32 devices in a mesh: atoms: 8 (over z, y), chan: 4 (over x, core).
Axes of the slice: x: 2, y: 2, z: 4, core: 2. Of those that a mesh axis runs over, the one named last changes fastest.
Arguments:
- positions: float32 [3, 4096], P(None, 'atoms'), may hold values from -2.5 to 2.5
- species: int32 [4096], P('atoms'), may hold values from 0 to 88
- neighbours: int32 [15, 4096], P(None, 'atoms'), may hold values from -1 to 4095, as said below
- labelled: int32 [4096], P('atoms'), may hold values from 0 to 1, as said below
- target_forces: float32 [3, 4096], P(None, 'atoms'), may hold values from -4 to 4
- embedding: float32 [89, 128], P(None, 'chan'), may hold values from -5 to 5
- bessel: float32 [2, 8, 64], replicated, may hold values from -2 to 2
- radial: float32 [2, 2, 64, 64], replicated, may hold values from -0.75 to 0.75
- filters: float32 [2, 4, 64, 128], P(None, None, None, 'chan'), may hold values from -0.75 to 0.75
- contract: float32 [2, 9, 128], P(None, None, 'chan'), may hold values from -2 to 2
- mixing: float32 [2, 128, 128], replicated, may hold values from -0.5 to 0.5
- readout: float32 [2, 16, 128], P(None, None, 'chan'), may hold values from -0.5 to 0.5
- energies: float32 [2, 16], replicated, may hold values from -1.5 to 1.5
- first_embedding: float32 [89, 128], P(None, 'chan'), may hold values from -1.9073486e-06 to 1.9073486e-06
- square_embedding: float32 [89, 128], P(None, 'chan'), may hold values from 7.5e-15 to 3e-14
- first_bessel: float32 [2, 8, 64], replicated, may hold values from -1.9073486e-06 to 1.9073486e-06
- square_bessel: float32 [2, 8, 64], replicated, may hold values from 7.5e-15 to 3e-14
- first_radial: float32 [2, 2, 64, 64], replicated, may hold values from -1.9073486e-06 to 1.9073486e-06
- square_radial: float32 [2, 2, 64, 64], replicated, may hold values from 7.5e-15 to 3e-14
- first_filters: float32 [2, 4, 64, 128], P(None, None, None, 'chan'), may hold values from -1.9073486e-06 to 1.9073486e-06
- square_filters: float32 [2, 4, 64, 128], P(None, None, None, 'chan'), may hold values from 7.5e-15 to 3e-14
- first_contract: float32 [2, 9, 128], P(None, None, 'chan'), may hold values from -1.9073486e-06 to 1.9073486e-06
- square_contract: float32 [2, 9, 128], P(None, None, 'chan'), may hold values from 7.5e-15 to 3e-14
- first_mixing: float32 [2, 128, 128], replicated, may hold values from -1.9073486e-06 to 1.9073486e-06
- square_mixing: float32 [2, 128, 128], replicated, may hold values from 7.5e-15 to 3e-14
- first_readout: float32 [2, 16, 128], P(None, None, 'chan'), may hold values from -1.9073486e-06 to 1.9073486e-06
- square_readout: float32 [2, 16, 128], P(None, None, 'chan'), may hold values from 7.5e-15 to 3e-14
- first_energies: float32 [2, 16], replicated, may hold values from -1.9073486e-06 to 1.9073486e-06
- square_energies: float32 [2, 16], replicated, may hold values from 7.5e-15 to 3e-14
Outputs:
- loss_parts: float32 [2], replicated
- forces: float32 [3, 4096], P(None, 'atoms')
- grad_norm: float32 [], replicated
- updated_embedding: float32 [89, 128], P(None, 'chan')
- moment_embedding: float32 [89, 128], P(None, 'chan')
- second_embedding: float32 [89, 128], P(None, 'chan')
- updated_bessel: float32 [2, 8, 64], replicated
- moment_bessel: float32 [2, 8, 64], replicated
- second_bessel: float32 [2, 8, 64], replicated
- updated_radial: float32 [2, 2, 64, 64], replicated
- moment_radial: float32 [2, 2, 64, 64], replicated
- second_radial: float32 [2, 2, 64, 64], replicated
- updated_filters: float32 [2, 4, 64, 128], P(None, None, None, 'chan')
- moment_filters: float32 [2, 4, 64, 128], P(None, None, None, 'chan')
- second_filters: float32 [2, 4, 64, 128], P(None, None, None, 'chan')
- updated_contract: float32 [2, 9, 128], P(None, None, 'chan')
- moment_contract: float32 [2, 9, 128], P(None, None, 'chan')
- second_contract: float32 [2, 9, 128], P(None, None, 'chan')
- updated_mixing: float32 [2, 128, 128], replicated
- moment_mixing: float32 [2, 128, 128], replicated
- second_mixing: float32 [2, 128, 128], replicated
- updated_readout: float32 [2, 16, 128], P(None, None, 'chan')
- moment_readout: float32 [2, 16, 128], P(None, None, 'chan')
- second_readout: float32 [2, 16, 128], P(None, None, 'chan')
- updated_energies: float32 [2, 16], replicated
- moment_energies: float32 [2, 16], replicated
- second_energies: float32 [2, 16], replicated
The draws below stay inside these ranges and needn't reach their ends.
Inputs may be any that keep to these rules, and one draw needn't show every extreme that they name: `neighbours`: molecules are runs of consecutive atoms of 1 to 16 atoms; each atom's slots list the other atoms of its molecule in increasing order, then -1. Every neighbour of an atom of a block lies within 8 atoms of that block. Atom 0 is always labelled.
All inputs are finite; a program needn't handle non-finite values.
Results may differ from the reference program's by a relative error of at most 0.0003.
Values sent between devices are 32-bit elements; how exact they have to be, the bound alone decides.
A program may use at most 320 MiB of HBM per device.

```python
import math
import jax
import jax.numpy as jnp
import numpy as np
from jax import lax

CHANNELS = 128
ELEMENTS = 89
NBESSEL = 8
RHIDDEN = 64
READ_UNITS = 16
LAYERS = 2
NBASIS = 9
SLOTS = 15
GHOST = 8
ADAM_STEP = 10
ATOM_DEV = 512
ATOMS = 4096


def draw_neighbours(key, part):
    key = jax.random.fold_in(key, 11)
    atom_index = jnp.arange(ATOMS, dtype=jnp.int32)
    phase = atom_index % 16
    inside = atom_index % ATOM_DEV
    coin = jax.random.randint(key, (ATOMS,), 0, 100)
    loose = (phase != 0) & (inside >= 9) & (inside < ATOM_DEV - 8)
    begins = (atom_index == 0) | (phase == 8) | loose & (coin < 35)
    first_atom = lax.cummax(jnp.where(begins, atom_index, 0), axis=0)
    next_begins = jnp.concatenate([begins[1:], jnp.ones((1,), dtype=bool)])
    closing = jnp.where(next_begins, atom_index, ATOMS - 1)
    last_atom = lax.cummin(closing, axis=0, reverse=True)
    slot = jnp.arange(SLOTS, dtype=jnp.int32)[:, None]
    shifted = (slot >= (atom_index - first_atom)[None, :]).astype(jnp.int32)
    target = first_atom[None, :] + slot + shifted
    return jnp.where(target <= last_atom[None, :], target, -1).astype(jnp.int32)


def draw_labelled(key, part):
    key = jax.random.fold_in(key, 23)
    atom_index = jnp.arange(ATOMS, dtype=jnp.int32)
    coin = jax.random.randint(key, (ATOMS,), 0, 1000)
    bound = 250 + 500 * atom_index // ATOMS
    return jnp.where((coin < bound) | (atom_index == 0), 1, 0).astype(jnp.int32)


def touch_ends(entries, key, least, largest):
    shape = entries.shape
    place = [jax.random.randint(jax.random.fold_in(key, axis), (), 0, shape[axis]) for axis in range(len(shape))]
    entries = entries.at[tuple(place)].set(least)
    longest = shape.index(max(shape))
    place[longest] = (place[longest] + 1) % shape[longest]
    return entries.at[tuple(place)].set(largest)


def steps_of(stream_key, extent, pieces, least, top_value):
    level = 1.0
    for axis_at, blocks in pieces:
        steps = jax.random.uniform(jax.random.fold_in(jax.random.fold_in(stream_key, 6), axis_at), (blocks,), jnp.float32, least / len(pieces), top_value / len(pieces))
        level = level * jnp.repeat(jnp.exp(steps), extent[axis_at] // blocks).reshape((-1,) + (1,) * (len(extent) - 1 - axis_at))
    return level


def rank_table(count, skew):
    portions = [(1 << 20) // math.isqrt(standing ** skew) + 1 for standing in range(1, count + 1)]
    scale = 1 + sum(portions) // (1 << 30)
    return np.cumsum(np.array([max(1, weight // scale) for weight in portions]))


def skewed_ids(stream_key, shape, number_of, lean):
    listing = rank_table(number_of, lean)
    pick = jax.random.randint(jax.random.fold_in(stream_key, 1), shape, 0, int(listing[number_of - 1]))
    standing = jnp.searchsorted(jnp.asarray(listing, jnp.int32), pick, side="right")
    return jax.random.permutation(jax.random.fold_in(stream_key, 2), number_of)[standing].astype(jnp.int32)


def gaussian(stream_key, dims, spread, reach, split=(), kind=jnp.bfloat16):
    array = spread * jax.random.normal(stream_key, dims, jnp.float32)
    if split:
        array = array * steps_of(stream_key, dims, split, -0.22, 0.18)
    return jnp.clip(array, -reach, reach).astype(kind)


def setup_inputs(seed: int = 0) -> dict:
    arg_keys = jax.random.split(jax.random.key(seed), 30)
    positions = jnp.clip(jax.random.uniform(arg_keys[0], (3, ATOMS), jnp.float32, -2.5, 2.5) * steps_of(arg_keys[0], (3, ATOMS), ((1, 8),), -0.4, 0.0), -2.5, 2.5)
    species = touch_ends(skewed_ids(arg_keys[1], (ATOMS,), ELEMENTS, 2), jax.random.fold_in(arg_keys[1], 3), 0, ELEMENTS - 1).astype(jnp.int32)
    neighbours = draw_neighbours(jax.random.fold_in(arg_keys[29], 71), 0)
    labelled = draw_labelled(jax.random.fold_in(arg_keys[29], 71), 0)
    target_forces = gaussian(arg_keys[4], (3, ATOMS), 1.0, 4.0, ((1, 8),), jnp.float32)
    embedding = gaussian(arg_keys[5], (ELEMENTS, CHANNELS), 1.0, 5.0, ((1, 4),), jnp.float32)
    bessel = gaussian(arg_keys[6], (LAYERS, NBESSEL, RHIDDEN), NBESSEL ** -0.5, 2.0, (), jnp.float32)
    radial = gaussian(arg_keys[7], (LAYERS, 2, RHIDDEN, RHIDDEN), RHIDDEN ** -0.5, 0.75, (), jnp.float32)
    filters = gaussian(arg_keys[8], (LAYERS, 4, RHIDDEN, CHANNELS), RHIDDEN ** -0.5, 0.75, ((3, 4),), jnp.float32)
    contract = gaussian(arg_keys[9], (LAYERS, NBASIS, CHANNELS), NBASIS ** -0.5, 2.0, ((2, 4),), jnp.float32)
    mixing = gaussian(arg_keys[10], (LAYERS, CHANNELS, CHANNELS), CHANNELS ** -0.5, 0.5, (), jnp.float32)
    readout = gaussian(arg_keys[11], (LAYERS, READ_UNITS, CHANNELS), CHANNELS ** -0.5, 0.5, ((2, 4),), jnp.float32)
    energies = gaussian(arg_keys[12], (LAYERS, READ_UNITS), READ_UNITS ** -0.5, 1.5, (), jnp.float32)
    first_embedding = gaussian(arg_keys[13], (ELEMENTS, CHANNELS), (3e-7), 1.9073486328125e-06, ((1, 4),), jnp.float32)
    square_embedding = jnp.clip(jnp.exp(math.log(2.99999994735501e-14) - 1.3862944 * jax.random.uniform(arg_keys[14], (ELEMENTS, CHANNELS), jnp.float32) ** steps_of(arg_keys[14], (ELEMENTS, CHANNELS), ((1, 4),), -0.2, 0.2)), 7.499999868387525e-15, 2.99999994735501e-14)
    first_bessel = gaussian(arg_keys[15], (LAYERS, NBESSEL, RHIDDEN), (3e-7), 1.9073486328125e-06, (), jnp.float32)
    square_bessel = jnp.clip(jnp.exp(jax.random.uniform(arg_keys[16], (LAYERS, NBESSEL, RHIDDEN), jnp.float32, math.log(7.499999868387525e-15), math.log(2.99999994735501e-14))), 7.499999868387525e-15, 2.99999994735501e-14)
    first_radial = gaussian(arg_keys[17], (LAYERS, 2, RHIDDEN, RHIDDEN), (3e-7), 1.9073486328125e-06, (), jnp.float32)
    square_radial = jnp.clip(jnp.exp(jax.random.uniform(arg_keys[18], (LAYERS, 2, RHIDDEN, RHIDDEN), jnp.float32, math.log(7.499999868387525e-15), math.log(2.99999994735501e-14))), 7.499999868387525e-15, 2.99999994735501e-14)
    first_filters = gaussian(arg_keys[19], (LAYERS, 4, RHIDDEN, CHANNELS), (3e-7), 1.9073486328125e-06, ((3, 4),), jnp.float32)
    square_filters = jnp.clip(jnp.exp(math.log(2.99999994735501e-14) - 1.3862944 * jax.random.uniform(arg_keys[20], (LAYERS, 4, RHIDDEN, CHANNELS), jnp.float32) ** steps_of(arg_keys[20], (LAYERS, 4, RHIDDEN, CHANNELS), ((3, 4),), -0.2, 0.2)), 7.499999868387525e-15, 2.99999994735501e-14)
    first_contract = gaussian(arg_keys[21], (LAYERS, NBASIS, CHANNELS), (3e-7), 1.9073486328125e-06, ((2, 4),), jnp.float32)
    square_contract = jnp.clip(jnp.exp(math.log(2.99999994735501e-14) - 1.3862944 * jax.random.uniform(arg_keys[22], (LAYERS, NBASIS, CHANNELS), jnp.float32) ** steps_of(arg_keys[22], (LAYERS, NBASIS, CHANNELS), ((2, 4),), -0.2, 0.2)), 7.499999868387525e-15, 2.99999994735501e-14)
    first_mixing = gaussian(arg_keys[23], (LAYERS, CHANNELS, CHANNELS), (3e-7), 1.9073486328125e-06, (), jnp.float32)
    square_mixing = jnp.clip(jnp.exp(jax.random.uniform(arg_keys[24], (LAYERS, CHANNELS, CHANNELS), jnp.float32, math.log(7.499999868387525e-15), math.log(2.99999994735501e-14))), 7.499999868387525e-15, 2.99999994735501e-14)
    first_readout = gaussian(arg_keys[25], (LAYERS, READ_UNITS, CHANNELS), (3e-7), 1.9073486328125e-06, ((2, 4),), jnp.float32)
    square_readout = jnp.clip(jnp.exp(math.log(2.99999994735501e-14) - 1.3862944 * jax.random.uniform(arg_keys[26], (LAYERS, READ_UNITS, CHANNELS), jnp.float32) ** steps_of(arg_keys[26], (LAYERS, READ_UNITS, CHANNELS), ((2, 4),), -0.2, 0.2)), 7.499999868387525e-15, 2.99999994735501e-14)
    first_energies = gaussian(arg_keys[27], (LAYERS, READ_UNITS), (3e-7), 1.9073486328125e-06, (), jnp.float32)
    square_energies = jnp.clip(jnp.exp(jax.random.uniform(arg_keys[28], (LAYERS, READ_UNITS), jnp.float32, math.log(7.499999868387525e-15), math.log(2.99999994735501e-14))), 7.499999868387525e-15, 2.99999994735501e-14)
    return dict(positions=positions, species=species, neighbours=neighbours, labelled=labelled, target_forces=target_forces, embedding=embedding, bessel=bessel, radial=radial, filters=filters, contract=contract, mixing=mixing, readout=readout, energies=energies, first_embedding=first_embedding, square_embedding=square_embedding, first_bessel=first_bessel, square_bessel=square_bessel, first_radial=first_radial, square_radial=square_radial, first_filters=first_filters, square_filters=square_filters, first_contract=first_contract, square_contract=square_contract, first_mixing=first_mixing, square_mixing=square_mixing, first_readout=first_readout, square_readout=square_readout, first_energies=first_energies, square_energies=square_energies)


@jax.custom_vjp
def low(v):
    return lax.optimization_barrier(v.astype(jnp.bfloat16)).astype(jnp.float32)

@jax.custom_vjp
def low_back(v):
    return v

def low_keep(v):
    return (low(v), None)

def low_pass(kept, grad):
    return (grad,)

def back_keep(v):
    return (v, None)

def back_low(kept, grad):
    return (low(grad),)
low.defvjp(low_keep, low_pass)
low_back.defvjp(back_keep, back_low)
HIGH = lax.Precision.HIGHEST
RCUT = 5.0
SMOOTH = 0.01
NEIGHBOURS_MEAN = 8.0
HUBER_DELTA = 1.0
CLIP_NORM = 0.001
RATE = 0.2
BETA_ONE = 0.9
BETA_TWO = 0.999
EPSILON = 1e-08
DECAY = 0.01

def harmonics(offset):
    along_x, along_y, along_z = (offset[0], offset[1], offset[2])
    radius_sq = along_x * along_x + along_y * along_y + along_z * along_z
    root_three = math.sqrt(3.0)
    parts = [jnp.ones_like(along_x), along_x, along_y, along_z, root_three * along_x * along_y, root_three * along_y * along_z, 0.5 * (3.0 * along_z * along_z - radius_sq), root_three * along_z * along_x, 0.5 * root_three * (along_x * along_x - along_y * along_y), math.sqrt(5.0 / 8.0) * along_y * (3.0 * along_x * along_x - along_y * along_y), math.sqrt(15.0) * along_x * along_y * along_z, math.sqrt(3.0 / 8.0) * along_y * (5.0 * along_z * along_z - radius_sq), 0.5 * along_z * (5.0 * along_z * along_z - 3.0 * radius_sq), math.sqrt(3.0 / 8.0) * along_x * (5.0 * along_z * along_z - radius_sq), 0.5 * math.sqrt(15.0) * along_z * (along_x * along_x - along_y * along_y), math.sqrt(5.0 / 8.0) * along_x * (along_x * along_x - 3.0 * along_y * along_y)]
    return jnp.stack(parts)

def radial_message(halo_feat, halo_pos, columns, valid_edge, bessel_weight, radial_weight, filter_weight, contract_weight):
    count_atoms = columns.shape[1]
    centre = halo_pos[:, GHOST:GHOST + count_atoms]
    offset = jnp.take(halo_pos, columns, axis=1) - centre[:, None, :]
    distance = jnp.sqrt(lax.optimization_barrier(jnp.sum(offset * offset, axis=0)) + SMOOTH)
    scaled = distance / RCUT
    orders = jnp.arange(1, NBESSEL + 1).astype(distance.dtype)
    bessel_basis = math.sqrt(2.0 / RCUT) * jnp.sin(math.pi * orders[:, None, None] * scaled[None]) / distance[None]
    envelope = 1.0 - 21.0 * scaled ** 5 + 35.0 * scaled ** 6 - 15.0 * scaled ** 7
    envelope = jnp.where(scaled < 1.0, envelope, 0.0) * valid_edge
    hidden = jax.nn.silu(jnp.einsum('nh,nka->hka', bessel_weight, bessel_basis, precision=HIGH))
    hidden = jax.nn.silu(jnp.einsum('gh,gka->hka', radial_weight[0], hidden, precision=HIGH))
    hidden = jax.nn.silu(jnp.einsum('gh,gka->hka', radial_weight[1], hidden, precision=HIGH))
    carried = jnp.take(halo_feat, columns, axis=1) * envelope[None]
    shapes = harmonics(offset / RCUT)
    blocks = []
    for degree in range(4):
        weighted = jnp.einsum('gc,gka->cka', filter_weight[degree], hidden, precision=HIGH) * carried
        section = shapes[degree * degree:(degree + 1) * (degree + 1)]
        blocks.append(jnp.einsum('cka,mka->mca', weighted, section, precision=HIGH) / NEIGHBOURS_MEAN)
    scalar = blocks[0][0]
    powers = [lax.optimization_barrier(jnp.sum(blocks[degree] * blocks[degree], axis=0)) for degree in (1, 2, 3)]
    products = jnp.stack([scalar, scalar * scalar] + powers + [scalar * scalar * scalar] + [scalar * squared for squared in powers])
    return jnp.einsum('kc,kca->ca', contract_weight, products, precision=HIGH)

def adamw(weight, gradient, first, second, scale):
    clipped = gradient * scale
    moment = BETA_ONE * first + (1.0 - BETA_ONE) * clipped
    second_new = BETA_TWO * second + (1.0 - BETA_TWO) * clipped * clipped
    corrected_first = moment / (1.0 - BETA_ONE ** ADAM_STEP)
    corrected_second = second_new / (1.0 - BETA_TWO ** ADAM_STEP)
    updated = weight - RATE * (corrected_first / (jnp.sqrt(corrected_second) + EPSILON) + DECAY * weight)
    return (updated, moment, second_new)

def reference(positions, species, neighbours, labelled, target_forces, embedding, bessel, radial, filters, contract, mixing, readout, energies, first_embedding, square_embedding, first_bessel, square_bessel, first_radial, square_radial, first_filters, square_filters, first_contract, square_contract, first_mixing, square_mixing, first_readout, square_readout, first_energies, square_energies):
    blocks_count = ATOMS // ATOM_DEV
    atom_index = jnp.arange(ATOMS).astype(jnp.int32)
    block_base = atom_index // ATOM_DEV * ATOM_DEV
    valid_bool = neighbours >= 0
    columns = jnp.where(valid_bool, neighbours - block_base[None, :] + GHOST, 0).astype(jnp.int32)
    valid_edge = valid_bool.astype(positions.dtype)
    column_blocks = columns.reshape(SLOTS, blocks_count, ATOM_DEV).transpose(1, 0, 2)
    valid_blocks = valid_edge.reshape(SLOTS, blocks_count, ATOM_DEV).transpose(1, 0, 2)
    block_ids = jnp.arange(blocks_count).astype(jnp.int32)
    one_hot = (species[None, :] == jnp.arange(ELEMENTS).astype(jnp.int32)[:, None]).astype(positions.dtype)
    labelled_float = labelled.astype(positions.dtype)
    label_total = jnp.sum(labelled_float)

    def energy_total(weights, coords):
        table, bessel_w, radial_w, filter_w, contract_w, mixing_w, readout_w, energies_w = weights
        features = jnp.dot(table.T, one_hot, precision=HIGH)
        padded_pos = jnp.pad(coords, ((0, 0), (GHOST, GHOST)))
        total = jnp.zeros((), coords.dtype)
        for layer_index in range(LAYERS):
            padded = jnp.pad(features, ((0, 0), (GHOST, GHOST)))
            inner = (bessel_w[layer_index], radial_w[layer_index], filter_w[layer_index], contract_w[layer_index])

            def one_block(inputs):
                block_id, block_cols, block_valid = inputs
                start = (block_id * ATOM_DEV).astype(jnp.int32)
                halo_feat = lax.dynamic_slice_in_dim(padded, start, ATOM_DEV + 2 * GHOST, 1)
                halo_pos = lax.dynamic_slice_in_dim(padded_pos, start, ATOM_DEV + 2 * GHOST, 1)
                return radial_message(halo_feat, halo_pos, block_cols, block_valid, *inner)
            message = lax.map(jax.checkpoint(one_block), (block_ids, column_blocks, valid_blocks))
            message = message.transpose(1, 0, 2).reshape(CHANNELS, ATOMS)
            features = features + jnp.dot(mixing_w[layer_index], message, precision=HIGH)
            summed = jnp.dot(readout_w[layer_index], features, precision=HIGH)
            total = total + jnp.sum(energies_w[layer_index][:, None] * jax.nn.silu(summed))
        return total

    def force_loss(weights):
        primal, pullback = jax.vjp(lambda coords: energy_total(weights, coords), positions)
        forces = -pullback(jnp.ones_like(primal))[0]
        diff = forces - target_forces
        magnitude = jnp.abs(diff)
        huber = jnp.where(magnitude <= HUBER_DELTA, 0.5 * diff * diff, HUBER_DELTA * (magnitude - 0.5 * HUBER_DELTA))
        loss_sum = jnp.sum(labelled_float[None, :] * huber)
        return (loss_sum / label_total, (loss_sum, forces))
    weights = (embedding, bessel, radial, filters, contract, mixing, readout, energies)
    loss_value, pullback, auxiliary = jax.vjp(force_loss, weights, has_aux=True)
    gradients = pullback(jnp.ones_like(loss_value))[0]
    loss_sum, forces = auxiliary
    grad_norm = jnp.sqrt(sum((jnp.sum(gradient * gradient) for gradient in gradients)))
    scale = jnp.minimum(1.0, CLIP_NORM / (grad_norm + 1e-06))
    firsts = (first_embedding, first_bessel, first_radial, first_filters, first_contract, first_mixing, first_readout, first_energies)
    squares = (square_embedding, square_bessel, square_radial, square_filters, square_contract, square_mixing, square_readout, square_energies)
    results = []
    for weight, gradient, first, second in zip(weights, gradients, firsts, squares):
        results.extend(adamw(weight, gradient, first, second, scale))
    return tuple([jnp.stack([loss_sum, label_total]), forces, grad_norm] + results)
```

```python
import functools
import math

import jax
import jax.numpy as jnp
from jax import lax
from jax.experimental import pallas as pl
from jax.experimental.pallas import tpu as pltpu
from jax.sharding import PartitionSpec as P

ELEMENTS = 89
NBESSEL = 8
GHOST = 8
ADAM_STEP = 10

RCUT = 5.0
SMOOTH = 0.01
NEIGHBOURS_MEAN = 8.0
HUBER_DELTA = 1.0
CLIP_NORM = 0.001
RATE = 0.2
BETA_ONE = 0.9
BETA_TWO = 0.999
EPSILON = 1e-08
DECAY = 0.01

UNIT = 64
WINDOW = UNIT + 16
PAD = 16
ROWS = WINDOW + 2 * PAD
LANES = 128
DIRECTED = 15
PAIRS = 8
FLAT = PAIRS * WINDOW
DEGREES = [0] + [1] * 3 + [2] * 5 + [3] * 7
ELEMENT_ROWS = 96
EXACT = lax.Precision.HIGHEST
FINE = lax.Precision.HIGHEST


def mm(left, right, left_dim, right_dim, precision=FINE):
    return lax.dot_general(
        left,
        right,
        (((left_dim,), (right_dim,)), ((), ())),
        precision=precision,
        preferred_element_type=jnp.float32,
    )


def geometry(rel_x, rel_y, rel_z, valid):
    distance = jnp.sqrt(rel_x * rel_x + rel_y * rel_y + rel_z * rel_z + SMOOTH)
    scaled = distance * (1.0 / RCUT)
    square = scaled * scaled
    fifth = square * square * scaled
    envelope = 1.0 - fifth * (21.0 - 35.0 * scaled + 15.0 * square)
    envelope = jnp.where(scaled < 1.0, envelope, 0.0) * (valid * (1.0 / NEIGHBOURS_MEAN))
    x, y, z = rel_x * (1.0 / RCUT), rel_y * (1.0 / RCUT), rel_z * (1.0 / RCUT)
    radius_sq = x * x + y * y + z * z
    root_three = math.sqrt(3.0)
    parts = [
        x,
        y,
        z,
        root_three * x * y,
        root_three * y * z,
        0.5 * (3.0 * z * z - radius_sq),
        root_three * z * x,
        0.5 * root_three * (x * x - y * y),
        math.sqrt(5.0 / 8.0) * y * (3.0 * x * x - y * y),
        math.sqrt(15.0) * x * y * z,
        math.sqrt(3.0 / 8.0) * y * (5.0 * z * z - radius_sq),
        0.5 * z * (5.0 * z * z - 3.0 * radius_sq),
        math.sqrt(3.0 / 8.0) * x * (5.0 * z * z - radius_sq),
        0.5 * math.sqrt(15.0) * z * (x * x - y * y),
        math.sqrt(5.0 / 8.0) * x * (x * x - 3.0 * y * y),
    ]
    return tuple([envelope] + [envelope * part for part in parts]), distance


def tiles(body):
    def step(index, carry):
        body(pl.multiple_of(index * 8, 8))
        return carry

    lax.fori_loop(0, WINDOW // 8, step, 0)


def step_kernel(
    win_ref,
    emb_ref,
    bes_ref,
    rad_ref,
    fil_ref,
    con_ref,
    mix_ref,
    read_ref,
    en_ref,
    force_ref,
    stat_ref,
    g_emb,
    g_bes,
    g_rad,
    g_fil,
    g_con,
    g_mix,
    g_read,
    g_en,
    ye,
    dye,
    ahead_mask,
    back_mask,
    featp,
    dfeatp,
    fj,
    dfj,
    fdir,
    dfdir,
    fpair,
    fbdir,
    fjb,
    wb,
    fbp,
    amat,
    damat,
    msg,
    msgb,
    dmsg,
    gsum,
    ycol,
    hid,
    hidb,
    hidt,
    bess,
    gcon,
):
    f32 = jnp.float32

    @pl.when(pl.program_id(0) == 0)
    def _():
        for ref in (g_emb, g_bes, g_rad, g_fil, g_con, g_mix, g_read, g_en, stat_ref):
            ref[...] = jnp.zeros_like(ref)
        featp[...] = jnp.zeros_like(featp)
        dfeatp[...] = jnp.zeros_like(dfeatp)
        for ref in (fpair, fbdir, fjb):
            for start in (0, PAD + WINDOW):
                ref[:, start : start + PAD, :] = jnp.zeros((ref.shape[0], PAD, LANES), f32)

    inner = pl.ds(PAD, WINDOW)

    def row(index):
        return win_ref[0, index : index + 1, :]

    def both_sides(value):
        wide = jnp.broadcast_to(value, (16, LANES))
        back = pltpu.roll(wide, 1, 1, stride=1, stride_axis=0)
        ahead = pltpu.roll(wide, 113, 1, stride=1, stride_axis=0)
        return back, ahead

    first, species, labelled = row(3), row(4), row(5)
    own = jnp.where((first >= 0.0) & (first < float(UNIT)), 1.0, 0.0)
    slot_row = lax.broadcasted_iota(jnp.int32, (16, LANES), 0)
    back_first, ahead_first = both_sides(first)
    may = (slot_row < DIRECTED) & (jnp.broadcast_to(own, (16, LANES)) > 0.0)
    is_back = may & (back_first == first)
    is_ahead = may & (ahead_first == first)
    back_f = jnp.where(is_back, 1.0, 0.0)
    ahead_f = jnp.where(is_ahead, 1.0, 0.0)
    valid = back_f + ahead_f

    def relative(value):
        back, ahead = both_sides(value)
        there = jnp.where(is_ahead, ahead, back)
        return jnp.where(valid > 0.0, there - value, 0.0)

    rel = [relative(row(i)) for i in range(3)]
    (shapes, distance), geometry_pull = jax.vjp(lambda a, b, c: geometry(a, b, c, valid), *rel)

    def spread(values, dest):
        ycol[...] = jnp.concatenate(values, axis=0).T

        def body(r):
            wide = ycol[pl.ds(r, 8), :]
            for slot in range(DIRECTED):
                for lm in range(16):
                    at = lm * 16 + slot
                    dest[slot * 16 + lm, pl.ds(r, 8), :] = jnp.broadcast_to(
                        wide[:, at : at + 1], (8, LANES)
                    )

        tiles(body)

    spread(shapes, ye)
    mask_cols = jnp.concatenate([ahead_f, back_f, jnp.zeros((96, LANES), f32)], axis=0).T
    for slot in range(DIRECTED):
        ahead_mask[slot] = jnp.broadcast_to(mask_cols[:WINDOW, slot : slot + 1], (WINDOW, LANES))
        back_mask[slot] = jnp.broadcast_to(
            mask_cols[:WINDOW, 16 + slot : 17 + slot], (WINDOW, LANES)
        )

    flat_lane = lax.broadcasted_iota(jnp.int32, (1, FLAT), 1)
    flat_slot = jnp.zeros((1, FLAT), jnp.int32)
    for slot in range(1, PAIRS):
        flat_slot = flat_slot + jnp.where(flat_lane >= slot * WINDOW, 1, 0)
    flat_atom = flat_lane - flat_slot * WINDOW
    take = jnp.where(
        lax.broadcasted_iota(jnp.int32, (LANES, FLAT), 0) == flat_atom, 1.0, 0.0
    ).astype(f32)
    slot_mask = lax.broadcasted_iota(jnp.int32, (PAIRS, FLAT), 0) == flat_slot

    def flatten(value):
        wide = mm(value, take, 1, 0, EXACT)
        return jnp.sum(jnp.where(slot_mask, wide, 0.0), axis=0, keepdims=True)

    def unflatten(value):
        wide = jnp.where(slot_mask, jnp.broadcast_to(value, (PAIRS, FLAT)), 0.0)
        return mm(wide, take, 1, 1, EXACT)

    flat_distance = flatten(distance[:PAIRS])
    order = (lax.broadcasted_iota(jnp.int32, (NBESSEL, FLAT), 0) + 1).astype(f32)
    omega = order * (math.pi / RCUT)
    angle = omega * flat_distance
    inverse = 1.0 / flat_distance
    root = math.sqrt(2.0 / RCUT)
    basis = root * jnp.sin(angle) * inverse
    bess[0] = basis
    bess[1] = (root * omega * jnp.cos(angle) - basis) * inverse

    def silu_parts(z):
        sig = 1.0 / (1.0 + jnp.exp(-z))
        h = z * sig
        slope = sig + h * (1.0 - sig)
        curve = sig * (1.0 - sig) * (2.0 + z * (1.0 - 2.0 * sig))
        return h, slope, curve

    def all_filters(t):
        return jnp.concatenate([fil_ref[t, degree] for degree in range(4)], axis=1)

    def network(t):
        value = bess[0]
        for depth in range(3):
            weight = bes_ref[t] if depth == 0 else rad_ref[t, depth - 1]
            z = mm(weight, value, 0, 0)
            value, slope, curve = silu_parts(z)
            hid[t, depth] = value
            hid[t, 3 + depth] = slope
            hid[t, 6 + depth] = curve

    def directed_filters(t, hidden, dest):
        flat = mm(hidden, all_filters(t), 0, 0)
        for slot in range(PAIRS):
            for degree in range(4):
                piece = flat[slot * WINDOW : (slot + 1) * WINDOW, degree * LANES : (degree + 1) * LANES]
                fpair[slot * 4 + degree, inner, :] = piece
                if slot < 7:
                    dest[t, slot * 4 + degree] = piece
        for slot in range(7, DIRECTED):
            ahead = ahead_mask[slot] > 0.0
            for degree in range(4):
                at = (14 - slot) * 4 + degree
                if slot == 7:
                    value = jnp.where(
                        ahead, fpair[at, pl.ds(PAD + 8, WINDOW), :], fpair[at, inner, :]
                    )
                else:
                    value = jnp.where(
                        ahead,
                        fpair[at, pl.ds(PAD + 15 - slot, WINDOW), :],
                        fpair[at, pl.ds(PAD - 1 - slot, WINDOW), :],
                    )
                dest[t, slot * 4 + degree] = value

    def gather(source, dest):
        for slot in range(DIRECTED):
            dest[slot] = jnp.where(
                ahead_mask[slot] > 0.0,
                source[pl.ds(PAD + 15 - slot, WINDOW), :],
                source[pl.ds(PAD - 1 - slot, WINDOW), :],
            )

    def scattered():
        total = None
        for slot in range(DIRECTED):
            term = (
                ahead_mask[slot] * fjb[14 - slot, pl.ds(PAD + 15 - slot, WINDOW), :]
                + back_mask[slot] * fjb[14 - slot, pl.ds(PAD - 1 - slot, WINDOW), :]
            )
            total = term if total is None else total + term
        return total

    def folded(slot, degree):
        here = fbdir[slot * 4 + degree, inner, :]
        if slot == 7:
            return back_mask[7] * (here + fbdir[28 + degree, pl.ds(PAD - 8, WINDOW), :])
        at = (14 - slot) * 4 + degree
        return (
            here
            + ahead_mask[slot] * fbdir[at, pl.ds(PAD + 15 - slot, WINDOW), :]
            + back_mask[slot] * fbdir[at, pl.ds(PAD - 1 - slot, WINDOW), :]
        )

    def all_folded():
        return jnp.concatenate(
            [
                jnp.concatenate([folded(slot, degree) for degree in range(4)], axis=1)
                for slot in range(PAIRS)
            ],
            axis=0,
        )

    def contract_rows(t):
        return [con_ref[t, b : b + 1, :] for b in range(9)]

    def powers_of(a):
        return [
            sum(a[lm] * a[lm] for lm in range(degree * degree, (degree + 1) ** 2))
            for degree in (1, 2, 3)
        ]

    def alpha_of(c, s, p):
        return (
            c[0] + 2.0 * c[1] * s + 3.0 * c[5] * s * s + c[6] * p[0] + c[7] * p[1] + c[8] * p[2]
        )

    def beta_of(c, s):
        return [c[2 + i] + c[6 + i] * s for i in range(3)]

    def forward_messages(t):
        def body(r):
            at = pl.ds(r, 8)
            a = [None] * 16
            for slot in range(DIRECTED):
                there = fj[t, slot, at, :]
                for degree in range(4):
                    w = fdir[t, slot * 4 + degree, at, :] * there
                    for lm in range(degree * degree, (degree + 1) ** 2):
                        term = ye[slot * 16 + lm, at, :] * w
                        a[lm] = term if a[lm] is None else a[lm] + term
            for lm in range(16):
                amat[t, lm, at, :] = a[lm]
            c = contract_rows(t)
            s, p = a[0], powers_of(a)
            value = s * (c[0] + s * (c[1] + s * c[5]) + c[6] * p[0] + c[7] * p[1] + c[8] * p[2])
            msg[t, at, :] = value + c[2] * p[0] + c[3] * p[1] + c[4] * p[2]

        tiles(body)

    def backward_messages(t, to_features):
        lane = lax.broadcasted_iota(jnp.int32, (8, LANES), 1)

        def body(r):
            at = pl.ds(r, 8)
            padded = pl.ds(pl.multiple_of(r + PAD, 8), 8)
            a = [amat[t, lm, at, :] for lm in range(16)]
            c = contract_rows(t)
            up = msgb[t, at, :]
            s, p = a[0], powers_of(a)
            beta = beta_of(c, s)
            twice = [None] + [2.0 * up * beta[i] for i in range(3)]
            ab = [up * alpha_of(c, s, p)] + [twice[DEGREES[lm]] * a[lm] for lm in range(1, 16)]
            halves = [jnp.zeros((8, LANES), f32)] * 2
            for slot in range(DIRECTED):
                there = fj[t, slot, at, :]
                back = None
                for degree in range(4):
                    weight = fdir[t, slot * 4 + degree, at, :]
                    w = weight * there
                    total = None
                    for lm in range(degree * degree, (degree + 1) ** 2):
                        term = ye[slot * 16 + lm, at, :] * ab[lm]
                        total = term if total is None else total + term
                        col = lm * 16 + slot
                        reduced = jnp.sum(w * ab[lm], axis=1, keepdims=True)
                        halves[col // LANES] = jnp.where(
                            lane == col % LANES, reduced, halves[col // LANES]
                        )
                    wb[t, slot * 4 + degree, at, :] = total
                    fbdir[slot * 4 + degree, padded, :] = total * there
                    if to_features:
                        back = total * weight if back is None else back + total * weight
                if to_features:
                    fjb[slot, padded, :] = back
            gsum[at, :LANES] += halves[0]
            gsum[at, LANES:] += halves[1]

        tiles(body)

    def tangent_messages(t, moving):
        def body(r):
            at = pl.ds(r, 8)
            da = [None] * 16
            for slot in range(DIRECTED):
                there = fj[t, slot, at, :]
                for degree in range(4):
                    weight = fdir[t, slot * 4 + degree, at, :]
                    w = weight * there
                    dw = dfdir[t, slot * 4 + degree, at, :] * there
                    if moving:
                        dw = dw + weight * dfj[slot, at, :]
                    for lm in range(degree * degree, (degree + 1) ** 2):
                        term = ye[slot * 16 + lm, at, :] * dw + dye[slot * 16 + lm, at, :] * w
                        da[lm] = term if da[lm] is None else da[lm] + term
            a = [amat[t, lm, at, :] for lm in range(16)]
            for lm in range(16):
                damat[t, lm, at, :] = da[lm]
            c = contract_rows(t)
            s, p = a[0], powers_of(a)
            beta = beta_of(c, s)
            value = alpha_of(c, s, p) * da[0]
            for i in range(3):
                degree = i + 1
                dp = 2.0 * sum(a[lm] * da[lm] for lm in range(degree * degree, (degree + 1) ** 2))
                value = value + beta[i] * dp
            dmsg[t, at, :] = value

        tiles(body)

    def tangent_backward(t, moving):
        gcon[...] = jnp.zeros_like(gcon)

        def body(r):
            at = pl.ds(r, 8)
            padded = pl.ds(pl.multiple_of(r + PAD, 8), 8)
            a = [amat[t, lm, at, :] for lm in range(16)]
            da = [damat[t, lm, at, :] for lm in range(16)]
            c = contract_rows(t)
            up, dup = msgb[t, at, :], dmsgb_of(at)
            s, ds, p = a[0], da[0], powers_of(a)
            dp = [
                2.0 * sum(a[lm] * da[lm] for lm in range(degree * degree, (degree + 1) ** 2))
                for degree in (1, 2, 3)
            ]
            alpha, beta = alpha_of(c, s, p), beta_of(c, s)
            dalpha = (
                2.0 * c[1] * ds
                + 6.0 * c[5] * s * ds
                + c[6] * dp[0]
                + c[7] * dp[1]
                + c[8] * dp[2]
            )
            pb = [None] + [2.0 * up * beta[i] for i in range(3)]
            dpb = [None] + [2.0 * (dup * beta[i] + up * c[6 + i] * ds) for i in range(3)]
            ab = [up * alpha] + [pb[DEGREES[lm]] * a[lm] for lm in range(1, 16)]
            dab = [dup * alpha + up * dalpha] + [
                pb[DEGREES[lm]] * da[lm] + dpb[DEGREES[lm]] * a[lm] for lm in range(1, 16)
            ]
            products = [(s, ds), (s * s, 2.0 * s * ds)]
            products += [(p[i], dp[i]) for i in range(3)]
            products += [(s * s * s, 3.0 * s * s * ds)]
            products += [(s * p[i], ds * p[i] + s * dp[i]) for i in range(3)]
            for b, (point, direction) in enumerate(products):
                gcon[b] += dup * point + up * direction
            for slot in range(DIRECTED):
                there = fj[t, slot, at, :]
                back = None
                for degree in range(4):
                    total = None
                    for lm in range(degree * degree, (degree + 1) ** 2):
                        term = ye[slot * 16 + lm, at, :] * dab[lm] + dye[slot * 16 + lm, at, :] * ab[lm]
                        total = term if total is None else total + term
                    was = wb[t, slot * 4 + degree, at, :]
                    value = total * there
                    if moving:
                        value = value + was * dfj[slot, at, :]
                    fbdir[slot * 4 + degree, padded, :] = value
                    term = (
                        total * fdir[t, slot * 4 + degree, at, :]
                        + was * dfdir[t, slot * 4 + degree, at, :]
                    )
                    back = term if back is None else back + term
                fjb[slot, padded, :] = back

        tiles(body)
        for b in range(9):
            g_con[t, b : b + 1, :] -= jnp.sum(gcon[b], axis=0, keepdims=True)

    def dmsgb_of(at):
        return msgb[2, at, :]

    hot = jnp.where(
        lax.broadcasted_iota(jnp.int32, (ELEMENT_ROWS, LANES), 0).astype(f32) == species, 1.0, 0.0
    )[:, :WINDOW]
    own_lane = own[:, :WINDOW]
    featp[0, inner, :] = mm(hot, emb_ref[...], 0, 0, EXACT)
    sums = []
    for t in range(2):
        network(t)
        directed_filters(t, hid[t, 2], fdir)
        gather(featp.at[t], fj.at[t])
        forward_messages(t)
        featp[t + 1, inner, :] = featp[t, inner, :] + mm(msg[t], mix_ref[t], 1, 1)
        sums.append(mm(read_ref[t], featp[t + 1, inner, :], 1, 1))

    gsum[...] = jnp.zeros_like(gsum)
    sum_bars, feat_bars = [], [None, None]
    flat_bar = None
    for t in range(2):
        _, slope, _ = silu_parts(sums[t])
        sum_bars.append(own_lane * en_ref[t] * slope)
    feat_bar = None
    for t in (1, 0):
        read_back = mm(sum_bars[t], read_ref[t], 0, 0)
        feat_bar = read_back if feat_bar is None else feat_bar + read_back
        feat_bars[t] = feat_bar
        msgb[t] = mm(feat_bar, mix_ref[t], 1, 0)
        backward_messages(t, t > 0)
        fbp[t] = all_folded()
        value = mm(all_filters(t), fbp[t], 1, 1)
        for depth in (2, 1, 0):
            hidb[t, depth] = value
            value = value * hid[t, 3 + depth]
            hidb[t, 3 + depth] = value
            weight = bes_ref[t] if depth == 0 else rad_ref[t, depth - 1]
            value = mm(weight, value, 1, 0)
        term = jnp.sum(value * bess[1], axis=0, keepdims=True)
        flat_bar = term if flat_bar is None else flat_bar + term
        if t > 0:
            feat_bar = feat_bar + scattered()

    turned = gsum[...].T
    shape_bars = tuple(turned[lm * 16 : lm * 16 + 16, :] for lm in range(16))
    distance_bar = jnp.concatenate([unflatten(flat_bar), jnp.zeros((8, LANES), f32)], axis=0)
    rel_bars = geometry_pull((shape_bars, distance_bar))
    flip = jnp.where(
        lax.broadcasted_iota(jnp.int32, (16, 16), 0) + lax.broadcasted_iota(jnp.int32, (16, 16), 1)
        == 14,
        1.0,
        0.0,
    ).astype(f32)
    slopes = []
    loss_row = jnp.zeros((1, LANES), f32)
    weight_row = own * labelled
    for i in range(3):
        bar = jnp.where(valid > 0.0, rel_bars[i], 0.0)
        reverse = mm(flip, bar, 1, 0, EXACT)
        back = pltpu.roll(reverse, 1, 1, stride=1, stride_axis=0)
        ahead = pltpu.roll(reverse, 113, 1, stride=1, stride_axis=0)
        arrived = jnp.where(is_ahead, ahead, jnp.where(is_back, back, 0.0))
        force = jnp.sum(bar - arrived, axis=0, keepdims=True)
        force_ref[0, i : i + 1, :] = force
        diff = force - row(8 + i)
        magnitude = jnp.abs(diff)
        huber = jnp.where(
            magnitude <= HUBER_DELTA,
            0.5 * diff * diff,
            HUBER_DELTA * (magnitude - 0.5 * HUBER_DELTA),
        )
        loss_row = loss_row + weight_row * huber
        slopes.append(weight_row * jnp.clip(diff, -HUBER_DELTA, HUBER_DELTA))
    force_ref[0, 3:8, :] = jnp.zeros((5, LANES), f32)
    stat_ref[0:1, :] += loss_row
    stat_ref[1:2, :] += weight_row

    drel = tuple(relative(value) for value in slopes)
    _, (dshapes, ddistance) = jax.jvp(
        lambda a, b, c: geometry(a, b, c, valid), tuple(rel), drel
    )
    spread(dshapes, dye)
    bess[2] = bess[1] * flatten(ddistance[:PAIRS])
    dsums = []
    dfeat = None
    for t in range(2):
        value = bess[2]
        for depth in range(3):
            weight = bes_ref[t] if depth == 0 else rad_ref[t, depth - 1]
            z = mm(weight, value, 0, 0)
            value = z * hid[t, 3 + depth]
            hidt[t, depth] = value
            hid[t, 6 + depth] = hid[t, 6 + depth] * z
        directed_filters(t, value, dfdir)
        if t > 0:
            dfeatp[inner, :] = dfeat
            gather(dfeatp, dfj)
        tangent_messages(t, t > 0)
        step = mm(dmsg[t], mix_ref[t], 1, 1)
        dfeat = step if dfeat is None else dfeat + step
        dsums.append((mm(read_ref[t], dfeat, 1, 1), dfeat))

    dfeat_bar = None
    for t in (1, 0):
        dsum, dfeat_after = dsums[t]
        act, slope, curve = silu_parts(sums[t])
        g_en[t] -= jnp.sum(own_lane * slope * dsum, axis=1, keepdims=True)
        dsum_bar = own_lane * en_ref[t] * curve * dsum
        g_read[t] -= mm(dsum_bar, featp[t + 1, inner, :], 1, 0) + mm(
            sum_bars[t], dfeat_after, 1, 0
        )
        read_back = mm(dsum_bar, read_ref[t], 0, 0)
        dfeat_bar = read_back if dfeat_bar is None else dfeat_bar + read_back
        g_mix[t] -= mm(dfeat_bar, msg[t], 0, 0) + mm(feat_bars[t], dmsg[t], 0, 0)
        msgb[2] = mm(dfeat_bar, mix_ref[t], 1, 0)
        tangent_backward(t, t > 0)
        dfbp = all_folded()
        g_fil[t] -= mm(hidt[t, 2], fbp[t], 1, 0) + mm(hid[t, 2], dfbp, 1, 0)
        value = mm(all_filters(t), dfbp, 1, 1)
        for depth in (2, 1, 0):
            value = value * hid[t, 3 + depth] + hidb[t, depth] * hid[t, 6 + depth]
            weight = bes_ref[t] if depth == 0 else rad_ref[t, depth - 1]
            before = bess[0] if depth == 0 else hid[t, depth - 1]
            dbefore = bess[2] if depth == 0 else hidt[t, depth - 1]
            grad = mm(dbefore, hidb[t, 3 + depth], 1, 1) + mm(before, value, 1, 1)
            if depth == 0:
                g_bes[t] -= grad
            else:
                g_rad[t, depth - 1] -= grad
                value = mm(weight, value, 1, 0)
        dfeat_bar = dfeat_bar + scattered()
    g_emb[...] -= mm(hot, dfeat_bar, 1, 0)


def local_step(windows, table, bessel, radial, filters, contract, mixing, readout, energies):
    units = windows.shape[0]
    f32 = jnp.float32
    vmem = pl.BlockSpec(memory_space=pltpu.VMEM)

    def scratch(*shape):
        return pltpu.VMEM(shape, f32)

    def out(*shape):
        return jax.ShapeDtypeStruct(shape, f32)

    return pl.pallas_call(
        step_kernel,
        grid=(units,),
        in_specs=[pl.BlockSpec((1, 16, LANES), lambda i: (i, 0, 0))] + [vmem] * 8,
        out_specs=[pl.BlockSpec((1, 8, LANES), lambda i: (i, 0, 0))] + [vmem] * 9,
        out_shape=[
            out(units, 8, LANES),
            out(8, LANES),
            out(ELEMENT_ROWS, LANES),
            out(2, NBESSEL, 64),
            out(2, 2, 64, 64),
            out(2, 64, 4 * LANES),
            out(2, 16, LANES),
            out(2, LANES, LANES),
            out(2, 16, LANES),
            out(2, 16, 1),
        ],
        scratch_shapes=[
            scratch(240, WINDOW, LANES),
            scratch(240, WINDOW, LANES),
            scratch(15, WINDOW, LANES),
            scratch(15, WINDOW, LANES),
            scratch(3, ROWS, LANES),
            scratch(ROWS, LANES),
            scratch(2, 15, WINDOW, LANES),
            scratch(15, WINDOW, LANES),
            scratch(2, 60, WINDOW, LANES),
            scratch(2, 60, WINDOW, LANES),
            scratch(32, ROWS, LANES),
            scratch(60, ROWS, LANES),
            scratch(15, ROWS, LANES),
            scratch(2, 60, WINDOW, LANES),
            scratch(2, FLAT, 4 * LANES),
            scratch(2, 16, WINDOW, LANES),
            scratch(2, 16, WINDOW, LANES),
            scratch(2, WINDOW, LANES),
            scratch(3, WINDOW, LANES),
            scratch(2, WINDOW, LANES),
            scratch(LANES, 2 * LANES),
            scratch(LANES, 2 * LANES),
            scratch(2, 9, 64, FLAT),
            scratch(2, 6, 64, FLAT),
            scratch(2, 3, 64, FLAT),
            scratch(3, NBESSEL, FLAT),
            scratch(9, 8, LANES),
        ],
        compiler_params=pltpu.CompilerParams(vmem_limit_bytes=62 * 1024 * 1024),
    )(windows, table, bessel, radial, filters, contract, mixing, readout, energies)


def adamw(weight, gradient, first, second, scale):
    clipped = gradient * scale
    moment = BETA_ONE * first + (1.0 - BETA_ONE) * clipped
    second_new = BETA_TWO * second + (1.0 - BETA_TWO) * clipped * clipped
    corrected_first = moment / (1.0 - BETA_ONE**ADAM_STEP)
    corrected_second = second_new / (1.0 - BETA_TWO**ADAM_STEP)
    updated = weight - RATE * (
        corrected_first / (jnp.sqrt(corrected_second) + EPSILON) + DECAY * weight
    )
    return (updated, moment, second_new)


def per_device(
    positions,
    species,
    neighbours,
    labelled,
    target_forces,
    embedding,
    bessel,
    radial,
    filters,
    contract,
    mixing,
    readout,
    energies,
    first_embedding,
    square_embedding,
    first_bessel,
    square_bessel,
    first_radial,
    square_radial,
    first_filters,
    square_filters,
    first_contract,
    square_contract,
    first_mixing,
    square_mixing,
    first_readout,
    square_readout,
    first_energies,
    square_energies,
):
    f32 = jnp.float32
    atom_count = positions.shape[1]
    local_chan = embedding.shape[1]
    blocks, groups = lax.axis_size("atoms"), lax.axis_size("chan")
    block, group = lax.axis_index("atoms"), lax.axis_index("chan")
    atom_base = block * atom_count
    share = atom_count // groups
    units = share // UNIT

    atom_index = atom_base + jnp.arange(atom_count, dtype=jnp.int32)
    leading = neighbours[0]
    first_atom = jnp.where((leading >= 0) & (leading < atom_index), leading, atom_index)
    packed = jnp.concatenate(
        [
            positions,
            (first_atom - atom_base).astype(f32)[None],
            species.astype(f32)[None],
            labelled.astype(f32)[None],
            jnp.zeros((2, atom_count), f32),
            target_forces,
            jnp.zeros((5, atom_count), f32),
        ],
        axis=0,
    )
    down = [(i + 1, i) for i in range(blocks - 1)]
    halo = lax.ppermute(packed[:, :GHOST], "atoms", down)
    halo_row = jnp.arange(16)[:, None] == 3
    halo = jnp.where(halo_row, jnp.where(block == blocks - 1, -1.0e6, halo + atom_count), halo)
    missing = jnp.where(jnp.arange(16)[:, None] == 3, -1.0e6, 0.0) * jnp.ones((1, LANES), f32)
    extended = jnp.concatenate([packed, halo, missing], axis=1)
    windows = []
    for unit in range(units):
        start = group * share + unit * UNIT
        window = lax.dynamic_slice(extended, (0, start), (16, WINDOW))
        shift = jnp.where(jnp.arange(16)[:, None] == 3, start.astype(f32), 0.0)
        window = window - shift
        windows.append(jnp.concatenate([window, missing[:, : LANES - WINDOW]], axis=1))
    windows = jnp.stack(windows)

    def whole(value):
        return lax.all_gather(value, "chan", axis=value.ndim - 1, tiled=True)

    table = jnp.concatenate(
        [whole(embedding), jnp.zeros((ELEMENT_ROWS - ELEMENTS, LANES), f32)], axis=0
    )
    force, stat, *grads = local_step(
        windows,
        table,
        bessel,
        radial,
        whole(filters),
        whole(contract),
        mixing,
        whole(readout),
        energies[:, :, None],
    )
    grad_embed, grad_bessel, grad_radial, grad_filters, grad_contract, grad_mixing = grads[:6]
    grad_readout, grad_vectors = grads[6:]
    grad_embed = grad_embed[:ELEMENTS]
    grad_filters = grad_filters.reshape(2, 64, 4, LANES).transpose(0, 2, 1, 3)
    grad_contract = grad_contract[:, :9]
    grad_vectors = grad_vectors[:, :, 0]

    canvas = jnp.zeros((3, atom_count + LANES), f32)
    for unit in range(units):
        start = group * share + unit * UNIT
        old = lax.dynamic_slice(canvas, (0, start), (3, WINDOW))
        canvas = lax.dynamic_update_slice(canvas, old + force[unit, :3, :WINDOW], (0, start))
    canvas = lax.psum(canvas, "chan")
    up = [(i, i + 1) for i in range(blocks - 1)]
    arrived = lax.ppermute(canvas[:, atom_count : atom_count + GHOST], "atoms", up)
    forces = canvas[:, :atom_count].at[:, :GHOST].add(arrived)

    def split(value):
        return lax.psum_scatter(value, "chan", scatter_dimension=value.ndim - 1, tiled=True)

    grad_embed, grad_filters, grad_contract, grad_readout = lax.psum(
        (split(grad_embed), split(grad_filters), split(grad_contract), split(grad_readout)),
        "atoms",
    )
    grad_bessel, grad_radial, grad_mixing, grad_vectors, loss_sum, label_total = lax.psum(
        (grad_bessel, grad_radial, grad_mixing, grad_vectors, jnp.sum(stat[0]), jnp.sum(stat[1])),
        ("atoms", "chan"),
    )
    gradients = [
        gradient / label_total
        for gradient in (
            grad_embed,
            grad_bessel,
            grad_radial,
            grad_filters,
            grad_contract,
            grad_mixing,
            grad_readout,
            grad_vectors,
        )
    ]
    squares_of = [jnp.sum(gradient * gradient) for gradient in gradients]
    split_squares = squares_of[0] + squares_of[3] + squares_of[4] + squares_of[6]
    whole_squares = squares_of[1] + squares_of[2] + squares_of[5] + squares_of[7]
    grad_norm = jnp.sqrt(lax.psum(split_squares, "chan") + whole_squares)
    scale = jnp.minimum(1.0, CLIP_NORM / (grad_norm + 1e-06))
    weights = (embedding, bessel, radial, filters, contract, mixing, readout, energies)
    firsts = (
        first_embedding,
        first_bessel,
        first_radial,
        first_filters,
        first_contract,
        first_mixing,
        first_readout,
        first_energies,
    )
    squares = (
        square_embedding,
        square_bessel,
        square_radial,
        square_filters,
        square_contract,
        square_mixing,
        square_readout,
        square_energies,
    )
    results = []
    for weight, gradient, first, second in zip(weights, gradients, firsts, squares):
        results.extend(adamw(weight, gradient, first, second, scale))
    return tuple([jnp.stack([loss_sum, label_total]), forces, grad_norm] + results)


def solution(mesh):
    whole = P()
    columns = P(None, "atoms")
    by_weight = [
        P(None, "chan"),
        whole,
        whole,
        P(None, None, None, "chan"),
        P(None, None, "chan"),
        whole,
        P(None, None, "chan"),
        whole,
    ]
    in_specs = [columns, P("atoms"), columns, P("atoms"), columns] + by_weight
    in_specs += [spec for spec in by_weight for _ in range(2)]
    out_specs = [whole, columns, whole] + [spec for spec in by_weight for _ in range(3)]
    return jax.shard_map(
        per_device,
        mesh=mesh,
        in_specs=tuple(in_specs),
        out_specs=tuple(out_specs),
        check_vma=False,
    )
```

```python
import functools
import math

import jax
import jax.numpy as jnp
from jax import lax
from jax.experimental import pallas as pl
from jax.experimental.pallas import tpu as pltpu
from jax.sharding import PartitionSpec as P

ELEMENTS = 89
NBESSEL = 8
GHOST = 8
ADAM_STEP = 10

RCUT = 5.0
SMOOTH = 0.01
NEIGHBOURS_MEAN = 8.0
HUBER_DELTA = 1.0
CLIP_NORM = 0.001
RATE = 0.2
BETA_ONE = 0.9
BETA_TWO = 0.999
EPSILON = 1e-08
DECAY = 0.01

UNIT = 64
WINDOW = UNIT + 16
PAD = 16
ROWS = WINDOW + 2 * PAD
LANES = 128
DIRECTED = 15
PAIRS = 8
FLAT = PAIRS * WINDOW
DEGREES = [0] + [1] * 3 + [2] * 5 + [3] * 7
ELEMENT_ROWS = 96
EXACT = lax.Precision.HIGHEST
FINE = lax.Precision.HIGHEST


def mm(left, right, left_dim, right_dim, precision=FINE):
    return lax.dot_general(
        left,
        right,
        (((left_dim,), (right_dim,)), ((), ())),
        precision=precision,
        preferred_element_type=jnp.float32,
    )


def geometry(rel_x, rel_y, rel_z, valid):
    distance = jnp.sqrt(rel_x * rel_x + rel_y * rel_y + rel_z * rel_z + SMOOTH)
    scaled = distance * (1.0 / RCUT)
    square = scaled * scaled
    fifth = square * square * scaled
    envelope = 1.0 - fifth * (21.0 - 35.0 * scaled + 15.0 * square)
    envelope = jnp.where(scaled < 1.0, envelope, 0.0) * (valid * (1.0 / NEIGHBOURS_MEAN))
    x, y, z = rel_x * (1.0 / RCUT), rel_y * (1.0 / RCUT), rel_z * (1.0 / RCUT)
    radius_sq = x * x + y * y + z * z
    root_three = math.sqrt(3.0)
    parts = [
        x,
        y,
        z,
        root_three * x * y,
        root_three * y * z,
        0.5 * (3.0 * z * z - radius_sq),
        root_three * z * x,
        0.5 * root_three * (x * x - y * y),
        math.sqrt(5.0 / 8.0) * y * (3.0 * x * x - y * y),
        math.sqrt(15.0) * x * y * z,
        math.sqrt(3.0 / 8.0) * y * (5.0 * z * z - radius_sq),
        0.5 * z * (5.0 * z * z - 3.0 * radius_sq),
        math.sqrt(3.0 / 8.0) * x * (5.0 * z * z - radius_sq),
        0.5 * math.sqrt(15.0) * z * (x * x - y * y),
        math.sqrt(5.0 / 8.0) * x * (x * x - 3.0 * y * y),
    ]
    return tuple([envelope] + [envelope * part for part in parts]), distance


def tiles(body):
    def step(index, carry):
        body(pl.multiple_of(index * 8, 8))
        return carry

    lax.fori_loop(0, WINDOW // 8, step, 0)


def step_kernel(
    win_ref,
    emb_ref,
    bes_ref,
    rad_ref,
    fil_ref,
    con_ref,
    mix_ref,
    read_ref,
    en_ref,
    force_ref,
    stat_ref,
    g_emb,
    g_bes,
    g_rad,
    g_fil,
    g_con,
    g_mix,
    g_read,
    g_en,
    ye,
    dye,
    ahead_mask,
    back_mask,
    featp,
    dfeatp,
    fj,
    dfj,
    fdir,
    dfdir,
    fpair,
    fbdir,
    fjb,
    wb,
    fbp,
    amat,
    damat,
    msg,
    msgb,
    dmsg,
    gsum,
    ycol,
    hid,
    hidb,
    hidt,
    bess,
    gcon,
):
    f32 = jnp.float32

    @pl.when(pl.program_id(0) == 0)
    def _():
        for ref in (g_emb, g_bes, g_rad, g_fil, g_con, g_mix, g_read, g_en, stat_ref):
            ref[...] = jnp.zeros_like(ref)
        featp[...] = jnp.zeros_like(featp)
        dfeatp[...] = jnp.zeros_like(dfeatp)
        for ref in (fpair, fbdir, fjb):
            for start in (0, PAD + WINDOW):
                ref[:, start : start + PAD, :] = jnp.zeros((ref.shape[0], PAD, LANES), f32)

    inner = pl.ds(PAD, WINDOW)

    def row(index):
        return win_ref[0, index : index + 1, :]

    def both_sides(value):
        wide = jnp.broadcast_to(value, (16, LANES))
        back = pltpu.roll(wide, 1, 1, stride=1, stride_axis=0)
        ahead = pltpu.roll(wide, 113, 1, stride=1, stride_axis=0)
        return back, ahead

    first, species, labelled = row(3), row(4), row(5)
    own = jnp.where((first >= 0.0) & (first < float(UNIT)), 1.0, 0.0)
    slot_row = lax.broadcasted_iota(jnp.int32, (16, LANES), 0)
    back_first, ahead_first = both_sides(first)
    may = (slot_row < DIRECTED) & (jnp.broadcast_to(own, (16, LANES)) > 0.0)
    is_back = may & (back_first == first)
    is_ahead = may & (ahead_first == first)
    back_f = jnp.where(is_back, 1.0, 0.0)
    ahead_f = jnp.where(is_ahead, 1.0, 0.0)
    valid = back_f + ahead_f

    def relative(value):
        back, ahead = both_sides(value)
        there = jnp.where(is_ahead, ahead, back)
        return jnp.where(valid > 0.0, there - value, 0.0)

    rel = [relative(row(i)) for i in range(3)]
    (shapes, distance), geometry_pull = jax.vjp(lambda a, b, c: geometry(a, b, c, valid), *rel)

    def spread(values, dest):
        ycol[...] = jnp.concatenate(values, axis=0).T

        def body(r):
            wide = ycol[pl.ds(r, 8), :]
            for slot in range(DIRECTED):
                for lm in range(16):
                    at = lm * 16 + slot
                    dest[slot * 16 + lm, pl.ds(r, 8), :] = jnp.broadcast_to(
                        wide[:, at : at + 1], (8, LANES)
                    )

        tiles(body)

    spread(shapes, ye)
    mask_cols = jnp.concatenate([ahead_f, back_f, jnp.zeros((96, LANES), f32)], axis=0).T
    for slot in range(DIRECTED):
        ahead_mask[slot] = jnp.broadcast_to(mask_cols[:WINDOW, slot : slot + 1], (WINDOW, LANES))
        back_mask[slot] = jnp.broadcast_to(
            mask_cols[:WINDOW, 16 + slot : 17 + slot], (WINDOW, LANES)
        )

    flat_lane = lax.broadcasted_iota(jnp.int32, (1, FLAT), 1)
    flat_slot = jnp.zeros((1, FLAT), jnp.int32)
    for slot in range(1, PAIRS):
        flat_slot = flat_slot + jnp.where(flat_lane >= slot * WINDOW, 1, 0)
    flat_atom = flat_lane - flat_slot * WINDOW
    take = jnp.where(
        lax.broadcasted_iota(jnp.int32, (LANES, FLAT), 0) == flat_atom, 1.0, 0.0
    ).astype(f32)
    slot_mask = lax.broadcasted_iota(jnp.int32, (PAIRS, FLAT), 0) == flat_slot

    def flatten(value):
        wide = mm(value, take, 1, 0, EXACT)
        return jnp.sum(jnp.where(slot_mask, wide, 0.0), axis=0, keepdims=True)

    def unflatten(value):
        wide = jnp.where(slot_mask, jnp.broadcast_to(value, (PAIRS, FLAT)), 0.0)
        return mm(wide, take, 1, 1, EXACT)

    flat_distance = flatten(distance[:PAIRS])
    order = (lax.broadcasted_iota(jnp.int32, (NBESSEL, FLAT), 0) + 1).astype(f32)
    omega = order * (math.pi / RCUT)
    angle = omega * flat_distance
    inverse = 1.0 / flat_distance
    root = math.sqrt(2.0 / RCUT)
    basis = root * jnp.sin(angle) * inverse
    bess[0] = basis
    bess[1] = (root * omega * jnp.cos(angle) - basis) * inverse

    def silu_parts(z):
        sig = 1.0 / (1.0 + jnp.exp(-z))
        h = z * sig
        slope = sig + h * (1.0 - sig)
        curve = sig * (1.0 - sig) * (2.0 + z * (1.0 - 2.0 * sig))
        return h, slope, curve

    def all_filters(t):
        return jnp.concatenate([fil_ref[t, degree] for degree in range(4)], axis=1)

    def network(t):
        value = bess[0]
        for depth in range(3):
            weight = bes_ref[t] if depth == 0 else rad_ref[t, depth - 1]
            z = mm(weight, value, 0, 0)
            value, slope, curve = silu_parts(z)
            hid[t, depth] = value
            hid[t, 3 + depth] = slope
            hid[t, 6 + depth] = curve

    def directed_filters(t, hidden, dest):
        flat = mm(hidden, all_filters(t), 0, 0)
        for slot in range(PAIRS):
            for degree in range(4):
                piece = flat[slot * WINDOW : (slot + 1) * WINDOW, degree * LANES : (degree + 1) * LANES]
                fpair[slot * 4 + degree, inner, :] = piece
                if slot < 7:
                    dest[t, slot * 4 + degree] = piece
        for slot in range(7, DIRECTED):
            ahead = ahead_mask[slot] > 0.0
            for degree in range(4):
                at = (14 - slot) * 4 + degree
                if slot == 7:
                    value = jnp.where(
                        ahead, fpair[at, pl.ds(PAD + 8, WINDOW), :], fpair[at, inner, :]
                    )
                else:
                    value = jnp.where(
                        ahead,
                        fpair[at, pl.ds(PAD + 15 - slot, WINDOW), :],
                        fpair[at, pl.ds(PAD - 1 - slot, WINDOW), :],
                    )
                dest[t, slot * 4 + degree] = value

    def gather(source, dest):
        for slot in range(DIRECTED):
            dest[slot] = jnp.where(
                ahead_mask[slot] > 0.0,
                source[pl.ds(PAD + 15 - slot, WINDOW), :],
                source[pl.ds(PAD - 1 - slot, WINDOW), :],
            )

    def scattered():
        total = None
        for slot in range(DIRECTED):
            term = (
                ahead_mask[slot] * fjb[14 - slot, pl.ds(PAD + 15 - slot, WINDOW), :]
                + back_mask[slot] * fjb[14 - slot, pl.ds(PAD - 1 - slot, WINDOW), :]
            )
            total = term if total is None else total + term
        return total

    def folded(slot, degree):
        here = fbdir[slot * 4 + degree, inner, :]
        if slot == 7:
            return back_mask[7] * (here + fbdir[28 + degree, pl.ds(PAD - 8, WINDOW), :])
        at = (14 - slot) * 4 + degree
        return (
            here
            + ahead_mask[slot] * fbdir[at, pl.ds(PAD + 15 - slot, WINDOW), :]
            + back_mask[slot] * fbdir[at, pl.ds(PAD - 1 - slot, WINDOW), :]
        )

    def all_folded():
        return jnp.concatenate(
            [
                jnp.concatenate([folded(slot, degree) for degree in range(4)], axis=1)
                for slot in range(PAIRS)
            ],
            axis=0,
        )

    def contract_rows(t):
        return [con_ref[t, b : b + 1, :] for b in range(9)]

    def powers_of(a):
        return [
            sum(a[lm] * a[lm] for lm in range(degree * degree, (degree + 1) ** 2))
            for degree in (1, 2, 3)
        ]

    def alpha_of(c, s, p):
        return (
            c[0] + 2.0 * c[1] * s + 3.0 * c[5] * s * s + c[6] * p[0] + c[7] * p[1] + c[8] * p[2]
        )

    def beta_of(c, s):
        return [c[2 + i] + c[6 + i] * s for i in range(3)]

    def forward_messages(t):
        def body(r):
            at = pl.ds(r, 8)
            a = [None] * 16
            for slot in range(DIRECTED):
                there = fj[t, slot, at, :]
                for degree in range(4):
                    w = fdir[t, slot * 4 + degree, at, :] * there
                    for lm in range(degree * degree, (degree + 1) ** 2):
                        term = ye[slot * 16 + lm, at, :] * w
                        a[lm] = term if a[lm] is None else a[lm] + term
            for lm in range(16):
                amat[t, lm, at, :] = a[lm]
            c = contract_rows(t)
            s, p = a[0], powers_of(a)
            value = s * (c[0] + s * (c[1] + s * c[5]) + c[6] * p[0] + c[7] * p[1] + c[8] * p[2])
            msg[t, at, :] = value + c[2] * p[0] + c[3] * p[1] + c[4] * p[2]

        tiles(body)

    def backward_messages(t, to_features):
        lane = lax.broadcasted_iota(jnp.int32, (8, LANES), 1)

        def body(r):
            at = pl.ds(r, 8)
            padded = pl.ds(pl.multiple_of(r + PAD, 8), 8)
            a = [amat[t, lm, at, :] for lm in range(16)]
            c = contract_rows(t)
            up = msgb[t, at, :]
            s, p = a[0], powers_of(a)
            beta = beta_of(c, s)
            twice = [None] + [2.0 * up * beta[i] for i in range(3)]
            ab = [up * alpha_of(c, s, p)] + [twice[DEGREES[lm]] * a[lm] for lm in range(1, 16)]
            halves = [jnp.zeros((8, LANES), f32)] * 2
            for slot in range(DIRECTED):
                there = fj[t, slot, at, :]
                back = None
                for degree in range(4):
                    weight = fdir[t, slot * 4 + degree, at, :]
                    w = weight * there
                    total = None
                    for lm in range(degree * degree, (degree + 1) ** 2):
                        term = ye[slot * 16 + lm, at, :] * ab[lm]
                        total = term if total is None else total + term
                        col = lm * 16 + slot
                        reduced = jnp.sum(w * ab[lm], axis=1, keepdims=True)
                        halves[col // LANES] = jnp.where(
                            lane == col % LANES, reduced, halves[col // LANES]
                        )
                    wb[t, slot * 4 + degree, at, :] = total
                    fbdir[slot * 4 + degree, padded, :] = total * there
                    if to_features:
                        back = total * weight if back is None else back + total * weight
                if to_features:
                    fjb[slot, padded, :] = back
            gsum[at, :LANES] += halves[0]
            gsum[at, LANES:] += halves[1]

        tiles(body)

    def tangent_messages(t, moving):
        def body(r):
            at = pl.ds(r, 8)
            da = [None] * 16
            for slot in range(DIRECTED):
                there = fj[t, slot, at, :]
                for degree in range(4):
                    weight = fdir[t, slot * 4 + degree, at, :]
                    w = weight * there
                    dw = dfdir[t, slot * 4 + degree, at, :] * there
                    if moving:
                        dw = dw + weight * dfj[slot, at, :]
                    for lm in range(degree * degree, (degree + 1) ** 2):
                        term = ye[slot * 16 + lm, at, :] * dw + dye[slot * 16 + lm, at, :] * w
                        da[lm] = term if da[lm] is None else da[lm] + term
            a = [amat[t, lm, at, :] for lm in range(16)]
            for lm in range(16):
                damat[t, lm, at, :] = da[lm]
            c = contract_rows(t)
            s, p = a[0], powers_of(a)
            beta = beta_of(c, s)
            value = alpha_of(c, s, p) * da[0]
            for i in range(3):
                degree = i + 1
                dp = 2.0 * sum(a[lm] * da[lm] for lm in range(degree * degree, (degree + 1) ** 2))
                value = value + beta[i] * dp
            dmsg[t, at, :] = value

        tiles(body)

    def tangent_backward(t, moving):
        gcon[...] = jnp.zeros_like(gcon)

        def body(r):
            at = pl.ds(r, 8)
            padded = pl.ds(pl.multiple_of(r + PAD, 8), 8)
            a = [amat[t, lm, at, :] for lm in range(16)]
            da = [damat[t, lm, at, :] for lm in range(16)]
            c = contract_rows(t)
            up, dup = msgb[t, at, :], dmsgb_of(at)
            s, ds, p = a[0], da[0], powers_of(a)
            dp = [
                2.0 * sum(a[lm] * da[lm] for lm in range(degree * degree, (degree + 1) ** 2))
                for degree in (1, 2, 3)
            ]
            alpha, beta = alpha_of(c, s, p), beta_of(c, s)
            dalpha = (
                2.0 * c[1] * ds
                + 6.0 * c[5] * s * ds
                + c[6] * dp[0]
                + c[7] * dp[1]
                + c[8] * dp[2]
            )
            pb = [None] + [2.0 * up * beta[i] for i in range(3)]
            dpb = [None] + [2.0 * (dup * beta[i] + up * c[6 + i] * ds) for i in range(3)]
            ab = [up * alpha] + [pb[DEGREES[lm]] * a[lm] for lm in range(1, 16)]
            dab = [dup * alpha + up * dalpha] + [
                pb[DEGREES[lm]] * da[lm] + dpb[DEGREES[lm]] * a[lm] for lm in range(1, 16)
            ]
            products = [(s, ds), (s * s, 2.0 * s * ds)]
            products += [(p[i], dp[i]) for i in range(3)]
            products += [(s * s * s, 3.0 * s * s * ds)]
            products += [(s * p[i], ds * p[i] + s * dp[i]) for i in range(3)]
            for b, (point, direction) in enumerate(products):
                gcon[b] += dup * point + up * direction
            for slot in range(DIRECTED):
                there = fj[t, slot, at, :]
                back = None
                for degree in range(4):
                    total = None
                    for lm in range(degree * degree, (degree + 1) ** 2):
                        term = ye[slot * 16 + lm, at, :] * dab[lm] + dye[slot * 16 + lm, at, :] * ab[lm]
                        total = term if total is None else total + term
                    was = wb[t, slot * 4 + degree, at, :]
                    value = total * there
                    if moving:
                        value = value + was * dfj[slot, at, :]
                    fbdir[slot * 4 + degree, padded, :] = value
                    term = (
                        total * fdir[t, slot * 4 + degree, at, :]
                        + was * dfdir[t, slot * 4 + degree, at, :]
                    )
                    back = term if back is None else back + term
                fjb[slot, padded, :] = back

        tiles(body)
        for b in range(9):
            g_con[t, b : b + 1, :] -= jnp.sum(gcon[b], axis=0, keepdims=True)

    def dmsgb_of(at):
        return msgb[2, at, :]

    hot = jnp.where(
        lax.broadcasted_iota(jnp.int32, (ELEMENT_ROWS, LANES), 0).astype(f32) == species, 1.0, 0.0
    )[:, :WINDOW]
    own_lane = own[:, :WINDOW]
    featp[0, inner, :] = mm(hot, emb_ref[...], 0, 0, EXACT)
    sums = []
    for t in range(2):
        network(t)
        directed_filters(t, hid[t, 2], fdir)
        gather(featp.at[t], fj.at[t])
        forward_messages(t)
        featp[t + 1, inner, :] = featp[t, inner, :] + mm(msg[t], mix_ref[t], 1, 1)
        sums.append(mm(read_ref[t], featp[t + 1, inner, :], 1, 1))

    gsum[...] = jnp.zeros_like(gsum)
    sum_bars, feat_bars = [], [None, None]
    flat_bar = None
    for t in range(2):
        _, slope, _ = silu_parts(sums[t])
        sum_bars.append(own_lane * en_ref[t] * slope)
    feat_bar = None
    for t in (1, 0):
        read_back = mm(sum_bars[t], read_ref[t], 0, 0)
        feat_bar = read_back if feat_bar is None else feat_bar + read_back
        feat_bars[t] = feat_bar
        msgb[t] = mm(feat_bar, mix_ref[t], 1, 0)
        backward_messages(t, t > 0)
        fbp[t] = all_folded()
        value = mm(all_filters(t), fbp[t], 1, 1)
        for depth in (2, 1, 0):
            hidb[t, depth] = value
            value = value * hid[t, 3 + depth]
            hidb[t, 3 + depth] = value
            weight = bes_ref[t] if depth == 0 else rad_ref[t, depth - 1]
            value = mm(weight, value, 1, 0)
        term = jnp.sum(value * bess[1], axis=0, keepdims=True)
        flat_bar = term if flat_bar is None else flat_bar + term
        if t > 0:
            feat_bar = feat_bar + scattered()

    turned = gsum[...].T
    shape_bars = tuple(turned[lm * 16 : lm * 16 + 16, :] for lm in range(16))
    distance_bar = jnp.concatenate([unflatten(flat_bar), jnp.zeros((8, LANES), f32)], axis=0)
    rel_bars = geometry_pull((shape_bars, distance_bar))
    flip = jnp.where(
        lax.broadcasted_iota(jnp.int32, (16, 16), 0) + lax.broadcasted_iota(jnp.int32, (16, 16), 1)
        == 14,
        1.0,
        0.0,
    ).astype(f32)
    slopes = []
    loss_row = jnp.zeros((1, LANES), f32)
    weight_row = own * labelled
    for i in range(3):
        bar = jnp.where(valid > 0.0, rel_bars[i], 0.0)
        reverse = mm(flip, bar, 1, 0, EXACT)
        back = pltpu.roll(reverse, 1, 1, stride=1, stride_axis=0)
        ahead = pltpu.roll(reverse, 113, 1, stride=1, stride_axis=0)
        arrived = jnp.where(is_ahead, ahead, jnp.where(is_back, back, 0.0))
        force = jnp.sum(bar - arrived, axis=0, keepdims=True)
        force_ref[0, i : i + 1, :] = force
        diff = force - row(8 + i)
        magnitude = jnp.abs(diff)
        huber = jnp.where(
            magnitude <= HUBER_DELTA,
            0.5 * diff * diff,
            HUBER_DELTA * (magnitude - 0.5 * HUBER_DELTA),
        )
        loss_row = loss_row + weight_row * huber
        slopes.append(weight_row * jnp.clip(diff, -HUBER_DELTA, HUBER_DELTA))
    force_ref[0, 3:8, :] = jnp.zeros((5, LANES), f32)
    stat_ref[0:1, :] += loss_row
    stat_ref[1:2, :] += weight_row

    drel = tuple(relative(value) for value in slopes)
    _, (dshapes, ddistance) = jax.jvp(
        lambda a, b, c: geometry(a, b, c, valid), tuple(rel), drel
    )
    spread(dshapes, dye)
    bess[2] = bess[1] * flatten(ddistance[:PAIRS])
    dsums = []
    dfeat = None
    for t in range(2):
        value = bess[2]
        for depth in range(3):
            weight = bes_ref[t] if depth == 0 else rad_ref[t, depth - 1]
            z = mm(weight, value, 0, 0)
            value = z * hid[t, 3 + depth]
            hidt[t, depth] = value
            hid[t, 6 + depth] = hid[t, 6 + depth] * z
        directed_filters(t, value, dfdir)
        if t > 0:
            dfeatp[inner, :] = dfeat
            gather(dfeatp, dfj)
        tangent_messages(t, t > 0)
        step = mm(dmsg[t], mix_ref[t], 1, 1)
        dfeat = step if dfeat is None else dfeat + step
        dsums.append((mm(read_ref[t], dfeat, 1, 1), dfeat))

    dfeat_bar = None
    for t in (1, 0):
        dsum, dfeat_after = dsums[t]
        act, slope, curve = silu_parts(sums[t])
        g_en[t] -= jnp.sum(own_lane * slope * dsum, axis=1, keepdims=True)
        dsum_bar = own_lane * en_ref[t] * curve * dsum
        g_read[t] -= mm(dsum_bar, featp[t + 1, inner, :], 1, 0) + mm(
            sum_bars[t], dfeat_after, 1, 0
        )
        read_back = mm(dsum_bar, read_ref[t], 0, 0)
        dfeat_bar = read_back if dfeat_bar is None else dfeat_bar + read_back
        g_mix[t] -= mm(dfeat_bar, msg[t], 0, 0) + mm(feat_bars[t], dmsg[t], 0, 0)
        msgb[2] = mm(dfeat_bar, mix_ref[t], 1, 0)
        tangent_backward(t, t > 0)
        dfbp = all_folded()
        g_fil[t] -= mm(hidt[t, 2], fbp[t], 1, 0) + mm(hid[t, 2], dfbp, 1, 0)
        value = mm(all_filters(t), dfbp, 1, 1)
        for depth in (2, 1, 0):
            value = value * hid[t, 3 + depth] + hidb[t, depth] * hid[t, 6 + depth]
            weight = bes_ref[t] if depth == 0 else rad_ref[t, depth - 1]
            before = bess[0] if depth == 0 else hid[t, depth - 1]
            dbefore = bess[2] if depth == 0 else hidt[t, depth - 1]
            grad = mm(dbefore, hidb[t, 3 + depth], 1, 1) + mm(before, value, 1, 1)
            if depth == 0:
                g_bes[t] -= grad
            else:
                g_rad[t, depth - 1] -= grad
                value = mm(weight, value, 1, 0)
        dfeat_bar = dfeat_bar + scattered()
    g_emb[...] -= mm(hot, dfeat_bar, 1, 0)


def local_step(windows, table, bessel, radial, filters, contract, mixing, readout, energies):
    units = windows.shape[0]
    f32 = jnp.float32
    vmem = pl.BlockSpec(memory_space=pltpu.VMEM)

    def scratch(*shape):
        return pltpu.VMEM(shape, f32)

    def out(*shape):
        return jax.ShapeDtypeStruct(shape, f32)

    return pl.pallas_call(
        step_kernel,
        grid=(units,),
        in_specs=[pl.BlockSpec((1, 16, LANES), lambda i: (i, 0, 0))] + [vmem] * 8,
        out_specs=[pl.BlockSpec((1, 8, LANES), lambda i: (i, 0, 0))] + [vmem] * 9,
        out_shape=[
            out(units, 8, LANES),
            out(8, LANES),
            out(ELEMENT_ROWS, LANES),
            out(2, NBESSEL, 64),
            out(2, 2, 64, 64),
            out(2, 64, 4 * LANES),
            out(2, 16, LANES),
            out(2, LANES, LANES),
            out(2, 16, LANES),
            out(2, 16, 1),
        ],
        scratch_shapes=[
            scratch(240, WINDOW, LANES),
            scratch(240, WINDOW, LANES),
            scratch(15, WINDOW, LANES),
            scratch(15, WINDOW, LANES),
            scratch(3, ROWS, LANES),
            scratch(ROWS, LANES),
            scratch(2, 15, WINDOW, LANES),
            scratch(15, WINDOW, LANES),
            scratch(2, 60, WINDOW, LANES),
            scratch(2, 60, WINDOW, LANES),
            scratch(32, ROWS, LANES),
            scratch(60, ROWS, LANES),
            scratch(15, ROWS, LANES),
            scratch(2, 60, WINDOW, LANES),
            scratch(2, FLAT, 4 * LANES),
            scratch(2, 16, WINDOW, LANES),
            scratch(2, 16, WINDOW, LANES),
            scratch(2, WINDOW, LANES),
            scratch(3, WINDOW, LANES),
            scratch(2, WINDOW, LANES),
            scratch(LANES, 2 * LANES),
            scratch(LANES, 2 * LANES),
            scratch(2, 9, 64, FLAT),
            scratch(2, 6, 64, FLAT),
            scratch(2, 3, 64, FLAT),
            scratch(3, NBESSEL, FLAT),
            scratch(9, 8, LANES),
        ],
        compiler_params=pltpu.CompilerParams(vmem_limit_bytes=62 * 1024 * 1024),
    )(windows, table, bessel, radial, filters, contract, mixing, readout, energies)


MESH = pl.DeviceIdType.MESH
GROUPS = 4
BLOCKS = 8
SHARE_LANES = LANES // GROUPS
BLOB = 168
PIECE = 272
SUB = 40
QUARTER = PIECE - BLOB


def dense(value):
    rows = value.shape[0] // GROUPS
    return jnp.concatenate([value[k * rows : (k + 1) * rows] for k in range(GROUPS)], axis=1)


def lanes_of(value, group):
    return value[:, group * SHARE_LANES : (group + 1) * SHARE_LANES]


def undense(pieces):
    return jnp.concatenate(
        [
            jnp.concatenate([lanes_of(piece, k) for piece in pieces], axis=1)
            for k in range(GROUPS)
        ],
        axis=0,
    )


def collect_kernel(
    pos_ref,
    spec_ref,
    neigh_ref,
    lab_ref,
    tgt_ref,
    emb_ref,
    fil_ref,
    con_ref,
    read_ref,
    win_ref,
    table_ref,
    full_ref,
    cont_ref,
    rd_ref,
    blob,
    padded,
    ext,
    halo,
    send_sem,
    recv_sem,
    halo_sem,
):
    block, group = lax.axis_index("atoms"), lax.axis_index("chan")
    count = pos_ref.shape[1]
    before = lax.rem(block + BLOCKS - 1, BLOCKS)
    after = lax.rem(block + 1, BLOCKS)
    peers = [lax.rem(group + offset, GROUPS) for offset in range(1, GROUPS)]
    barrier = pltpu.get_barrier_semaphore()
    for peer in peers:
        pl.semaphore_signal(barrier, inc=1, device_id={"chan": peer}, device_id_type=MESH)
    for other in (before, after):
        pl.semaphore_signal(barrier, inc=1, device_id={"atoms": other}, device_id_type=MESH)

    padded[...] = jnp.zeros_like(padded)
    padded[0:ELEMENTS, :] = emb_ref[...]
    for t in range(2):
        padded[96 + 16 * t : 105 + 16 * t, :] = con_ref[t]
    blob[group, 0:128, :] = dense(fil_ref[...].reshape(512, SHARE_LANES))
    blob[group, 128:152, :] = dense(padded[0:96, :])
    blob[group, 152:160, :] = dense(read_ref[...].reshape(32, SHARE_LANES))
    blob[group, 160:168, :] = dense(padded[96:128, :])

    atom = lax.broadcasted_iota(jnp.int32, (1, count), 1)
    leading = neigh_ref[0:1, :] - block * count
    first = jnp.where((neigh_ref[0:1, :] >= 0) & (leading < atom), leading, atom)
    ext[...] = jnp.zeros_like(ext)
    ext[0:3, 0:count] = pos_ref[...]
    ext[3:4, 0:count] = first.astype(jnp.float32)
    ext[4:5, 0:count] = spec_ref[...].astype(jnp.float32)
    ext[5:6, 0:count] = lab_ref[...].astype(jnp.float32)
    ext[8:11, 0:count] = tgt_ref[...]

    pl.semaphore_wait(barrier, GROUPS + 1)
    copies = []
    for at, peer in enumerate(peers):
        copies.append(
            pltpu.make_async_remote_copy(
                src_ref=blob.at[group],
                dst_ref=blob.at[group],
                send_sem=send_sem.at[at],
                recv_sem=recv_sem.at[group],
                device_id={"chan": peer},
                device_id_type=MESH,
            )
        )
    halo_copy = pltpu.make_async_remote_copy(
        src_ref=ext.at[:, 0:LANES],
        dst_ref=halo,
        send_sem=halo_sem.at[0],
        recv_sem=halo_sem.at[1],
        device_id={"atoms": before},
        device_id_type=MESH,
    )
    halo_copy.start()
    for copy in copies:
        copy.start()

    halo_copy.wait()
    kind = lax.broadcasted_iota(jnp.int32, (16, LANES), 0)
    lane = lax.broadcasted_iota(jnp.int32, (16, LANES), 1)
    there = (lane < GHOST) & (block < BLOCKS - 1)
    shifted = halo[...] + jnp.where(kind == 3, float(count), 0.0)
    nothing = jnp.where(kind == 3, -1.0e6, 0.0)
    ext[:, count : count + LANES] = jnp.where(there, shifted, nothing)
    share = count // GROUPS
    wide = ext[:, pl.ds(pl.multiple_of(group * share, LANES), 2 * LANES)]
    for unit in range(share // UNIT):
        view = wide if unit == 0 else pltpu.roll(wide, 2 * LANES - unit * UNIT, 1)
        view = view[:, :LANES]
        start = (group * share + unit * UNIT).astype(jnp.float32)
        view = view - jnp.where(kind == 3, start, 0.0)
        win_ref[unit] = jnp.where(lane < WINDOW, view, nothing)

    for at, peer in enumerate(peers):
        pltpu.make_async_remote_copy(
            src_ref=blob.at[peer],
            dst_ref=blob.at[peer],
            send_sem=send_sem.at[at],
            recv_sem=recv_sem.at[peer],
            device_id={"chan": peer},
            device_id_type=MESH,
        ).wait_recv()
    full_ref[...] = undense([blob[k, 0:128, :] for k in range(GROUPS)]).reshape(2, 4, 64, LANES)
    table_ref[...] = undense([blob[k, 128:152, :] for k in range(GROUPS)])
    rd_ref[...] = undense([blob[k, 152:160, :] for k in range(GROUPS)]).reshape(2, 16, LANES)
    cont_ref[...] = undense([blob[k, 160:168, :] for k in range(GROUPS)]).reshape(2, 16, LANES)
    for copy in copies:
        copy.wait_send()


def collect(positions, species, neighbours, labelled, targets, embedding, filters, contract, readout):
    f32 = jnp.float32
    count = positions.shape[1]
    vmem = pl.BlockSpec(memory_space=pltpu.VMEM)
    return pl.pallas_call(
        collect_kernel,
        in_specs=[vmem] * 9,
        out_specs=[vmem] * 5,
        out_shape=[
            jax.ShapeDtypeStruct((count // GROUPS // UNIT, 16, LANES), f32),
            jax.ShapeDtypeStruct((ELEMENT_ROWS, LANES), f32),
            jax.ShapeDtypeStruct((2, 4, 64, LANES), f32),
            jax.ShapeDtypeStruct((2, 16, LANES), f32),
            jax.ShapeDtypeStruct((2, 16, LANES), f32),
        ],
        scratch_shapes=[
            pltpu.VMEM((GROUPS, BLOB, LANES), f32),
            pltpu.VMEM((LANES, SHARE_LANES), f32),
            pltpu.VMEM((16, count + LANES), f32),
            pltpu.VMEM((16, LANES), f32),
            pltpu.SemaphoreType.DMA((GROUPS - 1,)),
            pltpu.SemaphoreType.DMA((GROUPS,)),
            pltpu.SemaphoreType.DMA((2,)),
        ],
        compiler_params=pltpu.CompilerParams(collective_id=0, has_side_effects=True),
    )(
        positions,
        species[None],
        neighbours,
        labelled[None],
        targets,
        embedding,
        filters,
        contract,
        readout,
    )


def reduce_kernel(
    force_ref,
    stat_ref,
    g_emb,
    g_bes,
    g_rad,
    g_fil,
    g_con,
    g_mix,
    g_read,
    g_en,
    forces_ref,
    own_ref,
    rest_ref,
    pieces,
    core_in,
    line_out,
    line_in,
    summed,
    sub_in,
    sub_out,
    total,
    quarters,
    windows,
    tail,
    tail_in,
    sems,
    sub_send,
    sub_recv,
    total_send,
    total_recv,
):
    f32 = jnp.float32
    block, group = lax.axis_index("atoms"), lax.axis_index("chan")
    line, core = group // 2, lax.rem(group, 2)
    core_peer = {"chan": line * 2 + (1 - core)}
    line_peer = {"chan": (1 - line) * 2 + core}
    others = [lax.rem(block + offset, BLOCKS) for offset in range(1, BLOCKS)]
    barrier = pltpu.get_barrier_semaphore()
    for peer in [core_peer, line_peer] + [{"atoms": other} for other in others]:
        pl.semaphore_signal(barrier, inc=1, device_id=peer, device_id_type=MESH)

    def copy(source, dest, at, peer):
        return pltpu.make_async_remote_copy(
            src_ref=source,
            dst_ref=dest,
            send_sem=sems.at[2 * at],
            recv_sem=sems.at[2 * at + 1],
            device_id=peer,
            device_id_type=MESH,
        )

    rows = lax.broadcasted_iota(jnp.int32, (16, LANES), 0)
    lanes = lax.broadcasted_iota(jnp.int32, (16, LANES), 1)
    vector = jnp.zeros((1, LANES), f32)
    for t in range(2):
        spread = jnp.broadcast_to(g_en[t], (16, LANES))
        vector = vector + jnp.sum(
            jnp.where(lanes == rows + 16 * t, spread, 0.0), axis=0, keepdims=True
        )
    inner = g_rad[...].reshape(256, 64)
    inner = jnp.concatenate([inner[:128], inner[128:]], axis=1)
    bessel = jnp.concatenate([g_bes[0], g_bes[1]], axis=1)
    for k in range(GROUPS):
        where = (k % 2, k // 2)
        for half in range(2):
            pieces[(*where, pl.ds(64 * half, 64), slice(None))] = jnp.concatenate(
                [
                    lanes_of(g_fil[j // 2, :, pl.ds(LANES * (2 * (j % 2) + half), LANES)], k)
                    for j in range(4)
                ],
                axis=1,
            )
        pieces[(*where, pl.ds(128, 24), slice(None))] = dense(lanes_of(g_emb[...], k))
        pieces[(*where, pl.ds(152, 8), slice(None))] = dense(
            lanes_of(g_read[...].reshape(32, LANES), k)
        )
        pieces[(*where, pl.ds(160, 8), slice(None))] = dense(
            lanes_of(g_con[...].reshape(32, LANES), k)
        )
        pieces[(*where, pl.ds(168, 64), slice(None))] = g_mix[k // 2, 64 * (k % 2) : 64 * (k % 2) + 64, :]
        pieces[(*where, pl.ds(232, 32), slice(None))] = inner[32 * k : 32 * k + 32]
        pieces[(*where, pl.ds(264, 8), slice(None))] = jnp.concatenate(
            [bessel[2 * k : 2 * k + 2], vector, stat_ref[0:2, :], jnp.zeros((3, LANES), f32)],
            axis=0,
        )
    windows[line, core] = force_ref[...]
    pl.semaphore_wait(barrier, BLOCKS + 1)

    core_copy = copy(pieces.at[1 - core], core_in, 0, core_peer)
    core_copy.start()
    core_force = copy(windows.at[line, core], windows.at[line, core], 1, core_peer)
    core_force.start()
    core_copy.wait()
    line_out[...] = pieces[core, 1 - line] + core_in[1 - line]
    line_copy = copy(line_out, line_in, 2, line_peer)
    line_copy.start()
    core_force.wait()
    line_force = copy(windows.at[line], windows.at[line], 3, line_peer)
    line_force.start()
    partial = pieces[core, line] + core_in[line]
    line_force.wait()

    lane8 = lax.broadcasted_iota(jnp.int32, (8, LANES), 1)
    canvas = [jnp.zeros((8, LANES), f32)] * 5
    for k in range(8):
        value = windows[k // 4, (k // 2) % 2, k % 2]
        if k % 2 == 0:
            canvas[k // 2] = canvas[k // 2] + value
        else:
            value = pltpu.roll(value, 64, 1)
            canvas[k // 2] = canvas[k // 2] + jnp.where(lane8 >= 64, value, 0.0)
            canvas[k // 2 + 1] = canvas[k // 2 + 1] + jnp.where(lane8 < 64, value, 0.0)
    tail[...] = canvas[4]
    tail_copy = copy(tail, tail_in, 4, {"atoms": others[0]})
    tail_copy.start()

    line_copy.wait()
    summed[7] = jnp.zeros((SUB, LANES), f32)
    partial = partial + line_in[...]
    for k in range(7):
        size = min(SUB, PIECE - k * SUB)
        summed[k, 0:size, :] = partial[k * SUB : k * SUB + size]
        if size < SUB:
            summed[k, size:SUB, :] = jnp.zeros((SUB - size, LANES), f32)

    def sub_copy(other, at):
        return pltpu.make_async_remote_copy(
            src_ref=summed.at[other],
            dst_ref=sub_in.at[block],
            send_sem=sub_send.at[at],
            recv_sem=sub_recv.at[block],
            device_id={"atoms": other},
            device_id_type=MESH,
        )

    def total_copy(other, at):
        return pltpu.make_async_remote_copy(
            src_ref=sub_out,
            dst_ref=total.at[block],
            send_sem=total_send.at[at],
            recv_sem=total_recv.at[block],
            device_id={"atoms": other},
            device_id_type=MESH,
        )

    def arrival(dest, recv, other):
        return pltpu.make_async_remote_copy(
            src_ref=sub_out,
            dst_ref=dest.at[other],
            send_sem=sub_send.at[0],
            recv_sem=recv.at[other],
            device_id={"atoms": other},
            device_id_type=MESH,
        )

    subs = [sub_copy(other, at) for at, other in enumerate(others)]
    for item in subs:
        item.start()
    value = summed[block]
    for other in others:
        arrival(sub_in, sub_recv, other).wait_recv()
        value = value + sub_in[other]
    sub_out[...] = value
    totals = [total_copy(other, at) for at, other in enumerate(others)]
    for item in totals:
        item.start()
    total[block] = value
    tail_copy.wait()
    forces = jnp.concatenate(canvas[:4], axis=1)
    edge = jnp.where((lane8 < GHOST) & (block > 0), tail_in[...], 0.0)
    forces_ref[...] = forces
    forces_ref[:, 0:LANES] = canvas[0] + edge
    for other in others:
        arrival(total, total_recv, other).wait_recv()
    for item in subs + totals:
        item.wait_send()

    everything = total[...].reshape(BLOCKS * SUB, LANES)
    own_ref[...] = everything[:BLOB]
    count = jnp.sum(everything[268:269], axis=1, keepdims=True)
    flat = everything[:266]
    energy_row = everything[266:267]
    squares = jnp.sum(flat * flat, axis=0, keepdims=True)
    squares = squares + (1.0 / GROUPS) * energy_row * energy_row
    squares = jnp.sum(squares, axis=1, keepdims=True)
    quarters[line, core] = everything[BLOB:PIECE]
    quarters[line, core, 101:102, :] = jnp.broadcast_to(squares, (1, LANES))
    line_quarter = copy(quarters.at[line, core], quarters.at[line, core], 5, line_peer)
    line_quarter.start()
    core_quarter = copy(quarters.at[line, core], quarters.at[line, core], 6, core_peer)
    core_quarter.start()
    line_quarter.wait()
    cross_quarter = copy(quarters.at[1 - line, core], quarters.at[1 - line, core], 7, core_peer)
    cross_quarter.start()
    core_quarter.wait()
    cross_quarter.wait()
    rest_ref[...] = quarters[...].reshape(GROUPS, QUARTER, LANES)


def reduce_all(force, stat, grads):
    f32 = jnp.float32
    vmem = pl.BlockSpec(memory_space=pltpu.VMEM)
    dma = pltpu.SemaphoreType.DMA
    return pl.pallas_call(
        reduce_kernel,
        in_specs=[vmem] * 10,
        out_specs=[vmem] * 3,
        out_shape=[
            jax.ShapeDtypeStruct((8, 4 * LANES), f32),
            jax.ShapeDtypeStruct((BLOB, LANES), f32),
            jax.ShapeDtypeStruct((GROUPS, QUARTER, LANES), f32),
        ],
        scratch_shapes=[
            pltpu.VMEM((2, 2, PIECE, LANES), f32),
            pltpu.VMEM((2, PIECE, LANES), f32),
            pltpu.VMEM((PIECE, LANES), f32),
            pltpu.VMEM((PIECE, LANES), f32),
            pltpu.VMEM((BLOCKS, SUB, LANES), f32),
            pltpu.VMEM((BLOCKS, SUB, LANES), f32),
            pltpu.VMEM((SUB, LANES), f32),
            pltpu.VMEM((BLOCKS, SUB, LANES), f32),
            pltpu.VMEM((2, 2, QUARTER, LANES), f32),
            pltpu.VMEM((2, 2, 2, 8, LANES), f32),
            pltpu.VMEM((8, LANES), f32),
            pltpu.VMEM((8, LANES), f32),
            dma((16,)),
            dma((BLOCKS - 1,)),
            dma((BLOCKS,)),
            dma((BLOCKS - 1,)),
            dma((BLOCKS,)),
        ],
        compiler_params=pltpu.CompilerParams(collective_id=1, has_side_effects=True),
    )(force, stat, *grads)


def adam_kernel(*refs):
    forces_in, own_ref, rest_ref = refs[:3]
    weights, moments = refs[3:11], refs[11:27]
    parts_ref, forces_ref, norm_ref = refs[27:30]
    results = refs[30:54]
    scratch = refs[54]
    rest = [rest_ref[k] for k in range(GROUPS)]
    stats = rest[0]
    loss = jnp.sum(stats[99:100], axis=1, keepdims=True)
    count = jnp.sum(stats[100:101], axis=1, keepdims=True)
    inverse = 1.0 / count
    squares = sum(rest[k][101:102, 0:1] for k in range(GROUPS))
    norm = jnp.sqrt(squares) * inverse
    factor = inverse * jnp.minimum(1.0, CLIP_NORM / (norm + 1e-06))
    norm_ref[...] = norm
    two = lax.broadcasted_iota(jnp.int32, (1, 2), 1)
    parts_ref[...] = jnp.where(two == 0, loss, count)
    forces_ref[...] = forces_in[0:3, :]

    def narrow(value):
        return jnp.concatenate([lanes_of(value, k) for k in range(GROUPS)], axis=0)

    fil = narrow(own_ref[0:128, :]).reshape(2, 4, 64, SHARE_LANES)
    emb = narrow(own_ref[128:152, :])
    read = narrow(own_ref[152:160, :]).reshape(2, 16, SHARE_LANES)
    scratch[...] = narrow(own_ref[160:168, :])
    con = [scratch[0:9, :], scratch[16:25, :]]
    mix = jnp.concatenate([rest[k][0:64] for k in range(GROUPS)], axis=0).reshape(2, LANES, LANES)
    inner = jnp.concatenate([rest[k][64:96] for k in range(GROUPS)], axis=0)
    inner = jnp.concatenate([inner[:, :64], inner[:, 64:]], axis=0).reshape(2, 2, 64, 64)
    bes = jnp.concatenate([rest[k][96:98] for k in range(GROUPS)], axis=0)
    bes = [bes[:, :64], bes[:, 64:]]
    vector = rest[0][98:99]
    vector = jnp.concatenate([vector[:, 0:16], vector[:, 16:32]], axis=0)

    def update(which, gradient, at):
        first, square = moments[2 * which], moments[2 * which + 1]
        weight = weights[which][at]
        clipped = gradient * factor
        moment = BETA_ONE * first[at] + (1.0 - BETA_ONE) * clipped
        second = BETA_TWO * square[at] + (1.0 - BETA_TWO) * clipped * clipped
        corrected_first = moment * (1.0 / (1.0 - BETA_ONE**ADAM_STEP))
        corrected_second = second * (1.0 / (1.0 - BETA_TWO**ADAM_STEP))
        updated = weight - RATE * (
            corrected_first / (jnp.sqrt(corrected_second) + EPSILON) + DECAY * weight
        )
        results[3 * which][at] = updated
        results[3 * which + 1][at] = moment
        results[3 * which + 2][at] = second

    everything = Ellipsis
    update(0, emb[:ELEMENTS], everything)
    for t in range(2):
        update(1, bes[t], t)
        update(4, con[t], t)
    update(2, inner, everything)
    update(3, fil, everything)
    update(5, mix, everything)
    update(6, read, everything)
    update(7, vector, everything)


def adam(forces, own, rest, weights, moments):
    f32 = jnp.float32
    vmem = pl.BlockSpec(memory_space=pltpu.VMEM)
    shapes = [(1, 2), (3, forces.shape[1]), (1, 1)]
    shapes += [weight.shape for weight in weights for _ in range(3)]
    return pl.pallas_call(
        adam_kernel,
        in_specs=[vmem] * 27,
        out_specs=[vmem] * 27,
        out_shape=[jax.ShapeDtypeStruct(shape, f32) for shape in shapes],
        scratch_shapes=[pltpu.VMEM((32, SHARE_LANES), f32)],
    )(forces, own, rest, *weights, *moments)


def adamw(weight, gradient, first, second, scale):
    clipped = gradient * scale
    moment = BETA_ONE * first + (1.0 - BETA_ONE) * clipped
    second_new = BETA_TWO * second + (1.0 - BETA_TWO) * clipped * clipped
    corrected_first = moment / (1.0 - BETA_ONE**ADAM_STEP)
    corrected_second = second_new / (1.0 - BETA_TWO**ADAM_STEP)
    updated = weight - RATE * (
        corrected_first / (jnp.sqrt(corrected_second) + EPSILON) + DECAY * weight
    )
    return (updated, moment, second_new)


def per_device(
    positions,
    species,
    neighbours,
    labelled,
    target_forces,
    embedding,
    bessel,
    radial,
    filters,
    contract,
    mixing,
    readout,
    energies,
    first_embedding,
    square_embedding,
    first_bessel,
    square_bessel,
    first_radial,
    square_radial,
    first_filters,
    square_filters,
    first_contract,
    square_contract,
    first_mixing,
    square_mixing,
    first_readout,
    square_readout,
    first_energies,
    square_energies,
):
    if (lax.axis_size("atoms"), lax.axis_size("chan")) == (BLOCKS, GROUPS):
        windows, table, full, cont, read = collect(
            positions,
            species,
            neighbours,
            labelled,
            target_forces,
            embedding,
            filters,
            contract,
            readout,
        )
        force, stat, *grads = local_step(
            windows, table, bessel, radial, full, cont, mixing, read, energies[:, :, None]
        )
        forces, own, rest = reduce_all(force, stat, grads)
        weights = (embedding, bessel, radial, filters, contract, mixing, readout, energies)
        moments = (
            first_embedding,
            square_embedding,
            first_bessel,
            square_bessel,
            first_radial,
            square_radial,
            first_filters,
            square_filters,
            first_contract,
            square_contract,
            first_mixing,
            square_mixing,
            first_readout,
            square_readout,
            first_energies,
            square_energies,
        )
        parts, forces, norm, *results = adam(forces, own, rest, weights, moments)
        return tuple([parts.reshape(2), forces, norm.reshape(())] + results)
    f32 = jnp.float32
    atom_count = positions.shape[1]
    local_chan = embedding.shape[1]
    blocks, groups = lax.axis_size("atoms"), lax.axis_size("chan")
    block, group = lax.axis_index("atoms"), lax.axis_index("chan")
    atom_base = block * atom_count
    share = atom_count // groups
    units = share // UNIT

    atom_index = atom_base + jnp.arange(atom_count, dtype=jnp.int32)
    leading = neighbours[0]
    first_atom = jnp.where((leading >= 0) & (leading < atom_index), leading, atom_index)
    packed = jnp.concatenate(
        [
            positions,
            (first_atom - atom_base).astype(f32)[None],
            species.astype(f32)[None],
            labelled.astype(f32)[None],
            jnp.zeros((2, atom_count), f32),
            target_forces,
            jnp.zeros((5, atom_count), f32),
        ],
        axis=0,
    )
    down = [(i + 1, i) for i in range(blocks - 1)]
    halo = lax.ppermute(packed[:, :GHOST], "atoms", down)
    halo_row = jnp.arange(16)[:, None] == 3
    halo = jnp.where(halo_row, jnp.where(block == blocks - 1, -1.0e6, halo + atom_count), halo)
    missing = jnp.where(jnp.arange(16)[:, None] == 3, -1.0e6, 0.0) * jnp.ones((1, LANES), f32)
    extended = jnp.concatenate([packed, halo, missing], axis=1)
    windows = []
    for unit in range(units):
        start = group * share + unit * UNIT
        window = lax.dynamic_slice(extended, (0, start), (16, WINDOW))
        shift = jnp.where(jnp.arange(16)[:, None] == 3, start.astype(f32), 0.0)
        window = window - shift
        windows.append(jnp.concatenate([window, missing[:, : LANES - WINDOW]], axis=1))
    windows = jnp.stack(windows)

    def whole(value):
        return lax.all_gather(value, "chan", axis=value.ndim - 1, tiled=True)

    table = jnp.concatenate(
        [whole(embedding), jnp.zeros((ELEMENT_ROWS - ELEMENTS, LANES), f32)], axis=0
    )
    force, stat, *grads = local_step(
        windows,
        table,
        bessel,
        radial,
        whole(filters),
        whole(contract),
        mixing,
        whole(readout),
        energies[:, :, None],
    )
    grad_embed, grad_bessel, grad_radial, grad_filters, grad_contract, grad_mixing = grads[:6]
    grad_readout, grad_vectors = grads[6:]
    grad_embed = grad_embed[:ELEMENTS]
    grad_filters = grad_filters.reshape(2, 64, 4, LANES).transpose(0, 2, 1, 3)
    grad_contract = grad_contract[:, :9]
    grad_vectors = grad_vectors[:, :, 0]

    canvas = jnp.zeros((3, atom_count + LANES), f32)
    for unit in range(units):
        start = group * share + unit * UNIT
        old = lax.dynamic_slice(canvas, (0, start), (3, WINDOW))
        canvas = lax.dynamic_update_slice(canvas, old + force[unit, :3, :WINDOW], (0, start))
    canvas = lax.psum(canvas, "chan")
    up = [(i, i + 1) for i in range(blocks - 1)]
    arrived = lax.ppermute(canvas[:, atom_count : atom_count + GHOST], "atoms", up)
    forces = canvas[:, :atom_count].at[:, :GHOST].add(arrived)

    def split(value):
        return lax.psum_scatter(value, "chan", scatter_dimension=value.ndim - 1, tiled=True)

    grad_embed, grad_filters, grad_contract, grad_readout = lax.psum(
        (split(grad_embed), split(grad_filters), split(grad_contract), split(grad_readout)),
        "atoms",
    )
    grad_bessel, grad_radial, grad_mixing, grad_vectors, loss_sum, label_total = lax.psum(
        (grad_bessel, grad_radial, grad_mixing, grad_vectors, jnp.sum(stat[0]), jnp.sum(stat[1])),
        ("atoms", "chan"),
    )
    gradients = [
        gradient / label_total
        for gradient in (
            grad_embed,
            grad_bessel,
            grad_radial,
            grad_filters,
            grad_contract,
            grad_mixing,
            grad_readout,
            grad_vectors,
        )
    ]
    squares_of = [jnp.sum(gradient * gradient) for gradient in gradients]
    split_squares = squares_of[0] + squares_of[3] + squares_of[4] + squares_of[6]
    whole_squares = squares_of[1] + squares_of[2] + squares_of[5] + squares_of[7]
    grad_norm = jnp.sqrt(lax.psum(split_squares, "chan") + whole_squares)
    scale = jnp.minimum(1.0, CLIP_NORM / (grad_norm + 1e-06))
    weights = (embedding, bessel, radial, filters, contract, mixing, readout, energies)
    firsts = (
        first_embedding,
        first_bessel,
        first_radial,
        first_filters,
        first_contract,
        first_mixing,
        first_readout,
        first_energies,
    )
    squares = (
        square_embedding,
        square_bessel,
        square_radial,
        square_filters,
        square_contract,
        square_mixing,
        square_readout,
        square_energies,
    )
    results = []
    for weight, gradient, first, second in zip(weights, gradients, firsts, squares):
        results.extend(adamw(weight, gradient, first, second, scale))
    return tuple([jnp.stack([loss_sum, label_total]), forces, grad_norm] + results)


def solution(mesh):
    whole = P()
    columns = P(None, "atoms")
    by_weight = [
        P(None, "chan"),
        whole,
        whole,
        P(None, None, None, "chan"),
        P(None, None, "chan"),
        whole,
        P(None, None, "chan"),
        whole,
    ]
    in_specs = [columns, P("atoms"), columns, P("atoms"), columns] + by_weight
    in_specs += [spec for spec in by_weight for _ in range(2)]
    out_specs = [whole, columns, whole] + [spec for spec in by_weight for _ in range(3)]
    return jax.shard_map(
        per_device,
        mesh=mesh,
        in_specs=tuple(in_specs),
        out_specs=tuple(out_specs),
        check_vma=False,
    )
```

```python
import functools
import math

import jax
import jax.numpy as jnp
from jax import lax
from jax.experimental import pallas as pl
from jax.experimental.pallas import tpu as pltpu
from jax.sharding import PartitionSpec as P

ELEMENTS = 89
NBESSEL = 8
GHOST = 8
ADAM_STEP = 10

RCUT = 5.0
SMOOTH = 0.01
NEIGHBOURS_MEAN = 8.0
HUBER_DELTA = 1.0
CLIP_NORM = 0.001
RATE = 0.2
BETA_ONE = 0.9
BETA_TWO = 0.999
EPSILON = 1e-08
DECAY = 0.01

UNIT = 64
WINDOW = UNIT + 16
PAD = 16
ROWS = WINDOW + 2 * PAD
LANES = 128
DIRECTED = 15
PAIRS = 8
FLAT = PAIRS * WINDOW
DEGREES = [0] + [1] * 3 + [2] * 5 + [3] * 7
EXACT = lax.Precision.HIGHEST

def shapes_of(x, y, z, root_three=math.sqrt(3.0)):
    xx, yy, zz = x * x, y * y, z * z
    xy, yz, zx = x * y, y * z, z * x
    both, less = xx + yy, xx - yy
    wide = 4.0 * zz - both
    return [
        x,
        y,
        z,
        root_three * xy,
        root_three * yz,
        zz - 0.5 * both,
        root_three * zx,
        (0.5 * root_three) * less,
        math.sqrt(5.0 / 8.0) * y * (3.0 * xx - yy),
        math.sqrt(15.0) * xy * z,
        math.sqrt(3.0 / 8.0) * y * wide,
        z * (zz - 1.5 * both),
        math.sqrt(3.0 / 8.0) * x * wide,
        (0.5 * math.sqrt(15.0)) * z * less,
        math.sqrt(5.0 / 8.0) * x * (xx - 3.0 * yy),
    ]


def radius_of(x, y, z, valid):
    distance = jnp.sqrt((x * x + y * y + z * z) * (RCUT * RCUT) + SMOOTH)
    scaled = distance * (1.0 / RCUT)
    square = scaled * scaled
    fifth = square * square * scaled
    envelope = 1.0 - fifth * (21.0 - 35.0 * scaled + 15.0 * square)
    envelope = jnp.where(scaled < 1.0, envelope, 0.0) * (valid * (1.0 / NEIGHBOURS_MEAN))
    return distance, envelope


def halves_of(value):
    high = value.astype(jnp.bfloat16)
    low = (value - high.astype(jnp.float32)).astype(jnp.bfloat16)
    return high, low


def dot(left, right, left_dim, right_dim):
    return lax.dot_general(
        left,
        right,
        (((left_dim,), (right_dim,)), ((), ())),
        preferred_element_type=jnp.float32,
    )


def fine(left, right, left_dim, right_dim):
    left_high, left_low = halves_of(left)
    right_high, right_low = halves_of(right)
    return (
        dot(left_high, right_high, left_dim, right_dim)
        + dot(left_low, right_high, left_dim, right_dim)
        + dot(left_high, right_low, left_dim, right_dim)
    )


def fine_rows(left, right):
    rows = left.shape[0]
    left_high, left_low = halves_of(left)
    right_high, right_low = halves_of(right)
    both = dot(jnp.concatenate([left_high, left_low], axis=0), right_high, 1, 1)
    return both[:rows] + both[rows:] + dot(left_high, right_low, 1, 1)


def triple(value):
    high, low = halves_of(value)
    return jnp.concatenate([high, high, low], axis=0)


def silu_parts(z):
    sig = 1.0 / (1.0 + jnp.exp(-z))
    h = z * sig
    slope = sig + h * (1.0 - sig)
    curve = sig * (1.0 - sig) * (2.0 + z * (1.0 - 2.0 * sig))
    return h, slope, curve


TILES = WINDOW // 8


def tiles(body):
    def step(index, carry):
        body(index, pl.multiple_of(index * 8, 8))
        return carry

    lax.fori_loop(0, TILES, step, 0)


def by_tile(value):
    return value.reshape(TILES, 8, LANES)


def members(degree):
    return range(degree * degree, (degree + 1) ** 2)


def step_kernel(
    win_ref,
    emb_ref,
    bes_ref,
    rad_ref,
    fil_ref,
    con_ref,
    mix_ref,
    read_ref,
    en_ref,
    force_ref,
    stat_ref,
    g_emb,
    g_bes,
    g_rad,
    g_fil,
    g_con,
    g_mix,
    g_read,
    g_en,
    yy,
    dyy,
    ahead_mask,
    back_mask,
    featp,
    dfeatp,
    fj,
    dfj,
    fdir,
    dfdir,
    flat,
    fbdir,
    fjb,
    wb,
    fbh,
    fbl,
    dfbh,
    dfbl,
    amat,
    damat,
    msg,
    msgb,
    dmsg,
    gsum,
    ycol,
    hid,
    hidb,
    hidu,
    hidt,
    bess,
    gcon,
    tab_w,
    bes_w,
    bes_b,
    rad_w,
    rad_b,
    fil_w,
    fil_b,
    take_w,
    g_tab,
    g_wide,
):
    f32, bf16 = jnp.float32, jnp.bfloat16

    @pl.when(pl.program_id(0) == 0)
    def _():
        for ref in (g_tab, g_wide, g_bes, g_rad, g_con, g_mix, g_read, g_en, stat_ref):
            ref[...] = jnp.zeros_like(ref)
        featp[...] = jnp.zeros_like(featp)
        dfeatp[...] = jnp.zeros_like(dfeatp)
        flat[0:PAD, :] = jnp.zeros((PAD, 4 * LANES), f32)
        flat[PAD + FLAT : 2 * PAD + FLAT, :] = jnp.zeros((PAD, 4 * LANES), f32)
        for ref in (fbdir, fjb):
            for start in (0, PAD + WINDOW):
                ref[:, start : start + PAD, :] = jnp.zeros((ref.shape[0], PAD, LANES), f32)
        tab_w[...] = jnp.concatenate(list(halves_of(emb_ref[...].T)), axis=0)
        for t in range(2):
            high, low = [value.astype(f32) for value in halves_of(bes_ref[t])]
            bes_w[t] = jnp.concatenate([high, low, high, jnp.zeros_like(high)], axis=0).T.astype(
                bf16
            )
            bes_b[t] = jnp.concatenate([high, low, high], axis=1).astype(bf16)
            for depth in range(2):
                high, low = [value.astype(f32) for value in halves_of(rad_ref[t, depth])]
                rad_b[t, depth] = jnp.concatenate([high, low, high], axis=1).astype(bf16)
                rad_w[t, depth] = jnp.concatenate([high, low, high], axis=0).T.astype(bf16)
            high, low = halves_of(fil_ref[t].reshape(4 * LANES, 64).T)
            fil_w[t] = jnp.concatenate([high, low, high], axis=0)
            fil_b[t] = jnp.concatenate([high, low], axis=0)

    inner = pl.ds(PAD, WINDOW)

    def row(index):
        return win_ref[0, index : index + 1, :]

    def both_sides(value):
        wide = jnp.broadcast_to(value, (16, LANES))
        back = pltpu.roll(wide, 1, 1, stride=1, stride_axis=0)
        ahead = pltpu.roll(wide, 113, 1, stride=1, stride_axis=0)
        return back, ahead

    first, species, labelled = row(3), row(4), row(5)
    own = jnp.where((first >= 0.0) & (first < float(UNIT)), 1.0, 0.0)
    slot_row = lax.broadcasted_iota(jnp.int32, (16, LANES), 0)
    back_first, ahead_first = both_sides(first)
    may = (slot_row < DIRECTED) & (jnp.broadcast_to(own, (16, LANES)) > 0.0)
    is_back = may & (back_first == first)
    is_ahead = may & (ahead_first == first)
    back_f = jnp.where(is_back, 1.0, 0.0)
    ahead_f = jnp.where(is_ahead, 1.0, 0.0)
    valid = back_f + ahead_f
    pair_valid = jnp.where(slot_row[:PAIRS] < 7, valid[:PAIRS], back_f[:PAIRS])

    def relative(value):
        back, ahead = both_sides(value)
        there = jnp.where(is_ahead, ahead, back)
        return jnp.where(valid > 0.0, there - value, 0.0) * (1.0 / RCUT)

    rel = tuple(relative(row(i)) for i in range(3))
    pair_rel = tuple(value[:PAIRS] for value in rel)
    (distance, envelope), radius_pull = jax.vjp(
        lambda a, b, c: radius_of(a, b, c, pair_valid), *pair_rel
    )

    def columns(values):
        rows = sum(value.shape[0] for value in values)
        values = list(values) + [jnp.zeros((LANES - rows, LANES), f32)]
        ycol[:, :LANES] = jnp.concatenate(values, axis=0).T

    columns(rel + (ahead_f, back_f))

    def spread_shapes(tile, r):
        at = pl.ds(r, 8)
        wide = ycol[at, :LANES]
        for slot in range(DIRECTED):
            x, y, z, ahead, back = [
                jnp.broadcast_to(wide[:, k * 16 + slot : k * 16 + slot + 1], (8, LANES))
                for k in range(5)
            ]
            for k, value in enumerate(shapes_of(x, y, z)):
                yy[tile, slot * 15 + k] = value
            ahead_mask[slot, at, :] = ahead
            back_mask[slot, at, :] = back

    tiles(spread_shapes)

    def spread_tangents(tile, r):
        at = pl.ds(r, 8)
        wide = ycol[at, :LANES]
        for slot in range(DIRECTED):
            direction = tuple(
                jnp.broadcast_to(wide[:, k * 16 + slot : k * 16 + slot + 1], (8, LANES))
                for k in range(3)
            )
            point = tuple(yy[tile, slot * 15 + k] for k in range(3))
            _, values = jax.jvp(shapes_of, point, direction)
            for k, value in enumerate(values):
                dyy[tile, slot * 15 + k] = value

    flat_lane = lax.broadcasted_iota(jnp.int32, (1, FLAT), 1)
    flat_slot = jnp.zeros((1, FLAT), jnp.int32)
    for slot in range(1, PAIRS):
        flat_slot = flat_slot + jnp.where(flat_lane >= slot * WINDOW, 1, 0)

    @pl.when(pl.program_id(0) == 0)
    def _():
        flat_atom = flat_lane - flat_slot * WINDOW
        take_w[...] = jnp.where(
            lax.broadcasted_iota(jnp.int32, (LANES, FLAT), 0) == flat_atom, 1.0, 0.0
        ).astype(bf16)

    slot_mask = lax.broadcasted_iota(jnp.int32, (PAIRS, FLAT), 0) == flat_slot

    def thirds(values):
        parts = []
        for value in values:
            for _ in range(3):
                part = value.astype(bf16).astype(f32)
                parts.append(part)
                value = value - part
        parts += [jnp.zeros_like(parts[0])] * (len(parts) % 2)
        return jnp.concatenate(parts, axis=0).astype(bf16)

    def joined(wide, count, masked):
        results = []
        for k in range(count):
            value = sum(wide[(3 * k + j) * PAIRS : (3 * k + j + 1) * PAIRS] for j in range(3))
            if masked:
                value = jnp.sum(jnp.where(slot_mask, value, 0.0), axis=0, keepdims=True)
            results.append(value)
        return results

    def flatten(values):
        return joined(dot(thirds(values), take_w[...], 1, 0), len(values), True)

    def unflatten(values):
        wide = [jnp.where(slot_mask, jnp.broadcast_to(v, (PAIRS, FLAT)), 0.0) for v in values]
        return joined(dot(thirds(wide), take_w[...], 1, 1), len(values), False)

    angle = distance * (math.pi / RCUT)
    flat_distance, flat_envelope, sine, cosine = flatten(
        [distance, envelope, jnp.sin(angle), jnp.cos(angle)]
    )
    order_row = lax.broadcasted_iota(jnp.int32, (NBESSEL, FLAT), 0)
    sines, cosines = [sine], [cosine]
    for k in range(1, NBESSEL):
        before = (0.0, 1.0) if k == 1 else (sines[k - 2], cosines[k - 2])
        sines.append(2.0 * cosine * sines[-1] - before[0])
        cosines.append(2.0 * cosine * cosines[-1] - before[1])

    def stacked(rows):
        value = jnp.broadcast_to(rows[0], (NBESSEL, FLAT))
        for k in range(1, NBESSEL):
            value = jnp.where(order_row == k, jnp.broadcast_to(rows[k], (NBESSEL, FLAT)), value)
        return value

    omega = (order_row + 1).astype(f32) * (math.pi / RCUT)
    inverse = 1.0 / flat_distance
    root = math.sqrt(2.0 / RCUT)
    basis = root * stacked(sines) * inverse
    bess[0] = basis
    bess[1] = (root * omega * stacked(cosines) - basis) * inverse

    def layer_in(t, depth, value):
        if depth == 0:
            high, low = [part.astype(f32) for part in halves_of(value)]
            wide = jnp.concatenate([high, high, low, jnp.zeros_like(high)], axis=0).astype(bf16)
            return dot(bes_w[t], wide, 1, 0)
        return dot(rad_w[t, depth - 1], triple(value), 1, 0)

    def layer_back(t, depth, value):
        weight = bes_b[t] if depth == 0 else rad_b[t, depth - 1]
        return dot(weight, triple(value), 1, 0)

    def network(t):
        value = bess[0]
        for depth in range(3):
            value, slope, curve = silu_parts(layer_in(t, depth, value))
            hid[t, depth] = value
            hid[t, 3 + depth] = slope
            hid[t, 6 + depth] = curve
        return value * flat_envelope

    def directed_filters(t, hidden, dest):
        flat[PAD : PAD + FLAT, :] = dot(triple(hidden), fil_w[t], 0, 0)
        for slot in range(DIRECTED):
            for degree in range(4):
                lanes = pl.ds(degree * LANES, LANES)
                if slot < 7:
                    value = flat[pl.ds(PAD + slot * WINDOW, WINDOW), lanes]
                else:
                    base = PAD + (14 - slot) * WINDOW
                    if slot == 7:
                        value = flat[pl.ds(base, WINDOW), lanes] + ahead_mask[slot] * (
                            flat[pl.ds(base + 8, WINDOW), lanes]
                        )
                    else:
                        value = (
                            ahead_mask[slot] * flat[pl.ds(base + 15 - slot, WINDOW), lanes]
                            + back_mask[slot] * flat[pl.ds(base - 1 - slot, WINDOW), lanes]
                        )
                dest[t, :, slot * 4 + degree] = by_tile(value)

    def gather(source, dest):
        for slot in range(DIRECTED):
            dest[:, slot] = by_tile(
                jnp.where(
                    ahead_mask[slot] > 0.0,
                    source[pl.ds(PAD + 15 - slot, WINDOW), :],
                    source[pl.ds(PAD - 1 - slot, WINDOW), :],
                )
            )

    def scattered():
        total = None
        for slot in range(DIRECTED):
            term = (
                ahead_mask[slot] * fjb[14 - slot, pl.ds(PAD + 15 - slot, WINDOW), :]
                + back_mask[slot] * fjb[14 - slot, pl.ds(PAD - 1 - slot, WINDOW), :]
            )
            total = term if total is None else total + term
        return total

    def all_folded(high_ref, low_ref):
        for slot in range(PAIRS):
            for degree in range(4):
                value = fbdir[slot * 4 + degree, inner, :]
                at = (14 - slot) * 4 + degree
                if slot == 7:
                    value = value + fbdir[at, pl.ds(PAD - 8, WINDOW), :]
                else:
                    value = value + jnp.where(
                        ahead_mask[slot] > 0.0,
                        fbdir[at, pl.ds(PAD + 15 - slot, WINDOW), :],
                        fbdir[at, pl.ds(PAD - 1 - slot, WINDOW), :],
                    )
                high, low = halves_of(value)
                lanes = pl.ds(degree * LANES, LANES)
                high_ref[pl.ds(slot * WINDOW, WINDOW), lanes] = high
                low_ref[pl.ds(slot * WINDOW, WINDOW), lanes] = low

    def filters_back(t, high_ref, low_ref):
        both = dot(fil_b[t], high_ref[...], 1, 1)
        return both[:64] + both[64:] + dot(fil_b[t, 0:64, :], low_ref[...], 1, 1)

    def filters_grad(hidden, high_ref, low_ref):
        high, low = halves_of(hidden)
        both = dot(jnp.concatenate([high, low], axis=0), high_ref[...], 1, 0)
        return both[:64] + both[64:] + dot(high, low_ref[...], 1, 0)

    def contract_rows(t):
        return [con_ref[t, b : b + 1, :] for b in range(9)]

    def powers_of(a):
        return [sum(a[lm] * a[lm] for lm in members(degree)) for degree in (1, 2, 3)]

    def alpha_of(c, s, p):
        return (
            c[0] + 2.0 * c[1] * s + 3.0 * c[5] * s * s + c[6] * p[0] + c[7] * p[1] + c[8] * p[2]
        )

    def beta_of(c, s):
        return [c[2 + i] + c[6 + i] * s for i in range(3)]

    def shape_at(ref, slot, lm, at):
        return ref[at, slot * 15 + lm - 1]

    def add(total, term):
        return term if total is None else total + term

    def forward_messages(t):
        def body(tile, r):
            at = pl.ds(r, 8)
            a = [None] * 16
            for slot in range(DIRECTED):
                there = fj[t, tile, slot]
                for degree in range(4):
                    w = fdir[t, tile, slot * 4 + degree] * there
                    if degree == 0:
                        a[0] = add(a[0], w)
                        continue
                    for lm in members(degree):
                        a[lm] = add(a[lm], shape_at(yy, slot, lm, tile) * w)
            for lm in range(16):
                amat[t, tile, lm] = a[lm]
            c = contract_rows(t)
            s, p = a[0], powers_of(a)
            value = s * (c[0] + s * (c[1] + s * c[5]) + c[6] * p[0] + c[7] * p[1] + c[8] * p[2])
            msg[t, at, :] = value + c[2] * p[0] + c[3] * p[1] + c[4] * p[2]

        tiles(body)

    def backward_messages(t, to_features):
        lane = lax.broadcasted_iota(jnp.int32, (8, LANES), 1)
        def body(tile, r):
            at = pl.ds(r, 8)
            padded = pl.ds(pl.multiple_of(r + PAD, 8), 8)
            a = [amat[t, tile, lm] for lm in range(16)]
            c = contract_rows(t)
            up = msgb[t, at, :]
            s, p = a[0], powers_of(a)
            beta = beta_of(c, s)
            twice = [None] + [2.0 * up * beta[i] for i in range(3)]
            ab = [up * alpha_of(c, s, p)] + [twice[DEGREES[lm]] * a[lm] for lm in range(1, 16)]
            half = [jnp.zeros((8, LANES), f32)] * 2
            for slot in range(DIRECTED):
                there = fj[t, tile, slot]
                back = None
                for degree in range(4):
                    weight = fdir[t, tile, slot * 4 + degree]
                    total = ab[0] if degree == 0 else None
                    if degree > 0:
                        w = weight * there
                        for lm in members(degree):
                            total = add(total, shape_at(yy, slot, lm, tile) * ab[lm])
                            col = slot * 16 + lm
                            reduced = jnp.sum(w * ab[lm], axis=1, keepdims=True)
                            half[col // LANES] = jnp.where(
                                lane == col % LANES, reduced, half[col // LANES]
                            )
                        wb[t, tile, slot * 3 + degree - 1] = total
                    fbdir[slot * 4 + degree, padded, :] = total * there
                    if to_features:
                        back = add(back, total * weight)
                if to_features:
                    fjb[slot, padded, :] = back
            gsum[at, :LANES] += half[0]
            gsum[at, LANES:] += half[1]

        tiles(body)

    def tangent_messages(t, moving):
        def body(tile, r):
            at = pl.ds(r, 8)
            da = [None] * 16
            for slot in range(DIRECTED):
                there = fj[t, tile, slot]
                for degree in range(4):
                    weight = fdir[t, tile, slot * 4 + degree]
                    dw = dfdir[t, tile, slot * 4 + degree] * there
                    if moving:
                        dw = dw + weight * dfj[tile, slot]
                    if degree == 0:
                        da[0] = add(da[0], dw)
                        continue
                    w = weight * there
                    for lm in members(degree):
                        term = shape_at(yy, slot, lm, tile) * dw + shape_at(dyy, slot, lm, tile) * w
                        da[lm] = add(da[lm], term)
            a = [amat[t, tile, lm] for lm in range(16)]
            for lm in range(16):
                damat[t, tile, lm] = da[lm]
            c = contract_rows(t)
            s, p = a[0], powers_of(a)
            beta = beta_of(c, s)
            value = alpha_of(c, s, p) * da[0]
            for i in range(3):
                value = value + beta[i] * (2.0 * sum(a[lm] * da[lm] for lm in members(i + 1)))
            dmsg[t, at, :] = value

        tiles(body)

    def tangent_backward(t, moving):
        gcon[...] = jnp.zeros_like(gcon)

        def body(tile, r):
            at = pl.ds(r, 8)
            padded = pl.ds(pl.multiple_of(r + PAD, 8), 8)
            a = [amat[t, tile, lm] for lm in range(16)]
            da = [damat[t, tile, lm] for lm in range(16)]
            c = contract_rows(t)
            up, dup = msgb[t, at, :], msgb[2, at, :]
            s, ds, p = a[0], da[0], powers_of(a)
            dp = [2.0 * sum(a[lm] * da[lm] for lm in members(degree)) for degree in (1, 2, 3)]
            alpha, beta = alpha_of(c, s, p), beta_of(c, s)
            dalpha = (
                2.0 * c[1] * ds
                + 6.0 * c[5] * s * ds
                + c[6] * dp[0]
                + c[7] * dp[1]
                + c[8] * dp[2]
            )
            pb = [None] + [2.0 * up * beta[i] for i in range(3)]
            dpb = [None] + [2.0 * (dup * beta[i] + up * c[6 + i] * ds) for i in range(3)]
            ab = [up * alpha] + [pb[DEGREES[lm]] * a[lm] for lm in range(1, 16)]
            dab = [dup * alpha + up * dalpha] + [
                pb[DEGREES[lm]] * da[lm] + dpb[DEGREES[lm]] * a[lm] for lm in range(1, 16)
            ]
            products = [(s, ds), (s * s, 2.0 * s * ds)]
            products += [(p[i], dp[i]) for i in range(3)]
            products += [(s * s * s, 3.0 * s * s * ds)]
            products += [(s * p[i], ds * p[i] + s * dp[i]) for i in range(3)]
            for b, (point, direction) in enumerate(products):
                gcon[b] += dup * point + up * direction
            for slot in range(DIRECTED):
                there = fj[t, tile, slot]
                back = None
                for degree in range(4):
                    if degree == 0:
                        was, total = ab[0], dab[0]
                    else:
                        was, total = wb[t, tile, slot * 3 + degree - 1], None
                        for lm in members(degree):
                            total = add(
                                total,
                                shape_at(yy, slot, lm, tile) * dab[lm]
                                + shape_at(dyy, slot, lm, tile) * ab[lm],
                            )
                    value = total * there
                    if moving:
                        value = value + was * dfj[tile, slot]
                    fbdir[slot * 4 + degree, padded, :] = value
                    back = add(
                        back,
                        total * fdir[t, tile, slot * 4 + degree]
                        + was * dfdir[t, tile, slot * 4 + degree],
                    )
                fjb[slot, padded, :] = back

        tiles(body)
        for b in range(9):
            g_con[t, b : b + 1, :] -= jnp.sum(gcon[b], axis=0, keepdims=True)

    hot = jnp.where(
        lax.broadcasted_iota(jnp.int32, (LANES, LANES), 0).astype(f32) == species, 1.0, 0.0
    )[:, :WINDOW].astype(bf16)
    own_lane = own[:, :WINDOW]
    featp[0, inner, :] = dot(jnp.concatenate([hot, hot], axis=0), tab_w[...], 0, 0)
    sums = []
    for t in range(2):
        directed_filters(t, network(t), fdir)
        gather(featp.at[t], fj.at[t])
        forward_messages(t)
        featp[t + 1, inner, :] = featp[t, inner, :] + fine(msg[t], mix_ref[t], 1, 1)
        sums.append(fine(read_ref[t], featp[t + 1, inner, :], 1, 1))

    gsum[...] = jnp.zeros_like(gsum)
    sum_bars, feat_bars = [], [None, None]
    diagonal = lax.broadcasted_iota(jnp.int32, (16, 16), 0) == lax.broadcasted_iota(
        jnp.int32, (16, 16), 1
    )
    vectors = [
        jnp.sum(
            jnp.where(diagonal, jnp.broadcast_to(en_ref[t : t + 1, :], (16, 16)), 0.0),
            axis=1,
            keepdims=True,
        )
        for t in range(2)
    ]
    flat_bar = envelope_bar = None
    for t in range(2):
        _, slope, _ = silu_parts(sums[t])
        sum_bars.append(own_lane * vectors[t] * slope)
    feat_bar = None
    for t in (1, 0):
        feat_bar = add(feat_bar, fine(sum_bars[t], read_ref[t], 0, 0))
        feat_bars[t] = feat_bar
        msgb[t] = fine(feat_bar, mix_ref[t], 1, 0)
        backward_messages(t, t > 0)
        all_folded(fbh.at[t], fbl.at[t])
        value = filters_back(t, fbh.at[t], fbl.at[t])
        hidu[t] = value
        envelope_bar = add(envelope_bar, jnp.sum(value * hid[t, 2], axis=0, keepdims=True))
        value = value * flat_envelope
        for depth in (2, 1, 0):
            hidb[t, depth] = value
            value = value * hid[t, 3 + depth]
            hidb[t, 3 + depth] = value
            value = layer_back(t, depth, value)
        flat_bar = add(flat_bar, jnp.sum(value * bess[1], axis=0, keepdims=True))
        if t > 0:
            feat_bar = feat_bar + scattered()

    ycol[...] = gsum[:, :LANES].T
    yrow = [ycol[pl.ds(lm, 8, stride=16), :] for lm in range(1, 16)]
    ycol[...] = gsum[:, LANES:].T
    yrow = [
        jnp.concatenate([yrow[lm - 1], ycol[pl.ds(lm, 8, stride=16), :]], axis=0)
        for lm in range(1, 16)
    ]
    _, shapes_pull = jax.vjp(shapes_of, *rel)
    rel_bars = shapes_pull(yrow)
    pair_bars = radius_pull(tuple(unflatten([flat_bar, envelope_bar])))
    flip = jnp.where(
        lax.broadcasted_iota(jnp.int32, (16, 16), 0) + lax.broadcasted_iota(jnp.int32, (16, 16), 1)
        == 14,
        1.0,
        0.0,
    ).astype(f32)
    slopes = []
    loss_row = jnp.zeros((1, LANES), f32)
    weight_row = own * labelled
    for i in range(3):
        bar = rel_bars[i] + jnp.concatenate([pair_bars[i], jnp.zeros((8, LANES), f32)], axis=0)
        bar = jnp.where(valid > 0.0, bar, 0.0) * (1.0 / RCUT)
        reverse = lax.dot_general(
            flip, bar, (((1,), (0,)), ((), ())), precision=EXACT, preferred_element_type=f32
        )
        back = pltpu.roll(reverse, 1, 1, stride=1, stride_axis=0)
        ahead = pltpu.roll(reverse, 113, 1, stride=1, stride_axis=0)
        arrived = jnp.where(is_ahead, ahead, jnp.where(is_back, back, 0.0))
        force = jnp.sum(bar - arrived, axis=0, keepdims=True)
        force_ref[0, i : i + 1, :] = force
        diff = force - row(8 + i)
        magnitude = jnp.abs(diff)
        huber = jnp.where(
            magnitude <= HUBER_DELTA,
            0.5 * diff * diff,
            HUBER_DELTA * (magnitude - 0.5 * HUBER_DELTA),
        )
        loss_row = loss_row + weight_row * huber
        slopes.append(weight_row * jnp.clip(diff, -HUBER_DELTA, HUBER_DELTA))
    force_ref[0, 3:8, :] = jnp.zeros((5, LANES), f32)
    stat_ref[0:1, :] += loss_row
    stat_ref[1:2, :] += weight_row

    drel = tuple(relative(value) for value in slopes)
    _, (ddistance, denvelope) = jax.jvp(
        lambda a, b, c: radius_of(a, b, c, pair_valid),
        pair_rel,
        tuple(value[:PAIRS] for value in drel),
    )
    columns(drel)
    tiles(spread_tangents)
    flat_ddistance, flat_denvelope = flatten([ddistance, denvelope])
    bess[2] = bess[1] * flat_ddistance
    dsums = []
    dfeat = None
    for t in range(2):
        value = bess[2]
        for depth in range(3):
            z = layer_in(t, depth, value)
            value = z * hid[t, 3 + depth]
            hid[t, 6 + depth] = hid[t, 6 + depth] * z
            if depth == 2:
                value = value * flat_envelope + hid[t, 2] * flat_denvelope
            hidt[t, depth] = value
        directed_filters(t, value, dfdir)
        if t > 0:
            dfeatp[inner, :] = dfeat
            gather(dfeatp, dfj)
        tangent_messages(t, t > 0)
        dfeat = add(dfeat, fine(dmsg[t], mix_ref[t], 1, 1))
        dsums.append((fine(read_ref[t], dfeat, 1, 1), dfeat))

    dfeat_bar = None
    for t in (1, 0):
        dsum, dfeat_after = dsums[t]
        _, slope, curve = silu_parts(sums[t])
        g_en[t] -= jnp.sum(own_lane * slope * dsum, axis=1, keepdims=True)
        dsum_bar = own_lane * vectors[t] * curve * dsum
        g_read[t] -= fine(dsum_bar, featp[t + 1, inner, :], 1, 0) + fine(
            sum_bars[t], dfeat_after, 1, 0
        )
        dfeat_bar = add(dfeat_bar, fine(dsum_bar, read_ref[t], 0, 0))
        g_mix[t] -= fine(dfeat_bar, msg[t], 0, 0) + fine(feat_bars[t], dmsg[t], 0, 0)
        msgb[2] = fine(dfeat_bar, mix_ref[t], 1, 0)
        tangent_backward(t, t > 0)
        all_folded(dfbh, dfbl)
        g_wide[t] += filters_grad(hidt[t, 2], fbh.at[t], fbl.at[t]) + filters_grad(
            hid[t, 2] * flat_envelope, dfbh, dfbl
        )
        value = filters_back(t, dfbh, dfbl) * flat_envelope + hidu[t] * flat_denvelope
        for depth in (2, 1, 0):
            value = value * hid[t, 3 + depth] + hidb[t, depth] * hid[t, 6 + depth]
            before = bess[0] if depth == 0 else hid[t, depth - 1]
            dbefore = bess[2] if depth == 0 else hidt[t, depth - 1]
            grad = fine_rows(
                jnp.concatenate([dbefore, before], axis=1),
                jnp.concatenate([hidb[t, 3 + depth], value], axis=1),
            )
            if depth == 0:
                g_bes[t] -= grad
            else:
                g_rad[t, depth - 1] -= grad
                value = layer_back(t, depth, value)
        dfeat_bar = dfeat_bar + scattered()
    high, low = halves_of(dfeat_bar)
    g_tab[...] += dot(hot, high, 1, 0) + dot(hot, low, 1, 0)

    @pl.when(pl.program_id(0) == pl.num_programs(0) - 1)
    def _():
        g_emb[...] = -g_tab[...].T
        for t in range(2):
            g_fil[t] = -g_wide[t].T.reshape(4, LANES, 64)


def local_step(windows, table, bessel, radial, filters, contract, mixing, readout, energies):
    units = windows.shape[0]
    f32, bf16 = jnp.float32, jnp.bfloat16
    vmem = pl.BlockSpec(memory_space=pltpu.VMEM)

    def scratch(*shape):
        return pltpu.VMEM(shape, f32)

    def short(*shape):
        return pltpu.VMEM(shape, bf16)

    def out(*shape):
        return jax.ShapeDtypeStruct(shape, f32)

    return pl.pallas_call(
        step_kernel,
        grid=(units,),
        in_specs=[pl.BlockSpec((1, 16, LANES), lambda i: (i, 0, 0))] + [vmem] * 8,
        out_specs=[pl.BlockSpec((1, 8, LANES), lambda i: (i, 0, 0))] + [vmem] * 9,
        out_shape=[
            out(units, 8, LANES),
            out(8, LANES),
            out(LANES, LANES),
            out(2, NBESSEL, 64),
            out(2, 2, 64, 64),
            out(2, 4, LANES, 64),
            out(2, 16, LANES),
            out(2, LANES, LANES),
            out(2, 16, LANES),
            out(2, 16, 1),
        ],
        scratch_shapes=[
            scratch(TILES, 225, 8, LANES),
            scratch(TILES, 225, 8, LANES),
            scratch(15, WINDOW, LANES),
            scratch(15, WINDOW, LANES),
            scratch(3, ROWS, LANES),
            scratch(ROWS, LANES),
            scratch(2, TILES, 15, 8, LANES),
            scratch(TILES, 15, 8, LANES),
            scratch(2, TILES, 60, 8, LANES),
            scratch(2, TILES, 60, 8, LANES),
            scratch(2 * PAD + FLAT, 4 * LANES),
            scratch(60, ROWS, LANES),
            scratch(15, ROWS, LANES),
            scratch(2, TILES, 45, 8, LANES),
            short(2, FLAT, 4 * LANES),
            short(2, FLAT, 4 * LANES),
            short(FLAT, 4 * LANES),
            short(FLAT, 4 * LANES),
            scratch(2, TILES, 16, 8, LANES),
            scratch(2, TILES, 16, 8, LANES),
            scratch(2, WINDOW, LANES),
            scratch(3, WINDOW, LANES),
            scratch(2, WINDOW, LANES),
            scratch(LANES, 2 * LANES),
            scratch(LANES, LANES),
            scratch(2, 9, 64, FLAT),
            scratch(2, 6, 64, FLAT),
            scratch(2, 64, FLAT),
            scratch(2, 3, 64, FLAT),
            scratch(3, NBESSEL, FLAT),
            scratch(9, 8, LANES),
            short(2 * LANES, LANES),
            short(2, 64, 4 * NBESSEL),
            short(2, NBESSEL, 192),
            short(2, 2, 64, 192),
            short(2, 2, 64, 192),
            short(2, 192, 4 * LANES),
            short(2, LANES, 4 * LANES),
            short(LANES, FLAT),
            scratch(LANES, LANES),
            scratch(2, 64, 4 * LANES),
        ],
        compiler_params=pltpu.CompilerParams(vmem_limit_bytes=62 * 1024 * 1024),
    )(windows, table, bessel, radial, filters, contract, mixing, readout, energies)


MESH = pl.DeviceIdType.MESH
GROUPS = 4
BLOCKS = 8
SHARE_LANES = LANES // GROUPS
BLOB = 176
PIECE = 280
SUB = 40
QUARTER = PIECE - BLOB


def dense(value):
    rows = value.shape[0] // GROUPS
    return jnp.concatenate([value[k * rows : (k + 1) * rows] for k in range(GROUPS)], axis=1)


def lanes_of(value, group):
    return value[:, group * SHARE_LANES : (group + 1) * SHARE_LANES]


def undense(pieces):
    return jnp.concatenate(
        [
            jnp.concatenate([lanes_of(piece, k) for piece in pieces], axis=1)
            for k in range(GROUPS)
        ],
        axis=0,
    )


def collect_kernel(
    pos_ref,
    spec_ref,
    neigh_ref,
    lab_ref,
    tgt_ref,
    emb_ref,
    fil_ref,
    con_ref,
    read_ref,
    win_ref,
    table_ref,
    full_ref,
    cont_ref,
    rd_ref,
    blob,
    padded,
    ext,
    halo,
    send_sem,
    recv_sem,
    halo_sem,
):
    block, group = lax.axis_index("atoms"), lax.axis_index("chan")
    count = pos_ref.shape[1]
    before = lax.rem(block + BLOCKS - 1, BLOCKS)
    after = lax.rem(block + 1, BLOCKS)
    peers = [lax.rem(group + offset, GROUPS) for offset in range(1, GROUPS)]
    barrier = pltpu.get_barrier_semaphore()
    for peer in peers:
        pl.semaphore_signal(barrier, inc=1, device_id={"chan": peer}, device_id_type=MESH)
    for other in (before, after):
        pl.semaphore_signal(barrier, inc=1, device_id={"atoms": other}, device_id_type=MESH)

    padded[...] = jnp.zeros_like(padded)
    for t in range(2):
        padded[16 * t : 16 * t + 9, :] = con_ref[:, t, :]
    table_ref[...] = jnp.zeros_like(table_ref)
    table_ref[0:SHARE_LANES, 0:ELEMENTS] = emb_ref[...]
    both = [fil_ref[t].reshape(LANES, 64) for t in range(2)]
    blob[group, 0:128, :] = jnp.concatenate(both, axis=1)
    blob[group, 128:160, :] = table_ref[0:SHARE_LANES, :]
    blob[group, 160:168, :] = dense(read_ref[...].reshape(32, SHARE_LANES))
    blob[group, 168:176, :] = dense(padded[...])

    atom = lax.broadcasted_iota(jnp.int32, (1, count), 1)
    leading = neigh_ref[0:1, :] - block * count
    first = jnp.where((neigh_ref[0:1, :] >= 0) & (leading < atom), leading, atom)
    ext[...] = jnp.zeros_like(ext)
    ext[0:3, 0:count] = pos_ref[...]
    ext[3:4, 0:count] = first.astype(jnp.float32)
    ext[4:5, 0:count] = spec_ref[...].astype(jnp.float32)
    ext[5:6, 0:count] = lab_ref[...].astype(jnp.float32)
    ext[8:11, 0:count] = tgt_ref[...]

    pl.semaphore_wait(barrier, GROUPS + 1)
    copies = []
    for at, peer in enumerate(peers):
        copies.append(
            pltpu.make_async_remote_copy(
                src_ref=blob.at[group],
                dst_ref=blob.at[group],
                send_sem=send_sem.at[at],
                recv_sem=recv_sem.at[group],
                device_id={"chan": peer},
                device_id_type=MESH,
            )
        )
    halo_copy = pltpu.make_async_remote_copy(
        src_ref=ext.at[:, 0:LANES],
        dst_ref=halo,
        send_sem=halo_sem.at[0],
        recv_sem=halo_sem.at[1],
        device_id={"atoms": before},
        device_id_type=MESH,
    )
    halo_copy.start()
    for copy in copies:
        copy.start()

    halo_copy.wait()
    kind = lax.broadcasted_iota(jnp.int32, (16, LANES), 0)
    lane = lax.broadcasted_iota(jnp.int32, (16, LANES), 1)
    there = (lane < GHOST) & (block < BLOCKS - 1)
    shifted = halo[...] + jnp.where(kind == 3, float(count), 0.0)
    nothing = jnp.where(kind == 3, -1.0e6, 0.0)
    ext[:, count : count + LANES] = jnp.where(there, shifted, nothing)
    share = count // GROUPS
    wide = ext[:, pl.ds(pl.multiple_of(group * share, LANES), 2 * LANES)]
    for unit in range(share // UNIT):
        view = wide if unit == 0 else pltpu.roll(wide, 2 * LANES - unit * UNIT, 1)
        view = view[:, :LANES]
        start = (group * share + unit * UNIT).astype(jnp.float32)
        view = view - jnp.where(kind == 3, start, 0.0)
        win_ref[unit] = jnp.where(lane < WINDOW, view, nothing)

    for at, peer in enumerate(peers):
        pltpu.make_async_remote_copy(
            src_ref=blob.at[peer],
            dst_ref=blob.at[peer],
            send_sem=send_sem.at[at],
            recv_sem=recv_sem.at[peer],
            device_id={"chan": peer},
            device_id_type=MESH,
        ).wait_recv()
    for k in range(GROUPS):
        part = pl.ds(k * SHARE_LANES, SHARE_LANES)
        for t in range(2):
            full_ref[t, :, part, :] = blob[k, 0:128, 64 * t : 64 * t + 64].reshape(
                4, SHARE_LANES, 64
            )
        table_ref[part, :] = blob[k, 128:160, :]
    rd_ref[...] = undense([blob[k, 160:168, :] for k in range(GROUPS)]).reshape(2, 16, LANES)
    cont_ref[...] = undense([blob[k, 168:176, :] for k in range(GROUPS)]).reshape(2, 16, LANES)
    for copy in copies:
        copy.wait_send()


def collect(positions, species, neighbours, labelled, targets, embedding, filters, contract, readout):
    f32 = jnp.float32
    count = positions.shape[1]
    vmem = pl.BlockSpec(memory_space=pltpu.VMEM)
    return pl.pallas_call(
        collect_kernel,
        in_specs=[vmem] * 9,
        out_specs=[vmem] * 5,
        out_shape=[
            jax.ShapeDtypeStruct((count // GROUPS // UNIT, 16, LANES), f32),
            jax.ShapeDtypeStruct((LANES, LANES), f32),
            jax.ShapeDtypeStruct((2, 4, LANES, 64), f32),
            jax.ShapeDtypeStruct((2, 16, LANES), f32),
            jax.ShapeDtypeStruct((2, 16, LANES), f32),
        ],
        scratch_shapes=[
            pltpu.VMEM((GROUPS, BLOB, LANES), f32),
            pltpu.VMEM((32, SHARE_LANES), f32),
            pltpu.VMEM((16, count + LANES), f32),
            pltpu.VMEM((16, LANES), f32),
            pltpu.SemaphoreType.DMA((GROUPS - 1,)),
            pltpu.SemaphoreType.DMA((GROUPS,)),
            pltpu.SemaphoreType.DMA((2,)),
        ],
        compiler_params=pltpu.CompilerParams(collective_id=0, has_side_effects=True),
    )(
        positions,
        species[None],
        neighbours,
        labelled[None],
        targets,
        embedding,
        filters,
        contract,
        readout,
    )


def reduce_kernel(
    force_ref,
    stat_ref,
    g_emb,
    g_bes,
    g_rad,
    g_fil,
    g_con,
    g_mix,
    g_read,
    g_en,
    forces_ref,
    own_ref,
    rest_ref,
    pieces,
    core_in,
    line_out,
    line_in,
    summed,
    sub_in,
    sub_out,
    total,
    quarters,
    windows,
    tail,
    tail_in,
    sems,
    sub_send,
    sub_recv,
    total_send,
    total_recv,
):
    f32 = jnp.float32
    block, group = lax.axis_index("atoms"), lax.axis_index("chan")
    line, core = group // 2, lax.rem(group, 2)
    core_peer = {"chan": line * 2 + (1 - core)}
    line_peer = {"chan": (1 - line) * 2 + core}
    others = [lax.rem(block + offset, BLOCKS) for offset in range(1, BLOCKS)]
    barrier = pltpu.get_barrier_semaphore()
    for peer in [core_peer, line_peer] + [{"atoms": other} for other in others]:
        pl.semaphore_signal(barrier, inc=1, device_id=peer, device_id_type=MESH)

    def copy(source, dest, at, peer):
        return pltpu.make_async_remote_copy(
            src_ref=source,
            dst_ref=dest,
            send_sem=sems.at[2 * at],
            recv_sem=sems.at[2 * at + 1],
            device_id=peer,
            device_id_type=MESH,
        )

    rows = lax.broadcasted_iota(jnp.int32, (16, LANES), 0)
    lanes = lax.broadcasted_iota(jnp.int32, (16, LANES), 1)
    vector = jnp.zeros((1, LANES), f32)
    for t in range(2):
        spread = jnp.broadcast_to(g_en[t], (16, LANES))
        vector = vector + jnp.sum(
            jnp.where(lanes == rows + 16 * t, spread, 0.0), axis=0, keepdims=True
        )
    inner = g_rad[...].reshape(256, 64)
    inner = jnp.concatenate([inner[:128], inner[128:]], axis=1)
    bessel = jnp.concatenate([g_bes[0], g_bes[1]], axis=1)
    for k in range(GROUPS):
        where = (k % 2, k // 2)
        part = pl.ds(k * SHARE_LANES, SHARE_LANES)
        both = [g_fil[t, :, part, :].reshape(LANES, 64) for t in range(2)]
        pieces[(*where, pl.ds(0, 128), slice(None))] = jnp.concatenate(both, axis=1)
        pieces[(*where, pl.ds(128, 32), slice(None))] = g_emb[part, :]
        pieces[(*where, pl.ds(160, 8), slice(None))] = dense(
            lanes_of(g_read[...].reshape(32, LANES), k)
        )
        pieces[(*where, pl.ds(168, 8), slice(None))] = dense(
            lanes_of(g_con[...].reshape(32, LANES), k)
        )
        pieces[(*where, pl.ds(176, 64), slice(None))] = g_mix[k // 2, 64 * (k % 2) : 64 * (k % 2) + 64, :]
        pieces[(*where, pl.ds(240, 32), slice(None))] = inner[32 * k : 32 * k + 32]
        pieces[(*where, pl.ds(272, 8), slice(None))] = jnp.concatenate(
            [bessel[2 * k : 2 * k + 2], vector, stat_ref[0:2, :], jnp.zeros((3, LANES), f32)],
            axis=0,
        )
    windows[line, core] = force_ref[...]
    pl.semaphore_wait(barrier, BLOCKS + 1)

    core_copy = copy(pieces.at[1 - core], core_in, 0, core_peer)
    core_copy.start()
    core_force = copy(windows.at[line, core], windows.at[line, core], 1, core_peer)
    core_force.start()
    core_copy.wait()
    line_out[...] = pieces[core, 1 - line] + core_in[1 - line]
    line_copy = copy(line_out, line_in, 2, line_peer)
    line_copy.start()
    core_force.wait()
    line_force = copy(windows.at[line], windows.at[line], 3, line_peer)
    line_force.start()
    partial = pieces[core, line] + core_in[line]
    line_force.wait()

    lane8 = lax.broadcasted_iota(jnp.int32, (8, LANES), 1)
    canvas = [jnp.zeros((8, LANES), f32)] * 5
    for k in range(8):
        value = windows[k // 4, (k // 2) % 2, k % 2]
        if k % 2 == 0:
            canvas[k // 2] = canvas[k // 2] + value
        else:
            value = pltpu.roll(value, 64, 1)
            canvas[k // 2] = canvas[k // 2] + jnp.where(lane8 >= 64, value, 0.0)
            canvas[k // 2 + 1] = canvas[k // 2 + 1] + jnp.where(lane8 < 64, value, 0.0)
    tail[...] = canvas[4]
    tail_copy = copy(tail, tail_in, 4, {"atoms": others[0]})
    tail_copy.start()

    line_copy.wait()
    summed[7] = jnp.zeros((SUB, LANES), f32)
    partial = partial + line_in[...]
    for k in range(7):
        size = min(SUB, PIECE - k * SUB)
        summed[k, 0:size, :] = partial[k * SUB : k * SUB + size]
        if size < SUB:
            summed[k, size:SUB, :] = jnp.zeros((SUB - size, LANES), f32)

    def sub_copy(other, at):
        return pltpu.make_async_remote_copy(
            src_ref=summed.at[other],
            dst_ref=sub_in.at[block],
            send_sem=sub_send.at[at],
            recv_sem=sub_recv.at[block],
            device_id={"atoms": other},
            device_id_type=MESH,
        )

    def total_copy(other, at):
        return pltpu.make_async_remote_copy(
            src_ref=sub_out,
            dst_ref=total.at[block],
            send_sem=total_send.at[at],
            recv_sem=total_recv.at[block],
            device_id={"atoms": other},
            device_id_type=MESH,
        )

    def arrival(dest, recv, other):
        return pltpu.make_async_remote_copy(
            src_ref=sub_out,
            dst_ref=dest.at[other],
            send_sem=sub_send.at[0],
            recv_sem=recv.at[other],
            device_id={"atoms": other},
            device_id_type=MESH,
        )

    subs = [sub_copy(other, at) for at, other in enumerate(others)]
    for item in subs:
        item.start()
    value = summed[block]
    for other in others:
        arrival(sub_in, sub_recv, other).wait_recv()
        value = value + sub_in[other]
    sub_out[...] = value
    totals = [total_copy(other, at) for at, other in enumerate(others)]
    for item in totals:
        item.start()
    total[block] = value
    tail_copy.wait()
    forces = jnp.concatenate(canvas[:4], axis=1)
    edge = jnp.where((lane8 < GHOST) & (block > 0), tail_in[...], 0.0)
    forces_ref[...] = forces
    forces_ref[:, 0:LANES] = canvas[0] + edge
    for other in others:
        arrival(total, total_recv, other).wait_recv()
    for item in subs + totals:
        item.wait_send()

    everything = total[...].reshape(BLOCKS * SUB, LANES)
    own_ref[...] = everything[:BLOB]
    flat = everything[:274]
    energy_row = everything[274:275]
    squares = jnp.sum(flat * flat, axis=0, keepdims=True)
    squares = squares + (1.0 / GROUPS) * energy_row * energy_row
    squares = jnp.sum(squares, axis=1, keepdims=True)
    quarters[line, core] = everything[BLOB:PIECE]
    quarters[line, core, 101:102, :] = jnp.broadcast_to(squares, (1, LANES))
    line_quarter = copy(quarters.at[line, core], quarters.at[line, core], 5, line_peer)
    line_quarter.start()
    core_quarter = copy(quarters.at[line, core], quarters.at[line, core], 6, core_peer)
    core_quarter.start()
    line_quarter.wait()
    cross_quarter = copy(quarters.at[1 - line, core], quarters.at[1 - line, core], 7, core_peer)
    cross_quarter.start()
    core_quarter.wait()
    cross_quarter.wait()
    rest_ref[...] = quarters[...].reshape(GROUPS, QUARTER, LANES)


def reduce_all(force, stat, grads):
    f32 = jnp.float32
    vmem = pl.BlockSpec(memory_space=pltpu.VMEM)
    dma = pltpu.SemaphoreType.DMA
    return pl.pallas_call(
        reduce_kernel,
        in_specs=[vmem] * 10,
        out_specs=[vmem] * 3,
        out_shape=[
            jax.ShapeDtypeStruct((8, 4 * LANES), f32),
            jax.ShapeDtypeStruct((BLOB, LANES), f32),
            jax.ShapeDtypeStruct((GROUPS, QUARTER, LANES), f32),
        ],
        scratch_shapes=[
            pltpu.VMEM((2, 2, PIECE, LANES), f32),
            pltpu.VMEM((2, PIECE, LANES), f32),
            pltpu.VMEM((PIECE, LANES), f32),
            pltpu.VMEM((PIECE, LANES), f32),
            pltpu.VMEM((BLOCKS, SUB, LANES), f32),
            pltpu.VMEM((BLOCKS, SUB, LANES), f32),
            pltpu.VMEM((SUB, LANES), f32),
            pltpu.VMEM((BLOCKS, SUB, LANES), f32),
            pltpu.VMEM((2, 2, QUARTER, LANES), f32),
            pltpu.VMEM((2, 2, 2, 8, LANES), f32),
            pltpu.VMEM((8, LANES), f32),
            pltpu.VMEM((8, LANES), f32),
            dma((16,)),
            dma((BLOCKS - 1,)),
            dma((BLOCKS,)),
            dma((BLOCKS - 1,)),
            dma((BLOCKS,)),
        ],
        compiler_params=pltpu.CompilerParams(collective_id=1, has_side_effects=True),
    )(force, stat, *grads)


def adam_kernel(*refs):
    forces_in, own_ref, rest_ref = refs[:3]
    weights, moments = refs[3:11], refs[11:27]
    parts_ref, forces_ref, norm_ref = refs[27:30]
    results = refs[30:54]
    scratch = refs[54]
    rest = [rest_ref[k] for k in range(GROUPS)]
    stats = rest[0]
    loss = jnp.sum(stats[99:100], axis=1, keepdims=True)
    count = jnp.sum(stats[100:101], axis=1, keepdims=True)
    inverse = 1.0 / count
    squares = sum(rest[k][101:102, 0:1] for k in range(GROUPS))
    norm = jnp.sqrt(squares) * inverse
    factor = inverse * jnp.minimum(1.0, CLIP_NORM / (norm + 1e-06))
    norm_ref[...] = norm
    two = lax.broadcasted_iota(jnp.int32, (1, 2), 1)
    parts_ref[...] = jnp.where(two == 0, loss, count)
    forces_ref[...] = forces_in[0:3, :]

    def narrow(value):
        return jnp.concatenate([lanes_of(value, k) for k in range(GROUPS)], axis=0)

    fil = [own_ref[0:128, 64 * t : 64 * t + 64].reshape(4, SHARE_LANES, 64) for t in range(2)]
    emb = own_ref[128:160, 0:ELEMENTS]
    read = narrow(own_ref[160:168, :]).reshape(2, 16, SHARE_LANES)
    scratch[...] = narrow(own_ref[168:176, :])
    con = [scratch[0:9, :], scratch[16:25, :]]
    mix = jnp.concatenate([rest[k][0:64] for k in range(GROUPS)], axis=0).reshape(2, LANES, LANES)
    inner = jnp.concatenate([rest[k][64:96] for k in range(GROUPS)], axis=0)
    inner = jnp.concatenate([inner[:, :64], inner[:, 64:]], axis=0).reshape(2, 2, 64, 64)
    bes = jnp.concatenate([rest[k][96:98] for k in range(GROUPS)], axis=0)
    bes = [bes[:, :64], bes[:, 64:]]
    vector = rest[0][98:99]
    vector = jnp.concatenate([vector[:, 0:16], vector[:, 16:32]], axis=0)

    def update(which, gradient, at):
        first, square = moments[2 * which], moments[2 * which + 1]
        weight = weights[which][at]
        clipped = gradient * factor
        moment = BETA_ONE * first[at] + (1.0 - BETA_ONE) * clipped
        second = BETA_TWO * square[at] + (1.0 - BETA_TWO) * clipped * clipped
        corrected_first = moment * (1.0 / (1.0 - BETA_ONE**ADAM_STEP))
        corrected_second = second * (1.0 / (1.0 - BETA_TWO**ADAM_STEP))
        updated = weight - RATE * (
            corrected_first / (jnp.sqrt(corrected_second) + EPSILON) + DECAY * weight
        )
        results[3 * which][at] = updated
        results[3 * which + 1][at] = moment
        results[3 * which + 2][at] = second

    everything = Ellipsis
    update(0, emb, everything)
    for t in range(2):
        update(1, bes[t], t)
        update(3, fil[t], t)
        update(4, con[t], (slice(None), t))
    update(2, inner, everything)
    update(5, mix, everything)
    update(6, read, everything)
    update(7, vector, everything)


def adam(forces, own, rest, weights, moments):
    f32 = jnp.float32
    vmem = pl.BlockSpec(memory_space=pltpu.VMEM)
    shapes = [(1, 2), (3, forces.shape[1]), (1, 1)]
    shapes += [weight.shape for weight in weights for _ in range(3)]
    return pl.pallas_call(
        adam_kernel,
        in_specs=[vmem] * 27,
        out_specs=[vmem] * 27,
        out_shape=[jax.ShapeDtypeStruct(shape, f32) for shape in shapes],
        scratch_shapes=[pltpu.VMEM((32, SHARE_LANES), f32)],
    )(forces, own, rest, *weights, *moments)


def adamw(weight, gradient, first, second, scale):
    clipped = gradient * scale
    moment = BETA_ONE * first + (1.0 - BETA_ONE) * clipped
    second_new = BETA_TWO * second + (1.0 - BETA_TWO) * clipped * clipped
    corrected_first = moment / (1.0 - BETA_ONE**ADAM_STEP)
    corrected_second = second_new / (1.0 - BETA_TWO**ADAM_STEP)
    updated = weight - RATE * (
        corrected_first / (jnp.sqrt(corrected_second) + EPSILON) + DECAY * weight
    )
    return (updated, moment, second_new)


def per_device(
    positions,
    species,
    neighbours,
    labelled,
    target_forces,
    embedding,
    bessel,
    radial,
    filters,
    contract,
    mixing,
    readout,
    energies,
    first_embedding,
    square_embedding,
    first_bessel,
    square_bessel,
    first_radial,
    square_radial,
    first_filters,
    square_filters,
    first_contract,
    square_contract,
    first_mixing,
    square_mixing,
    first_readout,
    square_readout,
    first_energies,
    square_energies,
):
    if (lax.axis_size("atoms"), lax.axis_size("chan")) == (BLOCKS, GROUPS):
        turns = [(1, 0), None, None, (0, 1, 3, 2), (1, 0, 2), None, None, None]

        def turned(value, order):
            return value if order is None else value.transpose(order)

        weights = (embedding, bessel, radial, filters, contract, mixing, readout, energies)
        weights = [turned(value, order) for value, order in zip(weights, turns)]
        moments = (
            first_embedding,
            square_embedding,
            first_bessel,
            square_bessel,
            first_radial,
            square_radial,
            first_filters,
            square_filters,
            first_contract,
            square_contract,
            first_mixing,
            square_mixing,
            first_readout,
            square_readout,
            first_energies,
            square_energies,
        )
        moments = [turned(value, turns[k // 2]) for k, value in enumerate(moments)]
        windows, table, full, cont, read = collect(
            positions,
            species,
            neighbours,
            labelled,
            target_forces,
            weights[0],
            weights[3],
            weights[4],
            readout,
        )
        force, stat, *grads = local_step(
            windows, table, bessel, radial, full, cont, mixing, read, energies
        )
        forces, own, rest = reduce_all(force, stat, grads)
        parts, forces, norm, *results = adam(forces, own, rest, weights, moments)
        results = [turned(value, turns[k // 3]) for k, value in enumerate(results)]
        return tuple([parts.reshape(2), forces, norm.reshape(())] + results)
    f32 = jnp.float32
    atom_count = positions.shape[1]
    local_chan = embedding.shape[1]
    blocks, groups = lax.axis_size("atoms"), lax.axis_size("chan")
    block, group = lax.axis_index("atoms"), lax.axis_index("chan")
    atom_base = block * atom_count
    share = atom_count // groups
    units = share // UNIT

    atom_index = atom_base + jnp.arange(atom_count, dtype=jnp.int32)
    leading = neighbours[0]
    first_atom = jnp.where((leading >= 0) & (leading < atom_index), leading, atom_index)
    packed = jnp.concatenate(
        [
            positions,
            (first_atom - atom_base).astype(f32)[None],
            species.astype(f32)[None],
            labelled.astype(f32)[None],
            jnp.zeros((2, atom_count), f32),
            target_forces,
            jnp.zeros((5, atom_count), f32),
        ],
        axis=0,
    )
    down = [(i + 1, i) for i in range(blocks - 1)]
    halo = lax.ppermute(packed[:, :GHOST], "atoms", down)
    halo_row = jnp.arange(16)[:, None] == 3
    halo = jnp.where(halo_row, jnp.where(block == blocks - 1, -1.0e6, halo + atom_count), halo)
    missing = jnp.where(jnp.arange(16)[:, None] == 3, -1.0e6, 0.0) * jnp.ones((1, LANES), f32)
    extended = jnp.concatenate([packed, halo, missing], axis=1)
    windows = []
    for unit in range(units):
        start = group * share + unit * UNIT
        window = lax.dynamic_slice(extended, (0, start), (16, WINDOW))
        shift = jnp.where(jnp.arange(16)[:, None] == 3, start.astype(f32), 0.0)
        window = window - shift
        windows.append(jnp.concatenate([window, missing[:, : LANES - WINDOW]], axis=1))
    windows = jnp.stack(windows)

    def whole(value):
        return lax.all_gather(value, "chan", axis=value.ndim - 1, tiled=True)

    table = jnp.concatenate(
        [whole(embedding), jnp.zeros((LANES - ELEMENTS, LANES), f32)], axis=0
    ).T
    force, stat, *grads = local_step(
        windows,
        table,
        bessel,
        radial,
        whole(filters).swapaxes(2, 3),
        jnp.pad(whole(contract), ((0, 0), (0, 7), (0, 0))),
        mixing,
        whole(readout),
        energies,
    )
    grad_embed, grad_bessel, grad_radial, grad_filters, grad_contract, grad_mixing = grads[:6]
    grad_readout, grad_vectors = grads[6:]
    grad_embed = grad_embed.T[:ELEMENTS]
    grad_filters = grad_filters.swapaxes(2, 3)
    grad_contract = grad_contract[:, :9]
    grad_vectors = grad_vectors[:, :, 0]

    canvas = jnp.zeros((3, atom_count + LANES), f32)
    for unit in range(units):
        start = group * share + unit * UNIT
        old = lax.dynamic_slice(canvas, (0, start), (3, WINDOW))
        canvas = lax.dynamic_update_slice(canvas, old + force[unit, :3, :WINDOW], (0, start))
    canvas = lax.psum(canvas, "chan")
    up = [(i, i + 1) for i in range(blocks - 1)]
    arrived = lax.ppermute(canvas[:, atom_count : atom_count + GHOST], "atoms", up)
    forces = canvas[:, :atom_count].at[:, :GHOST].add(arrived)

    def split(value):
        return lax.psum_scatter(value, "chan", scatter_dimension=value.ndim - 1, tiled=True)

    grad_embed, grad_filters, grad_contract, grad_readout = lax.psum(
        (split(grad_embed), split(grad_filters), split(grad_contract), split(grad_readout)),
        "atoms",
    )
    grad_bessel, grad_radial, grad_mixing, grad_vectors, loss_sum, label_total = lax.psum(
        (grad_bessel, grad_radial, grad_mixing, grad_vectors, jnp.sum(stat[0]), jnp.sum(stat[1])),
        ("atoms", "chan"),
    )
    gradients = [
        gradient / label_total
        for gradient in (
            grad_embed,
            grad_bessel,
            grad_radial,
            grad_filters,
            grad_contract,
            grad_mixing,
            grad_readout,
            grad_vectors,
        )
    ]
    squares_of = [jnp.sum(gradient * gradient) for gradient in gradients]
    split_squares = squares_of[0] + squares_of[3] + squares_of[4] + squares_of[6]
    whole_squares = squares_of[1] + squares_of[2] + squares_of[5] + squares_of[7]
    grad_norm = jnp.sqrt(lax.psum(split_squares, "chan") + whole_squares)
    scale = jnp.minimum(1.0, CLIP_NORM / (grad_norm + 1e-06))
    weights = (embedding, bessel, radial, filters, contract, mixing, readout, energies)
    firsts = (
        first_embedding,
        first_bessel,
        first_radial,
        first_filters,
        first_contract,
        first_mixing,
        first_readout,
        first_energies,
    )
    squares = (
        square_embedding,
        square_bessel,
        square_radial,
        square_filters,
        square_contract,
        square_mixing,
        square_readout,
        square_energies,
    )
    results = []
    for weight, gradient, first, second in zip(weights, gradients, firsts, squares):
        results.extend(adamw(weight, gradient, first, second, scale))
    return tuple([jnp.stack([loss_sum, label_total]), forces, grad_norm] + results)


def solution(mesh):
    whole = P()
    columns = P(None, "atoms")
    by_weight = [
        P(None, "chan"),
        whole,
        whole,
        P(None, None, None, "chan"),
        P(None, None, "chan"),
        whole,
        P(None, None, "chan"),
        whole,
    ]
    in_specs = [columns, P("atoms"), columns, P("atoms"), columns] + by_weight
    in_specs += [spec for spec in by_weight for _ in range(2)]
    out_specs = [whole, columns, whole] + [spec for spec in by_weight for _ in range(3)]
    return jax.shard_map(
        per_device,
        mesh=mesh,
        in_specs=tuple(in_specs),
        out_specs=tuple(out_specs),
        check_vma=False,
    )
```

```python
import functools
import math

import jax
import jax.numpy as jnp
from jax import lax
from jax.experimental import pallas as pl
from jax.experimental.pallas import tpu as pltpu
from jax.sharding import PartitionSpec as P

ELEMENTS = 89
NBESSEL = 8
GHOST = 8
ADAM_STEP = 10

RCUT = 5.0
SMOOTH = 0.01
NEIGHBOURS_MEAN = 8.0
HUBER_DELTA = 1.0
CLIP_NORM = 0.001
RATE = 0.2
BETA_ONE = 0.9
BETA_TWO = 0.999
EPSILON = 1e-08
DECAY = 0.01

UNIT = 64
WINDOW = UNIT + 16
LANES = 128
DIRECTED = 15
TILES = WINDOW // 8
CHUNK = 80
EDGE_BLOCKS = 2 * CHUNK
FLAT = 8 * CHUNK
DEGREES = [0] + [1] * 3 + [2] * 5 + [3] * 7
EXACT = lax.Precision.HIGHEST

def shapes_of(x, y, z, root_three=math.sqrt(3.0)):
    xx, yy, zz = x * x, y * y, z * z
    xy, yz, zx = x * y, y * z, z * x
    both, less = xx + yy, xx - yy
    wide = 4.0 * zz - both
    return [
        x,
        y,
        z,
        root_three * xy,
        root_three * yz,
        zz - 0.5 * both,
        root_three * zx,
        (0.5 * root_three) * less,
        math.sqrt(5.0 / 8.0) * y * (3.0 * xx - yy),
        math.sqrt(15.0) * xy * z,
        math.sqrt(3.0 / 8.0) * y * wide,
        z * (zz - 1.5 * both),
        math.sqrt(3.0 / 8.0) * x * wide,
        (0.5 * math.sqrt(15.0)) * z * less,
        math.sqrt(5.0 / 8.0) * x * (xx - 3.0 * yy),
    ]


def radius_of(x, y, z, valid):
    distance = jnp.sqrt((x * x + y * y + z * z) * (RCUT * RCUT) + SMOOTH)
    scaled = distance * (1.0 / RCUT)
    square = scaled * scaled
    fifth = square * square * scaled
    envelope = 1.0 - fifth * (21.0 - 35.0 * scaled + 15.0 * square)
    envelope = jnp.where(scaled < 1.0, envelope, 0.0) * (valid * (1.0 / NEIGHBOURS_MEAN))
    return distance, envelope


def halves_of(value):
    high = value.astype(jnp.bfloat16)
    low = (value - high.astype(jnp.float32)).astype(jnp.bfloat16)
    return high, low


def dot(left, right, left_dim, right_dim):
    return lax.dot_general(
        left,
        right,
        (((left_dim,), (right_dim,)), ((), ())),
        preferred_element_type=jnp.float32,
    )


def fine(left, right, left_dim, right_dim):
    left_high, left_low = halves_of(left)
    right_high, right_low = halves_of(right)
    return (
        dot(left_high, right_high, left_dim, right_dim)
        + dot(left_low, right_high, left_dim, right_dim)
        + dot(left_high, right_low, left_dim, right_dim)
    )


def fine_rows(left, right):
    rows = left.shape[0]
    left_high, left_low = halves_of(left)
    right_high, right_low = halves_of(right)
    both = dot(jnp.concatenate([left_high, left_low], axis=0), right_high, 1, 1)
    return both[:rows] + both[rows:] + dot(left_high, right_low, 1, 1)


def triple(value):
    high, low = halves_of(value)
    return jnp.concatenate([high, high, low], axis=0)


def add(total, term):
    return term if total is None else total + term


def members(degree):
    return range(degree * degree, (degree + 1) ** 2)


def thirds(values):
    parts = []
    for value in values:
        for _ in range(3):
            part = value.astype(jnp.bfloat16).astype(jnp.float32)
            parts.append(part)
            value = value - part
    parts += [jnp.zeros_like(parts[0])] * (16 - len(parts))
    return jnp.concatenate(parts, axis=0).astype(jnp.bfloat16)


def joined(rows, count):
    return [
        rows[3 * k : 3 * k + 1] + rows[3 * k + 1 : 3 * k + 2] + rows[3 * k + 2 : 3 * k + 3]
        for k in range(count)
    ]


def sine_cosine(angle):
    half = 0.5 * angle - (0.5 * math.pi)
    square = half * half
    sine = cosine = 0.0
    for k in range(6, -1, -1):
        cosine = cosine * square + (-1) ** k / math.factorial(2 * k)
        if k < 6:
            sine = sine * square + (-1) ** k / math.factorial(2 * k + 1)
    sine = sine * half
    return -2.0 * sine * cosine, 2.0 * sine * sine - 1.0


def step_kernel(
    win_ref,
    emb_ref,
    bes_ref,
    rad_ref,
    fil_ref,
    con_ref,
    mix_ref,
    read_ref,
    en_ref,
    force_ref,
    stat_ref,
    g_emb,
    g_bes,
    g_rad,
    g_fil,
    g_con,
    g_mix,
    g_read,
    g_en,
    begin_ref,
    yy,
    dyy,
    feats,
    dfeats,
    fj,
    dfj,
    fdir,
    dfdir,
    fb,
    fjb,
    wb,
    amat,
    damat,
    msg,
    msgb,
    dmsg,
    zs,
    sg,
    dz,
    hidb,
    hidu,
    bess,
    rows_ref,
    turn_ref,
    hot_j,
    hot_d,
    turned_j,
    turned_d,
    barrow,
    gcon,
    tab_w,
    bes_w,
    bes_b,
    rad_w,
    rad_b,
    fil_w,
    fil_b,
    g_tab,
    g_wide,
):
    f32, bf16, i32 = jnp.float32, jnp.bfloat16, jnp.int32
    gsum = dfj

    @pl.when(pl.program_id(0) == 0)
    def _():
        for ref in (g_tab, g_wide, g_bes, g_rad, g_con, g_mix, g_read, g_en, stat_ref):
            ref[...] = jnp.zeros_like(ref)
        for ref in (feats, dfeats, msg, dmsg, fjb, gsum):
            ref[...] = jnp.zeros_like(ref)

        def clear(block, carry):
            fb[0, block] = jnp.zeros((4, 8, LANES), f32)
            fb[1, block] = jnp.zeros((4, 8, LANES), f32)
            return carry

        lax.fori_loop(0, EDGE_BLOCKS, clear, 0)
        tab_w[...] = jnp.concatenate(list(halves_of(emb_ref[...].T)), axis=0)
        for t in range(2):
            high, low = [value.astype(f32) for value in halves_of(bes_ref[t])]
            bes_w[t] = jnp.concatenate([high, low, high, jnp.zeros_like(high)], axis=0).T.astype(
                bf16
            )
            bes_b[t] = jnp.concatenate([high, low, high], axis=1).astype(bf16)
            for depth in range(2):
                high, low = [value.astype(f32) for value in halves_of(rad_ref[t, depth])]
                rad_b[t, depth] = jnp.concatenate([high, low, high], axis=1).astype(bf16)
                rad_w[t, depth] = jnp.concatenate([high, low, high], axis=0).T.astype(bf16)
            high, low = halves_of(fil_ref[t].reshape(4 * LANES, 64).T)
            fil_w[t] = jnp.concatenate([high, low, high], axis=0)
            fil_b[t] = jnp.concatenate([high, low], axis=0)

    def both_sides(value):
        wide = jnp.broadcast_to(value, (16, LANES))
        back = pltpu.roll(wide, 1, 1, stride=1, stride_axis=0)
        ahead = pltpu.roll(wide, 113, 1, stride=1, stride_axis=0)
        return back, ahead

    first = win_ref[0, 3:4, :]
    own = jnp.where((first >= 0.0) & (first < float(UNIT)), 1.0, 0.0)
    slot_row = lax.broadcasted_iota(i32, (16, LANES), 0)
    back_first, ahead_first = both_sides(first)
    same = (slot_row < DIRECTED) & ((back_first == first) | (ahead_first == first))
    count = jnp.sum(jnp.where(same, 1.0, 0.0), axis=0, keepdims=True) * own

    line = lax.broadcasted_iota(i32, (LANES, LANES), 0)
    place = lax.broadcasted_iota(i32, (LANES, LANES), 1)
    key = jnp.broadcast_to(count + own, (LANES, LANES))
    other = key.T
    ahead_of = (other > key) | ((other == key) & (line < place))
    rank = jnp.sum(jnp.where(ahead_of, 1.0, 0.0), axis=0, keepdims=True)
    order_t = jnp.where(line.astype(f32) == rank, 1.0, 0.0).astype(bf16)
    index = lax.broadcasted_iota(i32, (1, LANES), 1).astype(f32)
    wide = jnp.concatenate(
        [win_ref[0], count, index, jnp.zeros((14, LANES), f32)], axis=0
    )
    high, middle = halves_of(wide)
    low = (wide - high.astype(f32) - middle.astype(f32)).astype(bf16)
    moved = dot(jnp.concatenate([high, middle, low], axis=0), order_t, 1, 1)
    turn_ref[0:32, :] = moved[0:32] + moved[32:64] + moved[64:96]

    def row(index):
        return turn_ref[index : index + 1, :]

    first, species, labelled = row(3), row(4), row(5)
    count, atom_id = row(16), row(17)
    own = jnp.where((first >= 0.0) & (first < float(UNIT)), 1.0, 0.0)
    atom_names = jnp.broadcast_to(atom_id, (LANES, LANES)).T[:, 0:1]

    lane_row = lax.broadcasted_iota(i32, (1, LANES), 1)
    used = lax.shift_right_logical(jnp.max(jnp.where(own > 0.0, lane_row, 0)) + 8, 3)
    begins, pairs = [jnp.int32(0)], []
    begin_ref[0] = 0
    for tile in range(TILES):
        mine = (lane_row >= 8 * tile) & (lane_row < 8 * tile + 8)
        most = jnp.max(jnp.where(mine, count, 0.0)).astype(i32)
        pairs.append(lax.shift_right_logical(most + 1, 1))
        begins.append(begins[-1] + pairs[-1])
        begin_ref[tile + 1] = begins[-1]
    total = begins[-1]
    chunks = jnp.where(2 * total > CHUNK, 2, 1)

    def each_chunk(body):
        def step(chunk, carry):
            body(chunk, pl.ds(chunk * CHUNK, CHUNK))
            return carry

        lax.fori_loop(0, chunks, step, 0)

    def each_tile(body):
        def step(tile, carry):
            body(tile, pl.ds(pl.multiple_of(tile * 8, 8), 8))
            return carry

        lax.fori_loop(0, used, step, 0)

    def each_block(tile, body, carry):
        return lax.fori_loop(
            begin_ref[tile],
            begin_ref[tile + 1],
            lambda pair, held: body(2 * pair + 1, body(2 * pair, held)),
            carry,
        )

    def each_edge_block(body):
        def step(four, carry):
            for k in range(4):
                body(4 * four + k)
            return carry

        lax.fori_loop(0, lax.shift_right_logical(2 * total + 3, 2), step, 0)

    def natural(values):
        wide = jnp.concatenate(
            [jnp.broadcast_to(value, (LANES, LANES)).T for value in values], axis=1
        )
        high, middle = halves_of(wide)
        low = (wide - high.astype(f32) - middle.astype(f32)).astype(bf16)
        return jnp.concatenate([high, middle], axis=0), low

    def spread(chunk, blocks, parts, dest):
        left = turned_d[chunk]
        wide = dot(jnp.concatenate([left, left], axis=1), parts[0], 1, 0) + dot(
            left, parts[1], 1, 0
        )
        for k in range(3):
            dest[blocks, k] = wide[:, k * LANES : (k + 1) * LANES].reshape(CHUNK, 8, LANES)

    def layer_in(t, depth, value):
        if depth == 0:
            high, low = [part.astype(f32) for part in halves_of(value)]
            wide = jnp.concatenate([high, high, low, jnp.zeros_like(high)], axis=0).astype(bf16)
            return dot(bes_w[t], wide, 1, 0)
        return dot(rad_w[t, depth - 1], triple(value), 1, 0)

    def layer_back(t, depth, value):
        weight = bes_b[t] if depth == 0 else rad_b[t, depth - 1]
        return dot(weight, triple(value), 1, 0)

    def parts_of(t, chunk, depth):
        z, sig = zs[t, chunk, depth], sg[t, chunk, depth]
        h, rest = z * sig, 1.0 - sig
        return h, sig + h * rest, sig * rest * (2.0 + z - 2.0 * h)

    def sigmoid(z):
        return 0.5 * jnp.tanh(0.5 * z) + 0.5

    def filters_to(t, hidden, blocks, dest):
        wide = dot(triple(hidden), fil_w[t], 0, 0)
        for degree in range(4):
            dest[t, blocks, degree] = wide[:, degree * LANES : (degree + 1) * LANES].reshape(
                CHUNK, 8, LANES
            )

    def filters_back(t, high, low):
        both = dot(fil_b[t], high, 1, 1)
        return both[:64] + both[64:] + dot(fil_b[t, 0:64, :], low, 1, 1)

    def filters_grad(hidden, wide_high, wide_low):
        high, low = halves_of(hidden)
        both = dot(jnp.concatenate([high, low], axis=0), wide_high, 1, 0)
        return both[:64] + both[64:] + dot(high, wide_low, 1, 0)

    def filter_bars(t, blocks):
        parts = [
            halves_of(fb[t, blocks, degree].reshape(FLAT, LANES)) for degree in range(4)
        ]
        return [jnp.concatenate([part[k] for part in parts], axis=1) for k in range(2)]

    position_parts = natural([row(k) * (1.0 / RCUT) for k in range(3)])
    position_rows = thirds([row(k) * (1.0 / RCUT) for k in range(3)])
    atom_rows = jnp.concatenate(
        [first * own, count, atom_id, jnp.zeros((13, LANES), f32)], axis=0
    ).astype(bf16)
    begin_blocks = [2 * value for value in begins]

    def geometry(chunk, blocks):
        edge = lax.broadcasted_iota(i32, (1, FLAT), 1) + chunk * FLAT
        block = lax.shift_right_logical(edge, 3)
        tile = jnp.zeros_like(edge)
        base = jnp.zeros_like(edge)
        for k in range(1, TILES):
            past = block >= begin_blocks[k]
            tile = tile + jnp.where(past, 1, 0)
            base = base + jnp.where(past, 2 * pairs[k - 1], 0)
        atom = (tile * 8 + (edge & 7)).astype(f32)
        number = (block - base).astype(f32)
        atom_column = lax.broadcasted_iota(i32, (LANES, FLAT), 0).astype(f32)
        hot = jnp.where(atom_column == atom, 1.0, 0.0).astype(bf16)
        known = dot(atom_rows, hot, 1, 0)
        there = known[0:1] + number
        there = there + jnp.where(there >= known[2:3], 1.0, 0.0)
        valid = jnp.where(number < known[1:2], 1.0, 0.0)
        hot = jnp.where(atom_names == jnp.where(valid > 0.0, there, -1.0), 1.0, 0.0)
        difference = hot - jnp.where(
            atom_column == jnp.where(valid > 0.0, atom, -1.0), 1.0, 0.0
        )
        hot_j[chunk] = hot.astype(bf16)
        hot_d[chunk] = difference.astype(bf16)
        turned_j[chunk] = hot.T.astype(bf16)
        turned_d[chunk] = difference.T.astype(bf16)
        spread(chunk, blocks, position_parts, yy)
        rel = joined(dot(position_rows, hot_d[chunk], 1, 0), 3)
        distance, envelope = radius_of(*rel, valid)
        for k, value in enumerate(rel + [valid, envelope]):
            rows_ref[chunk, k : k + 1, :] = value
        sine, cosine = sine_cosine(distance * (math.pi / RCUT))
        sines, cosines = [sine], [cosine]
        for k in range(1, NBESSEL):
            before = (0.0, 1.0) if k == 1 else (sines[k - 2], cosines[k - 2])
            sines.append(2.0 * cosine * sines[-1] - before[0])
            cosines.append(2.0 * cosine * cosines[-1] - before[1])
        inverse = 1.0 / distance
        root = math.sqrt(2.0 / RCUT)
        for k in range(NBESSEL):
            basis = root * sines[k] * inverse
            bess[chunk, 0, k : k + 1, :] = basis
            bess[chunk, 1, k : k + 1, :] = (
                root * ((k + 1) * math.pi / RCUT) * cosines[k] - basis
            ) * inverse
        values = [bess[chunk, 0]] * 2
        for depth in range(3):
            for t in range(2):
                z = layer_in(t, depth, values[t])
                sig = sigmoid(z)
                zs[t, chunk, depth] = z
                sg[t, chunk, depth] = sig
                values[t] = z * sig
        for t in range(2):
            filters_to(t, values[t] * envelope, blocks, fdir)

    each_chunk(geometry)

    def point_shapes(block):
        values = shapes_of(*[yy[block, k] for k in range(3)])
        for k in range(3, 15):
            yy[block, k] = values[k]

    each_edge_block(point_shapes)

    def gather_from(value, dest):
        both = jnp.concatenate(list(halves_of(value)), axis=1)

        def body(chunk, blocks):
            wide = dot(turned_j[chunk], both, 1, 0)
            dest[blocks] = (wide[:, :LANES] + wide[:, LANES:]).reshape(CHUNK, 8, LANES)

        each_chunk(body)

    def scattered(chunk, blocks):
        high, low = halves_of(fjb[blocks].reshape(FLAT, LANES))
        return dot(hot_j[chunk], high, 1, 0) + dot(hot_j[chunk], low, 1, 0)

    def contract_rows(t):
        return [con_ref[t, b : b + 1, :] for b in range(9)]

    def powers_of(a):
        return [sum(a[lm] * a[lm] for lm in members(degree)) for degree in (1, 2, 3)]

    def alpha_of(c, s, p):
        return (
            c[0] + 2.0 * c[1] * s + 3.0 * c[5] * s * s + c[6] * p[0] + c[7] * p[1] + c[8] * p[2]
        )

    def beta_of(c, s):
        return [c[2 + i] + c[6 + i] * s for i in range(3)]

    zeros16 = tuple(jnp.zeros((8, LANES), f32) for _ in range(16))

    def forward_messages(t):
        def body(tile, at):
            def edges(block, a):
                a = list(a)
                there = fj[t, block]
                for degree in range(4):
                    w = fdir[t, block, degree] * there
                    if degree == 0:
                        a[0] = a[0] + w
                        continue
                    for lm in members(degree):
                        a[lm] = a[lm] + yy[block, lm - 1] * w
                return tuple(a)

            a = each_block(tile, edges, zeros16)
            for lm in range(16):
                amat[t, tile, lm] = a[lm]
            c = contract_rows(t)
            s, p = a[0], powers_of(a)
            value = s * (c[0] + s * (c[1] + s * c[5]) + c[6] * p[0] + c[7] * p[1] + c[8] * p[2])
            msg[t, at, :] = value + c[2] * p[0] + c[3] * p[1] + c[4] * p[2]

        each_tile(body)

    def backward_messages(t):
        lane = lax.broadcasted_iota(i32, (8, LANES), 1)

        def body(tile, at):
            a = [amat[t, tile, lm] for lm in range(16)]
            c = contract_rows(t)
            up = msgb[t, at, :]
            s, p = a[0], powers_of(a)
            beta = beta_of(c, s)
            twice = [None] + [2.0 * up * beta[i] for i in range(3)]
            ab = [up * alpha_of(c, s, p)] + [twice[DEGREES[lm]] * a[lm] for lm in range(1, 16)]

            def edges(block, carry):
                there = fj[t, block]
                back = None
                turned = gsum[block] if t == 0 else jnp.zeros((8, LANES), f32)
                for degree in range(4):
                    weight = fdir[t, block, degree]
                    bar = ab[0] if degree == 0 else None
                    if degree > 0:
                        w = weight * there
                        for lm in members(degree):
                            bar = add(bar, yy[block, lm - 1] * ab[lm])
                            reduced = jnp.sum(w * ab[lm], axis=1, keepdims=True)
                            if t == 0:
                                reduced = turned + reduced
                            turned = jnp.where(lane == lm, reduced, turned)
                        wb[t, block, degree - 1] = bar
                    fb[t, block, degree] = bar * there
                    if t > 0:
                        back = add(back, bar * weight)
                if t > 0:
                    fjb[block] = back
                gsum[block] = turned
                return carry

            each_block(tile, edges, 0)

        each_tile(body)

    def tangent_messages(t):
        def body(tile, at):
            def edges(block, da):
                da = list(da)
                there = fj[t, block]
                for degree in range(4):
                    weight = fdir[t, block, degree]
                    dw = dfdir[t, block, degree] * there
                    if t > 0:
                        dw = dw + weight * dfj[block]
                    if degree == 0:
                        da[0] = da[0] + dw
                        continue
                    w = weight * there
                    for lm in members(degree):
                        da[lm] = da[lm] + (yy[block, lm - 1] * dw + dyy[block, lm - 1] * w)
                return tuple(da)

            da = each_block(tile, edges, zeros16)
            a = [amat[t, tile, lm] for lm in range(16)]
            for lm in range(16):
                damat[t, tile, lm] = da[lm]
            c = contract_rows(t)
            s, p = a[0], powers_of(a)
            beta = beta_of(c, s)
            value = alpha_of(c, s, p) * da[0]
            for i in range(3):
                value = value + beta[i] * (2.0 * sum(a[lm] * da[lm] for lm in members(i + 1)))
            dmsg[t, at, :] = value

        each_tile(body)

    def tangent_backward(t):
        gcon[...] = jnp.zeros_like(gcon)

        def body(tile, at):
            a = [amat[t, tile, lm] for lm in range(16)]
            da = [damat[t, tile, lm] for lm in range(16)]
            c = contract_rows(t)
            up, dup = msgb[t, at, :], msgb[2, at, :]
            s, ds, p = a[0], da[0], powers_of(a)
            dp = [2.0 * sum(a[lm] * da[lm] for lm in members(degree)) for degree in (1, 2, 3)]
            alpha, beta = alpha_of(c, s, p), beta_of(c, s)
            dalpha = (
                2.0 * c[1] * ds
                + 6.0 * c[5] * s * ds
                + c[6] * dp[0]
                + c[7] * dp[1]
                + c[8] * dp[2]
            )
            pb = [None] + [2.0 * up * beta[i] for i in range(3)]
            dpb = [None] + [2.0 * (dup * beta[i] + up * c[6 + i] * ds) for i in range(3)]
            ab = [up * alpha] + [pb[DEGREES[lm]] * a[lm] for lm in range(1, 16)]
            dab = [dup * alpha + up * dalpha] + [
                pb[DEGREES[lm]] * da[lm] + dpb[DEGREES[lm]] * a[lm] for lm in range(1, 16)
            ]
            products = [(s, ds), (s * s, 2.0 * s * ds)]
            products += [(p[i], dp[i]) for i in range(3)]
            products += [(s * s * s, 3.0 * s * s * ds)]
            products += [(s * p[i], ds * p[i] + s * dp[i]) for i in range(3)]
            for b, (point, direction) in enumerate(products):
                gcon[b] += dup * point + up * direction

            def edges(block, carry):
                there = fj[t, block]
                back = None
                for degree in range(4):
                    if degree == 0:
                        was, bar = ab[0], dab[0]
                    else:
                        was, bar = wb[t, block, degree - 1], None
                        for lm in members(degree):
                            bar = add(
                                bar, yy[block, lm - 1] * dab[lm] + dyy[block, lm - 1] * ab[lm]
                            )
                    value = bar * there
                    if t > 0:
                        value = value + was * dfj[block]
                    fb[t, block, degree] = value
                    back = add(
                        back, bar * fdir[t, block, degree] + was * dfdir[t, block, degree]
                    )
                fjb[block] = back
                return carry

            each_block(tile, edges, 0)

        each_tile(body)
        for b in range(9):
            g_con[t, b : b + 1, :] -= jnp.sum(gcon[b], axis=0, keepdims=True)

    inner = slice(0, WINDOW)
    hot_element = jnp.where(
        lax.broadcasted_iota(i32, (LANES, LANES), 0).astype(f32) == species, 1.0, 0.0
    )[:, :WINDOW].astype(bf16)
    own_lane = own[:, :WINDOW]
    feats[0, inner, :] = dot(
        jnp.concatenate([hot_element, hot_element], axis=0), tab_w[...], 0, 0
    )
    sums = []
    for t in range(2):
        gather_from(feats[t], fj.at[t])
        forward_messages(t)
        feats[t + 1, inner, :] = feats[t, inner, :] + fine(msg[t], mix_ref[t], 1, 1)
        sums.append(fine(read_ref[t], feats[t + 1, inner, :], 1, 1))

    diagonal = lax.broadcasted_iota(i32, (16, 16), 0) == lax.broadcasted_iota(i32, (16, 16), 1)
    sum_bars, feat_bars, slopes_read, curves_read = [], [None, None], [], []
    for t in range(2):
        vector = jnp.sum(
            jnp.where(diagonal, jnp.broadcast_to(en_ref[t : t + 1, :], (16, 16)), 0.0),
            axis=1,
            keepdims=True,
        )
        sig = sigmoid(sums[t])
        h, rest = sums[t] * sig, 1.0 - sig
        slopes_read.append(own_lane * (sig + h * rest))
        curves_read.append(own_lane * vector * (sig * rest * (2.0 + sums[t] - 2.0 * h)))
        sum_bars.append(vector * slopes_read[t])

    def scatter_all():
        msgb[3] = jnp.zeros((WINDOW, LANES), f32)

        def body(chunk, blocks):
            msgb[3] += scattered(chunk, blocks)[:WINDOW]

        each_chunk(body)
        return msgb[3]

    feat_bar = None
    for t in (1, 0):
        feat_bar = add(feat_bar, fine(sum_bars[t], read_ref[t], 0, 0))
        feat_bars[t] = feat_bar
        msgb[t] = fine(feat_bar, mix_ref[t], 1, 0)
        backward_messages(t)
        if t > 0:
            feat_bar = feat_bar + scatter_all()

    barrow[...] = jnp.zeros_like(barrow)

    def geometry_back(chunk, blocks):
        envelope = rows_ref[chunk, 4:5, :]
        values, envelope_bar, distance_bar = [], None, None
        for t in range(2):
            high, low = filter_bars(t, blocks)
            value = filters_back(t, high, low)
            hidu[t, chunk] = value
            h, _, _ = parts_of(t, chunk, 2)
            envelope_bar = add(envelope_bar, jnp.sum(value * h, axis=0, keepdims=True))
            values.append(value * envelope)
        for depth in (2, 1, 0):
            for t in range(2):
                hidb[t, chunk, depth] = values[t]
                _, slope, _ = parts_of(t, chunk, depth)
                values[t] = layer_back(t, depth, values[t] * slope)
        distance_bar = jnp.sum((values[0] + values[1]) * bess[chunk, 1], axis=0, keepdims=True)
        rel = tuple(rows_ref[chunk, k : k + 1, :] for k in range(3))
        valid = rows_ref[chunk, 3:4, :]
        _, radius_pull = jax.vjp(lambda a, b, c: radius_of(a, b, c, valid), *rel)
        radius_bars = radius_pull((distance_bar, envelope_bar))
        turned = gsum[blocks].reshape(FLAT, LANES).T
        _, shapes_pull = jax.vjp(shapes_of, *rel)
        shape_bars = shapes_pull([turned[lm : lm + 1, :] for lm in range(1, 16)])
        bars = [
            jnp.where(valid > 0.0, radius_bars[k] + shape_bars[k], 0.0) * (1.0 / RCUT)
            for k in range(3)
        ]
        for k, value in enumerate(joined(dot(thirds(bars), hot_d[chunk], 1, 1), 3)):
            barrow[k : k + 1, :] += value

    each_chunk(geometry_back)

    slopes = []
    loss_row = jnp.zeros((1, LANES), f32)
    weight_row = own * labelled
    for k in range(3):
        force = -barrow[k : k + 1, :]
        diff = force - row(8 + k)
        magnitude = jnp.abs(diff)
        huber = jnp.where(
            magnitude <= HUBER_DELTA,
            0.5 * diff * diff,
            HUBER_DELTA * (magnitude - 0.5 * HUBER_DELTA),
        )
        loss_row = loss_row + weight_row * huber
        slopes.append(weight_row * jnp.clip(diff, -HUBER_DELTA, HUBER_DELTA) * (1.0 / RCUT))
    unordered = dot(thirds([-barrow[k : k + 1, :] for k in range(3)]), order_t, 1, 0)
    for k, value in enumerate(joined(unordered, 3)):
        force_ref[0, k : k + 1, :] = value
    force_ref[0, 3:8, :] = jnp.zeros((5, LANES), f32)
    stat_ref[0:1, :] += loss_row
    stat_ref[1:2, :] += weight_row

    slope_parts = natural(slopes)
    slope_rows = thirds(slopes)

    def geometry_tangent(chunk, blocks):
        spread(chunk, blocks, slope_parts, dyy)
        rel = tuple(rows_ref[chunk, k : k + 1, :] for k in range(3))
        valid, envelope = rows_ref[chunk, 3:4, :], rows_ref[chunk, 4:5, :]
        drel = tuple(joined(dot(slope_rows, hot_d[chunk], 1, 0), 3))
        _, (ddistance, denvelope) = jax.jvp(
            lambda a, b, c: radius_of(a, b, c, valid), rel, drel
        )
        rows_ref[chunk, 5:6, :] = denvelope
        dbasis = bess[chunk, 1] * ddistance
        bess[chunk, 2] = dbasis
        values = [dbasis] * 2
        for depth in range(3):
            for t in range(2):
                z = layer_in(t, depth, values[t])
                dz[t, chunk, depth] = z
                h, slope, _ = parts_of(t, chunk, depth)
                values[t] = slope * z
                if depth == 2:
                    values[t] = values[t] * envelope + h * denvelope
        for t in range(2):
            filters_to(t, values[t], blocks, dfdir)
            high, low = filter_bars(t, blocks)
            g_wide[t] += filters_grad(values[t], high, low)

    each_chunk(geometry_tangent)

    def tangent_shapes(block):
        point = tuple(yy[block, k] for k in range(3))
        direction = tuple(dyy[block, k] for k in range(3))
        _, values = jax.jvp(shapes_of, point, direction)
        for k in range(3, 15):
            dyy[block, k] = values[k]

    each_edge_block(tangent_shapes)

    dsums = []
    dfeat = None
    for t in range(2):
        if t > 0:
            dfeats[inner, :] = dfeat
            gather_from(dfeats[...], dfj)
        tangent_messages(t)
        dfeat = add(dfeat, fine(dmsg[t], mix_ref[t], 1, 1))
        dsums.append((fine(read_ref[t], dfeat, 1, 1), dfeat))

    dfeat_bar = None
    for t in (1, 0):
        dsum, dfeat_after = dsums[t]
        g_en[t] -= jnp.sum(slopes_read[t] * dsum, axis=1, keepdims=True)
        dsum_bar = curves_read[t] * dsum
        g_read[t] -= fine(dsum_bar, feats[t + 1, inner, :], 1, 0) + fine(
            sum_bars[t], dfeat_after, 1, 0
        )
        dfeat_bar = add(dfeat_bar, fine(dsum_bar, read_ref[t], 0, 0))
        g_mix[t] -= fine(dfeat_bar, msg[t], 0, 0) + fine(feat_bars[t], dmsg[t], 0, 0)
        msgb[2] = fine(dfeat_bar, mix_ref[t], 1, 0)
        tangent_backward(t)
        dfeat_bar = dfeat_bar + scatter_all()
    high, low = halves_of(dfeat_bar)
    g_tab[...] += dot(hot_element, high, 1, 0) + dot(hot_element, low, 1, 0)

    def network_grads(chunk, blocks):
        envelope, denvelope = rows_ref[chunk, 4:5, :], rows_ref[chunk, 5:6, :]
        values = []
        for t in range(2):
            high, low = filter_bars(t, blocks)
            h, _, _ = parts_of(t, chunk, 2)
            g_wide[t] += filters_grad(h * envelope, high, low)
            values.append(filters_back(t, high, low) * envelope + hidu[t, chunk] * denvelope)
        for depth in (2, 1, 0):
            for t in range(2):
                _, slope, curve = parts_of(t, chunk, depth)
                bar = hidb[t, chunk, depth]
                value = values[t] * slope + bar * curve * dz[t, chunk, depth]
                if depth == 0:
                    before, dbefore = bess[chunk, 0], bess[chunk, 2]
                else:
                    before, slope_before, _ = parts_of(t, chunk, depth - 1)
                    dbefore = slope_before * dz[t, chunk, depth - 1]
                grad = fine_rows(
                    jnp.concatenate([dbefore, before], axis=1),
                    jnp.concatenate([bar * slope, value], axis=1),
                )
                if depth == 0:
                    g_bes[t] -= grad
                else:
                    g_rad[t, depth - 1] -= grad
                    values[t] = layer_back(t, depth, value)

    each_chunk(network_grads)

    @pl.when(pl.program_id(0) == pl.num_programs(0) - 1)
    def _():
        g_emb[...] = -g_tab[...].T
        for t in range(2):
            g_fil[t] = -g_wide[t].T.reshape(4, LANES, 64)


def local_step(windows, table, bessel, radial, filters, contract, mixing, readout, energies):
    units = windows.shape[0]
    f32, bf16 = jnp.float32, jnp.bfloat16
    vmem = pl.BlockSpec(memory_space=pltpu.VMEM)

    def scratch(*shape):
        return pltpu.VMEM(shape, f32)

    def short(*shape):
        return pltpu.VMEM(shape, bf16)

    def out(*shape):
        return jax.ShapeDtypeStruct(shape, f32)

    edges, parts = EDGE_BLOCKS, EDGE_BLOCKS // CHUNK
    return pl.pallas_call(
        step_kernel,
        grid=(units,),
        in_specs=[pl.BlockSpec((1, 16, LANES), lambda i: (i, 0, 0))] + [vmem] * 8,
        out_specs=[pl.BlockSpec((1, 8, LANES), lambda i: (i, 0, 0))] + [vmem] * 9,
        out_shape=[
            out(units, 8, LANES),
            out(8, LANES),
            out(LANES, LANES),
            out(2, NBESSEL, 64),
            out(2, 2, 64, 64),
            out(2, 4, LANES, 64),
            out(2, 16, LANES),
            out(2, LANES, LANES),
            out(2, 16, LANES),
            out(2, 16, 1),
        ],
        scratch_shapes=[
            pltpu.SMEM((16,), jnp.int32),
            scratch(edges, 15, 8, LANES),
            scratch(edges, 15, 8, LANES),
            scratch(3, LANES, LANES),
            scratch(LANES, LANES),
            scratch(2, edges, 8, LANES),
            scratch(edges, 8, LANES),
            scratch(2, edges, 4, 8, LANES),
            scratch(2, edges, 4, 8, LANES),
            scratch(2, edges, 4, 8, LANES),
            scratch(edges, 8, LANES),
            scratch(2, edges, 3, 8, LANES),
            scratch(2, TILES, 16, 8, LANES),
            scratch(2, TILES, 16, 8, LANES),
            scratch(2, WINDOW, LANES),
            scratch(4, WINDOW, LANES),
            scratch(2, WINDOW, LANES),
            scratch(2, parts, 3, 64, FLAT),
            scratch(2, parts, 3, 64, FLAT),
            scratch(2, parts, 3, 64, FLAT),
            scratch(2, parts, 3, 64, FLAT),
            scratch(2, parts, 64, FLAT),
            scratch(parts, 3, NBESSEL, FLAT),
            scratch(parts, 8, FLAT),
            scratch(LANES, LANES),
            short(parts, LANES, FLAT),
            short(parts, LANES, FLAT),
            short(parts, FLAT, LANES),
            short(parts, FLAT, LANES),
            scratch(8, LANES),
            scratch(9, 8, LANES),
            short(2 * LANES, LANES),
            short(2, 64, 4 * NBESSEL),
            short(2, NBESSEL, 192),
            short(2, 2, 64, 192),
            short(2, 2, 64, 192),
            short(2, 192, 4 * LANES),
            short(2, LANES, 4 * LANES),
            scratch(LANES, LANES),
            scratch(2, 64, 4 * LANES),
        ],
        compiler_params=pltpu.CompilerParams(vmem_limit_bytes=60 * 1024 * 1024),
    )(windows, table, bessel, radial, filters, contract, mixing, readout, energies)


MESH = pl.DeviceIdType.MESH
GROUPS = 4
BLOCKS = 8
SHARE_LANES = LANES // GROUPS
BLOB = 176
PIECE = 280
SUB = 40
QUARTER = PIECE - BLOB


def dense(value):
    rows = value.shape[0] // GROUPS
    return jnp.concatenate([value[k * rows : (k + 1) * rows] for k in range(GROUPS)], axis=1)


def lanes_of(value, group):
    return value[:, group * SHARE_LANES : (group + 1) * SHARE_LANES]


def undense(pieces):
    return jnp.concatenate(
        [
            jnp.concatenate([lanes_of(piece, k) for piece in pieces], axis=1)
            for k in range(GROUPS)
        ],
        axis=0,
    )


def collect_kernel(
    pos_ref,
    spec_ref,
    neigh_ref,
    lab_ref,
    tgt_ref,
    emb_ref,
    fil_ref,
    con_ref,
    read_ref,
    win_ref,
    table_ref,
    full_ref,
    cont_ref,
    rd_ref,
    blob,
    padded,
    ext,
    halo,
    send_sem,
    recv_sem,
    halo_sem,
):
    block, group = lax.axis_index("atoms"), lax.axis_index("chan")
    count = pos_ref.shape[1]
    before = lax.rem(block + BLOCKS - 1, BLOCKS)
    after = lax.rem(block + 1, BLOCKS)
    peers = [lax.rem(group + offset, GROUPS) for offset in range(1, GROUPS)]
    barrier = pltpu.get_barrier_semaphore()
    for peer in peers:
        pl.semaphore_signal(barrier, inc=1, device_id={"chan": peer}, device_id_type=MESH)
    for other in (before, after):
        pl.semaphore_signal(barrier, inc=1, device_id={"atoms": other}, device_id_type=MESH)

    padded[...] = jnp.zeros_like(padded)
    for t in range(2):
        padded[16 * t : 16 * t + 9, :] = con_ref[:, t, :]
    table_ref[...] = jnp.zeros_like(table_ref)
    table_ref[0:SHARE_LANES, 0:ELEMENTS] = emb_ref[...]
    both = [fil_ref[t].reshape(LANES, 64) for t in range(2)]
    blob[group, 0:128, :] = jnp.concatenate(both, axis=1)
    blob[group, 128:160, :] = table_ref[0:SHARE_LANES, :]
    blob[group, 160:168, :] = dense(read_ref[...].reshape(32, SHARE_LANES))
    blob[group, 168:176, :] = dense(padded[...])

    atom = lax.broadcasted_iota(jnp.int32, (1, count), 1)
    leading = neigh_ref[0:1, :] - block * count
    first = jnp.where((neigh_ref[0:1, :] >= 0) & (leading < atom), leading, atom)
    ext[...] = jnp.zeros_like(ext)
    ext[0:3, 0:count] = pos_ref[...]
    ext[3:4, 0:count] = first.astype(jnp.float32)
    ext[4:5, 0:count] = spec_ref[...].astype(jnp.float32)
    ext[5:6, 0:count] = lab_ref[...].astype(jnp.float32)
    ext[8:11, 0:count] = tgt_ref[...]

    pl.semaphore_wait(barrier, GROUPS + 1)
    copies = []
    for at, peer in enumerate(peers):
        copies.append(
            pltpu.make_async_remote_copy(
                src_ref=blob.at[group],
                dst_ref=blob.at[group],
                send_sem=send_sem.at[at],
                recv_sem=recv_sem.at[group],
                device_id={"chan": peer},
                device_id_type=MESH,
            )
        )
    halo_copy = pltpu.make_async_remote_copy(
        src_ref=ext.at[:, 0:LANES],
        dst_ref=halo,
        send_sem=halo_sem.at[0],
        recv_sem=halo_sem.at[1],
        device_id={"atoms": before},
        device_id_type=MESH,
    )
    halo_copy.start()
    for copy in copies:
        copy.start()

    halo_copy.wait()
    kind = lax.broadcasted_iota(jnp.int32, (16, LANES), 0)
    lane = lax.broadcasted_iota(jnp.int32, (16, LANES), 1)
    there = (lane < GHOST) & (block < BLOCKS - 1)
    shifted = halo[...] + jnp.where(kind == 3, float(count), 0.0)
    nothing = jnp.where(kind == 3, -1.0e6, 0.0)
    ext[:, count : count + LANES] = jnp.where(there, shifted, nothing)
    share = count // GROUPS
    wide = ext[:, pl.ds(pl.multiple_of(group * share, LANES), 2 * LANES)]
    for unit in range(share // UNIT):
        view = wide if unit == 0 else pltpu.roll(wide, 2 * LANES - unit * UNIT, 1)
        view = view[:, :LANES]
        start = (group * share + unit * UNIT).astype(jnp.float32)
        view = view - jnp.where(kind == 3, start, 0.0)
        win_ref[unit] = jnp.where(lane < WINDOW, view, nothing)

    for at, peer in enumerate(peers):
        pltpu.make_async_remote_copy(
            src_ref=blob.at[peer],
            dst_ref=blob.at[peer],
            send_sem=send_sem.at[at],
            recv_sem=recv_sem.at[peer],
            device_id={"chan": peer},
            device_id_type=MESH,
        ).wait_recv()
    for k in range(GROUPS):
        part = pl.ds(k * SHARE_LANES, SHARE_LANES)
        for t in range(2):
            full_ref[t, :, part, :] = blob[k, 0:128, 64 * t : 64 * t + 64].reshape(
                4, SHARE_LANES, 64
            )
        table_ref[part, :] = blob[k, 128:160, :]
    rd_ref[...] = undense([blob[k, 160:168, :] for k in range(GROUPS)]).reshape(2, 16, LANES)
    cont_ref[...] = undense([blob[k, 168:176, :] for k in range(GROUPS)]).reshape(2, 16, LANES)
    for copy in copies:
        copy.wait_send()


def collect(positions, species, neighbours, labelled, targets, embedding, filters, contract, readout):
    f32 = jnp.float32
    count = positions.shape[1]
    vmem = pl.BlockSpec(memory_space=pltpu.VMEM)
    return pl.pallas_call(
        collect_kernel,
        in_specs=[vmem] * 9,
        out_specs=[vmem] * 5,
        out_shape=[
            jax.ShapeDtypeStruct((count // GROUPS // UNIT, 16, LANES), f32),
            jax.ShapeDtypeStruct((LANES, LANES), f32),
            jax.ShapeDtypeStruct((2, 4, LANES, 64), f32),
            jax.ShapeDtypeStruct((2, 16, LANES), f32),
            jax.ShapeDtypeStruct((2, 16, LANES), f32),
        ],
        scratch_shapes=[
            pltpu.VMEM((GROUPS, BLOB, LANES), f32),
            pltpu.VMEM((32, SHARE_LANES), f32),
            pltpu.VMEM((16, count + LANES), f32),
            pltpu.VMEM((16, LANES), f32),
            pltpu.SemaphoreType.DMA((GROUPS - 1,)),
            pltpu.SemaphoreType.DMA((GROUPS,)),
            pltpu.SemaphoreType.DMA((2,)),
        ],
        compiler_params=pltpu.CompilerParams(collective_id=0, has_side_effects=True),
    )(
        positions,
        species[None],
        neighbours,
        labelled[None],
        targets,
        embedding,
        filters,
        contract,
        readout,
    )


def reduce_kernel(
    force_ref,
    stat_ref,
    g_emb,
    g_bes,
    g_rad,
    g_fil,
    g_con,
    g_mix,
    g_read,
    g_en,
    forces_ref,
    own_ref,
    rest_ref,
    pieces,
    core_in,
    line_out,
    line_in,
    summed,
    sub_in,
    sub_out,
    total,
    quarters,
    windows,
    tail,
    tail_in,
    sems,
    sub_send,
    sub_recv,
    total_send,
    total_recv,
):
    f32 = jnp.float32
    block, group = lax.axis_index("atoms"), lax.axis_index("chan")
    line, core = group // 2, lax.rem(group, 2)
    core_peer = {"chan": line * 2 + (1 - core)}
    line_peer = {"chan": (1 - line) * 2 + core}
    others = [lax.rem(block + offset, BLOCKS) for offset in range(1, BLOCKS)]
    barrier = pltpu.get_barrier_semaphore()
    for peer in [core_peer, line_peer] + [{"atoms": other} for other in others]:
        pl.semaphore_signal(barrier, inc=1, device_id=peer, device_id_type=MESH)

    def copy(source, dest, at, peer):
        return pltpu.make_async_remote_copy(
            src_ref=source,
            dst_ref=dest,
            send_sem=sems.at[2 * at],
            recv_sem=sems.at[2 * at + 1],
            device_id=peer,
            device_id_type=MESH,
        )

    rows = lax.broadcasted_iota(jnp.int32, (16, LANES), 0)
    lanes = lax.broadcasted_iota(jnp.int32, (16, LANES), 1)
    vector = jnp.zeros((1, LANES), f32)
    for t in range(2):
        spread = jnp.broadcast_to(g_en[t], (16, LANES))
        vector = vector + jnp.sum(
            jnp.where(lanes == rows + 16 * t, spread, 0.0), axis=0, keepdims=True
        )
    inner = g_rad[...].reshape(256, 64)
    inner = jnp.concatenate([inner[:128], inner[128:]], axis=1)
    bessel = jnp.concatenate([g_bes[0], g_bes[1]], axis=1)
    for k in range(GROUPS):
        where = (k % 2, k // 2)
        part = pl.ds(k * SHARE_LANES, SHARE_LANES)
        both = [g_fil[t, :, part, :].reshape(LANES, 64) for t in range(2)]
        pieces[(*where, pl.ds(0, 128), slice(None))] = jnp.concatenate(both, axis=1)
        pieces[(*where, pl.ds(128, 32), slice(None))] = g_emb[part, :]
        pieces[(*where, pl.ds(160, 8), slice(None))] = dense(
            lanes_of(g_read[...].reshape(32, LANES), k)
        )
        pieces[(*where, pl.ds(168, 8), slice(None))] = dense(
            lanes_of(g_con[...].reshape(32, LANES), k)
        )
        pieces[(*where, pl.ds(176, 64), slice(None))] = g_mix[k // 2, 64 * (k % 2) : 64 * (k % 2) + 64, :]
        pieces[(*where, pl.ds(240, 32), slice(None))] = inner[32 * k : 32 * k + 32]
        pieces[(*where, pl.ds(272, 8), slice(None))] = jnp.concatenate(
            [bessel[2 * k : 2 * k + 2], vector, stat_ref[0:2, :], jnp.zeros((3, LANES), f32)],
            axis=0,
        )
    windows[line, core] = force_ref[...]
    pl.semaphore_wait(barrier, BLOCKS + 1)

    core_copy = copy(pieces.at[1 - core], core_in, 0, core_peer)
    core_copy.start()
    core_force = copy(windows.at[line, core], windows.at[line, core], 1, core_peer)
    core_force.start()
    core_copy.wait()
    line_out[...] = pieces[core, 1 - line] + core_in[1 - line]
    line_copy = copy(line_out, line_in, 2, line_peer)
    line_copy.start()
    core_force.wait()
    line_force = copy(windows.at[line], windows.at[line], 3, line_peer)
    line_force.start()
    partial = pieces[core, line] + core_in[line]
    line_force.wait()

    lane8 = lax.broadcasted_iota(jnp.int32, (8, LANES), 1)
    canvas = [jnp.zeros((8, LANES), f32)] * 5
    for k in range(8):
        value = windows[k // 4, (k // 2) % 2, k % 2]
        if k % 2 == 0:
            canvas[k // 2] = canvas[k // 2] + value
        else:
            value = pltpu.roll(value, 64, 1)
            canvas[k // 2] = canvas[k // 2] + jnp.where(lane8 >= 64, value, 0.0)
            canvas[k // 2 + 1] = canvas[k // 2 + 1] + jnp.where(lane8 < 64, value, 0.0)
    tail[...] = canvas[4]
    tail_copy = copy(tail, tail_in, 4, {"atoms": others[0]})
    tail_copy.start()

    line_copy.wait()
    summed[7] = jnp.zeros((SUB, LANES), f32)
    partial = partial + line_in[...]
    for k in range(7):
        size = min(SUB, PIECE - k * SUB)
        summed[k, 0:size, :] = partial[k * SUB : k * SUB + size]
        if size < SUB:
            summed[k, size:SUB, :] = jnp.zeros((SUB - size, LANES), f32)

    def sub_copy(other, at):
        return pltpu.make_async_remote_copy(
            src_ref=summed.at[other],
            dst_ref=sub_in.at[block],
            send_sem=sub_send.at[at],
            recv_sem=sub_recv.at[block],
            device_id={"atoms": other},
            device_id_type=MESH,
        )

    def total_copy(other, at):
        return pltpu.make_async_remote_copy(
            src_ref=sub_out,
            dst_ref=total.at[block],
            send_sem=total_send.at[at],
            recv_sem=total_recv.at[block],
            device_id={"atoms": other},
            device_id_type=MESH,
        )

    def arrival(dest, recv, other):
        return pltpu.make_async_remote_copy(
            src_ref=sub_out,
            dst_ref=dest.at[other],
            send_sem=sub_send.at[0],
            recv_sem=recv.at[other],
            device_id={"atoms": other},
            device_id_type=MESH,
        )

    subs = [sub_copy(other, at) for at, other in enumerate(others)]
    for item in subs:
        item.start()
    value = summed[block]
    for other in others:
        arrival(sub_in, sub_recv, other).wait_recv()
        value = value + sub_in[other]
    sub_out[...] = value
    totals = [total_copy(other, at) for at, other in enumerate(others)]
    for item in totals:
        item.start()
    total[block] = value
    tail_copy.wait()
    forces = jnp.concatenate(canvas[:4], axis=1)
    edge = jnp.where((lane8 < GHOST) & (block > 0), tail_in[...], 0.0)
    forces_ref[...] = forces
    forces_ref[:, 0:LANES] = canvas[0] + edge
    for other in others:
        arrival(total, total_recv, other).wait_recv()
    for item in subs + totals:
        item.wait_send()

    everything = total[...].reshape(BLOCKS * SUB, LANES)
    own_ref[...] = everything[:BLOB]
    flat = everything[:274]
    energy_row = everything[274:275]
    squares = jnp.sum(flat * flat, axis=0, keepdims=True)
    squares = squares + (1.0 / GROUPS) * energy_row * energy_row
    squares = jnp.sum(squares, axis=1, keepdims=True)
    quarters[line, core] = everything[BLOB:PIECE]
    quarters[line, core, 101:102, :] = jnp.broadcast_to(squares, (1, LANES))
    line_quarter = copy(quarters.at[line, core], quarters.at[line, core], 5, line_peer)
    line_quarter.start()
    core_quarter = copy(quarters.at[line, core], quarters.at[line, core], 6, core_peer)
    core_quarter.start()
    line_quarter.wait()
    cross_quarter = copy(quarters.at[1 - line, core], quarters.at[1 - line, core], 7, core_peer)
    cross_quarter.start()
    core_quarter.wait()
    cross_quarter.wait()
    rest_ref[...] = quarters[...].reshape(GROUPS, QUARTER, LANES)


def reduce_all(force, stat, grads):
    f32 = jnp.float32
    vmem = pl.BlockSpec(memory_space=pltpu.VMEM)
    dma = pltpu.SemaphoreType.DMA
    return pl.pallas_call(
        reduce_kernel,
        in_specs=[vmem] * 10,
        out_specs=[vmem] * 3,
        out_shape=[
            jax.ShapeDtypeStruct((8, 4 * LANES), f32),
            jax.ShapeDtypeStruct((BLOB, LANES), f32),
            jax.ShapeDtypeStruct((GROUPS, QUARTER, LANES), f32),
        ],
        scratch_shapes=[
            pltpu.VMEM((2, 2, PIECE, LANES), f32),
            pltpu.VMEM((2, PIECE, LANES), f32),
            pltpu.VMEM((PIECE, LANES), f32),
            pltpu.VMEM((PIECE, LANES), f32),
            pltpu.VMEM((BLOCKS, SUB, LANES), f32),
            pltpu.VMEM((BLOCKS, SUB, LANES), f32),
            pltpu.VMEM((SUB, LANES), f32),
            pltpu.VMEM((BLOCKS, SUB, LANES), f32),
            pltpu.VMEM((2, 2, QUARTER, LANES), f32),
            pltpu.VMEM((2, 2, 2, 8, LANES), f32),
            pltpu.VMEM((8, LANES), f32),
            pltpu.VMEM((8, LANES), f32),
            dma((16,)),
            dma((BLOCKS - 1,)),
            dma((BLOCKS,)),
            dma((BLOCKS - 1,)),
            dma((BLOCKS,)),
        ],
        compiler_params=pltpu.CompilerParams(collective_id=1, has_side_effects=True),
    )(force, stat, *grads)


def adam_kernel(*refs):
    forces_in, own_ref, rest_ref = refs[:3]
    weights, moments = refs[3:11], refs[11:27]
    parts_ref, forces_ref, norm_ref = refs[27:30]
    results = refs[30:54]
    scratch = refs[54]
    rest = [rest_ref[k] for k in range(GROUPS)]
    stats = rest[0]
    loss = jnp.sum(stats[99:100], axis=1, keepdims=True)
    count = jnp.sum(stats[100:101], axis=1, keepdims=True)
    inverse = 1.0 / count
    squares = sum(rest[k][101:102, 0:1] for k in range(GROUPS))
    norm = jnp.sqrt(squares) * inverse
    factor = inverse * jnp.minimum(1.0, CLIP_NORM / (norm + 1e-06))
    norm_ref[...] = norm
    two = lax.broadcasted_iota(jnp.int32, (1, 2), 1)
    parts_ref[...] = jnp.where(two == 0, loss, count)
    forces_ref[...] = forces_in[0:3, :]

    def narrow(value):
        return jnp.concatenate([lanes_of(value, k) for k in range(GROUPS)], axis=0)

    fil = [own_ref[0:128, 64 * t : 64 * t + 64].reshape(4, SHARE_LANES, 64) for t in range(2)]
    emb = own_ref[128:160, 0:ELEMENTS]
    read = narrow(own_ref[160:168, :]).reshape(2, 16, SHARE_LANES)
    scratch[...] = narrow(own_ref[168:176, :])
    con = [scratch[0:9, :], scratch[16:25, :]]
    mix = jnp.concatenate([rest[k][0:64] for k in range(GROUPS)], axis=0).reshape(2, LANES, LANES)
    inner = jnp.concatenate([rest[k][64:96] for k in range(GROUPS)], axis=0)
    inner = jnp.concatenate([inner[:, :64], inner[:, 64:]], axis=0).reshape(2, 2, 64, 64)
    bes = jnp.concatenate([rest[k][96:98] for k in range(GROUPS)], axis=0)
    bes = [bes[:, :64], bes[:, 64:]]
    vector = rest[0][98:99]
    vector = jnp.concatenate([vector[:, 0:16], vector[:, 16:32]], axis=0)

    def update(which, gradient, at):
        first, square = moments[2 * which], moments[2 * which + 1]
        weight = weights[which][at]
        clipped = gradient * factor
        moment = BETA_ONE * first[at] + (1.0 - BETA_ONE) * clipped
        second = BETA_TWO * square[at] + (1.0 - BETA_TWO) * clipped * clipped
        corrected_first = moment * (1.0 / (1.0 - BETA_ONE**ADAM_STEP))
        corrected_second = second * (1.0 / (1.0 - BETA_TWO**ADAM_STEP))
        updated = weight - RATE * (
            corrected_first / (jnp.sqrt(corrected_second) + EPSILON) + DECAY * weight
        )
        results[3 * which][at] = updated
        results[3 * which + 1][at] = moment
        results[3 * which + 2][at] = second

    everything = Ellipsis
    update(0, emb, everything)
    for t in range(2):
        update(1, bes[t], t)
        update(3, fil[t], t)
        update(4, con[t], (slice(None), t))
    update(2, inner, everything)
    update(5, mix, everything)
    update(6, read, everything)
    update(7, vector, everything)


def adam(forces, own, rest, weights, moments):
    f32 = jnp.float32
    vmem = pl.BlockSpec(memory_space=pltpu.VMEM)
    shapes = [(1, 2), (3, forces.shape[1]), (1, 1)]
    shapes += [weight.shape for weight in weights for _ in range(3)]
    return pl.pallas_call(
        adam_kernel,
        in_specs=[vmem] * 27,
        out_specs=[vmem] * 27,
        out_shape=[jax.ShapeDtypeStruct(shape, f32) for shape in shapes],
        scratch_shapes=[pltpu.VMEM((32, SHARE_LANES), f32)],
    )(forces, own, rest, *weights, *moments)


def adamw(weight, gradient, first, second, scale):
    clipped = gradient * scale
    moment = BETA_ONE * first + (1.0 - BETA_ONE) * clipped
    second_new = BETA_TWO * second + (1.0 - BETA_TWO) * clipped * clipped
    corrected_first = moment / (1.0 - BETA_ONE**ADAM_STEP)
    corrected_second = second_new / (1.0 - BETA_TWO**ADAM_STEP)
    updated = weight - RATE * (
        corrected_first / (jnp.sqrt(corrected_second) + EPSILON) + DECAY * weight
    )
    return (updated, moment, second_new)


def per_device(
    positions,
    species,
    neighbours,
    labelled,
    target_forces,
    embedding,
    bessel,
    radial,
    filters,
    contract,
    mixing,
    readout,
    energies,
    first_embedding,
    square_embedding,
    first_bessel,
    square_bessel,
    first_radial,
    square_radial,
    first_filters,
    square_filters,
    first_contract,
    square_contract,
    first_mixing,
    square_mixing,
    first_readout,
    square_readout,
    first_energies,
    square_energies,
):
    if (lax.axis_size("atoms"), lax.axis_size("chan")) == (BLOCKS, GROUPS):
        turns = [(1, 0), None, None, (0, 1, 3, 2), (1, 0, 2), None, None, None]

        def turned(value, order):
            return value if order is None else value.transpose(order)

        weights = (embedding, bessel, radial, filters, contract, mixing, readout, energies)
        weights = [turned(value, order) for value, order in zip(weights, turns)]
        moments = (
            first_embedding,
            square_embedding,
            first_bessel,
            square_bessel,
            first_radial,
            square_radial,
            first_filters,
            square_filters,
            first_contract,
            square_contract,
            first_mixing,
            square_mixing,
            first_readout,
            square_readout,
            first_energies,
            square_energies,
        )
        moments = [turned(value, turns[k // 2]) for k, value in enumerate(moments)]
        windows, table, full, cont, read = collect(
            positions,
            species,
            neighbours,
            labelled,
            target_forces,
            weights[0],
            weights[3],
            weights[4],
            readout,
        )
        force, stat, *grads = local_step(
            windows, table, bessel, radial, full, cont, mixing, read, energies
        )
        forces, own, rest = reduce_all(force, stat, grads)
        parts, forces, norm, *results = adam(forces, own, rest, weights, moments)
        results = [turned(value, turns[k // 3]) for k, value in enumerate(results)]
        return tuple([parts.reshape(2), forces, norm.reshape(())] + results)
    f32 = jnp.float32
    atom_count = positions.shape[1]
    local_chan = embedding.shape[1]
    blocks, groups = lax.axis_size("atoms"), lax.axis_size("chan")
    block, group = lax.axis_index("atoms"), lax.axis_index("chan")
    atom_base = block * atom_count
    share = atom_count // groups
    units = share // UNIT

    atom_index = atom_base + jnp.arange(atom_count, dtype=jnp.int32)
    leading = neighbours[0]
    first_atom = jnp.where((leading >= 0) & (leading < atom_index), leading, atom_index)
    packed = jnp.concatenate(
        [
            positions,
            (first_atom - atom_base).astype(f32)[None],
            species.astype(f32)[None],
            labelled.astype(f32)[None],
            jnp.zeros((2, atom_count), f32),
            target_forces,
            jnp.zeros((5, atom_count), f32),
        ],
        axis=0,
    )
    down = [(i + 1, i) for i in range(blocks - 1)]
    halo = lax.ppermute(packed[:, :GHOST], "atoms", down)
    halo_row = jnp.arange(16)[:, None] == 3
    halo = jnp.where(halo_row, jnp.where(block == blocks - 1, -1.0e6, halo + atom_count), halo)
    missing = jnp.where(jnp.arange(16)[:, None] == 3, -1.0e6, 0.0) * jnp.ones((1, LANES), f32)
    extended = jnp.concatenate([packed, halo, missing], axis=1)
    windows = []
    for unit in range(units):
        start = group * share + unit * UNIT
        window = lax.dynamic_slice(extended, (0, start), (16, WINDOW))
        shift = jnp.where(jnp.arange(16)[:, None] == 3, start.astype(f32), 0.0)
        window = window - shift
        windows.append(jnp.concatenate([window, missing[:, : LANES - WINDOW]], axis=1))
    windows = jnp.stack(windows)

    def whole(value):
        return lax.all_gather(value, "chan", axis=value.ndim - 1, tiled=True)

    table = jnp.concatenate(
        [whole(embedding), jnp.zeros((LANES - ELEMENTS, LANES), f32)], axis=0
    ).T
    force, stat, *grads = local_step(
        windows,
        table,
        bessel,
        radial,
        whole(filters).swapaxes(2, 3),
        jnp.pad(whole(contract), ((0, 0), (0, 7), (0, 0))),
        mixing,
        whole(readout),
        energies,
    )
    grad_embed, grad_bessel, grad_radial, grad_filters, grad_contract, grad_mixing = grads[:6]
    grad_readout, grad_vectors = grads[6:]
    grad_embed = grad_embed.T[:ELEMENTS]
    grad_filters = grad_filters.swapaxes(2, 3)
    grad_contract = grad_contract[:, :9]
    grad_vectors = grad_vectors[:, :, 0]

    canvas = jnp.zeros((3, atom_count + LANES), f32)
    for unit in range(units):
        start = group * share + unit * UNIT
        old = lax.dynamic_slice(canvas, (0, start), (3, WINDOW))
        canvas = lax.dynamic_update_slice(canvas, old + force[unit, :3, :WINDOW], (0, start))
    canvas = lax.psum(canvas, "chan")
    up = [(i, i + 1) for i in range(blocks - 1)]
    arrived = lax.ppermute(canvas[:, atom_count : atom_count + GHOST], "atoms", up)
    forces = canvas[:, :atom_count].at[:, :GHOST].add(arrived)

    def split(value):
        return lax.psum_scatter(value, "chan", scatter_dimension=value.ndim - 1, tiled=True)

    grad_embed, grad_filters, grad_contract, grad_readout = lax.psum(
        (split(grad_embed), split(grad_filters), split(grad_contract), split(grad_readout)),
        "atoms",
    )
    grad_bessel, grad_radial, grad_mixing, grad_vectors, loss_sum, label_total = lax.psum(
        (grad_bessel, grad_radial, grad_mixing, grad_vectors, jnp.sum(stat[0]), jnp.sum(stat[1])),
        ("atoms", "chan"),
    )
    gradients = [
        gradient / label_total
        for gradient in (
            grad_embed,
            grad_bessel,
            grad_radial,
            grad_filters,
            grad_contract,
            grad_mixing,
            grad_readout,
            grad_vectors,
        )
    ]
    squares_of = [jnp.sum(gradient * gradient) for gradient in gradients]
    split_squares = squares_of[0] + squares_of[3] + squares_of[4] + squares_of[6]
    whole_squares = squares_of[1] + squares_of[2] + squares_of[5] + squares_of[7]
    grad_norm = jnp.sqrt(lax.psum(split_squares, "chan") + whole_squares)
    scale = jnp.minimum(1.0, CLIP_NORM / (grad_norm + 1e-06))
    weights = (embedding, bessel, radial, filters, contract, mixing, readout, energies)
    firsts = (
        first_embedding,
        first_bessel,
        first_radial,
        first_filters,
        first_contract,
        first_mixing,
        first_readout,
        first_energies,
    )
    squares = (
        square_embedding,
        square_bessel,
        square_radial,
        square_filters,
        square_contract,
        square_mixing,
        square_readout,
        square_energies,
    )
    results = []
    for weight, gradient, first, second in zip(weights, gradients, firsts, squares):
        results.extend(adamw(weight, gradient, first, second, scale))
    return tuple([jnp.stack([loss_sum, label_total]), forces, grad_norm] + results)


def solution(mesh):
    whole = P()
    columns = P(None, "atoms")
    by_weight = [
        P(None, "chan"),
        whole,
        whole,
        P(None, None, None, "chan"),
        P(None, None, "chan"),
        whole,
        P(None, None, "chan"),
        whole,
    ]
    in_specs = [columns, P("atoms"), columns, P("atoms"), columns] + by_weight
    in_specs += [spec for spec in by_weight for _ in range(2)]
    out_specs = [whole, columns, whole] + [spec for spec in by_weight for _ in range(3)]
    return jax.shard_map(
        per_device,
        mesh=mesh,
        in_specs=tuple(in_specs),
        out_specs=tuple(out_specs),
        check_vma=False,
    )
```

```python
import functools
import math

import jax
import jax.numpy as jnp
from jax import lax
from jax.experimental import pallas as pl
from jax.experimental.pallas import tpu as pltpu
from jax.sharding import PartitionSpec as P

ELEMENTS = 89
NBESSEL = 8
GHOST = 8
ADAM_STEP = 10

RCUT = 5.0
SMOOTH = 0.01
NEIGHBOURS_MEAN = 8.0
HUBER_DELTA = 1.0
CLIP_NORM = 0.001
RATE = 0.2
BETA_ONE = 0.9
BETA_TWO = 0.999
EPSILON = 1e-08
DECAY = 0.01

UNIT = 64
WINDOW = UNIT + 16
LANES = 128
DIRECTED = 15
TILES = WINDOW // 8
CHUNK = 80
EDGE_BLOCKS = 2 * CHUNK
FLAT = 8 * CHUNK
DEGREES = [0] + [1] * 3 + [2] * 5 + [3] * 7
EXACT = lax.Precision.HIGHEST

def shapes_of(x, y, z, root_three=math.sqrt(3.0)):
    xx, yy, zz = x * x, y * y, z * z
    xy, yz, zx = x * y, y * z, z * x
    both, less = xx + yy, xx - yy
    wide = 4.0 * zz - both
    return [
        x,
        y,
        z,
        root_three * xy,
        root_three * yz,
        zz - 0.5 * both,
        root_three * zx,
        (0.5 * root_three) * less,
        math.sqrt(5.0 / 8.0) * y * (3.0 * xx - yy),
        math.sqrt(15.0) * xy * z,
        math.sqrt(3.0 / 8.0) * y * wide,
        z * (zz - 1.5 * both),
        math.sqrt(3.0 / 8.0) * x * wide,
        (0.5 * math.sqrt(15.0)) * z * less,
        math.sqrt(5.0 / 8.0) * x * (xx - 3.0 * yy),
    ]


def slants_of(bar):
    third = 1.0 / math.sqrt(3.0)
    root = math.sqrt(3.0)
    a, b, c, d = (
        math.sqrt(5.0 / 8.0),
        math.sqrt(15.0),
        math.sqrt(3.0 / 8.0),
        0.5 * math.sqrt(15.0),
    )
    one = [[(0, bar[1])], [(0, bar[2])], [(0, bar[3])]]
    four, five, seven, eight = [root * bar[lm] for lm in (4, 5, 7, 8)]
    two = [
        [(2, four), (3, seven), (1, eight - bar[6])],
        [(1, four), (3, five), (2, -eight - bar[6])],
        [(2, five), (1, seven), (3, 2.0 * bar[6])],
    ]
    mixed = (b * third) * bar[10]
    three = [
        [
            (4, (6.0 * a * third) * bar[9] - (2.0 * c * third) * bar[11]),
            (5, mixed),
            (7, (2.0 * d * third) * bar[14] - root * bar[12]),
            (6, (4.0 * c) * bar[13]),
            (8, (6.0 * a * third) * bar[15] - (2.0 * c * third) * bar[13]),
        ],
        [
            (4, (-2.0 * c * third) * bar[13] - (6.0 * a * third) * bar[15]),
            (5, (-2.0 * d * third) * bar[14] - root * bar[12]),
            (7, mixed),
            (6, (4.0 * c) * bar[11]),
            (8, (6.0 * a * third) * bar[9] + (2.0 * c * third) * bar[11]),
        ],
        [
            (4, mixed),
            (5, (8.0 * c * third) * bar[11]),
            (7, (8.0 * c * third) * bar[13]),
            (6, 3.0 * bar[12]),
            (8, (2.0 * d * third) * bar[14]),
        ],
    ]
    return one, two, three


def radius_of(x, y, z, valid):
    distance = jnp.sqrt((x * x + y * y + z * z) * (RCUT * RCUT) + SMOOTH)
    scaled = distance * (1.0 / RCUT)
    square = scaled * scaled
    fifth = square * square * scaled
    envelope = 1.0 - fifth * (21.0 - 35.0 * scaled + 15.0 * square)
    envelope = jnp.where(scaled < 1.0, envelope, 0.0) * (valid * (1.0 / NEIGHBOURS_MEAN))
    return distance, envelope


def halves_of(value):
    high = value.astype(jnp.bfloat16)
    low = (value - high.astype(jnp.float32)).astype(jnp.bfloat16)
    return high, low


def dot(left, right, left_dim, right_dim):
    return lax.dot_general(
        left,
        right,
        (((left_dim,), (right_dim,)), ((), ())),
        preferred_element_type=jnp.float32,
    )


def fine(left, right, left_dim, right_dim):
    left_high, left_low = halves_of(left)
    right_high, right_low = halves_of(right)
    return (
        dot(left_high, right_high, left_dim, right_dim)
        + dot(left_low, right_high, left_dim, right_dim)
        + dot(left_high, right_low, left_dim, right_dim)
    )


def fine_rows(left, right):
    rows = left.shape[0]
    left_high, left_low = halves_of(left)
    right_high, right_low = halves_of(right)
    both = dot(jnp.concatenate([left_high, left_low], axis=0), right_high, 1, 1)
    return both[:rows] + both[rows:] + dot(left_high, right_low, 1, 1)


def triple(value):
    high, low = halves_of(value)
    return jnp.concatenate([high, high, low], axis=0)


def add(total, term):
    return term if total is None else total + term


def members(degree):
    return range(degree * degree, (degree + 1) ** 2)


def thirds(values):
    parts = []
    for value in values:
        for _ in range(3):
            part = value.astype(jnp.bfloat16).astype(jnp.float32)
            parts.append(part)
            value = value - part
    parts += [jnp.zeros_like(parts[0])] * (16 - len(parts))
    return jnp.concatenate(parts, axis=0).astype(jnp.bfloat16)


def joined(rows, count):
    return [
        rows[3 * k : 3 * k + 1] + rows[3 * k + 1 : 3 * k + 2] + rows[3 * k + 2 : 3 * k + 3]
        for k in range(count)
    ]


def sine_cosine(angle):
    half = 0.5 * angle - (0.5 * math.pi)
    square = half * half
    sine = cosine = 0.0
    for k in range(6, -1, -1):
        cosine = cosine * square + (-1) ** k / math.factorial(2 * k)
        if k < 6:
            sine = sine * square + (-1) ** k / math.factorial(2 * k + 1)
    sine = sine * half
    return -2.0 * sine * cosine, 2.0 * sine * sine - 1.0


def step_kernel(
    win_ref,
    emb_ref,
    bes_ref,
    rad_ref,
    fil_ref,
    con_ref,
    mix_ref,
    read_ref,
    en_ref,
    force_ref,
    stat_ref,
    g_emb,
    g_bes,
    g_rad,
    g_fil,
    g_con,
    g_mix,
    g_read,
    g_en,
    begin_ref,
    yy,
    dyy,
    feats,
    dfeats,
    fj,
    dfj,
    fdir,
    dfdir,
    fb,
    fjb,
    wb,
    pulls,
    amat,
    damat,
    msg,
    msgb,
    dmsg,
    zs,
    sg,
    dz,
    hidb,
    hidu,
    bess,
    rows_ref,
    turn_ref,
    hot_j,
    hot_d,
    turned_j,
    turned_d,
    barrow,
    gcon,
    tab_w,
    bes_w,
    bes_b,
    rad_w,
    rad_b,
    fil_w,
    fil_b,
    g_tab,
    g_wide,
):
    f32, bf16, i32 = jnp.float32, jnp.bfloat16, jnp.int32

    @pl.when(pl.program_id(0) == 0)
    def _():
        for ref in (g_tab, g_wide, g_bes, g_rad, g_con, g_mix, g_read, g_en, stat_ref):
            ref[...] = jnp.zeros_like(ref)
        for ref in (feats, dfeats, msg, dmsg, fjb, pulls):
            ref[...] = jnp.zeros_like(ref)

        def clear(sixteen, carry):
            for t in range(2):
                fb[t, pl.ds(16 * sixteen, 16)] = jnp.zeros((16, 4, 8, LANES), f32)
            return carry

        lax.fori_loop(0, EDGE_BLOCKS // 16, clear, 0)
        tab_w[...] = jnp.concatenate(list(halves_of(emb_ref[...].T)), axis=0)
        for t in range(2):
            high, low = [value.astype(f32) for value in halves_of(bes_ref[t])]
            bes_w[t] = jnp.concatenate([high, low, high, jnp.zeros_like(high)], axis=0).T.astype(
                bf16
            )
            bes_b[t] = jnp.concatenate([high, low, high], axis=1).astype(bf16)
            for depth in range(2):
                high, low = [value.astype(f32) for value in halves_of(rad_ref[t, depth])]
                rad_b[t, depth] = jnp.concatenate([high, low, high], axis=1).astype(bf16)
                rad_w[t, depth] = jnp.concatenate([high, low, high], axis=0).T.astype(bf16)
            high, low = halves_of(fil_ref[t].reshape(4 * LANES, 64).T)
            fil_w[t] = jnp.concatenate([high, low, high], axis=0)
            fil_b[t] = jnp.concatenate([high, low], axis=0)

    def both_sides(value):
        wide = jnp.broadcast_to(value, (16, LANES))
        back = pltpu.roll(wide, 1, 1, stride=1, stride_axis=0)
        ahead = pltpu.roll(wide, 113, 1, stride=1, stride_axis=0)
        return back, ahead

    first = win_ref[0, 3:4, :]
    own = jnp.where((first >= 0.0) & (first < float(UNIT)), 1.0, 0.0)
    slot_row = lax.broadcasted_iota(i32, (16, LANES), 0)
    back_first, ahead_first = both_sides(first)
    same = (slot_row < DIRECTED) & ((back_first == first) | (ahead_first == first))
    count = jnp.sum(jnp.where(same, 1.0, 0.0), axis=0, keepdims=True) * own

    line = lax.broadcasted_iota(i32, (LANES, LANES), 0)
    place = lax.broadcasted_iota(i32, (LANES, LANES), 1)
    key = jnp.broadcast_to(count + own, (LANES, LANES))
    other = key.T
    ahead_of = (other > key) | ((other == key) & (line < place))
    rank = jnp.sum(jnp.where(ahead_of, 1.0, 0.0), axis=0, keepdims=True)
    order_t = jnp.where(line.astype(f32) == rank, 1.0, 0.0).astype(bf16)
    index = lax.broadcasted_iota(i32, (1, LANES), 1).astype(f32)
    wide = jnp.concatenate(
        [win_ref[0], count, index, jnp.zeros((14, LANES), f32)], axis=0
    )
    high, middle = halves_of(wide)
    low = (wide - high.astype(f32) - middle.astype(f32)).astype(bf16)
    moved = dot(jnp.concatenate([high, middle, low], axis=0), order_t, 1, 1)
    turn_ref[0:32, :] = moved[0:32] + moved[32:64] + moved[64:96]

    def row(index):
        return turn_ref[index : index + 1, :]

    first, species, labelled = row(3), row(4), row(5)
    count, atom_id = row(16), row(17)
    own = jnp.where((first >= 0.0) & (first < float(UNIT)), 1.0, 0.0)
    atom_names = jnp.broadcast_to(atom_id, (LANES, LANES)).T[:, 0:1]

    lane_row = lax.broadcasted_iota(i32, (1, LANES), 1)
    used = lax.shift_right_logical(jnp.max(jnp.where(own > 0.0, lane_row, 0)) + 8, 3)
    begins, pairs = [jnp.int32(0)], []
    begin_ref[0] = 0
    for tile in range(TILES):
        mine = (lane_row >= 8 * tile) & (lane_row < 8 * tile + 8)
        most = jnp.max(jnp.where(mine, count, 0.0)).astype(i32)
        pairs.append(lax.shift_right_logical(most + 1, 1))
        begins.append(begins[-1] + pairs[-1])
        begin_ref[tile + 1] = begins[-1]
    total = begins[-1]
    chunks = jnp.where(2 * total > CHUNK, 2, 1)

    def each_chunk(body):
        def step(chunk, carry):
            body(chunk, pl.ds(chunk * CHUNK, CHUNK))
            return carry

        lax.fori_loop(0, chunks, step, 0)

    def each_tile(body):
        def step(tile, carry):
            body(tile, pl.ds(pl.multiple_of(tile * 8, 8), 8))
            return carry

        lax.fori_loop(0, used, step, 0)

    def each_block(tile, body, carry):
        return lax.fori_loop(
            begin_ref[tile],
            begin_ref[tile + 1],
            lambda pair, held: body(2 * pair + 1, body(2 * pair, held)),
            carry,
        )

    def each_edge_block(body):
        def step(four, carry):
            for k in range(4):
                body(4 * four + k)
            return carry

        lax.fori_loop(0, lax.shift_right_logical(2 * total + 3, 2), step, 0)

    def natural(values):
        wide = jnp.concatenate(
            [jnp.broadcast_to(value, (LANES, LANES)).T for value in values], axis=1
        )
        high, middle = halves_of(wide)
        low = (wide - high.astype(f32) - middle.astype(f32)).astype(bf16)
        return jnp.concatenate([high, middle], axis=0), low

    def spread(chunk, blocks, parts, dest):
        left = turned_d[chunk]
        wide = dot(jnp.concatenate([left, left], axis=1), parts[0], 1, 0) + dot(
            left, parts[1], 1, 0
        )
        for k in range(3):
            dest[blocks, k] = wide[:, k * LANES : (k + 1) * LANES].reshape(CHUNK, 8, LANES)

    def layer_in(t, depth, value):
        if depth == 0:
            high, low = [part.astype(f32) for part in halves_of(value)]
            wide = jnp.concatenate([high, high, low, jnp.zeros_like(high)], axis=0).astype(bf16)
            return dot(bes_w[t], wide, 1, 0)
        return dot(rad_w[t, depth - 1], triple(value), 1, 0)

    def layer_back(t, depth, value):
        weight = bes_b[t] if depth == 0 else rad_b[t, depth - 1]
        return dot(weight, triple(value), 1, 0)

    def parts_of(t, chunk, depth):
        z, sig = zs[t, chunk, depth], sg[t, chunk, depth]
        h, rest = z * sig, 1.0 - sig
        return h, sig + h * rest, sig * rest * (2.0 + z - 2.0 * h)

    def sigmoid(z):
        return 0.5 * jnp.tanh(0.5 * z) + 0.5

    def filters_to(t, hidden, blocks, dest):
        wide = dot(triple(hidden), fil_w[t], 0, 0)
        for degree in range(4):
            dest[t, blocks, degree] = wide[:, degree * LANES : (degree + 1) * LANES].reshape(
                CHUNK, 8, LANES
            )

    def filters_back(t, high, low):
        both = dot(fil_b[t], high, 1, 1)
        return both[:64] + both[64:] + dot(fil_b[t, 0:64, :], low, 1, 1)

    def filters_grad(hidden, wide_high, wide_low):
        high, low = halves_of(hidden)
        both = dot(jnp.concatenate([high, low], axis=0), wide_high, 1, 0)
        return both[:64] + both[64:] + dot(high, wide_low, 1, 0)

    def filter_bars(t, blocks):
        parts = [
            halves_of(fb[t, blocks, degree].reshape(FLAT, LANES)) for degree in range(4)
        ]
        return [jnp.concatenate([part[k] for part in parts], axis=1) for k in range(2)]

    position_parts = natural([row(k) * (1.0 / RCUT) for k in range(3)])
    position_rows = thirds([row(k) * (1.0 / RCUT) for k in range(3)])
    atom_rows = jnp.concatenate(
        [first * own, count, atom_id, jnp.zeros((13, LANES), f32)], axis=0
    ).astype(bf16)
    begin_blocks = [2 * value for value in begins]

    def geometry(chunk, blocks):
        edge = lax.broadcasted_iota(i32, (1, FLAT), 1) + chunk * FLAT
        block = lax.shift_right_logical(edge, 3)
        tile = jnp.zeros_like(edge)
        base = jnp.zeros_like(edge)
        for k in range(1, TILES):
            past = block >= begin_blocks[k]
            tile = tile + jnp.where(past, 1, 0)
            base = base + jnp.where(past, 2 * pairs[k - 1], 0)
        atom = (tile * 8 + (edge & 7)).astype(f32)
        number = (block - base).astype(f32)
        atom_column = lax.broadcasted_iota(i32, (LANES, FLAT), 0).astype(f32)
        hot = jnp.where(atom_column == atom, 1.0, 0.0).astype(bf16)
        known = dot(atom_rows, hot, 1, 0)
        there = known[0:1] + number
        there = there + jnp.where(there >= known[2:3], 1.0, 0.0)
        valid = jnp.where(number < known[1:2], 1.0, 0.0)
        hot = jnp.where(atom_names == jnp.where(valid > 0.0, there, -1.0), 1.0, 0.0)
        difference = hot - jnp.where(
            atom_column == jnp.where(valid > 0.0, atom, -1.0), 1.0, 0.0
        )
        hot_j[chunk] = hot.astype(bf16)
        hot_d[chunk] = difference.astype(bf16)
        turned_j[chunk] = hot.T.astype(bf16)
        turned_d[chunk] = difference.T.astype(bf16)
        spread(chunk, blocks, position_parts, yy)
        rel = joined(dot(position_rows, hot_d[chunk], 1, 0), 3)
        distance, envelope = radius_of(*rel, valid)
        for k, value in enumerate(rel + [valid, envelope]):
            rows_ref[chunk, k : k + 1, :] = value
        sine, cosine = sine_cosine(distance * (math.pi / RCUT))
        sines, cosines = [sine], [cosine]
        for k in range(1, NBESSEL):
            before = (0.0, 1.0) if k == 1 else (sines[k - 2], cosines[k - 2])
            sines.append(2.0 * cosine * sines[-1] - before[0])
            cosines.append(2.0 * cosine * cosines[-1] - before[1])
        inverse = 1.0 / distance
        root = math.sqrt(2.0 / RCUT)
        for k in range(NBESSEL):
            basis = root * sines[k] * inverse
            bess[chunk, 0, k : k + 1, :] = basis
            bess[chunk, 1, k : k + 1, :] = (
                root * ((k + 1) * math.pi / RCUT) * cosines[k] - basis
            ) * inverse
        values = [bess[chunk, 0]] * 2
        for depth in range(3):
            for t in range(2):
                z = layer_in(t, depth, values[t])
                sig = sigmoid(z)
                zs[t, chunk, depth] = z
                sg[t, chunk, depth] = sig
                values[t] = z * sig
        for t in range(2):
            filters_to(t, values[t] * envelope, blocks, fdir)

    each_chunk(geometry)

    def point_shapes(block):
        values = shapes_of(*[yy[block, k] for k in range(3)])
        for k in range(3, 15):
            yy[block, k] = values[k]

    each_edge_block(point_shapes)

    def gather_from(value, dest):
        both = jnp.concatenate(list(halves_of(value)), axis=1)

        def body(chunk, blocks):
            wide = dot(turned_j[chunk], both, 1, 0)
            dest[blocks] = (wide[:, :LANES] + wide[:, LANES:]).reshape(CHUNK, 8, LANES)

        each_chunk(body)

    def scattered(chunk, blocks):
        high, low = halves_of(fjb[blocks].reshape(FLAT, LANES))
        return dot(hot_j[chunk], high, 1, 0) + dot(hot_j[chunk], low, 1, 0)

    def contract_rows(t):
        return [con_ref[t, b : b + 1, :] for b in range(9)]

    def powers_of(a):
        return [sum(a[lm] * a[lm] for lm in members(degree)) for degree in (1, 2, 3)]

    def alpha_of(c, s, p):
        return (
            c[0] + 2.0 * c[1] * s + 3.0 * c[5] * s * s + c[6] * p[0] + c[7] * p[1] + c[8] * p[2]
        )

    def beta_of(c, s):
        return [c[2 + i] + c[6 + i] * s for i in range(3)]

    zeros16 = tuple(jnp.zeros((8, LANES), f32) for _ in range(16))

    def forward_messages(t):
        def body(tile, at):
            def edges(block, a):
                a = list(a)
                there = fj[t, block]
                for degree in range(4):
                    w = fdir[t, block, degree] * there
                    if degree == 0:
                        a[0] = a[0] + w
                        continue
                    for lm in members(degree):
                        a[lm] = a[lm] + yy[block, lm - 1] * w
                return tuple(a)

            a = each_block(tile, edges, zeros16)
            for lm in range(16):
                amat[t, tile, lm] = a[lm]
            c = contract_rows(t)
            s, p = a[0], powers_of(a)
            value = s * (c[0] + s * (c[1] + s * c[5]) + c[6] * p[0] + c[7] * p[1] + c[8] * p[2])
            msg[t, at, :] = value + c[2] * p[0] + c[3] * p[1] + c[4] * p[2]

        each_tile(body)

    def backward_messages(t):
        def body(tile, at):
            a = [amat[t, tile, lm] for lm in range(16)]
            c = contract_rows(t)
            up = msgb[t, at, :]
            s, p = a[0], powers_of(a)
            beta = beta_of(c, s)
            twice = [None] + [2.0 * up * beta[i] for i in range(3)]
            ab = [up * alpha_of(c, s, p)] + [twice[DEGREES[lm]] * a[lm] for lm in range(1, 16)]
            slant = slants_of(ab)

            def edges(block, carry):
                there = fj[t, block]
                back = None
                shape = [None] + [yy[block, lm - 1] for lm in range(1, 16)]
                pull = [None] * 3
                for degree in range(4):
                    weight = fdir[t, block, degree]
                    bar = ab[0] if degree == 0 else None
                    if degree > 0:
                        w = weight * there
                        for lm in members(degree):
                            bar = add(bar, shape[lm] * ab[lm])
                        for k in range(3):
                            moved = None
                            for lm, value in slant[degree - 1][k]:
                                moved = add(moved, value if lm == 0 else shape[lm] * value)
                            pull[k] = add(pull[k], w * moved)
                        wb[t, block, degree - 1] = bar
                    fb[t, block, degree] = bar * there
                    if t > 0:
                        back = add(back, bar * weight)
                if t > 0:
                    fjb[block] = back
                for k in range(3):
                    pulls[block, k] = pull[k] if t > 0 else pulls[block, k] + pull[k]
                return carry

            each_block(tile, edges, 0)

        each_tile(body)

    def tangent_messages(t):
        def body(tile, at):
            def edges(block, da):
                da = list(da)
                there = fj[t, block]
                for degree in range(4):
                    weight = fdir[t, block, degree]
                    dw = dfdir[t, block, degree] * there
                    if t > 0:
                        dw = dw + weight * dfj[block]
                    if degree == 0:
                        da[0] = da[0] + dw
                        continue
                    w = weight * there
                    for lm in members(degree):
                        da[lm] = da[lm] + (yy[block, lm - 1] * dw + dyy[block, lm - 1] * w)
                return tuple(da)

            da = each_block(tile, edges, zeros16)
            a = [amat[t, tile, lm] for lm in range(16)]
            for lm in range(16):
                damat[t, tile, lm] = da[lm]
            c = contract_rows(t)
            s, p = a[0], powers_of(a)
            beta = beta_of(c, s)
            value = alpha_of(c, s, p) * da[0]
            for i in range(3):
                value = value + beta[i] * (2.0 * sum(a[lm] * da[lm] for lm in members(i + 1)))
            dmsg[t, at, :] = value

        each_tile(body)

    def tangent_backward(t):
        gcon[...] = jnp.zeros_like(gcon)

        def body(tile, at):
            a = [amat[t, tile, lm] for lm in range(16)]
            da = [damat[t, tile, lm] for lm in range(16)]
            c = contract_rows(t)
            up, dup = msgb[t, at, :], msgb[2, at, :]
            s, ds, p = a[0], da[0], powers_of(a)
            dp = [2.0 * sum(a[lm] * da[lm] for lm in members(degree)) for degree in (1, 2, 3)]
            alpha, beta = alpha_of(c, s, p), beta_of(c, s)
            dalpha = (
                2.0 * c[1] * ds
                + 6.0 * c[5] * s * ds
                + c[6] * dp[0]
                + c[7] * dp[1]
                + c[8] * dp[2]
            )
            pb = [None] + [2.0 * up * beta[i] for i in range(3)]
            dpb = [None] + [2.0 * (dup * beta[i] + up * c[6 + i] * ds) for i in range(3)]
            ab = [up * alpha] + [pb[DEGREES[lm]] * a[lm] for lm in range(1, 16)]
            dab = [dup * alpha + up * dalpha] + [
                pb[DEGREES[lm]] * da[lm] + dpb[DEGREES[lm]] * a[lm] for lm in range(1, 16)
            ]
            products = [(s, ds), (s * s, 2.0 * s * ds)]
            products += [(p[i], dp[i]) for i in range(3)]
            products += [(s * s * s, 3.0 * s * s * ds)]
            products += [(s * p[i], ds * p[i] + s * dp[i]) for i in range(3)]
            for b, (point, direction) in enumerate(products):
                gcon[b] += dup * point + up * direction

            def edges(block, carry):
                there = fj[t, block]
                back = None
                for degree in range(4):
                    if degree == 0:
                        was, bar = ab[0], dab[0]
                    else:
                        was, bar = wb[t, block, degree - 1], None
                        for lm in members(degree):
                            bar = add(
                                bar, yy[block, lm - 1] * dab[lm] + dyy[block, lm - 1] * ab[lm]
                            )
                    value = bar * there
                    if t > 0:
                        value = value + was * dfj[block]
                    fb[t, block, degree] = value
                    back = add(
                        back, bar * fdir[t, block, degree] + was * dfdir[t, block, degree]
                    )
                fjb[block] = back
                return carry

            each_block(tile, edges, 0)

        each_tile(body)
        for b in range(9):
            g_con[t, b : b + 1, :] -= jnp.sum(gcon[b], axis=0, keepdims=True)

    inner = slice(0, WINDOW)
    hot_element = jnp.where(
        lax.broadcasted_iota(i32, (LANES, LANES), 0).astype(f32) == species, 1.0, 0.0
    )[:, :WINDOW].astype(bf16)
    own_lane = own[:, :WINDOW]
    feats[0, inner, :] = dot(
        jnp.concatenate([hot_element, hot_element], axis=0), tab_w[...], 0, 0
    )
    sums = []
    for t in range(2):
        gather_from(feats[t], fj.at[t])
        forward_messages(t)
        feats[t + 1, inner, :] = feats[t, inner, :] + fine(msg[t], mix_ref[t], 1, 1)
        sums.append(fine(read_ref[t], feats[t + 1, inner, :], 1, 1))

    diagonal = lax.broadcasted_iota(i32, (16, 16), 0) == lax.broadcasted_iota(i32, (16, 16), 1)
    sum_bars, feat_bars, slopes_read, curves_read = [], [None, None], [], []
    for t in range(2):
        vector = jnp.sum(
            jnp.where(diagonal, jnp.broadcast_to(en_ref[t : t + 1, :], (16, 16)), 0.0),
            axis=1,
            keepdims=True,
        )
        sig = sigmoid(sums[t])
        h, rest = sums[t] * sig, 1.0 - sig
        slopes_read.append(own_lane * (sig + h * rest))
        curves_read.append(own_lane * vector * (sig * rest * (2.0 + sums[t] - 2.0 * h)))
        sum_bars.append(vector * slopes_read[t])

    def scatter_all():
        msgb[3] = jnp.zeros((WINDOW, LANES), f32)

        def body(chunk, blocks):
            msgb[3] += scattered(chunk, blocks)[:WINDOW]

        each_chunk(body)
        return msgb[3]

    feat_bar = None
    for t in (1, 0):
        feat_bar = add(feat_bar, fine(sum_bars[t], read_ref[t], 0, 0))
        feat_bars[t] = feat_bar
        msgb[t] = fine(feat_bar, mix_ref[t], 1, 0)
        backward_messages(t)
        if t > 0:
            feat_bar = feat_bar + scatter_all()

    barrow[...] = jnp.zeros_like(barrow)

    def geometry_back(chunk, blocks):
        envelope = rows_ref[chunk, 4:5, :]
        values, envelope_bar, distance_bar = [], None, None
        for t in range(2):
            high, low = filter_bars(t, blocks)
            value = filters_back(t, high, low)
            hidu[t, chunk] = value
            h, _, _ = parts_of(t, chunk, 2)
            envelope_bar = add(envelope_bar, jnp.sum(value * h, axis=0, keepdims=True))
            values.append(value * envelope)
        for depth in (2, 1, 0):
            for t in range(2):
                hidb[t, chunk, depth] = values[t]
                _, slope, _ = parts_of(t, chunk, depth)
                values[t] = layer_back(t, depth, values[t] * slope)
        distance_bar = jnp.sum((values[0] + values[1]) * bess[chunk, 1], axis=0, keepdims=True)
        rel = tuple(rows_ref[chunk, k : k + 1, :] for k in range(3))
        valid = rows_ref[chunk, 3:4, :]
        _, radius_pull = jax.vjp(lambda a, b, c: radius_of(a, b, c, valid), *rel)
        radius_bars = radius_pull((distance_bar, envelope_bar))
        ones = jnp.ones((16, LANES), bf16)
        shape_bars = []
        for k in range(3):
            high, low = halves_of(pulls[blocks, k].reshape(FLAT, LANES))
            shape_bars.append((dot(ones, high, 1, 1) + dot(ones, low, 1, 1))[0:1])
        bars = [
            jnp.where(valid > 0.0, radius_bars[k] + shape_bars[k], 0.0) * (1.0 / RCUT)
            for k in range(3)
        ]
        for k, value in enumerate(joined(dot(thirds(bars), hot_d[chunk], 1, 1), 3)):
            barrow[k : k + 1, :] += value

    each_chunk(geometry_back)

    slopes = []
    loss_row = jnp.zeros((1, LANES), f32)
    weight_row = own * labelled
    for k in range(3):
        force = -barrow[k : k + 1, :]
        diff = force - row(8 + k)
        magnitude = jnp.abs(diff)
        huber = jnp.where(
            magnitude <= HUBER_DELTA,
            0.5 * diff * diff,
            HUBER_DELTA * (magnitude - 0.5 * HUBER_DELTA),
        )
        loss_row = loss_row + weight_row * huber
        slopes.append(weight_row * jnp.clip(diff, -HUBER_DELTA, HUBER_DELTA) * (1.0 / RCUT))
    unordered = dot(thirds([-barrow[k : k + 1, :] for k in range(3)]), order_t, 1, 0)
    for k, value in enumerate(joined(unordered, 3)):
        force_ref[0, k : k + 1, :] = value
    force_ref[0, 3:8, :] = jnp.zeros((5, LANES), f32)
    stat_ref[0:1, :] += loss_row
    stat_ref[1:2, :] += weight_row

    slope_parts = natural(slopes)
    slope_rows = thirds(slopes)

    def geometry_tangent(chunk, blocks):
        spread(chunk, blocks, slope_parts, dyy)
        rel = tuple(rows_ref[chunk, k : k + 1, :] for k in range(3))
        valid, envelope = rows_ref[chunk, 3:4, :], rows_ref[chunk, 4:5, :]
        drel = tuple(joined(dot(slope_rows, hot_d[chunk], 1, 0), 3))
        _, (ddistance, denvelope) = jax.jvp(
            lambda a, b, c: radius_of(a, b, c, valid), rel, drel
        )
        rows_ref[chunk, 5:6, :] = denvelope
        dbasis = bess[chunk, 1] * ddistance
        bess[chunk, 2] = dbasis
        values = [dbasis] * 2
        for depth in range(3):
            for t in range(2):
                z = layer_in(t, depth, values[t])
                dz[t, chunk, depth] = z
                h, slope, _ = parts_of(t, chunk, depth)
                values[t] = slope * z
                if depth == 2:
                    values[t] = values[t] * envelope + h * denvelope
        for t in range(2):
            filters_to(t, values[t], blocks, dfdir)
            high, low = filter_bars(t, blocks)
            g_wide[t] += filters_grad(values[t], high, low)

    each_chunk(geometry_tangent)

    def tangent_shapes(block):
        point = tuple(yy[block, k] for k in range(3))
        direction = tuple(dyy[block, k] for k in range(3))
        _, values = jax.jvp(shapes_of, point, direction)
        for k in range(3, 15):
            dyy[block, k] = values[k]

    each_edge_block(tangent_shapes)

    dsums = []
    dfeat = None
    for t in range(2):
        if t > 0:
            dfeats[inner, :] = dfeat
            gather_from(dfeats[...], dfj)
        tangent_messages(t)
        dfeat = add(dfeat, fine(dmsg[t], mix_ref[t], 1, 1))
        dsums.append((fine(read_ref[t], dfeat, 1, 1), dfeat))

    dfeat_bar = None
    for t in (1, 0):
        dsum, dfeat_after = dsums[t]
        g_en[t] -= jnp.sum(slopes_read[t] * dsum, axis=1, keepdims=True)
        dsum_bar = curves_read[t] * dsum
        g_read[t] -= fine(dsum_bar, feats[t + 1, inner, :], 1, 0) + fine(
            sum_bars[t], dfeat_after, 1, 0
        )
        dfeat_bar = add(dfeat_bar, fine(dsum_bar, read_ref[t], 0, 0))
        g_mix[t] -= fine(dfeat_bar, msg[t], 0, 0) + fine(feat_bars[t], dmsg[t], 0, 0)
        msgb[2] = fine(dfeat_bar, mix_ref[t], 1, 0)
        tangent_backward(t)
        dfeat_bar = dfeat_bar + scatter_all()
    high, low = halves_of(dfeat_bar)
    g_tab[...] += dot(hot_element, high, 1, 0) + dot(hot_element, low, 1, 0)

    def network_grads(chunk, blocks):
        envelope, denvelope = rows_ref[chunk, 4:5, :], rows_ref[chunk, 5:6, :]
        values = []
        for t in range(2):
            high, low = filter_bars(t, blocks)
            h, _, _ = parts_of(t, chunk, 2)
            g_wide[t] += filters_grad(h * envelope, high, low)
            values.append(filters_back(t, high, low) * envelope + hidu[t, chunk] * denvelope)
        for depth in (2, 1, 0):
            for t in range(2):
                _, slope, curve = parts_of(t, chunk, depth)
                bar = hidb[t, chunk, depth]
                value = values[t] * slope + bar * curve * dz[t, chunk, depth]
                if depth == 0:
                    before, dbefore = bess[chunk, 0], bess[chunk, 2]
                else:
                    before, slope_before, _ = parts_of(t, chunk, depth - 1)
                    dbefore = slope_before * dz[t, chunk, depth - 1]
                grad = fine_rows(
                    jnp.concatenate([dbefore, before], axis=1),
                    jnp.concatenate([bar * slope, value], axis=1),
                )
                if depth == 0:
                    g_bes[t] -= grad
                else:
                    g_rad[t, depth - 1] -= grad
                    values[t] = layer_back(t, depth, value)

    each_chunk(network_grads)

    @pl.when(pl.program_id(0) == pl.num_programs(0) - 1)
    def _():
        g_emb[...] = -g_tab[...].T
        for t in range(2):
            g_fil[t] = -g_wide[t].T.reshape(4, LANES, 64)


def local_step(windows, table, bessel, radial, filters, contract, mixing, readout, energies):
    units = windows.shape[0]
    f32, bf16 = jnp.float32, jnp.bfloat16
    vmem = pl.BlockSpec(memory_space=pltpu.VMEM)

    def scratch(*shape):
        return pltpu.VMEM(shape, f32)

    def short(*shape):
        return pltpu.VMEM(shape, bf16)

    def out(*shape):
        return jax.ShapeDtypeStruct(shape, f32)

    edges, parts = EDGE_BLOCKS, EDGE_BLOCKS // CHUNK
    return pl.pallas_call(
        step_kernel,
        grid=(units,),
        in_specs=[pl.BlockSpec((1, 16, LANES), lambda i: (i, 0, 0))] + [vmem] * 8,
        out_specs=[pl.BlockSpec((1, 8, LANES), lambda i: (i, 0, 0))] + [vmem] * 9,
        out_shape=[
            out(units, 8, LANES),
            out(8, LANES),
            out(LANES, LANES),
            out(2, NBESSEL, 64),
            out(2, 2, 64, 64),
            out(2, 4, LANES, 64),
            out(2, 16, LANES),
            out(2, LANES, LANES),
            out(2, 16, LANES),
            out(2, 16, 1),
        ],
        scratch_shapes=[
            pltpu.SMEM((16,), jnp.int32),
            scratch(edges, 15, 8, LANES),
            scratch(edges, 15, 8, LANES),
            scratch(3, LANES, LANES),
            scratch(LANES, LANES),
            scratch(2, edges, 8, LANES),
            scratch(edges, 8, LANES),
            scratch(2, edges, 4, 8, LANES),
            scratch(2, edges, 4, 8, LANES),
            scratch(2, edges, 4, 8, LANES),
            scratch(edges, 8, LANES),
            scratch(2, edges, 3, 8, LANES),
            scratch(edges, 3, 8, LANES),
            scratch(2, TILES, 16, 8, LANES),
            scratch(2, TILES, 16, 8, LANES),
            scratch(2, WINDOW, LANES),
            scratch(4, WINDOW, LANES),
            scratch(2, WINDOW, LANES),
            scratch(2, parts, 3, 64, FLAT),
            scratch(2, parts, 3, 64, FLAT),
            scratch(2, parts, 3, 64, FLAT),
            scratch(2, parts, 3, 64, FLAT),
            scratch(2, parts, 64, FLAT),
            scratch(parts, 3, NBESSEL, FLAT),
            scratch(parts, 8, FLAT),
            scratch(LANES, LANES),
            short(parts, LANES, FLAT),
            short(parts, LANES, FLAT),
            short(parts, FLAT, LANES),
            short(parts, FLAT, LANES),
            scratch(8, LANES),
            scratch(9, 8, LANES),
            short(2 * LANES, LANES),
            short(2, 64, 4 * NBESSEL),
            short(2, NBESSEL, 192),
            short(2, 2, 64, 192),
            short(2, 2, 64, 192),
            short(2, 192, 4 * LANES),
            short(2, LANES, 4 * LANES),
            scratch(LANES, LANES),
            scratch(2, 64, 4 * LANES),
        ],
        compiler_params=pltpu.CompilerParams(vmem_limit_bytes=60 * 1024 * 1024),
    )(windows, table, bessel, radial, filters, contract, mixing, readout, energies)


MESH = pl.DeviceIdType.MESH
GROUPS = 4
BLOCKS = 8
SHARE_LANES = LANES // GROUPS
BLOB = 176
PIECE = 280
SUB = 40
QUARTER = PIECE - BLOB


def dense(value):
    rows = value.shape[0] // GROUPS
    return jnp.concatenate([value[k * rows : (k + 1) * rows] for k in range(GROUPS)], axis=1)


def lanes_of(value, group):
    return value[:, group * SHARE_LANES : (group + 1) * SHARE_LANES]


def undense(pieces):
    return jnp.concatenate(
        [
            jnp.concatenate([lanes_of(piece, k) for piece in pieces], axis=1)
            for k in range(GROUPS)
        ],
        axis=0,
    )


def collect_kernel(
    pos_ref,
    spec_ref,
    neigh_ref,
    lab_ref,
    tgt_ref,
    emb_ref,
    fil_ref,
    con_ref,
    read_ref,
    win_ref,
    table_ref,
    full_ref,
    cont_ref,
    rd_ref,
    blob,
    padded,
    ext,
    halo,
    send_sem,
    recv_sem,
    halo_sem,
):
    block, group = lax.axis_index("atoms"), lax.axis_index("chan")
    count = pos_ref.shape[1]
    before = lax.rem(block + BLOCKS - 1, BLOCKS)
    after = lax.rem(block + 1, BLOCKS)
    peers = [lax.rem(group + offset, GROUPS) for offset in range(1, GROUPS)]
    barrier = pltpu.get_barrier_semaphore()
    for peer in peers:
        pl.semaphore_signal(barrier, inc=1, device_id={"chan": peer}, device_id_type=MESH)
    for other in (before, after):
        pl.semaphore_signal(barrier, inc=1, device_id={"atoms": other}, device_id_type=MESH)

    padded[...] = jnp.zeros_like(padded)
    for t in range(2):
        padded[16 * t : 16 * t + 9, :] = con_ref[:, t, :]
    table_ref[...] = jnp.zeros_like(table_ref)
    table_ref[0:SHARE_LANES, 0:ELEMENTS] = emb_ref[...]
    both = [fil_ref[t].reshape(LANES, 64) for t in range(2)]
    blob[group, 0:128, :] = jnp.concatenate(both, axis=1)
    blob[group, 128:160, :] = table_ref[0:SHARE_LANES, :]
    blob[group, 160:168, :] = dense(read_ref[...].reshape(32, SHARE_LANES))
    blob[group, 168:176, :] = dense(padded[...])

    atom = lax.broadcasted_iota(jnp.int32, (1, count), 1)
    leading = neigh_ref[0:1, :] - block * count
    first = jnp.where((neigh_ref[0:1, :] >= 0) & (leading < atom), leading, atom)
    ext[...] = jnp.zeros_like(ext)
    ext[0:3, 0:count] = pos_ref[...]
    ext[3:4, 0:count] = first.astype(jnp.float32)
    ext[4:5, 0:count] = spec_ref[...].astype(jnp.float32)
    ext[5:6, 0:count] = lab_ref[...].astype(jnp.float32)
    ext[8:11, 0:count] = tgt_ref[...]

    pl.semaphore_wait(barrier, GROUPS + 1)
    copies = []
    for at, peer in enumerate(peers):
        copies.append(
            pltpu.make_async_remote_copy(
                src_ref=blob.at[group],
                dst_ref=blob.at[group],
                send_sem=send_sem.at[at],
                recv_sem=recv_sem.at[group],
                device_id={"chan": peer},
                device_id_type=MESH,
            )
        )
    halo_copy = pltpu.make_async_remote_copy(
        src_ref=ext.at[:, 0:LANES],
        dst_ref=halo,
        send_sem=halo_sem.at[0],
        recv_sem=halo_sem.at[1],
        device_id={"atoms": before},
        device_id_type=MESH,
    )
    halo_copy.start()
    for copy in copies:
        copy.start()

    halo_copy.wait()
    kind = lax.broadcasted_iota(jnp.int32, (16, LANES), 0)
    lane = lax.broadcasted_iota(jnp.int32, (16, LANES), 1)
    there = (lane < GHOST) & (block < BLOCKS - 1)
    shifted = halo[...] + jnp.where(kind == 3, float(count), 0.0)
    nothing = jnp.where(kind == 3, -1.0e6, 0.0)
    ext[:, count : count + LANES] = jnp.where(there, shifted, nothing)
    share = count // GROUPS
    wide = ext[:, pl.ds(pl.multiple_of(group * share, LANES), 2 * LANES)]
    for unit in range(share // UNIT):
        view = wide if unit == 0 else pltpu.roll(wide, 2 * LANES - unit * UNIT, 1)
        view = view[:, :LANES]
        start = (group * share + unit * UNIT).astype(jnp.float32)
        view = view - jnp.where(kind == 3, start, 0.0)
        win_ref[unit] = jnp.where(lane < WINDOW, view, nothing)

    for at, peer in enumerate(peers):
        pltpu.make_async_remote_copy(
            src_ref=blob.at[peer],
            dst_ref=blob.at[peer],
            send_sem=send_sem.at[at],
            recv_sem=recv_sem.at[peer],
            device_id={"chan": peer},
            device_id_type=MESH,
        ).wait_recv()
    for k in range(GROUPS):
        part = pl.ds(k * SHARE_LANES, SHARE_LANES)
        for t in range(2):
            full_ref[t, :, part, :] = blob[k, 0:128, 64 * t : 64 * t + 64].reshape(
                4, SHARE_LANES, 64
            )
        table_ref[part, :] = blob[k, 128:160, :]
    rd_ref[...] = undense([blob[k, 160:168, :] for k in range(GROUPS)]).reshape(2, 16, LANES)
    cont_ref[...] = undense([blob[k, 168:176, :] for k in range(GROUPS)]).reshape(2, 16, LANES)
    for copy in copies:
        copy.wait_send()


def collect(positions, species, neighbours, labelled, targets, embedding, filters, contract, readout):
    f32 = jnp.float32
    count = positions.shape[1]
    vmem = pl.BlockSpec(memory_space=pltpu.VMEM)
    return pl.pallas_call(
        collect_kernel,
        in_specs=[vmem] * 9,
        out_specs=[vmem] * 5,
        out_shape=[
            jax.ShapeDtypeStruct((count // GROUPS // UNIT, 16, LANES), f32),
            jax.ShapeDtypeStruct((LANES, LANES), f32),
            jax.ShapeDtypeStruct((2, 4, LANES, 64), f32),
            jax.ShapeDtypeStruct((2, 16, LANES), f32),
            jax.ShapeDtypeStruct((2, 16, LANES), f32),
        ],
        scratch_shapes=[
            pltpu.VMEM((GROUPS, BLOB, LANES), f32),
            pltpu.VMEM((32, SHARE_LANES), f32),
            pltpu.VMEM((16, count + LANES), f32),
            pltpu.VMEM((16, LANES), f32),
            pltpu.SemaphoreType.DMA((GROUPS - 1,)),
            pltpu.SemaphoreType.DMA((GROUPS,)),
            pltpu.SemaphoreType.DMA((2,)),
        ],
        compiler_params=pltpu.CompilerParams(collective_id=0, has_side_effects=True),
    )(
        positions,
        species[None],
        neighbours,
        labelled[None],
        targets,
        embedding,
        filters,
        contract,
        readout,
    )


def reduce_kernel(
    force_ref,
    stat_ref,
    g_emb,
    g_bes,
    g_rad,
    g_fil,
    g_con,
    g_mix,
    g_read,
    g_en,
    forces_ref,
    own_ref,
    rest_ref,
    pieces,
    core_in,
    line_out,
    line_in,
    summed,
    sub_in,
    sub_out,
    total,
    quarters,
    windows,
    tail,
    tail_in,
    sems,
    sub_send,
    sub_recv,
    total_send,
    total_recv,
):
    f32 = jnp.float32
    block, group = lax.axis_index("atoms"), lax.axis_index("chan")
    line, core = group // 2, lax.rem(group, 2)
    core_peer = {"chan": line * 2 + (1 - core)}
    line_peer = {"chan": (1 - line) * 2 + core}
    others = [lax.rem(block + offset, BLOCKS) for offset in range(1, BLOCKS)]
    barrier = pltpu.get_barrier_semaphore()
    for peer in [core_peer, line_peer] + [{"atoms": other} for other in others]:
        pl.semaphore_signal(barrier, inc=1, device_id=peer, device_id_type=MESH)

    def copy(source, dest, at, peer):
        return pltpu.make_async_remote_copy(
            src_ref=source,
            dst_ref=dest,
            send_sem=sems.at[2 * at],
            recv_sem=sems.at[2 * at + 1],
            device_id=peer,
            device_id_type=MESH,
        )

    rows = lax.broadcasted_iota(jnp.int32, (16, LANES), 0)
    lanes = lax.broadcasted_iota(jnp.int32, (16, LANES), 1)
    vector = jnp.zeros((1, LANES), f32)
    for t in range(2):
        spread = jnp.broadcast_to(g_en[t], (16, LANES))
        vector = vector + jnp.sum(
            jnp.where(lanes == rows + 16 * t, spread, 0.0), axis=0, keepdims=True
        )
    inner = g_rad[...].reshape(256, 64)
    inner = jnp.concatenate([inner[:128], inner[128:]], axis=1)
    bessel = jnp.concatenate([g_bes[0], g_bes[1]], axis=1)
    for k in range(GROUPS):
        where = (k % 2, k // 2)
        part = pl.ds(k * SHARE_LANES, SHARE_LANES)
        both = [g_fil[t, :, part, :].reshape(LANES, 64) for t in range(2)]
        pieces[(*where, pl.ds(0, 128), slice(None))] = jnp.concatenate(both, axis=1)
        pieces[(*where, pl.ds(128, 32), slice(None))] = g_emb[part, :]
        pieces[(*where, pl.ds(160, 8), slice(None))] = dense(
            lanes_of(g_read[...].reshape(32, LANES), k)
        )
        pieces[(*where, pl.ds(168, 8), slice(None))] = dense(
            lanes_of(g_con[...].reshape(32, LANES), k)
        )
        pieces[(*where, pl.ds(176, 64), slice(None))] = g_mix[k // 2, 64 * (k % 2) : 64 * (k % 2) + 64, :]
        pieces[(*where, pl.ds(240, 32), slice(None))] = inner[32 * k : 32 * k + 32]
        pieces[(*where, pl.ds(272, 8), slice(None))] = jnp.concatenate(
            [bessel[2 * k : 2 * k + 2], vector, stat_ref[0:2, :], jnp.zeros((3, LANES), f32)],
            axis=0,
        )
    windows[line, core] = force_ref[...]
    pl.semaphore_wait(barrier, BLOCKS + 1)

    core_copy = copy(pieces.at[1 - core], core_in, 0, core_peer)
    core_copy.start()
    core_force = copy(windows.at[line, core], windows.at[line, core], 1, core_peer)
    core_force.start()
    core_copy.wait()
    line_out[...] = pieces[core, 1 - line] + core_in[1 - line]
    line_copy = copy(line_out, line_in, 2, line_peer)
    line_copy.start()
    core_force.wait()
    line_force = copy(windows.at[line], windows.at[line], 3, line_peer)
    line_force.start()
    partial = pieces[core, line] + core_in[line]
    line_force.wait()

    lane8 = lax.broadcasted_iota(jnp.int32, (8, LANES), 1)
    canvas = [jnp.zeros((8, LANES), f32)] * 5
    for k in range(8):
        value = windows[k // 4, (k // 2) % 2, k % 2]
        if k % 2 == 0:
            canvas[k // 2] = canvas[k // 2] + value
        else:
            value = pltpu.roll(value, 64, 1)
            canvas[k // 2] = canvas[k // 2] + jnp.where(lane8 >= 64, value, 0.0)
            canvas[k // 2 + 1] = canvas[k // 2 + 1] + jnp.where(lane8 < 64, value, 0.0)
    tail[...] = canvas[4]
    tail_copy = copy(tail, tail_in, 4, {"atoms": others[0]})
    tail_copy.start()

    line_copy.wait()
    summed[7] = jnp.zeros((SUB, LANES), f32)
    partial = partial + line_in[...]
    for k in range(7):
        size = min(SUB, PIECE - k * SUB)
        summed[k, 0:size, :] = partial[k * SUB : k * SUB + size]
        if size < SUB:
            summed[k, size:SUB, :] = jnp.zeros((SUB - size, LANES), f32)

    def sub_copy(other, at):
        return pltpu.make_async_remote_copy(
            src_ref=summed.at[other],
            dst_ref=sub_in.at[block],
            send_sem=sub_send.at[at],
            recv_sem=sub_recv.at[block],
            device_id={"atoms": other},
            device_id_type=MESH,
        )

    def total_copy(other, at):
        return pltpu.make_async_remote_copy(
            src_ref=sub_out,
            dst_ref=total.at[block],
            send_sem=total_send.at[at],
            recv_sem=total_recv.at[block],
            device_id={"atoms": other},
            device_id_type=MESH,
        )

    def arrival(dest, recv, other):
        return pltpu.make_async_remote_copy(
            src_ref=sub_out,
            dst_ref=dest.at[other],
            send_sem=sub_send.at[0],
            recv_sem=recv.at[other],
            device_id={"atoms": other},
            device_id_type=MESH,
        )

    subs = [sub_copy(other, at) for at, other in enumerate(others)]
    for item in subs:
        item.start()
    value = summed[block]
    for other in others:
        arrival(sub_in, sub_recv, other).wait_recv()
        value = value + sub_in[other]
    sub_out[...] = value
    totals = [total_copy(other, at) for at, other in enumerate(others)]
    for item in totals:
        item.start()
    total[block] = value
    tail_copy.wait()
    forces = jnp.concatenate(canvas[:4], axis=1)
    edge = jnp.where((lane8 < GHOST) & (block > 0), tail_in[...], 0.0)
    forces_ref[...] = forces
    forces_ref[:, 0:LANES] = canvas[0] + edge
    for other in others:
        arrival(total, total_recv, other).wait_recv()
    for item in subs + totals:
        item.wait_send()

    everything = total[...].reshape(BLOCKS * SUB, LANES)
    own_ref[...] = everything[:BLOB]
    flat = everything[:274]
    energy_row = everything[274:275]
    squares = jnp.sum(flat * flat, axis=0, keepdims=True)
    squares = squares + (1.0 / GROUPS) * energy_row * energy_row
    squares = jnp.sum(squares, axis=1, keepdims=True)
    quarters[line, core] = everything[BLOB:PIECE]
    quarters[line, core, 101:102, :] = jnp.broadcast_to(squares, (1, LANES))
    line_quarter = copy(quarters.at[line, core], quarters.at[line, core], 5, line_peer)
    line_quarter.start()
    core_quarter = copy(quarters.at[line, core], quarters.at[line, core], 6, core_peer)
    core_quarter.start()
    line_quarter.wait()
    cross_quarter = copy(quarters.at[1 - line, core], quarters.at[1 - line, core], 7, core_peer)
    cross_quarter.start()
    core_quarter.wait()
    cross_quarter.wait()
    rest_ref[...] = quarters[...].reshape(GROUPS, QUARTER, LANES)


def reduce_all(force, stat, grads):
    f32 = jnp.float32
    vmem = pl.BlockSpec(memory_space=pltpu.VMEM)
    dma = pltpu.SemaphoreType.DMA
    return pl.pallas_call(
        reduce_kernel,
        in_specs=[vmem] * 10,
        out_specs=[vmem] * 3,
        out_shape=[
            jax.ShapeDtypeStruct((8, 4 * LANES), f32),
            jax.ShapeDtypeStruct((BLOB, LANES), f32),
            jax.ShapeDtypeStruct((GROUPS, QUARTER, LANES), f32),
        ],
        scratch_shapes=[
            pltpu.VMEM((2, 2, PIECE, LANES), f32),
            pltpu.VMEM((2, PIECE, LANES), f32),
            pltpu.VMEM((PIECE, LANES), f32),
            pltpu.VMEM((PIECE, LANES), f32),
            pltpu.VMEM((BLOCKS, SUB, LANES), f32),
            pltpu.VMEM((BLOCKS, SUB, LANES), f32),
            pltpu.VMEM((SUB, LANES), f32),
            pltpu.VMEM((BLOCKS, SUB, LANES), f32),
            pltpu.VMEM((2, 2, QUARTER, LANES), f32),
            pltpu.VMEM((2, 2, 2, 8, LANES), f32),
            pltpu.VMEM((8, LANES), f32),
            pltpu.VMEM((8, LANES), f32),
            dma((16,)),
            dma((BLOCKS - 1,)),
            dma((BLOCKS,)),
            dma((BLOCKS - 1,)),
            dma((BLOCKS,)),
        ],
        compiler_params=pltpu.CompilerParams(collective_id=1, has_side_effects=True),
    )(force, stat, *grads)


def adam_kernel(*refs):
    forces_in, own_ref, rest_ref = refs[:3]
    weights, moments = refs[3:11], refs[11:27]
    parts_ref, forces_ref, norm_ref = refs[27:30]
    results = refs[30:54]
    scratch = refs[54]
    rest = [rest_ref[k] for k in range(GROUPS)]
    stats = rest[0]
    loss = jnp.sum(stats[99:100], axis=1, keepdims=True)
    count = jnp.sum(stats[100:101], axis=1, keepdims=True)
    inverse = 1.0 / count
    squares = sum(rest[k][101:102, 0:1] for k in range(GROUPS))
    norm = jnp.sqrt(squares) * inverse
    factor = inverse * jnp.minimum(1.0, CLIP_NORM / (norm + 1e-06))
    norm_ref[...] = norm
    two = lax.broadcasted_iota(jnp.int32, (1, 2), 1)
    parts_ref[...] = jnp.where(two == 0, loss, count)
    forces_ref[...] = forces_in[0:3, :]

    def narrow(value):
        return jnp.concatenate([lanes_of(value, k) for k in range(GROUPS)], axis=0)

    fil = [own_ref[0:128, 64 * t : 64 * t + 64].reshape(4, SHARE_LANES, 64) for t in range(2)]
    emb = own_ref[128:160, 0:ELEMENTS]
    read = narrow(own_ref[160:168, :]).reshape(2, 16, SHARE_LANES)
    scratch[...] = narrow(own_ref[168:176, :])
    con = [scratch[0:9, :], scratch[16:25, :]]
    mix = jnp.concatenate([rest[k][0:64] for k in range(GROUPS)], axis=0).reshape(2, LANES, LANES)
    inner = jnp.concatenate([rest[k][64:96] for k in range(GROUPS)], axis=0)
    inner = jnp.concatenate([inner[:, :64], inner[:, 64:]], axis=0).reshape(2, 2, 64, 64)
    bes = jnp.concatenate([rest[k][96:98] for k in range(GROUPS)], axis=0)
    bes = [bes[:, :64], bes[:, 64:]]
    vector = rest[0][98:99]
    vector = jnp.concatenate([vector[:, 0:16], vector[:, 16:32]], axis=0)

    def update(which, gradient, at):
        first, square = moments[2 * which], moments[2 * which + 1]
        weight = weights[which][at]
        clipped = gradient * factor
        moment = BETA_ONE * first[at] + (1.0 - BETA_ONE) * clipped
        second = BETA_TWO * square[at] + (1.0 - BETA_TWO) * clipped * clipped
        corrected_first = moment * (1.0 / (1.0 - BETA_ONE**ADAM_STEP))
        corrected_second = second * (1.0 / (1.0 - BETA_TWO**ADAM_STEP))
        updated = weight - RATE * (
            corrected_first / (jnp.sqrt(corrected_second) + EPSILON) + DECAY * weight
        )
        results[3 * which][at] = updated
        results[3 * which + 1][at] = moment
        results[3 * which + 2][at] = second

    everything = Ellipsis
    update(0, emb, everything)
    for t in range(2):
        update(1, bes[t], t)
        update(3, fil[t], t)
        update(4, con[t], (slice(None), t))
    update(2, inner, everything)
    update(5, mix, everything)
    update(6, read, everything)
    update(7, vector, everything)


def adam(forces, own, rest, weights, moments):
    f32 = jnp.float32
    vmem = pl.BlockSpec(memory_space=pltpu.VMEM)
    shapes = [(1, 2), (3, forces.shape[1]), (1, 1)]
    shapes += [weight.shape for weight in weights for _ in range(3)]
    return pl.pallas_call(
        adam_kernel,
        in_specs=[vmem] * 27,
        out_specs=[vmem] * 27,
        out_shape=[jax.ShapeDtypeStruct(shape, f32) for shape in shapes],
        scratch_shapes=[pltpu.VMEM((32, SHARE_LANES), f32)],
    )(forces, own, rest, *weights, *moments)


def adamw(weight, gradient, first, second, scale):
    clipped = gradient * scale
    moment = BETA_ONE * first + (1.0 - BETA_ONE) * clipped
    second_new = BETA_TWO * second + (1.0 - BETA_TWO) * clipped * clipped
    corrected_first = moment / (1.0 - BETA_ONE**ADAM_STEP)
    corrected_second = second_new / (1.0 - BETA_TWO**ADAM_STEP)
    updated = weight - RATE * (
        corrected_first / (jnp.sqrt(corrected_second) + EPSILON) + DECAY * weight
    )
    return (updated, moment, second_new)


def per_device(
    positions,
    species,
    neighbours,
    labelled,
    target_forces,
    embedding,
    bessel,
    radial,
    filters,
    contract,
    mixing,
    readout,
    energies,
    first_embedding,
    square_embedding,
    first_bessel,
    square_bessel,
    first_radial,
    square_radial,
    first_filters,
    square_filters,
    first_contract,
    square_contract,
    first_mixing,
    square_mixing,
    first_readout,
    square_readout,
    first_energies,
    square_energies,
):
    if (lax.axis_size("atoms"), lax.axis_size("chan")) == (BLOCKS, GROUPS):
        turns = [(1, 0), None, None, (0, 1, 3, 2), (1, 0, 2), None, None, None]

        def turned(value, order):
            return value if order is None else value.transpose(order)

        weights = (embedding, bessel, radial, filters, contract, mixing, readout, energies)
        weights = [turned(value, order) for value, order in zip(weights, turns)]
        moments = (
            first_embedding,
            square_embedding,
            first_bessel,
            square_bessel,
            first_radial,
            square_radial,
            first_filters,
            square_filters,
            first_contract,
            square_contract,
            first_mixing,
            square_mixing,
            first_readout,
            square_readout,
            first_energies,
            square_energies,
        )
        moments = [turned(value, turns[k // 2]) for k, value in enumerate(moments)]
        windows, table, full, cont, read = collect(
            positions,
            species,
            neighbours,
            labelled,
            target_forces,
            weights[0],
            weights[3],
            weights[4],
            readout,
        )
        force, stat, *grads = local_step(
            windows, table, bessel, radial, full, cont, mixing, read, energies
        )
        forces, own, rest = reduce_all(force, stat, grads)
        parts, forces, norm, *results = adam(forces, own, rest, weights, moments)
        results = [turned(value, turns[k // 3]) for k, value in enumerate(results)]
        return tuple([parts.reshape(2), forces, norm.reshape(())] + results)
    f32 = jnp.float32
    atom_count = positions.shape[1]
    local_chan = embedding.shape[1]
    blocks, groups = lax.axis_size("atoms"), lax.axis_size("chan")
    block, group = lax.axis_index("atoms"), lax.axis_index("chan")
    atom_base = block * atom_count
    share = atom_count // groups
    units = share // UNIT

    atom_index = atom_base + jnp.arange(atom_count, dtype=jnp.int32)
    leading = neighbours[0]
    first_atom = jnp.where((leading >= 0) & (leading < atom_index), leading, atom_index)
    packed = jnp.concatenate(
        [
            positions,
            (first_atom - atom_base).astype(f32)[None],
            species.astype(f32)[None],
            labelled.astype(f32)[None],
            jnp.zeros((2, atom_count), f32),
            target_forces,
            jnp.zeros((5, atom_count), f32),
        ],
        axis=0,
    )
    down = [(i + 1, i) for i in range(blocks - 1)]
    halo = lax.ppermute(packed[:, :GHOST], "atoms", down)
    halo_row = jnp.arange(16)[:, None] == 3
    halo = jnp.where(halo_row, jnp.where(block == blocks - 1, -1.0e6, halo + atom_count), halo)
    missing = jnp.where(jnp.arange(16)[:, None] == 3, -1.0e6, 0.0) * jnp.ones((1, LANES), f32)
    extended = jnp.concatenate([packed, halo, missing], axis=1)
    windows = []
    for unit in range(units):
        start = group * share + unit * UNIT
        window = lax.dynamic_slice(extended, (0, start), (16, WINDOW))
        shift = jnp.where(jnp.arange(16)[:, None] == 3, start.astype(f32), 0.0)
        window = window - shift
        windows.append(jnp.concatenate([window, missing[:, : LANES - WINDOW]], axis=1))
    windows = jnp.stack(windows)

    def whole(value):
        return lax.all_gather(value, "chan", axis=value.ndim - 1, tiled=True)

    table = jnp.concatenate(
        [whole(embedding), jnp.zeros((LANES - ELEMENTS, LANES), f32)], axis=0
    ).T
    force, stat, *grads = local_step(
        windows,
        table,
        bessel,
        radial,
        whole(filters).swapaxes(2, 3),
        jnp.pad(whole(contract), ((0, 0), (0, 7), (0, 0))),
        mixing,
        whole(readout),
        energies,
    )
    grad_embed, grad_bessel, grad_radial, grad_filters, grad_contract, grad_mixing = grads[:6]
    grad_readout, grad_vectors = grads[6:]
    grad_embed = grad_embed.T[:ELEMENTS]
    grad_filters = grad_filters.swapaxes(2, 3)
    grad_contract = grad_contract[:, :9]
    grad_vectors = grad_vectors[:, :, 0]

    canvas = jnp.zeros((3, atom_count + LANES), f32)
    for unit in range(units):
        start = group * share + unit * UNIT
        old = lax.dynamic_slice(canvas, (0, start), (3, WINDOW))
        canvas = lax.dynamic_update_slice(canvas, old + force[unit, :3, :WINDOW], (0, start))
    canvas = lax.psum(canvas, "chan")
    up = [(i, i + 1) for i in range(blocks - 1)]
    arrived = lax.ppermute(canvas[:, atom_count : atom_count + GHOST], "atoms", up)
    forces = canvas[:, :atom_count].at[:, :GHOST].add(arrived)

    def split(value):
        return lax.psum_scatter(value, "chan", scatter_dimension=value.ndim - 1, tiled=True)

    grad_embed, grad_filters, grad_contract, grad_readout = lax.psum(
        (split(grad_embed), split(grad_filters), split(grad_contract), split(grad_readout)),
        "atoms",
    )
    grad_bessel, grad_radial, grad_mixing, grad_vectors, loss_sum, label_total = lax.psum(
        (grad_bessel, grad_radial, grad_mixing, grad_vectors, jnp.sum(stat[0]), jnp.sum(stat[1])),
        ("atoms", "chan"),
    )
    gradients = [
        gradient / label_total
        for gradient in (
            grad_embed,
            grad_bessel,
            grad_radial,
            grad_filters,
            grad_contract,
            grad_mixing,
            grad_readout,
            grad_vectors,
        )
    ]
    squares_of = [jnp.sum(gradient * gradient) for gradient in gradients]
    split_squares = squares_of[0] + squares_of[3] + squares_of[4] + squares_of[6]
    whole_squares = squares_of[1] + squares_of[2] + squares_of[5] + squares_of[7]
    grad_norm = jnp.sqrt(lax.psum(split_squares, "chan") + whole_squares)
    scale = jnp.minimum(1.0, CLIP_NORM / (grad_norm + 1e-06))
    weights = (embedding, bessel, radial, filters, contract, mixing, readout, energies)
    firsts = (
        first_embedding,
        first_bessel,
        first_radial,
        first_filters,
        first_contract,
        first_mixing,
        first_readout,
        first_energies,
    )
    squares = (
        square_embedding,
        square_bessel,
        square_radial,
        square_filters,
        square_contract,
        square_mixing,
        square_readout,
        square_energies,
    )
    results = []
    for weight, gradient, first, second in zip(weights, gradients, firsts, squares):
        results.extend(adamw(weight, gradient, first, second, scale))
    return tuple([jnp.stack([loss_sum, label_total]), forces, grad_norm] + results)


def solution(mesh):
    whole = P()
    columns = P(None, "atoms")
    by_weight = [
        P(None, "chan"),
        whole,
        whole,
        P(None, None, None, "chan"),
        P(None, None, "chan"),
        whole,
        P(None, None, "chan"),
        whole,
    ]
    in_specs = [columns, P("atoms"), columns, P("atoms"), columns] + by_weight
    in_specs += [spec for spec in by_weight for _ in range(2)]
    out_specs = [whole, columns, whole] + [spec for spec in by_weight for _ in range(3)]
    return jax.shard_map(
        per_device,
        mesh=mesh,
        in_specs=tuple(in_specs),
        out_specs=tuple(out_specs),
        check_vma=False,
    )
```

```python
import functools
import math

import jax
import jax.numpy as jnp
from jax import lax
from jax.experimental import pallas as pl
from jax.experimental.pallas import tpu as pltpu
from jax.sharding import PartitionSpec as P

ELEMENTS = 89
NBESSEL = 8
GHOST = 8
ADAM_STEP = 10

RCUT = 5.0
SMOOTH = 0.01
NEIGHBOURS_MEAN = 8.0
HUBER_DELTA = 1.0
CLIP_NORM = 0.001
RATE = 0.2
BETA_ONE = 0.9
BETA_TWO = 0.999
EPSILON = 1e-08
DECAY = 0.01

UNIT = 64
WINDOW = UNIT + 16
LANES = 128
DIRECTED = 15
TILES = WINDOW // 8
CHUNK = 80
EDGE_BLOCKS = 2 * CHUNK
FLAT = 8 * CHUNK
DEGREES = [0] + [1] * 3 + [2] * 5 + [3] * 7
EXACT = lax.Precision.HIGHEST

def shapes_of(x, y, z, root_three=math.sqrt(3.0)):
    xx, yy, zz = x * x, y * y, z * z
    xy, yz, zx = x * y, y * z, z * x
    both, less = xx + yy, xx - yy
    wide = 4.0 * zz - both
    return [
        x,
        y,
        z,
        root_three * xy,
        root_three * yz,
        zz - 0.5 * both,
        root_three * zx,
        (0.5 * root_three) * less,
        math.sqrt(5.0 / 8.0) * y * (3.0 * xx - yy),
        math.sqrt(15.0) * xy * z,
        math.sqrt(3.0 / 8.0) * y * wide,
        z * (zz - 1.5 * both),
        math.sqrt(3.0 / 8.0) * x * wide,
        (0.5 * math.sqrt(15.0)) * z * less,
        math.sqrt(5.0 / 8.0) * x * (xx - 3.0 * yy),
    ]


def slants_of(bar):
    third = 1.0 / math.sqrt(3.0)
    root = math.sqrt(3.0)
    a, b, c, d = (
        math.sqrt(5.0 / 8.0),
        math.sqrt(15.0),
        math.sqrt(3.0 / 8.0),
        0.5 * math.sqrt(15.0),
    )
    one = [[(0, bar[1])], [(0, bar[2])], [(0, bar[3])]]
    four, five, seven, eight = [root * bar[lm] for lm in (4, 5, 7, 8)]
    two = [
        [(2, four), (3, seven), (1, eight - bar[6])],
        [(1, four), (3, five), (2, -eight - bar[6])],
        [(2, five), (1, seven), (3, 2.0 * bar[6])],
    ]
    mixed = (b * third) * bar[10]
    three = [
        [
            (4, (6.0 * a * third) * bar[9] - (2.0 * c * third) * bar[11]),
            (5, mixed),
            (7, (2.0 * d * third) * bar[14] - root * bar[12]),
            (6, (4.0 * c) * bar[13]),
            (8, (6.0 * a * third) * bar[15] - (2.0 * c * third) * bar[13]),
        ],
        [
            (4, (-2.0 * c * third) * bar[13] - (6.0 * a * third) * bar[15]),
            (5, (-2.0 * d * third) * bar[14] - root * bar[12]),
            (7, mixed),
            (6, (4.0 * c) * bar[11]),
            (8, (6.0 * a * third) * bar[9] + (2.0 * c * third) * bar[11]),
        ],
        [
            (4, mixed),
            (5, (8.0 * c * third) * bar[11]),
            (7, (8.0 * c * third) * bar[13]),
            (6, 3.0 * bar[12]),
            (8, (2.0 * d * third) * bar[14]),
        ],
    ]
    return one, two, three


def radius_of(x, y, z, valid):
    distance = jnp.sqrt((x * x + y * y + z * z) * (RCUT * RCUT) + SMOOTH)
    scaled = distance * (1.0 / RCUT)
    square = scaled * scaled
    fifth = square * square * scaled
    envelope = 1.0 - fifth * (21.0 - 35.0 * scaled + 15.0 * square)
    envelope = jnp.where(scaled < 1.0, envelope, 0.0) * (valid * (1.0 / NEIGHBOURS_MEAN))
    return distance, envelope


def halves_of(value):
    high = value.astype(jnp.bfloat16)
    low = (value - high.astype(jnp.float32)).astype(jnp.bfloat16)
    return high, low


def dot(left, right, left_dim, right_dim):
    return lax.dot_general(
        left,
        right,
        (((left_dim,), (right_dim,)), ((), ())),
        preferred_element_type=jnp.float32,
    )


def fine(left, right, left_dim, right_dim):
    left_high, left_low = halves_of(left)
    right_high, right_low = halves_of(right)
    rows = left.shape[0]
    if left_dim == 1 and rows % 16 == 0:
        both = dot(jnp.concatenate([left_high, left_low], axis=0), right_high, 1, right_dim)
        return both[:rows] + both[rows:] + dot(left_high, right_low, 1, right_dim)
    return (
        dot(left_high, right_high, left_dim, right_dim)
        + dot(left_low, right_high, left_dim, right_dim)
        + dot(left_high, right_low, left_dim, right_dim)
    )


def fine_rows(left, right):
    rows = left.shape[0]
    left_high, left_low = halves_of(left)
    right_high, right_low = halves_of(right)
    both = dot(jnp.concatenate([left_high, left_low], axis=0), right_high, 1, 1)
    return both[:rows] + both[rows:] + dot(left_high, right_low, 1, 1)


def triple(value):
    high, low = halves_of(value)
    return jnp.concatenate([high, high, low], axis=0)


def add(total, term):
    return term if total is None else total + term


def members(degree):
    return range(degree * degree, (degree + 1) ** 2)


def thirds(values):
    parts = []
    for value in values:
        for _ in range(3):
            part = value.astype(jnp.bfloat16).astype(jnp.float32)
            parts.append(part)
            value = value - part
    parts += [jnp.zeros_like(parts[0])] * (16 - len(parts))
    return jnp.concatenate(parts, axis=0).astype(jnp.bfloat16)


def joined(rows, count):
    return [
        rows[3 * k : 3 * k + 1] + rows[3 * k + 1 : 3 * k + 2] + rows[3 * k + 2 : 3 * k + 3]
        for k in range(count)
    ]


def sine_cosine(angle):
    half = 0.5 * angle - (0.5 * math.pi)
    square = half * half
    sine = cosine = 0.0
    for k in range(6, -1, -1):
        cosine = cosine * square + (-1) ** k / math.factorial(2 * k)
        if k < 6:
            sine = sine * square + (-1) ** k / math.factorial(2 * k + 1)
    sine = sine * half
    return -2.0 * sine * cosine, 2.0 * sine * sine - 1.0


def both_sides(value):
    wide = jnp.broadcast_to(value, (16, LANES))
    back = pltpu.roll(wide, 1, 1, stride=1, stride_axis=0)
    ahead = pltpu.roll(wide, 113, 1, stride=1, stride_axis=0)
    return back, ahead


def neighbour_counts(first):
    own = jnp.where((first >= 0.0) & (first < float(UNIT)), 1.0, 0.0)
    slot_row = lax.broadcasted_iota(jnp.int32, (16, LANES), 0)
    back_first, ahead_first = both_sides(first)
    same = (slot_row < DIRECTED) & ((back_first == first) | (ahead_first == first))
    return jnp.sum(jnp.where(same, 1.0, 0.0), axis=0, keepdims=True) * own, own


def step_kernel(
    win_ref,
    emb_ref,
    bes_ref,
    rad_ref,
    fil_ref,
    con_ref,
    mix_ref,
    read_ref,
    en_ref,
    force_ref,
    stat_ref,
    g_emb,
    g_bes,
    g_rad,
    g_fil,
    g_con,
    g_mix,
    g_read,
    g_en,
    begin_ref,
    yy,
    dyy,
    feats,
    dfeats,
    fj,
    dfj,
    fdir,
    dfdir,
    fb,
    fjb,
    wb,
    amat,
    damat,
    msg,
    msgb,
    dmsg,
    zs,
    sg,
    dz,
    hidb,
    hidu,
    bess,
    rows_ref,
    turn_ref,
    hot_j,
    hot_d,
    turned_j,
    turned_d,
    barrow,
    gcon,
    tab_w,
    bes_w,
    bes_b,
    rad_w,
    rad_b,
    fil_w,
    fil_b,
    g_tab,
    g_wide,
):
    f32, bf16, i32 = jnp.float32, jnp.bfloat16, jnp.int32
    pulls = dyy

    @pl.when(pl.program_id(0) == 0)
    def _():
        for ref in (g_tab, g_wide, g_bes, g_rad, g_con, g_mix, g_read, g_en, stat_ref):
            ref[...] = jnp.zeros_like(ref)
        for ref in (feats, dfeats, fjb):
            ref[...] = jnp.zeros_like(ref)

        def clear(sixteen, carry):
            for t in range(2):
                fb[t, pl.ds(16 * sixteen, 16)] = jnp.zeros((16, 4, 8, LANES), f32)
            return carry

        lax.fori_loop(0, EDGE_BLOCKS // 16, clear, 0)
        tab_w[...] = jnp.concatenate(list(halves_of(emb_ref[...].T)), axis=0)
        for t in range(2):
            high, low = [value.astype(f32) for value in halves_of(bes_ref[t])]
            bes_w[t] = jnp.concatenate([high, low, high, jnp.zeros_like(high)], axis=0).T.astype(
                bf16
            )
            bes_b[t] = jnp.concatenate([high, low, high], axis=1).astype(bf16)
            for depth in range(2):
                high, low = [value.astype(f32) for value in halves_of(rad_ref[t, depth])]
                rad_b[t, depth] = jnp.concatenate([high, low, high], axis=1).astype(bf16)
                rad_w[t, depth] = jnp.concatenate([high, low, high], axis=0).T.astype(bf16)
            high, low = halves_of(fil_ref[t].reshape(4 * LANES, 64).T)
            fil_w[t] = jnp.concatenate([high, low, high], axis=0)
            fil_b[t] = jnp.concatenate([high, low], axis=0)

    count, own = neighbour_counts(win_ref[0, 3:4, :])

    line = lax.broadcasted_iota(i32, (LANES, LANES), 0)
    place = lax.broadcasted_iota(i32, (LANES, LANES), 1)
    key = jnp.broadcast_to(count + own, (LANES, LANES))
    other = key.T
    ahead_of = (other > key) | ((other == key) & (line < place))
    rank = jnp.sum(jnp.where(ahead_of, 1.0, 0.0), axis=0, keepdims=True)
    order_t = jnp.where(line.astype(f32) == rank, 1.0, 0.0).astype(bf16)
    index = lax.broadcasted_iota(i32, (1, LANES), 1).astype(f32)
    wide = jnp.concatenate(
        [win_ref[0], count, index, jnp.zeros((14, LANES), f32)], axis=0
    )
    high, middle = halves_of(wide)
    low = (wide - high.astype(f32) - middle.astype(f32)).astype(bf16)
    moved = dot(jnp.concatenate([high, middle, low], axis=0), order_t, 1, 1)
    turn_ref[0:32, :] = moved[0:32] + moved[32:64] + moved[64:96]

    def row(index):
        return turn_ref[index : index + 1, :]

    first, species, labelled = row(3), row(4), row(5)
    count, atom_id = row(16), row(17)
    own = jnp.where((first >= 0.0) & (first < float(UNIT)), 1.0, 0.0)
    atom_names = jnp.broadcast_to(atom_id, (LANES, LANES)).T[:, 0:1]

    lane_row = lax.broadcasted_iota(i32, (1, LANES), 1)
    used = lax.shift_right_logical(jnp.max(jnp.where(count > 0.0, lane_row, -8)) + 8, 3)
    for ref in (msg, dmsg):
        ref[...] = jnp.zeros_like(ref)
    begins, pairs = [jnp.int32(0)], []
    begin_ref[0] = 0
    for tile in range(TILES):
        mine = (lane_row >= 8 * tile) & (lane_row < 8 * tile + 8)
        most = jnp.max(jnp.where(mine, count, 0.0)).astype(i32)
        pairs.append(lax.shift_right_logical(most + 1, 1))
        begins.append(begins[-1] + pairs[-1])
        begin_ref[tile + 1] = begins[-1]
    total = begins[-1]
    chunks = jnp.int32(1)
    for k in range(1, EDGE_BLOCKS // CHUNK):
        chunks = chunks + jnp.where(2 * total > k * CHUNK, 1, 0)

    def each_chunk(body):
        def step(chunk, carry):
            body(chunk, pl.ds(chunk * CHUNK, CHUNK))
            return carry

        lax.fori_loop(0, chunks, step, 0)

    def each_tile(body):
        def step(tile, carry):
            body(tile, pl.ds(pl.multiple_of(tile * 8, 8), 8))
            return carry

        lax.fori_loop(0, used, step, 0)

    def each_block(tile, body, carry):
        start, stop = begin_ref[tile], begin_ref[tile + 1]
        doubles = lax.shift_right_logical(stop - start, 1)

        def four(index, held):
            block = 2 * start + 4 * index
            for k in range(4):
                held = body(block + k, held)
            return held

        carry = lax.fori_loop(0, doubles, four, carry)
        return lax.fori_loop(
            start + 2 * doubles,
            stop,
            lambda pair, held: body(2 * pair + 1, body(2 * pair, held)),
            carry,
        )

    def each_edge_block(body):
        def step(four, carry):
            for k in range(4):
                body(4 * four + k)
            return carry

        lax.fori_loop(0, lax.shift_right_logical(2 * total + 3, 2), step, 0)

    def natural(values):
        wide = jnp.concatenate(
            [jnp.broadcast_to(value, (LANES, LANES)).T for value in values], axis=1
        )
        high, middle = halves_of(wide)
        low = (wide - high.astype(f32) - middle.astype(f32)).astype(bf16)
        return jnp.concatenate([high, middle], axis=0), low

    def spread(chunk, blocks, parts, dest):
        left = turned_d[chunk]
        wide = dot(jnp.concatenate([left, left], axis=1), parts[0], 1, 0) + dot(
            left, parts[1], 1, 0
        )
        for k in range(3):
            dest[blocks, k] = wide[:, k * LANES : (k + 1) * LANES].reshape(CHUNK, 8, LANES)

    def layer_in(t, depth, value):
        if depth == 0:
            high, low = [part.astype(f32) for part in halves_of(value)]
            wide = jnp.concatenate([high, high, low, jnp.zeros_like(high)], axis=0).astype(bf16)
            return dot(bes_w[t], wide, 1, 0)
        return dot(rad_w[t, depth - 1], triple(value), 1, 0)

    def layer_back(t, depth, value):
        weight = bes_b[t] if depth == 0 else rad_b[t, depth - 1]
        return dot(weight, triple(value), 1, 0)

    def parts_of(t, chunk, depth):
        z, sig = zs[t, chunk, depth], sg[t, chunk, depth]
        h, rest = z * sig, 1.0 - sig
        return h, sig + h * rest, sig * rest * (2.0 + z - 2.0 * h)

    def sigmoid(z):
        return 0.5 * jnp.tanh(0.5 * z) + 0.5

    def filters_to(t, hidden, blocks, dest):
        wide = dot(triple(hidden), fil_w[t], 0, 0)
        for degree in range(4):
            dest[t, blocks, degree] = wide[:, degree * LANES : (degree + 1) * LANES].reshape(
                CHUNK, 8, LANES
            )

    def filters_back(t, high, low):
        both = dot(fil_b[t], high, 1, 1)
        return both[:64] + both[64:] + dot(fil_b[t, 0:64, :], low, 1, 1)

    def filters_grad(hidden, wide_high, wide_low):
        high, low = halves_of(hidden)
        both = dot(jnp.concatenate([high, low], axis=0), wide_high, 1, 0)
        return both[:64] + both[64:] + dot(high, wide_low, 1, 0)

    def filter_bars(t, blocks):
        parts = [
            halves_of(fb[t, blocks, degree].reshape(FLAT, LANES)) for degree in range(4)
        ]
        return [jnp.concatenate([part[k] for part in parts], axis=1) for k in range(2)]

    position_parts = natural([row(k) * (1.0 / RCUT) for k in range(3)])
    position_rows = thirds([row(k) * (1.0 / RCUT) for k in range(3)])
    atom_rows = jnp.concatenate(
        [first * own, count, atom_id, jnp.zeros((13, LANES), f32)], axis=0
    ).astype(bf16)
    begin_blocks = [2 * value for value in begins]

    def geometry(chunk, blocks):
        edge = lax.broadcasted_iota(i32, (1, FLAT), 1) + chunk * FLAT
        block = lax.shift_right_logical(edge, 3)
        tile = jnp.zeros_like(edge)
        base = jnp.zeros_like(edge)
        for k in range(1, TILES):
            past = block >= begin_blocks[k]
            tile = tile + jnp.where(past, 1, 0)
            base = base + jnp.where(past, 2 * pairs[k - 1], 0)
        atom = (tile * 8 + (edge & 7)).astype(f32)
        number = (block - base).astype(f32)
        atom_column = lax.broadcasted_iota(i32, (LANES, FLAT), 0).astype(f32)
        hot = jnp.where(atom_column == atom, 1.0, 0.0).astype(bf16)
        known = dot(atom_rows, hot, 1, 0)
        there = known[0:1] + number
        there = there + jnp.where(there >= known[2:3], 1.0, 0.0)
        valid = jnp.where(number < known[1:2], 1.0, 0.0)
        hot = jnp.where(atom_names == jnp.where(valid > 0.0, there, -1.0), 1.0, 0.0)
        difference = hot - jnp.where(
            atom_column == jnp.where(valid > 0.0, atom, -1.0), 1.0, 0.0
        )
        hot_j[chunk] = hot.astype(bf16)
        hot_d[chunk] = difference.astype(bf16)
        turned_j[chunk] = hot.T.astype(bf16)
        turned_d[chunk] = difference.T.astype(bf16)
        spread(chunk, blocks, position_parts, yy)
        rel = joined(dot(position_rows, hot_d[chunk], 1, 0), 3)
        distance, envelope = radius_of(*rel, valid)
        for k, value in enumerate(rel + [valid, envelope]):
            rows_ref[chunk, k : k + 1, :] = value
        sine, cosine = sine_cosine(distance * (math.pi / RCUT))
        sines, cosines = [sine], [cosine]
        for k in range(1, NBESSEL):
            before = (0.0, 1.0) if k == 1 else (sines[k - 2], cosines[k - 2])
            sines.append(2.0 * cosine * sines[-1] - before[0])
            cosines.append(2.0 * cosine * cosines[-1] - before[1])
        inverse = 1.0 / distance
        root = math.sqrt(2.0 / RCUT)
        for k in range(NBESSEL):
            basis = root * sines[k] * inverse
            bess[chunk, 0, k : k + 1, :] = basis
            bess[chunk, 1, k : k + 1, :] = (
                root * ((k + 1) * math.pi / RCUT) * cosines[k] - basis
            ) * inverse
        values = [bess[chunk, 0]] * 2
        for depth in range(3):
            for t in range(2):
                z = layer_in(t, depth, values[t])
                sig = sigmoid(z)
                zs[t, chunk, depth] = z
                sg[t, chunk, depth] = sig
                values[t] = z * sig
        for t in range(2):
            filters_to(t, values[t] * envelope, blocks, fdir)

    each_chunk(geometry)

    def point_shapes(block):
        values = shapes_of(*[yy[block, k] for k in range(3)])
        for k in range(3, 15):
            yy[block, k] = values[k]

    each_edge_block(point_shapes)

    def gather_from(value, dest):
        both = jnp.concatenate(list(halves_of(value)), axis=1)

        def body(chunk, blocks):
            wide = dot(turned_j[chunk], both, 1, 0)
            dest[blocks] = (wide[:, :LANES] + wide[:, LANES:]).reshape(CHUNK, 8, LANES)

        each_chunk(body)

    def scattered(chunk, blocks):
        both = jnp.concatenate(list(halves_of(fjb[blocks].reshape(FLAT, LANES))), axis=1)
        wide = dot(hot_j[chunk], both, 1, 0)
        return wide[:, :LANES] + wide[:, LANES:]

    def contract_rows(t):
        return [con_ref[t, b : b + 1, :] for b in range(9)]

    def powers_of(a):
        return [sum(a[lm] * a[lm] for lm in members(degree)) for degree in (1, 2, 3)]

    def alpha_of(c, s, p):
        return (
            c[0] + 2.0 * c[1] * s + 3.0 * c[5] * s * s + c[6] * p[0] + c[7] * p[1] + c[8] * p[2]
        )

    def beta_of(c, s):
        return [c[2 + i] + c[6 + i] * s for i in range(3)]

    zeros16 = tuple(jnp.zeros((8, LANES), f32) for _ in range(16))

    def forward_messages(t):
        def body(tile, at):
            def edges(block, a):
                a = list(a)
                there = fj[t, block]
                for degree in range(4):
                    w = fdir[t, block, degree] * there
                    if degree == 0:
                        a[0] = a[0] + w
                        continue
                    for lm in members(degree):
                        a[lm] = a[lm] + yy[block, lm - 1] * w
                return tuple(a)

            a = each_block(tile, edges, zeros16)
            for lm in range(16):
                amat[t, tile, lm] = a[lm]
            c = contract_rows(t)
            s, p = a[0], powers_of(a)
            value = s * (c[0] + s * (c[1] + s * c[5]) + c[6] * p[0] + c[7] * p[1] + c[8] * p[2])
            msg[t, at, :] = value + c[2] * p[0] + c[3] * p[1] + c[4] * p[2]

        each_tile(body)

    def backward_messages(t):
        def body(tile, at):
            a = [amat[t, tile, lm] for lm in range(16)]
            c = contract_rows(t)
            up = msgb[t, at, :]
            s, p = a[0], powers_of(a)
            beta = beta_of(c, s)
            twice = [None] + [2.0 * up * beta[i] for i in range(3)]
            ab = [up * alpha_of(c, s, p)] + [twice[DEGREES[lm]] * a[lm] for lm in range(1, 16)]
            slant = slants_of(ab)

            def edges(block, carry):
                there = fj[t, block]
                back = None
                shape = [None] + [yy[block, lm - 1] for lm in range(1, 16)]
                pull = [None] * 3
                for degree in range(4):
                    weight = fdir[t, block, degree]
                    bar = ab[0] if degree == 0 else None
                    if degree > 0:
                        w = weight * there
                        for lm in members(degree):
                            bar = add(bar, shape[lm] * ab[lm])
                        for k in range(3):
                            moved = None
                            for lm, value in slant[degree - 1][k]:
                                moved = add(moved, value if lm == 0 else shape[lm] * value)
                            pull[k] = add(pull[k], w * moved)
                        wb[t, block, degree - 1] = bar
                    fb[t, block, degree] = bar * there
                    if t > 0:
                        back = add(back, bar * weight)
                if t > 0:
                    fjb[block] = back
                for k in range(3):
                    pulls[block, k] = pull[k] if t > 0 else pulls[block, k] + pull[k]
                return carry

            each_block(tile, edges, 0)

        each_tile(body)

    def tangent_messages(t):
        def body(tile, at):
            def edges(block, da):
                da = list(da)
                there = fj[t, block]
                for degree in range(4):
                    weight = fdir[t, block, degree]
                    dw = dfdir[t, block, degree] * there
                    if t > 0:
                        dw = dw + weight * dfj[block]
                    if degree == 0:
                        da[0] = da[0] + dw
                        continue
                    w = weight * there
                    for lm in members(degree):
                        da[lm] = da[lm] + (yy[block, lm - 1] * dw + dyy[block, lm - 1] * w)
                return tuple(da)

            da = each_block(tile, edges, zeros16)
            a = [amat[t, tile, lm] for lm in range(16)]
            for lm in range(16):
                damat[t, tile, lm] = da[lm]
            c = contract_rows(t)
            s, p = a[0], powers_of(a)
            beta = beta_of(c, s)
            value = alpha_of(c, s, p) * da[0]
            for i in range(3):
                value = value + beta[i] * (2.0 * sum(a[lm] * da[lm] for lm in members(i + 1)))
            dmsg[t, at, :] = value

        each_tile(body)

    def tangent_backward(t):
        gcon[...] = jnp.zeros_like(gcon)

        def body(tile, at):
            a = [amat[t, tile, lm] for lm in range(16)]
            da = [damat[t, tile, lm] for lm in range(16)]
            c = contract_rows(t)
            up, dup = msgb[t, at, :], msgb[2, at, :]
            s, ds, p = a[0], da[0], powers_of(a)
            dp = [2.0 * sum(a[lm] * da[lm] for lm in members(degree)) for degree in (1, 2, 3)]
            alpha, beta = alpha_of(c, s, p), beta_of(c, s)
            dalpha = (
                2.0 * c[1] * ds
                + 6.0 * c[5] * s * ds
                + c[6] * dp[0]
                + c[7] * dp[1]
                + c[8] * dp[2]
            )
            pb = [None] + [2.0 * up * beta[i] for i in range(3)]
            dpb = [None] + [2.0 * (dup * beta[i] + up * c[6 + i] * ds) for i in range(3)]
            ab = [up * alpha] + [pb[DEGREES[lm]] * a[lm] for lm in range(1, 16)]
            dab = [dup * alpha + up * dalpha] + [
                pb[DEGREES[lm]] * da[lm] + dpb[DEGREES[lm]] * a[lm] for lm in range(1, 16)
            ]
            products = [(s, ds), (s * s, 2.0 * s * ds)]
            products += [(p[i], dp[i]) for i in range(3)]
            products += [(s * s * s, 3.0 * s * s * ds)]
            products += [(s * p[i], ds * p[i] + s * dp[i]) for i in range(3)]
            for b, (point, direction) in enumerate(products):
                gcon[b] += dup * point + up * direction

            def edges(block, carry):
                there = fj[t, block]
                back = None
                for degree in range(4):
                    if degree == 0:
                        was, bar = ab[0], dab[0]
                    else:
                        was, bar = wb[t, block, degree - 1], None
                        for lm in members(degree):
                            bar = add(
                                bar, yy[block, lm - 1] * dab[lm] + dyy[block, lm - 1] * ab[lm]
                            )
                    value = bar * there
                    if t > 0:
                        value = value + was * dfj[block]
                    fb[t, block, degree] = value
                    back = add(
                        back, bar * fdir[t, block, degree] + was * dfdir[t, block, degree]
                    )
                fjb[block] = back
                return carry

            each_block(tile, edges, 0)

        each_tile(body)
        for b in range(9):
            g_con[t, b : b + 1, :] -= jnp.sum(gcon[b], axis=0, keepdims=True)

    inner = slice(0, WINDOW)
    hot_element = jnp.where(
        lax.broadcasted_iota(i32, (LANES, LANES), 0).astype(f32) == species, 1.0, 0.0
    )[:, :WINDOW].astype(bf16)
    own_lane = own[:, :WINDOW]
    feats[0, inner, :] = dot(
        jnp.concatenate([hot_element, hot_element], axis=0), tab_w[...], 0, 0
    )
    sums = []
    for t in range(2):
        gather_from(feats[t], fj.at[t])
        forward_messages(t)
        feats[t + 1, inner, :] = feats[t, inner, :] + fine(msg[t], mix_ref[t], 1, 1)
        sums.append(fine(read_ref[t], feats[t + 1, inner, :], 1, 1))

    diagonal = lax.broadcasted_iota(i32, (16, 16), 0) == lax.broadcasted_iota(i32, (16, 16), 1)
    sum_bars, feat_bars, slopes_read, curves_read = [], [None, None], [], []
    for t in range(2):
        vector = jnp.sum(
            jnp.where(diagonal, jnp.broadcast_to(en_ref[t : t + 1, :], (16, 16)), 0.0),
            axis=1,
            keepdims=True,
        )
        sig = sigmoid(sums[t])
        h, rest = sums[t] * sig, 1.0 - sig
        slopes_read.append(own_lane * (sig + h * rest))
        curves_read.append(own_lane * vector * (sig * rest * (2.0 + sums[t] - 2.0 * h)))
        sum_bars.append(vector * slopes_read[t])

    def scatter_all():
        msgb[3] = jnp.zeros((WINDOW, LANES), f32)

        def body(chunk, blocks):
            msgb[3] += scattered(chunk, blocks)[:WINDOW]

        each_chunk(body)
        return msgb[3]

    feat_bar = None
    for t in (1, 0):
        feat_bar = add(feat_bar, fine(sum_bars[t], read_ref[t], 0, 0))
        feat_bars[t] = feat_bar
        msgb[t] = fine(feat_bar, mix_ref[t], 1, 0)
        backward_messages(t)
        if t > 0:
            feat_bar = feat_bar + scatter_all()

    barrow[...] = jnp.zeros_like(barrow)

    def geometry_back(chunk, blocks):
        envelope = rows_ref[chunk, 4:5, :]
        values, envelope_bar, distance_bar = [], None, None
        for t in range(2):
            high, low = filter_bars(t, blocks)
            value = filters_back(t, high, low)
            hidu[t, chunk] = value
            h, _, _ = parts_of(t, chunk, 2)
            envelope_bar = add(envelope_bar, jnp.sum(value * h, axis=0, keepdims=True))
            values.append(value * envelope)
        for depth in (2, 1, 0):
            for t in range(2):
                hidb[t, chunk, depth] = values[t]
                _, slope, _ = parts_of(t, chunk, depth)
                values[t] = layer_back(t, depth, values[t] * slope)
        distance_bar = jnp.sum((values[0] + values[1]) * bess[chunk, 1], axis=0, keepdims=True)
        rel = tuple(rows_ref[chunk, k : k + 1, :] for k in range(3))
        valid = rows_ref[chunk, 3:4, :]
        _, radius_pull = jax.vjp(lambda a, b, c: radius_of(a, b, c, valid), *rel)
        radius_bars = radius_pull((distance_bar, envelope_bar))
        ones = jnp.ones((16, LANES), bf16)
        shape_bars = []
        for k in range(3):
            high, low = halves_of(pulls[blocks, k].reshape(FLAT, LANES))
            shape_bars.append((dot(ones, high, 1, 1) + dot(ones, low, 1, 1))[0:1])
        bars = [
            jnp.where(valid > 0.0, radius_bars[k] + shape_bars[k], 0.0) * (1.0 / RCUT)
            for k in range(3)
        ]
        for k, value in enumerate(joined(dot(thirds(bars), hot_d[chunk], 1, 1), 3)):
            barrow[k : k + 1, :] += value

    each_chunk(geometry_back)

    slopes = []
    loss_row = jnp.zeros((1, LANES), f32)
    weight_row = own * labelled
    for k in range(3):
        force = -barrow[k : k + 1, :]
        diff = force - row(8 + k)
        magnitude = jnp.abs(diff)
        huber = jnp.where(
            magnitude <= HUBER_DELTA,
            0.5 * diff * diff,
            HUBER_DELTA * (magnitude - 0.5 * HUBER_DELTA),
        )
        loss_row = loss_row + weight_row * huber
        slopes.append(weight_row * jnp.clip(diff, -HUBER_DELTA, HUBER_DELTA) * (1.0 / RCUT))
    unordered = dot(thirds([-barrow[k : k + 1, :] for k in range(3)]), order_t, 1, 0)
    for k, value in enumerate(joined(unordered, 3)):
        force_ref[0, k : k + 1, :] = value
    force_ref[0, 3:4, :] = win_ref[0, 6:7, :]
    force_ref[0, 4:8, :] = jnp.zeros((4, LANES), f32)
    stat_ref[0:1, :] += loss_row
    stat_ref[1:2, :] += weight_row

    slope_parts = natural(slopes)
    slope_rows = thirds(slopes)

    def geometry_tangent(chunk, blocks):
        spread(chunk, blocks, slope_parts, dyy)
        rel = tuple(rows_ref[chunk, k : k + 1, :] for k in range(3))
        valid, envelope = rows_ref[chunk, 3:4, :], rows_ref[chunk, 4:5, :]
        drel = tuple(joined(dot(slope_rows, hot_d[chunk], 1, 0), 3))
        _, (ddistance, denvelope) = jax.jvp(
            lambda a, b, c: radius_of(a, b, c, valid), rel, drel
        )
        rows_ref[chunk, 5:6, :] = denvelope
        dbasis = bess[chunk, 1] * ddistance
        bess[chunk, 2] = dbasis
        values = [dbasis] * 2
        for depth in range(3):
            for t in range(2):
                z = layer_in(t, depth, values[t])
                dz[t, chunk, depth] = z
                h, slope, _ = parts_of(t, chunk, depth)
                values[t] = slope * z
                if depth == 2:
                    values[t] = values[t] * envelope + h * denvelope
        for t in range(2):
            filters_to(t, values[t], blocks, dfdir)
            high, low = filter_bars(t, blocks)
            g_wide[t] += filters_grad(values[t], high, low)

    each_chunk(geometry_tangent)

    def tangent_shapes(block):
        point = tuple(yy[block, k] for k in range(3))
        direction = tuple(dyy[block, k] for k in range(3))
        _, values = jax.jvp(shapes_of, point, direction)
        for k in range(3, 15):
            dyy[block, k] = values[k]

    each_edge_block(tangent_shapes)

    dsums = []
    dfeat = None
    for t in range(2):
        if t > 0:
            dfeats[inner, :] = dfeat
            gather_from(dfeats[...], dfj)
        tangent_messages(t)
        dfeat = add(dfeat, fine(dmsg[t], mix_ref[t], 1, 1))
        dsums.append((fine(read_ref[t], dfeat, 1, 1), dfeat))

    dfeat_bar = None
    for t in (1, 0):
        dsum, dfeat_after = dsums[t]
        g_en[t] -= jnp.sum(slopes_read[t] * dsum, axis=1, keepdims=True)
        dsum_bar = curves_read[t] * dsum
        g_read[t] -= fine(dsum_bar, feats[t + 1, inner, :], 1, 0) + fine(
            sum_bars[t], dfeat_after, 1, 0
        )
        dfeat_bar = add(dfeat_bar, fine(dsum_bar, read_ref[t], 0, 0))
        g_mix[t] -= fine(dfeat_bar, msg[t], 0, 0) + fine(feat_bars[t], dmsg[t], 0, 0)
        msgb[2] = fine(dfeat_bar, mix_ref[t], 1, 0)
        tangent_backward(t)
        dfeat_bar = dfeat_bar + scatter_all()
    high, low = halves_of(dfeat_bar)
    g_tab[...] += dot(hot_element, high, 1, 0) + dot(hot_element, low, 1, 0)

    def network_grads(chunk, blocks):
        envelope, denvelope = rows_ref[chunk, 4:5, :], rows_ref[chunk, 5:6, :]
        values = []
        for t in range(2):
            high, low = filter_bars(t, blocks)
            h, _, _ = parts_of(t, chunk, 2)
            g_wide[t] += filters_grad(h * envelope, high, low)
            values.append(filters_back(t, high, low) * envelope + hidu[t, chunk] * denvelope)
        for depth in (2, 1, 0):
            for t in range(2):
                _, slope, curve = parts_of(t, chunk, depth)
                bar = hidb[t, chunk, depth]
                value = values[t] * slope + bar * curve * dz[t, chunk, depth]
                if depth == 0:
                    before, dbefore = bess[chunk, 0], bess[chunk, 2]
                else:
                    before, slope_before, _ = parts_of(t, chunk, depth - 1)
                    dbefore = slope_before * dz[t, chunk, depth - 1]
                grad = fine_rows(
                    jnp.concatenate([dbefore, before], axis=1),
                    jnp.concatenate([bar * slope, value], axis=1),
                )
                if depth == 0:
                    g_bes[t] -= grad
                else:
                    g_rad[t, depth - 1] -= grad
                    values[t] = layer_back(t, depth, value)

    each_chunk(network_grads)

    @pl.when(pl.program_id(0) == pl.num_programs(0) - 1)
    def _():
        g_emb[...] = -g_tab[...].T
        for t in range(2):
            g_fil[t] = -g_wide[t].T.reshape(4, LANES, 64)


def local_step(windows, table, bessel, radial, filters, contract, mixing, readout, energies):
    units = windows.shape[0]
    f32, bf16 = jnp.float32, jnp.bfloat16
    vmem = pl.BlockSpec(memory_space=pltpu.VMEM)

    def scratch(*shape):
        return pltpu.VMEM(shape, f32)

    def short(*shape):
        return pltpu.VMEM(shape, bf16)

    def out(*shape):
        return jax.ShapeDtypeStruct(shape, f32)

    edges, parts = EDGE_BLOCKS, EDGE_BLOCKS // CHUNK
    return pl.pallas_call(
        step_kernel,
        grid=(units,),
        in_specs=[pl.BlockSpec((1, 16, LANES), lambda i: (i, 0, 0))] + [vmem] * 8,
        out_specs=[pl.BlockSpec((1, 8, LANES), lambda i: (i, 0, 0))] + [vmem] * 9,
        out_shape=[
            out(units, 8, LANES),
            out(8, LANES),
            out(LANES, LANES),
            out(2, NBESSEL, 64),
            out(2, 2, 64, 64),
            out(2, 4, LANES, 64),
            out(2, 16, LANES),
            out(2, LANES, LANES),
            out(2, 16, LANES),
            out(2, 16, 1),
        ],
        scratch_shapes=[
            pltpu.SMEM((16,), jnp.int32),
            scratch(edges, 15, 8, LANES),
            scratch(edges, 15, 8, LANES),
            scratch(3, LANES, LANES),
            scratch(LANES, LANES),
            scratch(2, edges, 8, LANES),
            scratch(edges, 8, LANES),
            scratch(2, edges, 4, 8, LANES),
            scratch(2, edges, 4, 8, LANES),
            scratch(2, edges, 4, 8, LANES),
            scratch(edges, 8, LANES),
            scratch(2, edges, 3, 8, LANES),
            scratch(2, TILES, 16, 8, LANES),
            scratch(2, TILES, 16, 8, LANES),
            scratch(2, WINDOW, LANES),
            scratch(4, WINDOW, LANES),
            scratch(2, WINDOW, LANES),
            scratch(2, parts, 3, 64, FLAT),
            scratch(2, parts, 3, 64, FLAT),
            scratch(2, parts, 3, 64, FLAT),
            scratch(2, parts, 3, 64, FLAT),
            scratch(2, parts, 64, FLAT),
            scratch(parts, 3, NBESSEL, FLAT),
            scratch(parts, 8, FLAT),
            scratch(LANES, LANES),
            short(parts, LANES, FLAT),
            short(parts, LANES, FLAT),
            short(parts, FLAT, LANES),
            short(parts, FLAT, LANES),
            scratch(8, LANES),
            scratch(9, 8, LANES),
            short(2 * LANES, LANES),
            short(2, 64, 4 * NBESSEL),
            short(2, NBESSEL, 192),
            short(2, 2, 64, 192),
            short(2, 2, 64, 192),
            short(2, 192, 4 * LANES),
            short(2, LANES, 4 * LANES),
            scratch(LANES, LANES),
            scratch(2, 64, 4 * LANES),
        ],
        compiler_params=pltpu.CompilerParams(vmem_limit_bytes=60 * 1024 * 1024),
    )(windows, table, bessel, radial, filters, contract, mixing, readout, energies)


MESH = pl.DeviceIdType.MESH
GROUPS = 4
BLOCKS = 8
SHARE_LANES = LANES // GROUPS
BLOB = 176
PIECE = 280
SUB = 40
QUARTER = PIECE - BLOB


def dense(value):
    rows = value.shape[0] // GROUPS
    return jnp.concatenate([value[k * rows : (k + 1) * rows] for k in range(GROUPS)], axis=1)


def lanes_of(value, group):
    return value[:, group * SHARE_LANES : (group + 1) * SHARE_LANES]


def undense(pieces):
    return jnp.concatenate(
        [
            jnp.concatenate([lanes_of(piece, k) for piece in pieces], axis=1)
            for k in range(GROUPS)
        ],
        axis=0,
    )


def collect_kernel(
    pos_ref,
    spec_ref,
    neigh_ref,
    lab_ref,
    tgt_ref,
    emb_ref,
    fil_ref,
    con_ref,
    read_ref,
    win_ref,
    table_ref,
    full_ref,
    cont_ref,
    rd_ref,
    blob,
    padded,
    ext,
    halo,
    send_sem,
    recv_sem,
    halo_sem,
):
    block, group = lax.axis_index("atoms"), lax.axis_index("chan")
    count = pos_ref.shape[1]
    before = lax.rem(block + BLOCKS - 1, BLOCKS)
    after = lax.rem(block + 1, BLOCKS)
    peers = [lax.rem(group + offset, GROUPS) for offset in range(1, GROUPS)]
    barrier = pltpu.get_barrier_semaphore()
    for peer in peers:
        pl.semaphore_signal(barrier, inc=1, device_id={"chan": peer}, device_id_type=MESH)
    for other in (before, after):
        pl.semaphore_signal(barrier, inc=1, device_id={"atoms": other}, device_id_type=MESH)

    padded[...] = jnp.zeros_like(padded)
    for t in range(2):
        padded[16 * t : 16 * t + 9, :] = con_ref[:, t, :]
    table_ref[...] = jnp.zeros_like(table_ref)
    table_ref[0:SHARE_LANES, 0:ELEMENTS] = emb_ref[...]
    both = [fil_ref[t].reshape(LANES, 64) for t in range(2)]
    blob[group, 0:128, :] = jnp.concatenate(both, axis=1)
    blob[group, 128:160, :] = table_ref[0:SHARE_LANES, :]
    blob[group, 160:168, :] = dense(read_ref[...].reshape(32, SHARE_LANES))
    blob[group, 168:176, :] = dense(padded[...])

    atom = lax.broadcasted_iota(jnp.int32, (1, count), 1)
    leading = neigh_ref[0:1, :] - block * count
    first = jnp.where((neigh_ref[0:1, :] >= 0) & (leading < atom), leading, atom)
    ext[...] = jnp.zeros_like(ext)
    ext[0:3, 0:count] = pos_ref[...]
    ext[3:4, 0:count] = first.astype(jnp.float32)
    ext[4:5, 0:count] = spec_ref[...].astype(jnp.float32)
    ext[5:6, 0:count] = lab_ref[...].astype(jnp.float32)
    ext[8:11, 0:count] = tgt_ref[...]

    pl.semaphore_wait(barrier, GROUPS + 1)
    copies = []
    for at, peer in enumerate(peers):
        copies.append(
            pltpu.make_async_remote_copy(
                src_ref=blob.at[group],
                dst_ref=blob.at[group],
                send_sem=send_sem.at[at],
                recv_sem=recv_sem.at[group],
                device_id={"chan": peer},
                device_id_type=MESH,
            )
        )
    halo_copy = pltpu.make_async_remote_copy(
        src_ref=ext.at[:, 0:LANES],
        dst_ref=halo,
        send_sem=halo_sem.at[0],
        recv_sem=halo_sem.at[1],
        device_id={"atoms": before},
        device_id_type=MESH,
    )
    halo_copy.start()
    for copy in copies:
        copy.start()

    halo_copy.wait()
    kind = lax.broadcasted_iota(jnp.int32, (16, LANES), 0)
    lane = lax.broadcasted_iota(jnp.int32, (16, LANES), 1)
    there = (lane < GHOST) & (block < BLOCKS - 1)
    shifted = halo[...] + jnp.where(kind == 3, float(count), 0.0)
    nothing = jnp.where(kind == 3, -1.0e6, 0.0)
    ext[:, count : count + LANES] = jnp.where(there, shifted, nothing)
    units = count // UNIT
    views, loads = [], []
    for unit in range(units):
        wide = ext[:, LANES * (unit // 2) : LANES * (unit // 2) + 2 * LANES]
        if unit % 2 == 1:
            wide = pltpu.roll(wide, 2 * LANES - UNIT, 1)
        shift = jnp.where(kind == 3, float(unit * UNIT), 0.0)
        view = jnp.where(lane < WINDOW, wide[:, :LANES] - shift, nothing)
        views.append(jnp.where(kind == 6, float(unit), view))
        neighbours, _ = neighbour_counts(view[3:4, :])
        loads.append(jnp.sum(neighbours, axis=1, keepdims=True))
    ranks = []
    for unit in range(units):
        rank = jnp.zeros((1, 1), jnp.float32)
        for other in range(units):
            if other != unit:
                before_it = loads[other] >= loads[unit] if other < unit else loads[other] > loads[unit]
                rank = rank + jnp.where(before_it, 1.0, 0.0)
        ranks.append(rank)
    for slot in range(units // GROUPS):
        wanted = (group if slot == 0 else units - 1 - group).astype(jnp.float32)
        chosen = jnp.zeros((16, LANES), jnp.float32)
        for unit in range(units):
            chosen = chosen + jnp.where(ranks[unit] == wanted, views[unit], 0.0)
        win_ref[slot] = chosen

    for at, peer in enumerate(peers):
        pltpu.make_async_remote_copy(
            src_ref=blob.at[peer],
            dst_ref=blob.at[peer],
            send_sem=send_sem.at[at],
            recv_sem=recv_sem.at[peer],
            device_id={"chan": peer},
            device_id_type=MESH,
        ).wait_recv()
    for k in range(GROUPS):
        part = pl.ds(k * SHARE_LANES, SHARE_LANES)
        for t in range(2):
            full_ref[t, :, part, :] = blob[k, 0:128, 64 * t : 64 * t + 64].reshape(
                4, SHARE_LANES, 64
            )
        table_ref[part, :] = blob[k, 128:160, :]
    rd_ref[...] = undense([blob[k, 160:168, :] for k in range(GROUPS)]).reshape(2, 16, LANES)
    cont_ref[...] = undense([blob[k, 168:176, :] for k in range(GROUPS)]).reshape(2, 16, LANES)
    for copy in copies:
        copy.wait_send()


def collect(positions, species, neighbours, labelled, targets, embedding, filters, contract, readout):
    f32 = jnp.float32
    count = positions.shape[1]
    vmem = pl.BlockSpec(memory_space=pltpu.VMEM)
    return pl.pallas_call(
        collect_kernel,
        in_specs=[vmem] * 9,
        out_specs=[vmem] * 5,
        out_shape=[
            jax.ShapeDtypeStruct((count // GROUPS // UNIT, 16, LANES), f32),
            jax.ShapeDtypeStruct((LANES, LANES), f32),
            jax.ShapeDtypeStruct((2, 4, LANES, 64), f32),
            jax.ShapeDtypeStruct((2, 16, LANES), f32),
            jax.ShapeDtypeStruct((2, 16, LANES), f32),
        ],
        scratch_shapes=[
            pltpu.VMEM((GROUPS, BLOB, LANES), f32),
            pltpu.VMEM((32, SHARE_LANES), f32),
            pltpu.VMEM((16, count + LANES), f32),
            pltpu.VMEM((16, LANES), f32),
            pltpu.SemaphoreType.DMA((GROUPS - 1,)),
            pltpu.SemaphoreType.DMA((GROUPS,)),
            pltpu.SemaphoreType.DMA((2,)),
        ],
        compiler_params=pltpu.CompilerParams(collective_id=0, has_side_effects=True),
    )(
        positions,
        species[None],
        neighbours,
        labelled[None],
        targets,
        embedding,
        filters,
        contract,
        readout,
    )


def reduce_kernel(
    force_ref,
    stat_ref,
    g_emb,
    g_bes,
    g_rad,
    g_fil,
    g_con,
    g_mix,
    g_read,
    g_en,
    forces_ref,
    own_ref,
    rest_ref,
    pieces,
    core_in,
    line_out,
    line_in,
    summed,
    sub_in,
    sub_out,
    total,
    quarters,
    windows,
    tail,
    tail_in,
    sems,
    sub_send,
    sub_recv,
    total_send,
    total_recv,
):
    f32 = jnp.float32
    block, group = lax.axis_index("atoms"), lax.axis_index("chan")
    line, core = group // 2, lax.rem(group, 2)
    core_peer = {"chan": line * 2 + (1 - core)}
    line_peer = {"chan": (1 - line) * 2 + core}
    others = [lax.rem(block + offset, BLOCKS) for offset in range(1, BLOCKS)]
    barrier = pltpu.get_barrier_semaphore()
    for peer in [core_peer, line_peer] + [{"atoms": other} for other in others]:
        pl.semaphore_signal(barrier, inc=1, device_id=peer, device_id_type=MESH)

    def copy(source, dest, at, peer):
        return pltpu.make_async_remote_copy(
            src_ref=source,
            dst_ref=dest,
            send_sem=sems.at[2 * at],
            recv_sem=sems.at[2 * at + 1],
            device_id=peer,
            device_id_type=MESH,
        )

    rows = lax.broadcasted_iota(jnp.int32, (16, LANES), 0)
    lanes = lax.broadcasted_iota(jnp.int32, (16, LANES), 1)
    vector = jnp.zeros((1, LANES), f32)
    for t in range(2):
        spread = jnp.broadcast_to(g_en[t], (16, LANES))
        vector = vector + jnp.sum(
            jnp.where(lanes == rows + 16 * t, spread, 0.0), axis=0, keepdims=True
        )
    inner = g_rad[...].reshape(256, 64)
    inner = jnp.concatenate([inner[:128], inner[128:]], axis=1)
    bessel = jnp.concatenate([g_bes[0], g_bes[1]], axis=1)
    for k in range(GROUPS):
        where = (k % 2, k // 2)
        part = pl.ds(k * SHARE_LANES, SHARE_LANES)
        both = [g_fil[t, :, part, :].reshape(LANES, 64) for t in range(2)]
        pieces[(*where, pl.ds(0, 128), slice(None))] = jnp.concatenate(both, axis=1)
        pieces[(*where, pl.ds(128, 32), slice(None))] = g_emb[part, :]
        pieces[(*where, pl.ds(160, 8), slice(None))] = dense(
            lanes_of(g_read[...].reshape(32, LANES), k)
        )
        pieces[(*where, pl.ds(168, 8), slice(None))] = dense(
            lanes_of(g_con[...].reshape(32, LANES), k)
        )
        pieces[(*where, pl.ds(176, 64), slice(None))] = g_mix[k // 2, 64 * (k % 2) : 64 * (k % 2) + 64, :]
        pieces[(*where, pl.ds(240, 32), slice(None))] = inner[32 * k : 32 * k + 32]
        pieces[(*where, pl.ds(272, 8), slice(None))] = jnp.concatenate(
            [bessel[2 * k : 2 * k + 2], vector, stat_ref[0:2, :], jnp.zeros((3, LANES), f32)],
            axis=0,
        )
    windows[line, core] = force_ref[...]
    pl.semaphore_wait(barrier, BLOCKS + 1)

    core_copy = copy(pieces.at[1 - core], core_in, 0, core_peer)
    core_copy.start()
    core_force = copy(windows.at[line, core], windows.at[line, core], 1, core_peer)
    core_force.start()
    core_copy.wait()
    line_out[...] = pieces[core, 1 - line] + core_in[1 - line]
    line_copy = copy(line_out, line_in, 2, line_peer)
    line_copy.start()
    core_force.wait()
    line_force = copy(windows.at[line], windows.at[line], 3, line_peer)
    line_force.start()
    partial = pieces[core, line] + core_in[line]
    line_force.wait()

    lane8 = lax.broadcasted_iota(jnp.int32, (8, LANES), 1)
    canvas = [jnp.zeros((8, LANES), f32)] * 5
    held = [windows[k // 4, (k // 2) % 2, k % 2] for k in range(8)]
    for unit in range(8):
        value = jnp.zeros((8, LANES), f32)
        for item in held:
            value = value + jnp.where(item[3:4, :] == float(unit), item, 0.0)
        if unit % 2 == 0:
            canvas[unit // 2] = canvas[unit // 2] + value
        else:
            value = pltpu.roll(value, 64, 1)
            canvas[unit // 2] = canvas[unit // 2] + jnp.where(lane8 >= 64, value, 0.0)
            canvas[unit // 2 + 1] = canvas[unit // 2 + 1] + jnp.where(lane8 < 64, value, 0.0)
    tail[...] = canvas[4]
    tail_copy = copy(tail, tail_in, 4, {"atoms": others[0]})
    tail_copy.start()

    line_copy.wait()
    summed[7] = jnp.zeros((SUB, LANES), f32)
    partial = partial + line_in[...]
    for k in range(7):
        size = min(SUB, PIECE - k * SUB)
        summed[k, 0:size, :] = partial[k * SUB : k * SUB + size]
        if size < SUB:
            summed[k, size:SUB, :] = jnp.zeros((SUB - size, LANES), f32)

    def sub_copy(other, at):
        return pltpu.make_async_remote_copy(
            src_ref=summed.at[other],
            dst_ref=sub_in.at[block],
            send_sem=sub_send.at[at],
            recv_sem=sub_recv.at[block],
            device_id={"atoms": other},
            device_id_type=MESH,
        )

    def total_copy(other, at):
        return pltpu.make_async_remote_copy(
            src_ref=sub_out,
            dst_ref=total.at[block],
            send_sem=total_send.at[at],
            recv_sem=total_recv.at[block],
            device_id={"atoms": other},
            device_id_type=MESH,
        )

    def arrival(dest, recv, other):
        return pltpu.make_async_remote_copy(
            src_ref=sub_out,
            dst_ref=dest.at[other],
            send_sem=sub_send.at[0],
            recv_sem=recv.at[other],
            device_id={"atoms": other},
            device_id_type=MESH,
        )

    subs = [sub_copy(other, at) for at, other in enumerate(others)]
    for item in subs:
        item.start()
    value = summed[block]
    for other in others:
        arrival(sub_in, sub_recv, other).wait_recv()
        value = value + sub_in[other]
    sub_out[...] = value
    totals = [total_copy(other, at) for at, other in enumerate(others)]
    for item in totals:
        item.start()
    total[block] = value
    tail_copy.wait()
    forces = jnp.concatenate(canvas[:4], axis=1)
    edge = jnp.where((lane8 < GHOST) & (block > 0), tail_in[...], 0.0)
    forces_ref[...] = forces
    forces_ref[:, 0:LANES] = canvas[0] + edge
    for other in others:
        arrival(total, total_recv, other).wait_recv()
    for item in subs + totals:
        item.wait_send()

    everything = total[...].reshape(BLOCKS * SUB, LANES)
    own_ref[...] = everything[:BLOB]
    flat = everything[:274]
    energy_row = everything[274:275]
    squares = jnp.sum(flat * flat, axis=0, keepdims=True)
    squares = squares + (1.0 / GROUPS) * energy_row * energy_row
    squares = jnp.sum(squares, axis=1, keepdims=True)
    quarters[line, core] = everything[BLOB:PIECE]
    quarters[line, core, 101:102, :] = jnp.broadcast_to(squares, (1, LANES))
    line_quarter = copy(quarters.at[line, core], quarters.at[line, core], 5, line_peer)
    line_quarter.start()
    core_quarter = copy(quarters.at[line, core], quarters.at[line, core], 6, core_peer)
    core_quarter.start()
    line_quarter.wait()
    cross_quarter = copy(quarters.at[1 - line, core], quarters.at[1 - line, core], 7, core_peer)
    cross_quarter.start()
    core_quarter.wait()
    cross_quarter.wait()
    rest_ref[...] = quarters[...].reshape(GROUPS, QUARTER, LANES)


def reduce_all(force, stat, grads):
    f32 = jnp.float32
    vmem = pl.BlockSpec(memory_space=pltpu.VMEM)
    dma = pltpu.SemaphoreType.DMA
    return pl.pallas_call(
        reduce_kernel,
        in_specs=[vmem] * 10,
        out_specs=[vmem] * 3,
        out_shape=[
            jax.ShapeDtypeStruct((8, 4 * LANES), f32),
            jax.ShapeDtypeStruct((BLOB, LANES), f32),
            jax.ShapeDtypeStruct((GROUPS, QUARTER, LANES), f32),
        ],
        scratch_shapes=[
            pltpu.VMEM((2, 2, PIECE, LANES), f32),
            pltpu.VMEM((2, PIECE, LANES), f32),
            pltpu.VMEM((PIECE, LANES), f32),
            pltpu.VMEM((PIECE, LANES), f32),
            pltpu.VMEM((BLOCKS, SUB, LANES), f32),
            pltpu.VMEM((BLOCKS, SUB, LANES), f32),
            pltpu.VMEM((SUB, LANES), f32),
            pltpu.VMEM((BLOCKS, SUB, LANES), f32),
            pltpu.VMEM((2, 2, QUARTER, LANES), f32),
            pltpu.VMEM((2, 2, 2, 8, LANES), f32),
            pltpu.VMEM((8, LANES), f32),
            pltpu.VMEM((8, LANES), f32),
            dma((16,)),
            dma((BLOCKS - 1,)),
            dma((BLOCKS,)),
            dma((BLOCKS - 1,)),
            dma((BLOCKS,)),
        ],
        compiler_params=pltpu.CompilerParams(collective_id=1, has_side_effects=True),
    )(force, stat, *grads)


def adam_kernel(*refs):
    forces_in, own_ref, rest_ref = refs[:3]
    weights, moments = refs[3:11], refs[11:27]
    parts_ref, forces_ref, norm_ref = refs[27:30]
    results = refs[30:54]
    scratch = refs[54]
    rest = [rest_ref[k] for k in range(GROUPS)]
    stats = rest[0]
    loss = jnp.sum(stats[99:100], axis=1, keepdims=True)
    count = jnp.sum(stats[100:101], axis=1, keepdims=True)
    inverse = 1.0 / count
    squares = sum(rest[k][101:102, 0:1] for k in range(GROUPS))
    norm = jnp.sqrt(squares) * inverse
    factor = inverse * jnp.minimum(1.0, CLIP_NORM / (norm + 1e-06))
    norm_ref[...] = norm
    two = lax.broadcasted_iota(jnp.int32, (1, 2), 1)
    parts_ref[...] = jnp.where(two == 0, loss, count)
    forces_ref[...] = forces_in[0:3, :]

    def narrow(value):
        return jnp.concatenate([lanes_of(value, k) for k in range(GROUPS)], axis=0)

    fil = [own_ref[0:128, 64 * t : 64 * t + 64].reshape(4, SHARE_LANES, 64) for t in range(2)]
    emb = own_ref[128:160, 0:ELEMENTS]
    read = narrow(own_ref[160:168, :]).reshape(2, 16, SHARE_LANES)
    scratch[...] = narrow(own_ref[168:176, :])
    con = [scratch[0:9, :], scratch[16:25, :]]
    mix = jnp.concatenate([rest[k][0:64] for k in range(GROUPS)], axis=0).reshape(2, LANES, LANES)
    inner = jnp.concatenate([rest[k][64:96] for k in range(GROUPS)], axis=0)
    inner = jnp.concatenate([inner[:, :64], inner[:, 64:]], axis=0).reshape(2, 2, 64, 64)
    bes = jnp.concatenate([rest[k][96:98] for k in range(GROUPS)], axis=0)
    bes = [bes[:, :64], bes[:, 64:]]
    vector = rest[0][98:99]
    vector = jnp.concatenate([vector[:, 0:16], vector[:, 16:32]], axis=0)

    def update(which, gradient, at):
        first, square = moments[2 * which], moments[2 * which + 1]
        weight = weights[which][at]
        clipped = gradient * factor
        moment = BETA_ONE * first[at] + (1.0 - BETA_ONE) * clipped
        second = BETA_TWO * square[at] + (1.0 - BETA_TWO) * clipped * clipped
        corrected_first = moment * (1.0 / (1.0 - BETA_ONE**ADAM_STEP))
        corrected_second = second * (1.0 / (1.0 - BETA_TWO**ADAM_STEP))
        updated = weight - RATE * (
            corrected_first / (jnp.sqrt(corrected_second) + EPSILON) + DECAY * weight
        )
        results[3 * which][at] = updated
        results[3 * which + 1][at] = moment
        results[3 * which + 2][at] = second

    everything = Ellipsis
    update(0, emb, everything)
    for t in range(2):
        update(1, bes[t], t)
        update(3, fil[t], t)
        update(4, con[t], (slice(None), t))
    update(2, inner, everything)
    update(5, mix, everything)
    update(6, read, everything)
    update(7, vector, everything)


def adam(forces, own, rest, weights, moments):
    f32 = jnp.float32
    vmem = pl.BlockSpec(memory_space=pltpu.VMEM)
    shapes = [(1, 2), (3, forces.shape[1]), (1, 1)]
    shapes += [weight.shape for weight in weights for _ in range(3)]
    return pl.pallas_call(
        adam_kernel,
        in_specs=[vmem] * 27,
        out_specs=[vmem] * 27,
        out_shape=[jax.ShapeDtypeStruct(shape, f32) for shape in shapes],
        scratch_shapes=[pltpu.VMEM((32, SHARE_LANES), f32)],
    )(forces, own, rest, *weights, *moments)


def adamw(weight, gradient, first, second, scale):
    clipped = gradient * scale
    moment = BETA_ONE * first + (1.0 - BETA_ONE) * clipped
    second_new = BETA_TWO * second + (1.0 - BETA_TWO) * clipped * clipped
    corrected_first = moment / (1.0 - BETA_ONE**ADAM_STEP)
    corrected_second = second_new / (1.0 - BETA_TWO**ADAM_STEP)
    updated = weight - RATE * (
        corrected_first / (jnp.sqrt(corrected_second) + EPSILON) + DECAY * weight
    )
    return (updated, moment, second_new)


def per_device(
    positions,
    species,
    neighbours,
    labelled,
    target_forces,
    embedding,
    bessel,
    radial,
    filters,
    contract,
    mixing,
    readout,
    energies,
    first_embedding,
    square_embedding,
    first_bessel,
    square_bessel,
    first_radial,
    square_radial,
    first_filters,
    square_filters,
    first_contract,
    square_contract,
    first_mixing,
    square_mixing,
    first_readout,
    square_readout,
    first_energies,
    square_energies,
):
    if (lax.axis_size("atoms"), lax.axis_size("chan")) == (BLOCKS, GROUPS):
        turns = [(1, 0), None, None, (0, 1, 3, 2), (1, 0, 2), None, None, None]

        def turned(value, order):
            return value if order is None else value.transpose(order)

        weights = (embedding, bessel, radial, filters, contract, mixing, readout, energies)
        weights = [turned(value, order) for value, order in zip(weights, turns)]
        moments = (
            first_embedding,
            square_embedding,
            first_bessel,
            square_bessel,
            first_radial,
            square_radial,
            first_filters,
            square_filters,
            first_contract,
            square_contract,
            first_mixing,
            square_mixing,
            first_readout,
            square_readout,
            first_energies,
            square_energies,
        )
        moments = [turned(value, turns[k // 2]) for k, value in enumerate(moments)]
        windows, table, full, cont, read = collect(
            positions,
            species,
            neighbours,
            labelled,
            target_forces,
            weights[0],
            weights[3],
            weights[4],
            readout,
        )
        force, stat, *grads = local_step(
            windows, table, bessel, radial, full, cont, mixing, read, energies
        )
        forces, own, rest = reduce_all(force, stat, grads)
        parts, forces, norm, *results = adam(forces, own, rest, weights, moments)
        results = [turned(value, turns[k // 3]) for k, value in enumerate(results)]
        return tuple([parts.reshape(2), forces, norm.reshape(())] + results)
    f32 = jnp.float32
    atom_count = positions.shape[1]
    local_chan = embedding.shape[1]
    blocks, groups = lax.axis_size("atoms"), lax.axis_size("chan")
    block, group = lax.axis_index("atoms"), lax.axis_index("chan")
    atom_base = block * atom_count
    share = atom_count // groups
    units = share // UNIT

    atom_index = atom_base + jnp.arange(atom_count, dtype=jnp.int32)
    leading = neighbours[0]
    first_atom = jnp.where((leading >= 0) & (leading < atom_index), leading, atom_index)
    packed = jnp.concatenate(
        [
            positions,
            (first_atom - atom_base).astype(f32)[None],
            species.astype(f32)[None],
            labelled.astype(f32)[None],
            jnp.zeros((2, atom_count), f32),
            target_forces,
            jnp.zeros((5, atom_count), f32),
        ],
        axis=0,
    )
    down = [(i + 1, i) for i in range(blocks - 1)]
    halo = lax.ppermute(packed[:, :GHOST], "atoms", down)
    halo_row = jnp.arange(16)[:, None] == 3
    halo = jnp.where(halo_row, jnp.where(block == blocks - 1, -1.0e6, halo + atom_count), halo)
    missing = jnp.where(jnp.arange(16)[:, None] == 3, -1.0e6, 0.0) * jnp.ones((1, LANES), f32)
    extended = jnp.concatenate([packed, halo, missing], axis=1)
    windows = []
    for unit in range(units):
        start = group * share + unit * UNIT
        window = lax.dynamic_slice(extended, (0, start), (16, WINDOW))
        shift = jnp.where(jnp.arange(16)[:, None] == 3, start.astype(f32), 0.0)
        window = window - shift
        windows.append(jnp.concatenate([window, missing[:, : LANES - WINDOW]], axis=1))
    windows = jnp.stack(windows)

    def whole(value):
        return lax.all_gather(value, "chan", axis=value.ndim - 1, tiled=True)

    table = jnp.concatenate(
        [whole(embedding), jnp.zeros((LANES - ELEMENTS, LANES), f32)], axis=0
    ).T
    force, stat, *grads = local_step(
        windows,
        table,
        bessel,
        radial,
        whole(filters).swapaxes(2, 3),
        jnp.pad(whole(contract), ((0, 0), (0, 7), (0, 0))),
        mixing,
        whole(readout),
        energies,
    )
    grad_embed, grad_bessel, grad_radial, grad_filters, grad_contract, grad_mixing = grads[:6]
    grad_readout, grad_vectors = grads[6:]
    grad_embed = grad_embed.T[:ELEMENTS]
    grad_filters = grad_filters.swapaxes(2, 3)
    grad_contract = grad_contract[:, :9]
    grad_vectors = grad_vectors[:, :, 0]

    canvas = jnp.zeros((3, atom_count + LANES), f32)
    for unit in range(units):
        start = group * share + unit * UNIT
        old = lax.dynamic_slice(canvas, (0, start), (3, WINDOW))
        canvas = lax.dynamic_update_slice(canvas, old + force[unit, :3, :WINDOW], (0, start))
    canvas = lax.psum(canvas, "chan")
    up = [(i, i + 1) for i in range(blocks - 1)]
    arrived = lax.ppermute(canvas[:, atom_count : atom_count + GHOST], "atoms", up)
    forces = canvas[:, :atom_count].at[:, :GHOST].add(arrived)

    def split(value):
        return lax.psum_scatter(value, "chan", scatter_dimension=value.ndim - 1, tiled=True)

    grad_embed, grad_filters, grad_contract, grad_readout = lax.psum(
        (split(grad_embed), split(grad_filters), split(grad_contract), split(grad_readout)),
        "atoms",
    )
    grad_bessel, grad_radial, grad_mixing, grad_vectors, loss_sum, label_total = lax.psum(
        (grad_bessel, grad_radial, grad_mixing, grad_vectors, jnp.sum(stat[0]), jnp.sum(stat[1])),
        ("atoms", "chan"),
    )
    gradients = [
        gradient / label_total
        for gradient in (
            grad_embed,
            grad_bessel,
            grad_radial,
            grad_filters,
            grad_contract,
            grad_mixing,
            grad_readout,
            grad_vectors,
        )
    ]
    squares_of = [jnp.sum(gradient * gradient) for gradient in gradients]
    split_squares = squares_of[0] + squares_of[3] + squares_of[4] + squares_of[6]
    whole_squares = squares_of[1] + squares_of[2] + squares_of[5] + squares_of[7]
    grad_norm = jnp.sqrt(lax.psum(split_squares, "chan") + whole_squares)
    scale = jnp.minimum(1.0, CLIP_NORM / (grad_norm + 1e-06))
    weights = (embedding, bessel, radial, filters, contract, mixing, readout, energies)
    firsts = (
        first_embedding,
        first_bessel,
        first_radial,
        first_filters,
        first_contract,
        first_mixing,
        first_readout,
        first_energies,
    )
    squares = (
        square_embedding,
        square_bessel,
        square_radial,
        square_filters,
        square_contract,
        square_mixing,
        square_readout,
        square_energies,
    )
    results = []
    for weight, gradient, first, second in zip(weights, gradients, firsts, squares):
        results.extend(adamw(weight, gradient, first, second, scale))
    return tuple([jnp.stack([loss_sum, label_total]), forces, grad_norm] + results)


def solution(mesh):
    whole = P()
    columns = P(None, "atoms")
    by_weight = [
        P(None, "chan"),
        whole,
        whole,
        P(None, None, None, "chan"),
        P(None, None, "chan"),
        whole,
        P(None, None, "chan"),
        whole,
    ]
    in_specs = [columns, P("atoms"), columns, P("atoms"), columns] + by_weight
    in_specs += [spec for spec in by_weight for _ in range(2)]
    out_specs = [whole, columns, whole] + [spec for spec in by_weight for _ in range(3)]
    return jax.shard_map(
        per_device,
        mesh=mesh,
        in_specs=tuple(in_specs),
        out_specs=tuple(out_specs),
        check_vma=False,
    )
```

```python
import functools
import math

import jax
import jax.numpy as jnp
from jax import lax
from jax.experimental import pallas as pl
from jax.experimental.pallas import tpu as pltpu
from jax.sharding import PartitionSpec as P

ELEMENTS = 89
NBESSEL = 8
GHOST = 8
ADAM_STEP = 10

RCUT = 5.0
SMOOTH = 0.01
NEIGHBOURS_MEAN = 8.0
HUBER_DELTA = 1.0
CLIP_NORM = 0.001
RATE = 0.2
BETA_ONE = 0.9
BETA_TWO = 0.999
EPSILON = 1e-08
DECAY = 0.01

UNIT = 64
WINDOW = UNIT + 16
LANES = 128
DIRECTED = 15
TILES = WINDOW // 8
CHUNK = 80
EDGE_BLOCKS = 2 * CHUNK
FLAT = 8 * CHUNK
DEGREES = [0] + [1] * 3 + [2] * 5 + [3] * 7
EXACT = lax.Precision.HIGHEST

def shapes_of(x, y, z, root_three=math.sqrt(3.0)):
    xx, yy, zz = x * x, y * y, z * z
    xy, yz, zx = x * y, y * z, z * x
    both, less = xx + yy, xx - yy
    wide = 4.0 * zz - both
    return [
        x,
        y,
        z,
        root_three * xy,
        root_three * yz,
        zz - 0.5 * both,
        root_three * zx,
        (0.5 * root_three) * less,
        math.sqrt(5.0 / 8.0) * y * (3.0 * xx - yy),
        math.sqrt(15.0) * xy * z,
        math.sqrt(3.0 / 8.0) * y * wide,
        z * (zz - 1.5 * both),
        math.sqrt(3.0 / 8.0) * x * wide,
        (0.5 * math.sqrt(15.0)) * z * less,
        math.sqrt(5.0 / 8.0) * x * (xx - 3.0 * yy),
    ]


def slants_of(bar):
    third = 1.0 / math.sqrt(3.0)
    root = math.sqrt(3.0)
    a, b, c, d = (
        math.sqrt(5.0 / 8.0),
        math.sqrt(15.0),
        math.sqrt(3.0 / 8.0),
        0.5 * math.sqrt(15.0),
    )
    one = [[(0, bar[1])], [(0, bar[2])], [(0, bar[3])]]
    four, five, seven, eight = [root * bar[lm] for lm in (4, 5, 7, 8)]
    two = [
        [(2, four), (3, seven), (1, eight - bar[6])],
        [(1, four), (3, five), (2, -eight - bar[6])],
        [(2, five), (1, seven), (3, 2.0 * bar[6])],
    ]
    mixed = (b * third) * bar[10]
    three = [
        [
            (4, (6.0 * a * third) * bar[9] - (2.0 * c * third) * bar[11]),
            (5, mixed),
            (7, (2.0 * d * third) * bar[14] - root * bar[12]),
            (6, (4.0 * c) * bar[13]),
            (8, (6.0 * a * third) * bar[15] - (2.0 * c * third) * bar[13]),
        ],
        [
            (4, (-2.0 * c * third) * bar[13] - (6.0 * a * third) * bar[15]),
            (5, (-2.0 * d * third) * bar[14] - root * bar[12]),
            (7, mixed),
            (6, (4.0 * c) * bar[11]),
            (8, (6.0 * a * third) * bar[9] + (2.0 * c * third) * bar[11]),
        ],
        [
            (4, mixed),
            (5, (8.0 * c * third) * bar[11]),
            (7, (8.0 * c * third) * bar[13]),
            (6, 3.0 * bar[12]),
            (8, (2.0 * d * third) * bar[14]),
        ],
    ]
    return one, two, three


def radius_of(x, y, z, valid):
    distance = jnp.sqrt((x * x + y * y + z * z) * (RCUT * RCUT) + SMOOTH)
    scaled = distance * (1.0 / RCUT)
    square = scaled * scaled
    fifth = square * square * scaled
    envelope = 1.0 - fifth * (21.0 - 35.0 * scaled + 15.0 * square)
    envelope = jnp.where(scaled < 1.0, envelope, 0.0) * (valid * (1.0 / NEIGHBOURS_MEAN))
    return distance, envelope


def halves_of(value):
    high = value.astype(jnp.bfloat16)
    low = (value - high.astype(jnp.float32)).astype(jnp.bfloat16)
    return high, low


def dot(left, right, left_dim, right_dim):
    return lax.dot_general(
        left,
        right,
        (((left_dim,), (right_dim,)), ((), ())),
        preferred_element_type=jnp.float32,
    )


def fine(left, right, left_dim, right_dim):
    left_high, left_low = halves_of(left)
    right_high, right_low = halves_of(right)
    rows = left.shape[0]
    if left_dim == 1 and rows % 16 == 0:
        both = dot(jnp.concatenate([left_high, left_low], axis=0), right_high, 1, right_dim)
        return both[:rows] + both[rows:] + dot(left_high, right_low, 1, right_dim)
    return (
        dot(left_high, right_high, left_dim, right_dim)
        + dot(left_low, right_high, left_dim, right_dim)
        + dot(left_high, right_low, left_dim, right_dim)
    )


def fine_rows(left, right):
    rows = left.shape[0]
    left_high, left_low = halves_of(left)
    right_high, right_low = halves_of(right)
    both = dot(jnp.concatenate([left_high, left_low], axis=0), right_high, 1, 1)
    return both[:rows] + both[rows:] + dot(left_high, right_low, 1, 1)


def triple(value):
    high, low = halves_of(value)
    return jnp.concatenate([high, high, low], axis=0)


def add(total, term):
    return term if total is None else total + term


def members(degree):
    return range(degree * degree, (degree + 1) ** 2)


def thirds(values):
    parts = []
    for value in values:
        for _ in range(3):
            part = value.astype(jnp.bfloat16).astype(jnp.float32)
            parts.append(part)
            value = value - part
    parts += [jnp.zeros_like(parts[0])] * (16 - len(parts))
    return jnp.concatenate(parts, axis=0).astype(jnp.bfloat16)


def joined(rows, count):
    return [
        rows[3 * k : 3 * k + 1] + rows[3 * k + 1 : 3 * k + 2] + rows[3 * k + 2 : 3 * k + 3]
        for k in range(count)
    ]


def sine_cosine(angle):
    half = 0.5 * angle - (0.5 * math.pi)
    square = half * half
    sine = cosine = 0.0
    for k in range(6, -1, -1):
        cosine = cosine * square + (-1) ** k / math.factorial(2 * k)
        if k < 6:
            sine = sine * square + (-1) ** k / math.factorial(2 * k + 1)
    sine = sine * half
    return -2.0 * sine * cosine, 2.0 * sine * sine - 1.0


def both_sides(value):
    wide = jnp.broadcast_to(value, (16, LANES))
    back = pltpu.roll(wide, 1, 1, stride=1, stride_axis=0)
    ahead = pltpu.roll(wide, 113, 1, stride=1, stride_axis=0)
    return back, ahead


def neighbour_counts(first):
    own = jnp.where((first >= 0.0) & (first < float(UNIT)), 1.0, 0.0)
    slot_row = lax.broadcasted_iota(jnp.int32, (16, LANES), 0)
    back_first, ahead_first = both_sides(first)
    same = (slot_row < DIRECTED) & ((back_first == first) | (ahead_first == first))
    return jnp.sum(jnp.where(same, 1.0, 0.0), axis=0, keepdims=True) * own, own


def step_kernel(
    win_ref,
    emb_ref,
    bes_ref,
    rad_ref,
    fil_ref,
    con_ref,
    mix_ref,
    read_ref,
    en_ref,
    force_ref,
    stat_ref,
    g_emb,
    g_bes,
    g_rad,
    g_fil,
    g_con,
    g_mix,
    g_read,
    g_en,
    begin_ref,
    yy,
    dyy,
    feats,
    dfeats,
    fj,
    dfj,
    fdir,
    dfdir,
    fb,
    fjb,
    wb,
    amat,
    damat,
    msg,
    msgb,
    dmsg,
    zs,
    sg,
    dz,
    hidb,
    hidu,
    bess,
    rows_ref,
    turn_ref,
    hot_j,
    hot_d,
    turned_j,
    turned_d,
    barrow,
    gcon,
    tab_w,
    bes_w,
    bes_b,
    rad_w,
    rad_b,
    fil_w,
    fil_b,
):
    f32, bf16, i32 = jnp.float32, jnp.bfloat16, jnp.int32
    pulls = dyy

    @pl.when(pl.program_id(0) == 0)
    def _():
        for ref in (g_emb, g_fil, g_bes, g_rad, g_con, g_mix, g_read, g_en, stat_ref):
            ref[...] = jnp.zeros_like(ref)
        for ref in (feats, dfeats, fjb):
            ref[...] = jnp.zeros_like(ref)

        def clear(sixteen, carry):
            for t in range(2):
                fb[t, pl.ds(16 * sixteen, 16)] = jnp.zeros((16, 4, 8, LANES), f32)
            return carry

        lax.fori_loop(0, EDGE_BLOCKS // 16, clear, 0)
        tab_w[...] = jnp.concatenate(list(halves_of(emb_ref[...].T)), axis=0)
        for t in range(2):
            high, low = [value.astype(f32) for value in halves_of(bes_ref[t])]
            bes_w[t] = jnp.concatenate([high, low, high, jnp.zeros_like(high)], axis=0).T.astype(
                bf16
            )
            bes_b[t] = jnp.concatenate([high, low, high], axis=1).astype(bf16)
            for depth in range(2):
                high, low = [value.astype(f32) for value in halves_of(rad_ref[t, depth])]
                rad_b[t, depth] = jnp.concatenate([high, low, high], axis=1).astype(bf16)
                rad_w[t, depth] = jnp.concatenate([high, low, high], axis=0).T.astype(bf16)
            high, low = halves_of(fil_ref[t].reshape(4 * LANES, 64).T)
            fil_w[t] = jnp.concatenate([high, low, high], axis=0)
            fil_b[t] = jnp.concatenate([high, low], axis=0)

    count, own = neighbour_counts(win_ref[0, 3:4, :])

    line = lax.broadcasted_iota(i32, (LANES, LANES), 0)
    place = lax.broadcasted_iota(i32, (LANES, LANES), 1)
    key = jnp.broadcast_to(count + own, (LANES, LANES))
    other = key.T
    ahead_of = (other > key) | ((other == key) & (line < place))
    rank = jnp.sum(jnp.where(ahead_of, 1.0, 0.0), axis=0, keepdims=True)
    order_t = jnp.where(line.astype(f32) == rank, 1.0, 0.0).astype(bf16)
    index = lax.broadcasted_iota(i32, (1, LANES), 1).astype(f32)
    wide = jnp.concatenate(
        [win_ref[0], count, index, jnp.zeros((14, LANES), f32)], axis=0
    )
    high, middle = halves_of(wide)
    low = (wide - high.astype(f32) - middle.astype(f32)).astype(bf16)
    moved = dot(jnp.concatenate([high, middle, low], axis=0), order_t, 1, 1)
    turn_ref[0:32, :] = moved[0:32] + moved[32:64] + moved[64:96]

    def row(index):
        return turn_ref[index : index + 1, :]

    first, species, labelled = row(3), row(4), row(5)
    count, atom_id = row(16), row(17)
    own = jnp.where((first >= 0.0) & (first < float(UNIT)), 1.0, 0.0)
    atom_names = jnp.broadcast_to(atom_id, (LANES, LANES)).T[:, 0:1]

    lane_row = lax.broadcasted_iota(i32, (1, LANES), 1)
    used = lax.shift_right_logical(jnp.max(jnp.where(count > 0.0, lane_row, -8)) + 8, 3)
    for ref in (msg, dmsg):
        ref[...] = jnp.zeros_like(ref)
    begins, pairs = [jnp.int32(0)], []
    begin_ref[0] = 0
    for tile in range(TILES):
        mine = (lane_row >= 8 * tile) & (lane_row < 8 * tile + 8)
        most = jnp.max(jnp.where(mine, count, 0.0)).astype(i32)
        pairs.append(lax.shift_right_logical(most + 1, 1))
        begins.append(begins[-1] + pairs[-1])
        begin_ref[tile + 1] = begins[-1]
    total = begins[-1]
    chunks = jnp.int32(1)
    for k in range(1, EDGE_BLOCKS // CHUNK):
        chunks = chunks + jnp.where(2 * total > k * CHUNK, 1, 0)

    def each_chunk(body):
        def step(chunk, carry):
            body(chunk, pl.ds(chunk * CHUNK, CHUNK))
            return carry

        lax.fori_loop(0, chunks, step, 0)

    def each_tile(body):
        def step(tile, carry):
            body(tile, pl.ds(pl.multiple_of(tile * 8, 8), 8))
            return carry

        lax.fori_loop(0, used, step, 0)

    def each_block(tile, body, carry):
        start, stop = begin_ref[tile], begin_ref[tile + 1]
        doubles = lax.shift_right_logical(stop - start, 1)

        def four(index, held):
            block = 2 * start + 4 * index
            for k in range(4):
                held = body(block + k, held)
            return held

        carry = lax.fori_loop(0, doubles, four, carry)
        return lax.fori_loop(
            start + 2 * doubles,
            stop,
            lambda pair, held: body(2 * pair + 1, body(2 * pair, held)),
            carry,
        )

    def each_edge_block(body):
        def step(four, carry):
            for k in range(4):
                body(4 * four + k)
            return carry

        lax.fori_loop(0, lax.shift_right_logical(2 * total + 3, 2), step, 0)

    def natural(values):
        wide = jnp.concatenate(
            [jnp.broadcast_to(value, (LANES, LANES)).T for value in values], axis=1
        )
        high, middle = halves_of(wide)
        low = (wide - high.astype(f32) - middle.astype(f32)).astype(bf16)
        return jnp.concatenate([high, middle], axis=0), low

    def spread(chunk, blocks, parts, dest):
        left = turned_d[chunk]
        wide = dot(jnp.concatenate([left, left], axis=1), parts[0], 1, 0) + dot(
            left, parts[1], 1, 0
        )
        for k in range(3):
            dest[blocks, k] = wide[:, k * LANES : (k + 1) * LANES].reshape(CHUNK, 8, LANES)

    def layer_in(t, depth, value):
        if depth == 0:
            high, low = [part.astype(f32) for part in halves_of(value)]
            wide = jnp.concatenate([high, high, low, jnp.zeros_like(high)], axis=0).astype(bf16)
            return dot(bes_w[t], wide, 1, 0)
        return dot(rad_w[t, depth - 1], triple(value), 1, 0)

    def layer_back(t, depth, value):
        weight = bes_b[t] if depth == 0 else rad_b[t, depth - 1]
        return dot(weight, triple(value), 1, 0)

    def parts_of(t, chunk, depth):
        z, sig = zs[t, chunk, depth], sg[t, chunk, depth]
        h, rest = z * sig, 1.0 - sig
        return h, sig + h * rest, sig * rest * (2.0 + z - 2.0 * h)

    def sigmoid(z):
        return 0.5 * jnp.tanh(0.5 * z) + 0.5

    def filters_to(t, hidden, blocks, dest):
        wide = dot(triple(hidden), fil_w[t], 0, 0)
        for degree in range(4):
            dest[t, blocks, degree] = wide[:, degree * LANES : (degree + 1) * LANES].reshape(
                CHUNK, 8, LANES
            )

    def filters_back(t, high, low):
        both = dot(fil_b[t], high, 1, 1)
        return both[:64] + both[64:] + dot(fil_b[t, 0:64, :], low, 1, 1)

    def filters_grad(hidden, wide_high, wide_low):
        high, low = halves_of(hidden)
        both = dot(jnp.concatenate([high, low], axis=0), wide_high, 1, 0)
        return both[:64] + both[64:] + dot(high, wide_low, 1, 0)

    def filter_bars(t, blocks):
        parts = [
            halves_of(fb[t, blocks, degree].reshape(FLAT, LANES)) for degree in range(4)
        ]
        return [jnp.concatenate([part[k] for part in parts], axis=1) for k in range(2)]

    position_parts = natural([row(k) * (1.0 / RCUT) for k in range(3)])
    position_rows = thirds([row(k) * (1.0 / RCUT) for k in range(3)])
    atom_rows = jnp.concatenate(
        [first * own, count, atom_id, jnp.zeros((13, LANES), f32)], axis=0
    ).astype(bf16)
    begin_blocks = [2 * value for value in begins]

    def geometry(chunk, blocks):
        edge = lax.broadcasted_iota(i32, (1, FLAT), 1) + chunk * FLAT
        block = lax.shift_right_logical(edge, 3)
        tile = jnp.zeros_like(edge)
        base = jnp.zeros_like(edge)
        for k in range(1, TILES):
            past = block >= begin_blocks[k]
            tile = tile + jnp.where(past, 1, 0)
            base = base + jnp.where(past, 2 * pairs[k - 1], 0)
        atom = (tile * 8 + (edge & 7)).astype(f32)
        number = (block - base).astype(f32)
        atom_column = lax.broadcasted_iota(i32, (LANES, FLAT), 0).astype(f32)
        hot = jnp.where(atom_column == atom, 1.0, 0.0).astype(bf16)
        known = dot(atom_rows, hot, 1, 0)
        there = known[0:1] + number
        there = there + jnp.where(there >= known[2:3], 1.0, 0.0)
        valid = jnp.where(number < known[1:2], 1.0, 0.0)
        hot = jnp.where(atom_names == jnp.where(valid > 0.0, there, -1.0), 1.0, 0.0)
        difference = hot - jnp.where(
            atom_column == jnp.where(valid > 0.0, atom, -1.0), 1.0, 0.0
        )
        hot_j[chunk] = hot.astype(bf16)
        hot_d[chunk] = difference.astype(bf16)
        turned_j[chunk] = hot.T.astype(bf16)
        turned_d[chunk] = difference.T.astype(bf16)
        spread(chunk, blocks, position_parts, yy)
        rel = joined(dot(position_rows, hot_d[chunk], 1, 0), 3)
        distance, envelope = radius_of(*rel, valid)
        for k, value in enumerate(rel + [valid, envelope]):
            rows_ref[chunk, k : k + 1, :] = value
        sine, cosine = sine_cosine(distance * (math.pi / RCUT))
        sines, cosines = [sine], [cosine]
        for k in range(1, NBESSEL):
            before = (0.0, 1.0) if k == 1 else (sines[k - 2], cosines[k - 2])
            sines.append(2.0 * cosine * sines[-1] - before[0])
            cosines.append(2.0 * cosine * cosines[-1] - before[1])
        inverse = 1.0 / distance
        root = math.sqrt(2.0 / RCUT)
        for k in range(NBESSEL):
            basis = root * sines[k] * inverse
            bess[chunk, 0, k : k + 1, :] = basis
            bess[chunk, 1, k : k + 1, :] = (
                root * ((k + 1) * math.pi / RCUT) * cosines[k] - basis
            ) * inverse
        values = [bess[chunk, 0]] * 2
        for depth in range(3):
            for t in range(2):
                z = layer_in(t, depth, values[t])
                sig = sigmoid(z)
                zs[t, chunk, depth] = z
                sg[t, chunk, depth] = sig
                values[t] = z * sig
        for t in range(2):
            filters_to(t, values[t] * envelope, blocks, fdir)

    each_chunk(geometry)

    def point_shapes(block):
        values = shapes_of(*[yy[block, k] for k in range(3)])
        for k in range(3, 15):
            yy[block, k] = values[k]

    each_edge_block(point_shapes)

    def gather_from(value, dest):
        both = jnp.concatenate(list(halves_of(value)), axis=1)

        def body(chunk, blocks):
            wide = dot(turned_j[chunk], both, 1, 0)
            dest[blocks] = (wide[:, :LANES] + wide[:, LANES:]).reshape(CHUNK, 8, LANES)

        each_chunk(body)

    def scattered(chunk, blocks):
        both = jnp.concatenate(list(halves_of(fjb[blocks].reshape(FLAT, LANES))), axis=1)
        wide = dot(hot_j[chunk], both, 1, 0)
        return wide[:, :LANES] + wide[:, LANES:]

    def contract_rows(t):
        return [con_ref[t, b : b + 1, :] for b in range(9)]

    def powers_of(a):
        return [sum(a[lm] * a[lm] for lm in members(degree)) for degree in (1, 2, 3)]

    def alpha_of(c, s, p):
        return (
            c[0] + 2.0 * c[1] * s + 3.0 * c[5] * s * s + c[6] * p[0] + c[7] * p[1] + c[8] * p[2]
        )

    def beta_of(c, s):
        return [c[2 + i] + c[6 + i] * s for i in range(3)]

    zeros16 = tuple(jnp.zeros((8, LANES), f32) for _ in range(16))

    def forward_messages(t):
        def body(tile, at):
            def edges(block, a):
                a = list(a)
                there = fj[t, block]
                for degree in range(4):
                    w = fdir[t, block, degree] * there
                    if degree == 0:
                        a[0] = a[0] + w
                        continue
                    for lm in members(degree):
                        a[lm] = a[lm] + yy[block, lm - 1] * w
                return tuple(a)

            a = each_block(tile, edges, zeros16)
            for lm in range(16):
                amat[t, tile, lm] = a[lm]
            c = contract_rows(t)
            s, p = a[0], powers_of(a)
            value = s * (c[0] + s * (c[1] + s * c[5]) + c[6] * p[0] + c[7] * p[1] + c[8] * p[2])
            msg[t, at, :] = value + c[2] * p[0] + c[3] * p[1] + c[4] * p[2]

        each_tile(body)

    def backward_messages(t):
        def body(tile, at):
            a = [amat[t, tile, lm] for lm in range(16)]
            c = contract_rows(t)
            up = msgb[t, at, :]
            s, p = a[0], powers_of(a)
            beta = beta_of(c, s)
            twice = [None] + [2.0 * up * beta[i] for i in range(3)]
            ab = [up * alpha_of(c, s, p)] + [twice[DEGREES[lm]] * a[lm] for lm in range(1, 16)]
            slant = slants_of(ab)

            def edges(block, carry):
                there = fj[t, block]
                back = None
                shape = [None] + [yy[block, lm - 1] for lm in range(1, 16)]
                pull = [None] * 3
                for degree in range(4):
                    weight = fdir[t, block, degree]
                    bar = ab[0] if degree == 0 else None
                    if degree > 0:
                        w = weight * there
                        for lm in members(degree):
                            bar = add(bar, shape[lm] * ab[lm])
                        for k in range(3):
                            moved = None
                            for lm, value in slant[degree - 1][k]:
                                moved = add(moved, value if lm == 0 else shape[lm] * value)
                            pull[k] = add(pull[k], w * moved)
                        wb[t, block, degree - 1] = bar
                    fb[t, block, degree] = bar * there
                    if t > 0:
                        back = add(back, bar * weight)
                if t > 0:
                    fjb[block] = back
                for k in range(3):
                    pulls[block, k] = pull[k] if t > 0 else pulls[block, k] + pull[k]
                return carry

            each_block(tile, edges, 0)

        each_tile(body)

    def tangent_messages(t):
        def body(tile, at):
            def edges(block, da):
                da = list(da)
                there = fj[t, block]
                for degree in range(4):
                    weight = fdir[t, block, degree]
                    dw = dfdir[t, block, degree] * there
                    if t > 0:
                        dw = dw + weight * dfj[block]
                    if degree == 0:
                        da[0] = da[0] + dw
                        continue
                    w = weight * there
                    for lm in members(degree):
                        da[lm] = da[lm] + (yy[block, lm - 1] * dw + dyy[block, lm - 1] * w)
                return tuple(da)

            da = each_block(tile, edges, zeros16)
            a = [amat[t, tile, lm] for lm in range(16)]
            for lm in range(16):
                damat[t, tile, lm] = da[lm]
            c = contract_rows(t)
            s, p = a[0], powers_of(a)
            beta = beta_of(c, s)
            value = alpha_of(c, s, p) * da[0]
            for i in range(3):
                value = value + beta[i] * (2.0 * sum(a[lm] * da[lm] for lm in members(i + 1)))
            dmsg[t, at, :] = value

        each_tile(body)

    def tangent_backward(t):
        gcon[...] = jnp.zeros_like(gcon)

        def body(tile, at):
            a = [amat[t, tile, lm] for lm in range(16)]
            da = [damat[t, tile, lm] for lm in range(16)]
            c = contract_rows(t)
            up, dup = msgb[t, at, :], msgb[2, at, :]
            s, ds, p = a[0], da[0], powers_of(a)
            dp = [2.0 * sum(a[lm] * da[lm] for lm in members(degree)) for degree in (1, 2, 3)]
            alpha, beta = alpha_of(c, s, p), beta_of(c, s)
            dalpha = (
                2.0 * c[1] * ds
                + 6.0 * c[5] * s * ds
                + c[6] * dp[0]
                + c[7] * dp[1]
                + c[8] * dp[2]
            )
            pb = [None] + [2.0 * up * beta[i] for i in range(3)]
            dpb = [None] + [2.0 * (dup * beta[i] + up * c[6 + i] * ds) for i in range(3)]
            ab = [up * alpha] + [pb[DEGREES[lm]] * a[lm] for lm in range(1, 16)]
            dab = [dup * alpha + up * dalpha] + [
                pb[DEGREES[lm]] * da[lm] + dpb[DEGREES[lm]] * a[lm] for lm in range(1, 16)
            ]
            products = [(s, ds), (s * s, 2.0 * s * ds)]
            products += [(p[i], dp[i]) for i in range(3)]
            products += [(s * s * s, 3.0 * s * s * ds)]
            products += [(s * p[i], ds * p[i] + s * dp[i]) for i in range(3)]
            for b, (point, direction) in enumerate(products):
                gcon[b] += dup * point + up * direction

            def edges(block, carry):
                there = fj[t, block]
                back = None
                for degree in range(4):
                    if degree == 0:
                        was, bar = ab[0], dab[0]
                    else:
                        was, bar = wb[t, block, degree - 1], None
                        for lm in members(degree):
                            bar = add(
                                bar, yy[block, lm - 1] * dab[lm] + dyy[block, lm - 1] * ab[lm]
                            )
                    value = bar * there
                    if t > 0:
                        value = value + was * dfj[block]
                    fb[t, block, degree] = value
                    back = add(
                        back, bar * fdir[t, block, degree] + was * dfdir[t, block, degree]
                    )
                fjb[block] = back
                return carry

            each_block(tile, edges, 0)

        each_tile(body)
        for b in range(9):
            g_con[t, b : b + 1, :] -= jnp.sum(gcon[b], axis=0, keepdims=True)

    inner = slice(0, WINDOW)
    hot_element = jnp.where(
        lax.broadcasted_iota(i32, (LANES, LANES), 0).astype(f32) == species, 1.0, 0.0
    )[:, :WINDOW].astype(bf16)
    own_lane = own[:, :WINDOW]
    feats[0, inner, :] = dot(
        jnp.concatenate([hot_element, hot_element], axis=0), tab_w[...], 0, 0
    )
    sums = []
    for t in range(2):
        gather_from(feats[t], fj.at[t])
        forward_messages(t)
        feats[t + 1, inner, :] = feats[t, inner, :] + fine(msg[t], mix_ref[t], 1, 1)
        sums.append(fine(read_ref[t], feats[t + 1, inner, :], 1, 1))

    diagonal = lax.broadcasted_iota(i32, (16, 16), 0) == lax.broadcasted_iota(i32, (16, 16), 1)
    sum_bars, feat_bars, slopes_read, curves_read = [], [None, None], [], []
    for t in range(2):
        vector = jnp.sum(
            jnp.where(diagonal, jnp.broadcast_to(en_ref[t : t + 1, :], (16, 16)), 0.0),
            axis=1,
            keepdims=True,
        )
        sig = sigmoid(sums[t])
        h, rest = sums[t] * sig, 1.0 - sig
        slopes_read.append(own_lane * (sig + h * rest))
        curves_read.append(own_lane * vector * (sig * rest * (2.0 + sums[t] - 2.0 * h)))
        sum_bars.append(vector * slopes_read[t])

    def scatter_all():
        msgb[3] = jnp.zeros((WINDOW, LANES), f32)

        def body(chunk, blocks):
            msgb[3] += scattered(chunk, blocks)[:WINDOW]

        each_chunk(body)
        return msgb[3]

    feat_bar = None
    for t in (1, 0):
        feat_bar = add(feat_bar, fine(sum_bars[t], read_ref[t], 0, 0))
        feat_bars[t] = feat_bar
        msgb[t] = fine(feat_bar, mix_ref[t], 1, 0)
        backward_messages(t)
        if t > 0:
            feat_bar = feat_bar + scatter_all()

    barrow[...] = jnp.zeros_like(barrow)

    def geometry_back(chunk, blocks):
        envelope = rows_ref[chunk, 4:5, :]
        values, envelope_bar, distance_bar = [], None, None
        for t in range(2):
            high, low = filter_bars(t, blocks)
            value = filters_back(t, high, low)
            hidu[t, chunk] = value
            h, _, _ = parts_of(t, chunk, 2)
            envelope_bar = add(envelope_bar, jnp.sum(value * h, axis=0, keepdims=True))
            values.append(value * envelope)
        for depth in (2, 1, 0):
            for t in range(2):
                hidb[t, chunk, depth] = values[t]
                _, slope, _ = parts_of(t, chunk, depth)
                values[t] = layer_back(t, depth, values[t] * slope)
        distance_bar = jnp.sum((values[0] + values[1]) * bess[chunk, 1], axis=0, keepdims=True)
        rel = tuple(rows_ref[chunk, k : k + 1, :] for k in range(3))
        valid = rows_ref[chunk, 3:4, :]
        _, radius_pull = jax.vjp(lambda a, b, c: radius_of(a, b, c, valid), *rel)
        radius_bars = radius_pull((distance_bar, envelope_bar))
        ones = jnp.ones((16, LANES), bf16)
        shape_bars = []
        for k in range(3):
            high, low = halves_of(pulls[blocks, k].reshape(FLAT, LANES))
            shape_bars.append((dot(ones, high, 1, 1) + dot(ones, low, 1, 1))[0:1])
        bars = [
            jnp.where(valid > 0.0, radius_bars[k] + shape_bars[k], 0.0) * (1.0 / RCUT)
            for k in range(3)
        ]
        for k, value in enumerate(joined(dot(thirds(bars), hot_d[chunk], 1, 1), 3)):
            barrow[k : k + 1, :] += value

    each_chunk(geometry_back)

    slopes = []
    loss_row = jnp.zeros((1, LANES), f32)
    weight_row = own * labelled
    for k in range(3):
        force = -barrow[k : k + 1, :]
        diff = force - row(8 + k)
        magnitude = jnp.abs(diff)
        huber = jnp.where(
            magnitude <= HUBER_DELTA,
            0.5 * diff * diff,
            HUBER_DELTA * (magnitude - 0.5 * HUBER_DELTA),
        )
        loss_row = loss_row + weight_row * huber
        slopes.append(weight_row * jnp.clip(diff, -HUBER_DELTA, HUBER_DELTA) * (1.0 / RCUT))
    unordered = dot(thirds([-barrow[k : k + 1, :] for k in range(3)]), order_t, 1, 0)
    for k, value in enumerate(joined(unordered, 3)):
        force_ref[0, k : k + 1, :] = value
    force_ref[0, 3:4, :] = win_ref[0, 6:7, :]
    force_ref[0, 4:8, :] = jnp.zeros((4, LANES), f32)
    stat_ref[0:1, :] += loss_row
    stat_ref[1:2, :] += weight_row

    slope_parts = natural(slopes)
    slope_rows = thirds(slopes)

    def geometry_tangent(chunk, blocks):
        spread(chunk, blocks, slope_parts, dyy)
        rel = tuple(rows_ref[chunk, k : k + 1, :] for k in range(3))
        valid, envelope = rows_ref[chunk, 3:4, :], rows_ref[chunk, 4:5, :]
        drel = tuple(joined(dot(slope_rows, hot_d[chunk], 1, 0), 3))
        _, (ddistance, denvelope) = jax.jvp(
            lambda a, b, c: radius_of(a, b, c, valid), rel, drel
        )
        rows_ref[chunk, 5:6, :] = denvelope
        dbasis = bess[chunk, 1] * ddistance
        bess[chunk, 2] = dbasis
        values = [dbasis] * 2
        for depth in range(3):
            for t in range(2):
                z = layer_in(t, depth, values[t])
                dz[t, chunk, depth] = z
                h, slope, _ = parts_of(t, chunk, depth)
                values[t] = slope * z
                if depth == 2:
                    values[t] = values[t] * envelope + h * denvelope
        for t in range(2):
            filters_to(t, values[t], blocks, dfdir)
            high, low = filter_bars(t, blocks)
            g_fil[t] -= filters_grad(values[t], high, low)

    each_chunk(geometry_tangent)

    def tangent_shapes(block):
        point = tuple(yy[block, k] for k in range(3))
        direction = tuple(dyy[block, k] for k in range(3))
        _, values = jax.jvp(shapes_of, point, direction)
        for k in range(3, 15):
            dyy[block, k] = values[k]

    each_edge_block(tangent_shapes)

    dsums = []
    dfeat = None
    for t in range(2):
        if t > 0:
            dfeats[inner, :] = dfeat
            gather_from(dfeats[...], dfj)
        tangent_messages(t)
        dfeat = add(dfeat, fine(dmsg[t], mix_ref[t], 1, 1))
        dsums.append((fine(read_ref[t], dfeat, 1, 1), dfeat))

    dfeat_bar = None
    for t in (1, 0):
        dsum, dfeat_after = dsums[t]
        g_en[t] -= jnp.sum(slopes_read[t] * dsum, axis=1, keepdims=True)
        dsum_bar = curves_read[t] * dsum
        g_read[t] -= fine(dsum_bar, feats[t + 1, inner, :], 1, 0) + fine(
            sum_bars[t], dfeat_after, 1, 0
        )
        dfeat_bar = add(dfeat_bar, fine(dsum_bar, read_ref[t], 0, 0))
        g_mix[t] -= fine(dfeat_bar, msg[t], 0, 0) + fine(feat_bars[t], dmsg[t], 0, 0)
        msgb[2] = fine(dfeat_bar, mix_ref[t], 1, 0)
        tangent_backward(t)
        dfeat_bar = dfeat_bar + scatter_all()
    high, low = halves_of(dfeat_bar)
    g_emb[...] -= dot(hot_element, high, 1, 0) + dot(hot_element, low, 1, 0)

    def network_grads(chunk, blocks):
        envelope, denvelope = rows_ref[chunk, 4:5, :], rows_ref[chunk, 5:6, :]
        values = []
        for t in range(2):
            high, low = filter_bars(t, blocks)
            h, _, _ = parts_of(t, chunk, 2)
            g_fil[t] -= filters_grad(h * envelope, high, low)
            values.append(filters_back(t, high, low) * envelope + hidu[t, chunk] * denvelope)
        for depth in (2, 1, 0):
            for t in range(2):
                _, slope, curve = parts_of(t, chunk, depth)
                bar = hidb[t, chunk, depth]
                value = values[t] * slope + bar * curve * dz[t, chunk, depth]
                if depth == 0:
                    before, dbefore = bess[chunk, 0], bess[chunk, 2]
                else:
                    before, slope_before, _ = parts_of(t, chunk, depth - 1)
                    dbefore = slope_before * dz[t, chunk, depth - 1]
                grad = fine_rows(dbefore, bar * slope) + fine_rows(before, value)
                if depth == 0:
                    g_bes[t] -= grad
                else:
                    g_rad[t, depth - 1] -= grad
                    values[t] = layer_back(t, depth, value)

    each_chunk(network_grads)


def local_step(windows, table, bessel, radial, filters, contract, mixing, readout, energies):
    units = windows.shape[0]
    f32, bf16 = jnp.float32, jnp.bfloat16
    vmem = pl.BlockSpec(memory_space=pltpu.VMEM)

    def scratch(*shape):
        return pltpu.VMEM(shape, f32)

    def short(*shape):
        return pltpu.VMEM(shape, bf16)

    def out(*shape):
        return jax.ShapeDtypeStruct(shape, f32)

    edges, parts = EDGE_BLOCKS, EDGE_BLOCKS // CHUNK
    return pl.pallas_call(
        step_kernel,
        grid=(units,),
        in_specs=[pl.BlockSpec((1, 16, LANES), lambda i: (i, 0, 0))] + [vmem] * 8,
        out_specs=[pl.BlockSpec((1, 8, LANES), lambda i: (i, 0, 0))] + [vmem] * 9,
        out_shape=[
            out(units, 8, LANES),
            out(8, LANES),
            out(LANES, LANES),
            out(2, NBESSEL, 64),
            out(2, 2, 64, 64),
            out(2, 64, 4 * LANES),
            out(2, 16, LANES),
            out(2, LANES, LANES),
            out(2, 16, LANES),
            out(2, 16, 1),
        ],
        scratch_shapes=[
            pltpu.SMEM((16,), jnp.int32),
            scratch(edges, 15, 8, LANES),
            scratch(edges, 15, 8, LANES),
            scratch(3, LANES, LANES),
            scratch(LANES, LANES),
            scratch(2, edges, 8, LANES),
            scratch(edges, 8, LANES),
            scratch(2, edges, 4, 8, LANES),
            scratch(2, edges, 4, 8, LANES),
            scratch(2, edges, 4, 8, LANES),
            scratch(edges, 8, LANES),
            scratch(2, edges, 3, 8, LANES),
            scratch(2, TILES, 16, 8, LANES),
            scratch(2, TILES, 16, 8, LANES),
            scratch(2, WINDOW, LANES),
            scratch(4, WINDOW, LANES),
            scratch(2, WINDOW, LANES),
            scratch(2, parts, 3, 64, FLAT),
            scratch(2, parts, 3, 64, FLAT),
            scratch(2, parts, 3, 64, FLAT),
            scratch(2, parts, 3, 64, FLAT),
            scratch(2, parts, 64, FLAT),
            scratch(parts, 3, NBESSEL, FLAT),
            scratch(parts, 8, FLAT),
            scratch(LANES, LANES),
            short(parts, LANES, FLAT),
            short(parts, LANES, FLAT),
            short(parts, FLAT, LANES),
            short(parts, FLAT, LANES),
            scratch(8, LANES),
            scratch(9, 8, LANES),
            short(2 * LANES, LANES),
            short(2, 64, 4 * NBESSEL),
            short(2, NBESSEL, 192),
            short(2, 2, 64, 192),
            short(2, 2, 64, 192),
            short(2, 192, 4 * LANES),
            short(2, LANES, 4 * LANES),
        ],
        compiler_params=pltpu.CompilerParams(vmem_limit_bytes=60 * 1024 * 1024),
    )(windows, table, bessel, radial, filters, contract, mixing, readout, energies)


MESH = pl.DeviceIdType.MESH
GROUPS = 4
BLOCKS = 8
SHARE_LANES = LANES // GROUPS
BLOB = 176
PIECE = 280
SUB = 40
QUARTER = PIECE - BLOB


def dense(value):
    rows = value.shape[0] // GROUPS
    return jnp.concatenate([value[k * rows : (k + 1) * rows] for k in range(GROUPS)], axis=1)


def lanes_of(value, group):
    return value[:, group * SHARE_LANES : (group + 1) * SHARE_LANES]


def undense(pieces):
    return jnp.concatenate(
        [
            jnp.concatenate([lanes_of(piece, k) for piece in pieces], axis=1)
            for k in range(GROUPS)
        ],
        axis=0,
    )


def collect_kernel(
    pos_ref,
    spec_ref,
    neigh_ref,
    lab_ref,
    tgt_ref,
    emb_ref,
    fil_ref,
    con_ref,
    read_ref,
    win_ref,
    table_ref,
    full_ref,
    cont_ref,
    rd_ref,
    blob,
    padded,
    ext,
    halo,
    send_sem,
    recv_sem,
    halo_sem,
):
    block, group = lax.axis_index("atoms"), lax.axis_index("chan")
    count = pos_ref.shape[1]
    before = lax.rem(block + BLOCKS - 1, BLOCKS)
    after = lax.rem(block + 1, BLOCKS)
    twin = lax.rem(group + 1 - 2 * lax.rem(group, 2) + GROUPS, GROUPS)
    peers = [lax.rem(group + 2, GROUPS), GROUPS - 1 - group, twin]
    barrier = pltpu.get_barrier_semaphore()
    for peer in peers:
        pl.semaphore_signal(barrier, inc=1, device_id={"chan": peer}, device_id_type=MESH)
    for other in (before, after):
        pl.semaphore_signal(barrier, inc=1, device_id={"atoms": other}, device_id_type=MESH)

    padded[...] = jnp.zeros_like(padded)
    for t in range(2):
        padded[16 * t : 16 * t + 9, :] = con_ref[:, t, :]
    table_ref[...] = jnp.zeros_like(table_ref)
    table_ref[0:SHARE_LANES, 0:ELEMENTS] = emb_ref[...]
    both = [fil_ref[t].reshape(LANES, 64) for t in range(2)]
    blob[group, 0:128, :] = jnp.concatenate(both, axis=1)
    blob[group, 128:160, :] = table_ref[0:SHARE_LANES, :]
    blob[group, 160:168, :] = dense(read_ref[...].reshape(32, SHARE_LANES))
    blob[group, 168:176, :] = dense(padded[...])

    atom = lax.broadcasted_iota(jnp.int32, (1, count), 1)
    leading = neigh_ref[0:1, :] - block * count
    first = jnp.where((neigh_ref[0:1, :] >= 0) & (leading < atom), leading, atom)
    ext[...] = jnp.zeros_like(ext)
    ext[0:3, 0:count] = pos_ref[...]
    ext[3:4, 0:count] = first.astype(jnp.float32)
    ext[4:5, 0:count] = spec_ref[...].astype(jnp.float32)
    ext[5:6, 0:count] = lab_ref[...].astype(jnp.float32)
    ext[8:11, 0:count] = tgt_ref[...]

    pl.semaphore_wait(barrier, GROUPS + 1)
    copies = []
    for at, peer in enumerate(peers):
        copies.append(
            pltpu.make_async_remote_copy(
                src_ref=blob.at[group],
                dst_ref=blob.at[group],
                send_sem=send_sem.at[at],
                recv_sem=recv_sem.at[group],
                device_id={"chan": peer},
                device_id_type=MESH,
            )
        )
    halo_copy = pltpu.make_async_remote_copy(
        src_ref=ext.at[:, 0:LANES],
        dst_ref=halo,
        send_sem=halo_sem.at[0],
        recv_sem=halo_sem.at[1],
        device_id={"atoms": before},
        device_id_type=MESH,
    )
    for copy in copies:
        copy.start()
    halo_copy.start()

    halo_copy.wait()
    kind = lax.broadcasted_iota(jnp.int32, (16, LANES), 0)
    lane = lax.broadcasted_iota(jnp.int32, (16, LANES), 1)
    there = (lane < GHOST) & (block < BLOCKS - 1)
    shifted = halo[...] + jnp.where(kind == 3, float(count), 0.0)
    nothing = jnp.where(kind == 3, -1.0e6, 0.0)
    ext[:, count : count + LANES] = jnp.where(there, shifted, nothing)
    units = count // UNIT
    views, loads = [], []
    for unit in range(units):
        wide = ext[:, LANES * (unit // 2) : LANES * (unit // 2) + 2 * LANES]
        if unit % 2 == 1:
            wide = pltpu.roll(wide, 2 * LANES - UNIT, 1)
        shift = jnp.where(kind == 3, float(unit * UNIT), 0.0)
        view = jnp.where(lane < WINDOW, wide[:, :LANES] - shift, nothing)
        views.append(jnp.where(kind == 6, float(unit), view))
        neighbours, _ = neighbour_counts(view[3:4, :])
        loads.append(jnp.sum(neighbours, axis=1, keepdims=True))
    ranks = []
    for unit in range(units):
        rank = jnp.zeros((1, 1), jnp.float32)
        for other in range(units):
            if other != unit:
                before_it = loads[other] >= loads[unit] if other < unit else loads[other] > loads[unit]
                rank = rank + jnp.where(before_it, 1.0, 0.0)
        ranks.append(rank)
    for slot in range(units // GROUPS):
        wanted = (group if slot == 0 else units - 1 - group).astype(jnp.float32)
        chosen = jnp.zeros((16, LANES), jnp.float32)
        for unit in range(units):
            chosen = chosen + jnp.where(ranks[unit] == wanted, views[unit], 0.0)
        win_ref[slot] = chosen

    for at, peer in enumerate(peers):
        pltpu.make_async_remote_copy(
            src_ref=blob.at[peer],
            dst_ref=blob.at[peer],
            send_sem=send_sem.at[at],
            recv_sem=recv_sem.at[peer],
            device_id={"chan": peer},
            device_id_type=MESH,
        ).wait_recv()
    for k in range(GROUPS):
        part = pl.ds(k * SHARE_LANES, SHARE_LANES)
        for t in range(2):
            full_ref[t, :, part, :] = blob[k, 0:128, 64 * t : 64 * t + 64].reshape(
                4, SHARE_LANES, 64
            )
        table_ref[part, :] = blob[k, 128:160, :]
    rd_ref[...] = undense([blob[k, 160:168, :] for k in range(GROUPS)]).reshape(2, 16, LANES)
    cont_ref[...] = undense([blob[k, 168:176, :] for k in range(GROUPS)]).reshape(2, 16, LANES)
    for copy in copies:
        copy.wait_send()


def collect(positions, species, neighbours, labelled, targets, embedding, filters, contract, readout):
    f32 = jnp.float32
    count = positions.shape[1]
    vmem = pl.BlockSpec(memory_space=pltpu.VMEM)
    return pl.pallas_call(
        collect_kernel,
        in_specs=[vmem] * 9,
        out_specs=[vmem] * 5,
        out_shape=[
            jax.ShapeDtypeStruct((count // GROUPS // UNIT, 16, LANES), f32),
            jax.ShapeDtypeStruct((LANES, LANES), f32),
            jax.ShapeDtypeStruct((2, 4, LANES, 64), f32),
            jax.ShapeDtypeStruct((2, 16, LANES), f32),
            jax.ShapeDtypeStruct((2, 16, LANES), f32),
        ],
        scratch_shapes=[
            pltpu.VMEM((GROUPS, BLOB, LANES), f32),
            pltpu.VMEM((32, SHARE_LANES), f32),
            pltpu.VMEM((16, count + LANES), f32),
            pltpu.VMEM((16, LANES), f32),
            pltpu.SemaphoreType.DMA((GROUPS - 1,)),
            pltpu.SemaphoreType.DMA((GROUPS,)),
            pltpu.SemaphoreType.DMA((2,)),
        ],
        compiler_params=pltpu.CompilerParams(collective_id=0, has_side_effects=True),
    )(
        positions,
        species[None],
        neighbours,
        labelled[None],
        targets,
        embedding,
        filters,
        contract,
        readout,
    )


def reduce_kernel(
    force_ref,
    stat_ref,
    g_emb,
    g_bes,
    g_rad,
    g_fil,
    g_con,
    g_mix,
    g_read,
    g_en,
    forces_ref,
    own_ref,
    rest_ref,
    pieces,
    core_in,
    line_out,
    line_in,
    summed,
    sub_in,
    sub_out,
    total,
    quarters,
    windows,
    tail,
    tail_in,
    sems,
    table_t,
    filters_t,
    sub_send,
    sub_recv,
    total_send,
    total_recv,
):
    f32 = jnp.float32
    block, group = lax.axis_index("atoms"), lax.axis_index("chan")
    line, core = group // 2, lax.rem(group, 2)
    core_peer = {"chan": line * 2 + (1 - core)}
    line_peer = {"chan": (1 - line) * 2 + core}
    others = [lax.rem(block + offset, BLOCKS) for offset in range(1, BLOCKS)]
    barrier = pltpu.get_barrier_semaphore()
    for peer in [core_peer, line_peer] + [{"atoms": other} for other in others]:
        pl.semaphore_signal(barrier, inc=1, device_id=peer, device_id_type=MESH)

    def copy(source, dest, at, peer):
        return pltpu.make_async_remote_copy(
            src_ref=source,
            dst_ref=dest,
            send_sem=sems.at[2 * at],
            recv_sem=sems.at[2 * at + 1],
            device_id=peer,
            device_id_type=MESH,
        )

    rows = lax.broadcasted_iota(jnp.int32, (16, LANES), 0)
    lanes = lax.broadcasted_iota(jnp.int32, (16, LANES), 1)
    vector = jnp.zeros((1, LANES), f32)
    for t in range(2):
        spread = jnp.broadcast_to(g_en[t], (16, LANES))
        vector = vector + jnp.sum(
            jnp.where(lanes == rows + 16 * t, spread, 0.0), axis=0, keepdims=True
        )
    table_t[...] = g_emb[...].T
    for t in range(2):
        filters_t[t] = g_fil[t].T.reshape(4, LANES, 64)
    inner = g_rad[...].reshape(256, 64)
    inner = jnp.concatenate([inner[:128], inner[128:]], axis=1)
    bessel = jnp.concatenate([g_bes[0], g_bes[1]], axis=1)
    for k in range(GROUPS):
        where = (k % 2, k // 2)
        part = pl.ds(k * SHARE_LANES, SHARE_LANES)
        both = [filters_t[t, :, part, :].reshape(LANES, 64) for t in range(2)]
        pieces[(*where, pl.ds(0, 128), slice(None))] = jnp.concatenate(both, axis=1)
        pieces[(*where, pl.ds(128, 32), slice(None))] = table_t[part, :]
        pieces[(*where, pl.ds(160, 8), slice(None))] = dense(
            lanes_of(g_read[...].reshape(32, LANES), k)
        )
        pieces[(*where, pl.ds(168, 8), slice(None))] = dense(
            lanes_of(g_con[...].reshape(32, LANES), k)
        )
        pieces[(*where, pl.ds(176, 64), slice(None))] = g_mix[k // 2, 64 * (k % 2) : 64 * (k % 2) + 64, :]
        pieces[(*where, pl.ds(240, 32), slice(None))] = inner[32 * k : 32 * k + 32]
        pieces[(*where, pl.ds(272, 8), slice(None))] = jnp.concatenate(
            [bessel[2 * k : 2 * k + 2], vector, stat_ref[0:2, :], jnp.zeros((3, LANES), f32)],
            axis=0,
        )
    windows[line, core] = force_ref[...]
    pl.semaphore_wait(barrier, BLOCKS + 1)

    core_copy = copy(pieces.at[1 - core], core_in, 0, core_peer)
    core_copy.start()
    core_force = copy(windows.at[line, core], windows.at[line, core], 1, core_peer)
    core_force.start()
    core_copy.wait()
    line_out[...] = pieces[core, 1 - line] + core_in[1 - line]
    line_copy = copy(line_out, line_in, 2, line_peer)
    line_copy.start()
    core_force.wait()
    line_force = copy(windows.at[line], windows.at[line], 3, line_peer)
    line_force.start()
    partial = pieces[core, line] + core_in[line]
    line_force.wait()

    lane8 = lax.broadcasted_iota(jnp.int32, (8, LANES), 1)
    canvas = [jnp.zeros((8, LANES), f32)] * 5
    held = [windows[k // 4, (k // 2) % 2, k % 2] for k in range(8)]
    for unit in range(8):
        value = jnp.zeros((8, LANES), f32)
        for item in held:
            value = value + jnp.where(item[3:4, :] == float(unit), item, 0.0)
        if unit % 2 == 0:
            canvas[unit // 2] = canvas[unit // 2] + value
        else:
            value = pltpu.roll(value, 64, 1)
            canvas[unit // 2] = canvas[unit // 2] + jnp.where(lane8 >= 64, value, 0.0)
            canvas[unit // 2 + 1] = canvas[unit // 2 + 1] + jnp.where(lane8 < 64, value, 0.0)
    tail[...] = canvas[4]
    tail_copy = copy(tail, tail_in, 4, {"atoms": others[0]})
    tail_copy.start()

    line_copy.wait()
    summed[7] = jnp.zeros((SUB, LANES), f32)
    partial = partial + line_in[...]
    for k in range(7):
        size = min(SUB, PIECE - k * SUB)
        summed[k, 0:size, :] = partial[k * SUB : k * SUB + size]
        if size < SUB:
            summed[k, size:SUB, :] = jnp.zeros((SUB - size, LANES), f32)

    def sub_copy(other, at):
        return pltpu.make_async_remote_copy(
            src_ref=summed.at[other],
            dst_ref=sub_in.at[block],
            send_sem=sub_send.at[at],
            recv_sem=sub_recv.at[block],
            device_id={"atoms": other},
            device_id_type=MESH,
        )

    def total_copy(other, at):
        return pltpu.make_async_remote_copy(
            src_ref=sub_out,
            dst_ref=total.at[block],
            send_sem=total_send.at[at],
            recv_sem=total_recv.at[block],
            device_id={"atoms": other},
            device_id_type=MESH,
        )

    def arrival(dest, recv, other):
        return pltpu.make_async_remote_copy(
            src_ref=sub_out,
            dst_ref=dest.at[other],
            send_sem=sub_send.at[0],
            recv_sem=recv.at[other],
            device_id={"atoms": other},
            device_id_type=MESH,
        )

    subs = [sub_copy(other, at) for at, other in enumerate(others)]
    for item in subs:
        item.start()
    value = summed[block]
    for other in others:
        arrival(sub_in, sub_recv, other).wait_recv()
        value = value + sub_in[other]
    sub_out[...] = value
    totals = [total_copy(other, at) for at, other in enumerate(others)]
    for item in totals:
        item.start()
    total[block] = value
    tail_copy.wait()
    forces = jnp.concatenate(canvas[:4], axis=1)
    edge = jnp.where((lane8 < GHOST) & (block > 0), tail_in[...], 0.0)
    forces_ref[...] = forces
    forces_ref[:, 0:LANES] = canvas[0] + edge
    for other in others:
        arrival(total, total_recv, other).wait_recv()
    for item in subs + totals:
        item.wait_send()

    everything = total[...].reshape(BLOCKS * SUB, LANES)
    own_ref[...] = everything[:BLOB]
    flat = everything[:274]
    energy_row = everything[274:275]
    squares = jnp.sum(flat * flat, axis=0, keepdims=True)
    squares = squares + (1.0 / GROUPS) * energy_row * energy_row
    squares = jnp.sum(squares, axis=1, keepdims=True)
    quarters[line, core] = everything[BLOB:PIECE]
    quarters[line, core, 101:102, :] = jnp.broadcast_to(squares, (1, LANES))
    line_quarter = copy(quarters.at[line, core], quarters.at[line, core], 5, line_peer)
    line_quarter.start()
    core_quarter = copy(quarters.at[line, core], quarters.at[line, core], 6, core_peer)
    core_quarter.start()
    line_quarter.wait()
    cross_quarter = copy(quarters.at[1 - line, core], quarters.at[1 - line, core], 7, core_peer)
    cross_quarter.start()
    core_quarter.wait()
    cross_quarter.wait()
    rest_ref[...] = quarters[...].reshape(GROUPS, QUARTER, LANES)


def reduce_all(force, stat, grads):
    f32 = jnp.float32
    vmem = pl.BlockSpec(memory_space=pltpu.VMEM)
    dma = pltpu.SemaphoreType.DMA
    return pl.pallas_call(
        reduce_kernel,
        in_specs=[vmem] * 10,
        out_specs=[vmem] * 3,
        out_shape=[
            jax.ShapeDtypeStruct((8, 4 * LANES), f32),
            jax.ShapeDtypeStruct((BLOB, LANES), f32),
            jax.ShapeDtypeStruct((GROUPS, QUARTER, LANES), f32),
        ],
        scratch_shapes=[
            pltpu.VMEM((2, 2, PIECE, LANES), f32),
            pltpu.VMEM((2, PIECE, LANES), f32),
            pltpu.VMEM((PIECE, LANES), f32),
            pltpu.VMEM((PIECE, LANES), f32),
            pltpu.VMEM((BLOCKS, SUB, LANES), f32),
            pltpu.VMEM((BLOCKS, SUB, LANES), f32),
            pltpu.VMEM((SUB, LANES), f32),
            pltpu.VMEM((BLOCKS, SUB, LANES), f32),
            pltpu.VMEM((2, 2, QUARTER, LANES), f32),
            pltpu.VMEM((2, 2, 2, 8, LANES), f32),
            pltpu.VMEM((8, LANES), f32),
            pltpu.VMEM((8, LANES), f32),
            dma((16,)),
            pltpu.VMEM((LANES, LANES), f32),
            pltpu.VMEM((2, 4, LANES, 64), f32),
            dma((BLOCKS - 1,)),
            dma((BLOCKS,)),
            dma((BLOCKS - 1,)),
            dma((BLOCKS,)),
        ],
        compiler_params=pltpu.CompilerParams(collective_id=1, has_side_effects=True),
    )(force, stat, *grads)


def adam_kernel(*refs):
    forces_in, own_ref, rest_ref = refs[:3]
    weights, moments = refs[3:11], refs[11:27]
    parts_ref, forces_ref, norm_ref = refs[27:30]
    results = refs[30:54]
    scratch = refs[54]
    rest = [rest_ref[k] for k in range(GROUPS)]
    stats = rest[0]
    loss = jnp.sum(stats[99:100], axis=1, keepdims=True)
    count = jnp.sum(stats[100:101], axis=1, keepdims=True)
    inverse = 1.0 / count
    squares = sum(rest[k][101:102, 0:1] for k in range(GROUPS))
    norm = jnp.sqrt(squares) * inverse
    factor = inverse * jnp.minimum(1.0, CLIP_NORM / (norm + 1e-06))
    norm_ref[...] = norm
    two = lax.broadcasted_iota(jnp.int32, (1, 2), 1)
    parts_ref[...] = jnp.where(two == 0, loss, count)
    forces_ref[...] = forces_in[0:3, :]

    def narrow(value):
        return jnp.concatenate([lanes_of(value, k) for k in range(GROUPS)], axis=0)

    fil = [own_ref[0:128, 64 * t : 64 * t + 64].reshape(4, SHARE_LANES, 64) for t in range(2)]
    emb = own_ref[128:160, 0:ELEMENTS]
    read = narrow(own_ref[160:168, :]).reshape(2, 16, SHARE_LANES)
    scratch[...] = narrow(own_ref[168:176, :])
    con = [scratch[0:9, :], scratch[16:25, :]]
    mix = jnp.concatenate([rest[k][0:64] for k in range(GROUPS)], axis=0).reshape(2, LANES, LANES)
    inner = jnp.concatenate([rest[k][64:96] for k in range(GROUPS)], axis=0)
    inner = jnp.concatenate([inner[:, :64], inner[:, 64:]], axis=0).reshape(2, 2, 64, 64)
    bes = jnp.concatenate([rest[k][96:98] for k in range(GROUPS)], axis=0)
    bes = [bes[:, :64], bes[:, 64:]]
    vector = rest[0][98:99]
    vector = jnp.concatenate([vector[:, 0:16], vector[:, 16:32]], axis=0)

    def update(which, gradient, at):
        first, square = moments[2 * which], moments[2 * which + 1]
        weight = weights[which][at]
        clipped = gradient * factor
        moment = BETA_ONE * first[at] + (1.0 - BETA_ONE) * clipped
        second = BETA_TWO * square[at] + (1.0 - BETA_TWO) * clipped * clipped
        corrected_first = moment * (1.0 / (1.0 - BETA_ONE**ADAM_STEP))
        corrected_second = second * (1.0 / (1.0 - BETA_TWO**ADAM_STEP))
        updated = weight - RATE * (
            corrected_first / (jnp.sqrt(corrected_second) + EPSILON) + DECAY * weight
        )
        results[3 * which][at] = updated
        results[3 * which + 1][at] = moment
        results[3 * which + 2][at] = second

    everything = Ellipsis
    update(0, emb, everything)
    for t in range(2):
        update(1, bes[t], t)
        update(3, fil[t], t)
        update(4, con[t], (slice(None), t))
    update(2, inner, everything)
    update(5, mix, everything)
    update(6, read, everything)
    update(7, vector, everything)


def adam(forces, own, rest, weights, moments):
    f32 = jnp.float32
    vmem = pl.BlockSpec(memory_space=pltpu.VMEM)
    shapes = [(1, 2), (3, forces.shape[1]), (1, 1)]
    shapes += [weight.shape for weight in weights for _ in range(3)]
    return pl.pallas_call(
        adam_kernel,
        in_specs=[vmem] * 27,
        out_specs=[vmem] * 27,
        out_shape=[jax.ShapeDtypeStruct(shape, f32) for shape in shapes],
        scratch_shapes=[pltpu.VMEM((32, SHARE_LANES), f32)],
    )(forces, own, rest, *weights, *moments)


def adamw(weight, gradient, first, second, scale):
    clipped = gradient * scale
    moment = BETA_ONE * first + (1.0 - BETA_ONE) * clipped
    second_new = BETA_TWO * second + (1.0 - BETA_TWO) * clipped * clipped
    corrected_first = moment / (1.0 - BETA_ONE**ADAM_STEP)
    corrected_second = second_new / (1.0 - BETA_TWO**ADAM_STEP)
    updated = weight - RATE * (
        corrected_first / (jnp.sqrt(corrected_second) + EPSILON) + DECAY * weight
    )
    return (updated, moment, second_new)


def per_device(
    positions,
    species,
    neighbours,
    labelled,
    target_forces,
    embedding,
    bessel,
    radial,
    filters,
    contract,
    mixing,
    readout,
    energies,
    first_embedding,
    square_embedding,
    first_bessel,
    square_bessel,
    first_radial,
    square_radial,
    first_filters,
    square_filters,
    first_contract,
    square_contract,
    first_mixing,
    square_mixing,
    first_readout,
    square_readout,
    first_energies,
    square_energies,
):
    if (lax.axis_size("atoms"), lax.axis_size("chan")) == (BLOCKS, GROUPS):
        turns = [(1, 0), None, None, (0, 1, 3, 2), (1, 0, 2), None, None, None]

        def turned(value, order):
            return value if order is None else value.transpose(order)

        weights = (embedding, bessel, radial, filters, contract, mixing, readout, energies)
        weights = [turned(value, order) for value, order in zip(weights, turns)]
        moments = (
            first_embedding,
            square_embedding,
            first_bessel,
            square_bessel,
            first_radial,
            square_radial,
            first_filters,
            square_filters,
            first_contract,
            square_contract,
            first_mixing,
            square_mixing,
            first_readout,
            square_readout,
            first_energies,
            square_energies,
        )
        moments = [turned(value, turns[k // 2]) for k, value in enumerate(moments)]
        windows, table, full, cont, read = collect(
            positions,
            species,
            neighbours,
            labelled,
            target_forces,
            weights[0],
            weights[3],
            weights[4],
            readout,
        )
        force, stat, *grads = local_step(
            windows, table, bessel, radial, full, cont, mixing, read, energies
        )
        forces, own, rest = reduce_all(force, stat, grads)
        parts, forces, norm, *results = adam(forces, own, rest, weights, moments)
        results = [turned(value, turns[k // 3]) for k, value in enumerate(results)]
        return tuple([parts.reshape(2), forces, norm.reshape(())] + results)
    f32 = jnp.float32
    atom_count = positions.shape[1]
    local_chan = embedding.shape[1]
    blocks, groups = lax.axis_size("atoms"), lax.axis_size("chan")
    block, group = lax.axis_index("atoms"), lax.axis_index("chan")
    atom_base = block * atom_count
    share = atom_count // groups
    units = share // UNIT

    atom_index = atom_base + jnp.arange(atom_count, dtype=jnp.int32)
    leading = neighbours[0]
    first_atom = jnp.where((leading >= 0) & (leading < atom_index), leading, atom_index)
    packed = jnp.concatenate(
        [
            positions,
            (first_atom - atom_base).astype(f32)[None],
            species.astype(f32)[None],
            labelled.astype(f32)[None],
            jnp.zeros((2, atom_count), f32),
            target_forces,
            jnp.zeros((5, atom_count), f32),
        ],
        axis=0,
    )
    down = [(i + 1, i) for i in range(blocks - 1)]
    halo = lax.ppermute(packed[:, :GHOST], "atoms", down)
    halo_row = jnp.arange(16)[:, None] == 3
    halo = jnp.where(halo_row, jnp.where(block == blocks - 1, -1.0e6, halo + atom_count), halo)
    missing = jnp.where(jnp.arange(16)[:, None] == 3, -1.0e6, 0.0) * jnp.ones((1, LANES), f32)
    extended = jnp.concatenate([packed, halo, missing], axis=1)
    windows = []
    for unit in range(units):
        start = group * share + unit * UNIT
        window = lax.dynamic_slice(extended, (0, start), (16, WINDOW))
        shift = jnp.where(jnp.arange(16)[:, None] == 3, start.astype(f32), 0.0)
        window = window - shift
        windows.append(jnp.concatenate([window, missing[:, : LANES - WINDOW]], axis=1))
    windows = jnp.stack(windows)

    def whole(value):
        return lax.all_gather(value, "chan", axis=value.ndim - 1, tiled=True)

    table = jnp.concatenate(
        [whole(embedding), jnp.zeros((LANES - ELEMENTS, LANES), f32)], axis=0
    ).T
    force, stat, *grads = local_step(
        windows,
        table,
        bessel,
        radial,
        whole(filters).swapaxes(2, 3),
        jnp.pad(whole(contract), ((0, 0), (0, 7), (0, 0))),
        mixing,
        whole(readout),
        energies,
    )
    grad_embed, grad_bessel, grad_radial, grad_filters, grad_contract, grad_mixing = grads[:6]
    grad_readout, grad_vectors = grads[6:]
    grad_embed = grad_embed[:ELEMENTS]
    grad_filters = grad_filters.reshape(2, 64, 4, LANES).transpose(0, 2, 1, 3)
    grad_contract = grad_contract[:, :9]
    grad_vectors = grad_vectors[:, :, 0]

    canvas = jnp.zeros((3, atom_count + LANES), f32)
    for unit in range(units):
        start = group * share + unit * UNIT
        old = lax.dynamic_slice(canvas, (0, start), (3, WINDOW))
        canvas = lax.dynamic_update_slice(canvas, old + force[unit, :3, :WINDOW], (0, start))
    canvas = lax.psum(canvas, "chan")
    up = [(i, i + 1) for i in range(blocks - 1)]
    arrived = lax.ppermute(canvas[:, atom_count : atom_count + GHOST], "atoms", up)
    forces = canvas[:, :atom_count].at[:, :GHOST].add(arrived)

    def split(value):
        return lax.psum_scatter(value, "chan", scatter_dimension=value.ndim - 1, tiled=True)

    grad_embed, grad_filters, grad_contract, grad_readout = lax.psum(
        (split(grad_embed), split(grad_filters), split(grad_contract), split(grad_readout)),
        "atoms",
    )
    grad_bessel, grad_radial, grad_mixing, grad_vectors, loss_sum, label_total = lax.psum(
        (grad_bessel, grad_radial, grad_mixing, grad_vectors, jnp.sum(stat[0]), jnp.sum(stat[1])),
        ("atoms", "chan"),
    )
    gradients = [
        gradient / label_total
        for gradient in (
            grad_embed,
            grad_bessel,
            grad_radial,
            grad_filters,
            grad_contract,
            grad_mixing,
            grad_readout,
            grad_vectors,
        )
    ]
    squares_of = [jnp.sum(gradient * gradient) for gradient in gradients]
    split_squares = squares_of[0] + squares_of[3] + squares_of[4] + squares_of[6]
    whole_squares = squares_of[1] + squares_of[2] + squares_of[5] + squares_of[7]
    grad_norm = jnp.sqrt(lax.psum(split_squares, "chan") + whole_squares)
    scale = jnp.minimum(1.0, CLIP_NORM / (grad_norm + 1e-06))
    weights = (embedding, bessel, radial, filters, contract, mixing, readout, energies)
    firsts = (
        first_embedding,
        first_bessel,
        first_radial,
        first_filters,
        first_contract,
        first_mixing,
        first_readout,
        first_energies,
    )
    squares = (
        square_embedding,
        square_bessel,
        square_radial,
        square_filters,
        square_contract,
        square_mixing,
        square_readout,
        square_energies,
    )
    results = []
    for weight, gradient, first, second in zip(weights, gradients, firsts, squares):
        results.extend(adamw(weight, gradient, first, second, scale))
    return tuple([jnp.stack([loss_sum, label_total]), forces, grad_norm] + results)


def solution(mesh):
    whole = P()
    columns = P(None, "atoms")
    by_weight = [
        P(None, "chan"),
        whole,
        whole,
        P(None, None, None, "chan"),
        P(None, None, "chan"),
        whole,
        P(None, None, "chan"),
        whole,
    ]
    in_specs = [columns, P("atoms"), columns, P("atoms"), columns] + by_weight
    in_specs += [spec for spec in by_weight for _ in range(2)]
    out_specs = [whole, columns, whole] + [spec for spec in by_weight for _ in range(3)]
    return jax.shard_map(
        per_device,
        mesh=mesh,
        in_specs=tuple(in_specs),
        out_specs=tuple(out_specs),
        check_vma=False,
    )
```
